32 devices in a mesh: dp: 16 (over z, y, core), mp: 2 (over x).
Axes of the slice: x: 2, y: 2, z: 4, core: 2. Of those that a mesh axis runs over, the one named last changes fastest.
Arguments:
- inputs: bfloat16 [16, 1024, 512], P('dp', 'mp'), may hold values from -6 to 6
- lengths: int32 [16], P('dp'), may hold values from 768 to 1024, as said below
- gain_glu: float32 [512], replicated, may hold values from 0.5 to 1.5
- w_value: bfloat16 [512, 512], P(None, 'mp'), may hold values from -0.25 to 0.25
- w_gate: bfloat16 [512, 512], P(None, 'mp'), may hold values from -0.25 to 0.25
- gain_branch: float32 [512], replicated, may hold values from 0.5 to 1.5
- w_left: bfloat16 [512, 2048], P(None, 'mp'), may hold values from -0.25 to 0.25
- w_right: bfloat16 [3, 512, 256], P(None, None, 'mp'), may hold values from -0.15625 to 0.15625
- gain_mid: bfloat16 [2048], P('mp'), may hold values from 0.5 to 1.5
- w_depth: bfloat16 [9, 2048], P(None, 'mp'), may hold values from -2 to 2
- w_point: bfloat16 [2048, 256], P('mp'), may hold values from -0.125 to 0.125
- gain_attn: float32 [512], replicated, may hold values from 0.5 to 1.5
- w_qkv: bfloat16 [3, 512, 512], P(None, None, 'mp'), may hold values from -0.25 to 0.25
- w_out: bfloat16 [512, 512], P('mp'), may hold values from -4 to 4
- gain_ffn: float32 [512], replicated, may hold values from 0.5 to 1.5
- w_in: bfloat16 [512, 2048], P(None, 'mp'), may hold values from -0.25 to 0.25
- w_back: bfloat16 [2048, 512], P('mp'), may hold values from -0.125 to 0.125
- cotangent: bfloat16 [16, 1024, 512], P('dp', 'mp'), may hold values from -6 to 6
Outputs:
- outputs: bfloat16 [16, 1024, 512], P('dp', 'mp')
- grad_inputs: bfloat16 [16, 1024, 512], P('dp', 'mp')
- grad_gain_glu: float32 [512], replicated
- grad_w_value: float32 [512, 512], P(None, 'mp')
- grad_w_gate: float32 [512, 512], P(None, 'mp')
- grad_gain_branch: float32 [512], replicated
- grad_w_left: float32 [512, 2048], P(None, 'mp')
- grad_w_right: float32 [3, 512, 256], P(None, None, 'mp')
- grad_gain_mid: float32 [2048], P('mp')
- grad_w_depth: float32 [9, 2048], P(None, 'mp')
- grad_w_point: float32 [2048, 256], P('mp')
- grad_gain_attn: float32 [512], replicated
- grad_w_qkv: float32 [3, 512, 512], P(None, None, 'mp')
- grad_w_out: float32 [512, 512], P('mp')
- grad_gain_ffn: float32 [512], replicated
- grad_w_in: float32 [512, 2048], P(None, 'mp')
- grad_w_back: float32 [2048, 512], P('mp')
The draws below stay inside these ranges and needn't reach their ends.
Inputs may be any that keep to these rules, and one draw needn't show every extreme that they name: `lengths`: in each block of 1 sequence of one index of dp, one sequence, drawn from the seed, is 768 or more long; where a block holds two or more sequences, the others are 256 or more long. The least and the most are each taken by some sequence.
All inputs are finite; a program needn't handle non-finite values.
Results may differ from the reference program's by a relative error of at most 0.029.
Values may be sent and summed in bfloat16 or wider, within the bound.
No kernel may reach another device: no remote copies, remote signals or barrier semaphores. Data moves between devices by JAX's collectives and lax.ppermute only.
A program may use at most 192 MiB of HBM per device.

```python
import math
import jax
import jax.numpy as jnp
from jax import lax

D = 512
FF = 2048
HEADS = 8
HEAD_DIM = 64
RIGHT_W = 256
SEP_W = 256
CONV_TAPS = 3
SEP_TAPS = 9
LEN = 1024
SEQ_GRP = 1
SEQS = 16
N_MP = 2


def draw_lengths(key, part):
    key = jax.random.fold_in(key, 11)
    keys = jax.random.split(key, 5)
    groups = SEQS // SEQ_GRP
    long_low = LEN - LEN // (2 * N_MP)
    base_len = jax.random.randint(keys[0], (SEQS,), LEN // 4, LEN + 1)
    long_len = jax.random.randint(keys[1], (SEQS,), long_low, LEN + 1)
    chosen = jax.random.randint(keys[2], (groups,), 0, SEQ_GRP)
    slot_index = jnp.arange(SEQS) % SEQ_GRP
    group_index = jnp.arange(SEQS) // SEQ_GRP
    is_long = slot_index == chosen[group_index]
    result = jnp.where(is_long, long_len, base_len)
    low_group = jax.random.randint(keys[3], (), 0, groups)
    if SEQ_GRP > 1:
        high_group = jax.random.randint(keys[4], (), 0, groups)
        low_slot = low_group * SEQ_GRP + (chosen[low_group] + 1) % SEQ_GRP
        result = result.at[low_slot].set(LEN // 4)
        result = result.at[high_group * SEQ_GRP + chosen[high_group]].set(LEN)
    else:
        high_group = (low_group + 1 + jax.random.randint(keys[4], (), 0, groups - 1)) % groups
        result = result.at[low_group].set(long_low)
        result = result.at[high_group].set(LEN)
    return result.astype(jnp.int32)


def block_scale(rng, extent, cuts, least, top_value):
    gain = 1.0
    for dim, shards_of in cuts:
        draws = jax.random.uniform(jax.random.fold_in(jax.random.fold_in(rng, 6), dim), (shards_of,), jnp.float32, least / len(cuts), top_value / len(cuts))
        gain = gain * jnp.repeat(jnp.exp(draws), extent[dim] // shards_of).reshape((-1,) + (1,) * (len(extent) - 1 - dim))
    return gain


def scatter_about(own_key, extent, spread, bound, cuts=(), kind=jnp.bfloat16):
    factor_of = block_scale(own_key, extent, cuts, -0.22, 0.18) if cuts else 1.0
    array = jax.random.normal(own_key, extent, jnp.float32) * spread * factor_of
    return jnp.minimum(jnp.maximum(array, -bound), bound).astype(kind)


def setup_inputs(seed: int = 0) -> dict:
    seeds = jax.random.split(jax.random.key(seed), 19)
    inputs = scatter_about(seeds[0], (SEQS, LEN, D), 1.0, 6.0, ((0, 16), (1, 2)))
    lengths = draw_lengths(jax.random.fold_in(seeds[18], 71), 0)
    gain_glu = jnp.clip(1.0 + 0.1 * jax.random.normal(seeds[2], (D,), jnp.float32), 0.5, 1.5)
    w_value = scatter_about(seeds[3], (D, D), D ** -0.5, 0.25, ((1, 2),))
    w_gate = scatter_about(seeds[4], (D, D), D ** -0.5, 0.25, ((1, 2),))
    gain_branch = jnp.clip(1.0 + 0.1 * jax.random.normal(seeds[5], (D,), jnp.float32), 0.5, 1.5)
    w_left = scatter_about(seeds[6], (D, FF), D ** -0.5, 0.25, ((1, 2),))
    w_right = scatter_about(seeds[7], (CONV_TAPS, D, RIGHT_W), (CONV_TAPS * D) ** -0.5, 0.15625, ((2, 2),))
    gain_mid = jnp.clip(1.0 + 0.1 * jax.random.normal(seeds[8], (FF,), jnp.float32), 0.5, 1.5).astype(jnp.bfloat16)
    w_depth = scatter_about(seeds[9], (SEP_TAPS, FF), SEP_TAPS ** -0.5, 2.0, ((1, 2),))
    w_point = scatter_about(seeds[10], (FF, SEP_W), FF ** -0.5, 0.125, ((0, 2),))
    gain_attn = jnp.clip(1.0 + 0.1 * jax.random.normal(seeds[11], (D,), jnp.float32), 0.5, 1.5)
    w_qkv = scatter_about(seeds[12], (3, D, D), D ** -0.5, 0.25, ((2, 2),))
    w_out = scatter_about(seeds[13], (D, D), (max(1, D * 4 // LEN)) ** -0.5, 4.0, ((0, 2),))
    gain_ffn = jnp.clip(1.0 + 0.1 * jax.random.normal(seeds[14], (D,), jnp.float32), 0.5, 1.5)
    w_in = scatter_about(seeds[15], (D, FF), D ** -0.5, 0.25, ((1, 2),))
    w_back = scatter_about(seeds[16], (FF, D), FF ** -0.5, 0.125, ((0, 2),))
    cotangent = scatter_about(seeds[17], (SEQS, LEN, D), 1.0, 6.0, ((0, 16), (1, 2)))
    return {"inputs": inputs, "lengths": lengths, "gain_glu": gain_glu, "w_value": w_value, "w_gate": w_gate, "gain_branch": gain_branch, "w_left": w_left, "w_right": w_right, "gain_mid": gain_mid, "w_depth": w_depth, "w_point": w_point, "gain_attn": gain_attn, "w_qkv": w_qkv, "w_out": w_out, "gain_ffn": gain_ffn, "w_in": w_in, "w_back": w_back, "cotangent": cotangent}


highest = lax.Precision.HIGHEST
epsilon = 1e-06
negative_big = -1e+30

@jax.custom_vjp
def low(v):
    return lax.optimization_barrier(v.astype(jnp.bfloat16)).astype(jnp.float32)

@jax.custom_vjp
def low_back(v):
    return v

def low_keep(v):
    return (low(v), None)

def low_pass(kept, grad):
    return (grad,)

def back_keep(v):
    return (v, None)

def back_low(kept, grad):
    return (low(grad),)
low.defvjp(low_keep, low_pass)
low_back.defvjp(back_keep, back_low)

def project(values, weight):
    return jnp.einsum('...d,df->...f', values, weight, precision=highest)

def norm(values, gain_vec):
    centre = values - lax.optimization_barrier(jnp.mean(values, axis=-1, keepdims=True))
    return centre * lax.rsqrt(lax.optimization_barrier(jnp.mean(centre * centre, axis=-1, keepdims=True)) + epsilon) * gain_vec

def shifted(values, offset):
    margin = abs(offset)
    if margin == 0:
        return values
    padded = jnp.pad(values, ((0, 0), (margin, margin), (0, 0)))
    return lax.slice_in_dim(padded, margin + offset, margin + offset + values.shape[1], axis=1)

def place_right(right_vals, stride):
    filler = jnp.zeros(right_vals.shape + (stride - 1,), right_vals.dtype)
    joined = jnp.concatenate([right_vals[..., None], filler], axis=-1)
    return joined.reshape(right_vals.shape[:-1] + (right_vals.shape[-1] * stride,))

def layer(weights, values, valid_mask):
    gain_glu, w_value, w_gate, gain_branch, w_left, w_right, gain_mid, w_depth, w_point, gain_attn, w_qkv, w_out, gain_ffn, w_in, w_back = weights
    pad_mask = valid_mask.astype(values.dtype)[..., None]
    glu_in = low(norm(values, gain_glu))
    value_pre = low_back(project(glu_in, w_value))
    gate_pre = low_back(project(glu_in, w_gate))
    glu_out = low_back(low(value_pre * jax.nn.sigmoid(gate_pre)))
    resid_one = values + glu_out
    branch_in = low(pad_mask * norm(resid_one, gain_branch))
    left_act = jax.nn.silu(low_back(project(branch_in, w_left)))
    conv_taps = w_right.shape[0]
    conv_sum = project(shifted(branch_in, -(conv_taps // 2)), w_right[0])
    for tap_index in range(1, conv_taps):
        conv_sum = conv_sum + project(shifted(branch_in, tap_index - conv_taps // 2), w_right[tap_index])
    right_act = jax.nn.silu(low_back(conv_sum))
    mid = left_act + place_right(right_act, FF // RIGHT_W)
    depth_in = pad_mask * norm(mid, gain_mid)
    sep_taps = w_depth.shape[0]
    depth = shifted(depth_in, -(sep_taps // 2)) * w_depth[0]
    for tap_index in range(1, sep_taps):
        depth = depth + shifted(depth_in, tap_index - sep_taps // 2) * w_depth[tap_index]
    sep_out = low_back(project(low(depth), w_point))
    resid_two = resid_one + jnp.pad(sep_out, ((0, 0), (0, 0), (0, D - SEP_W)))
    attn_in = low(norm(resid_two, gain_attn))
    head_shape = (SEQ_GRP, LEN, HEADS, HEAD_DIM)
    queries = low_back(low(project(attn_in, w_qkv[0]))).reshape(head_shape)
    key_vecs = low_back(low(project(attn_in, w_qkv[1]))).reshape(head_shape)
    value_vecs = low_back(low(project(attn_in, w_qkv[2]))).reshape(head_shape)
    score_scale = 1.0 / math.sqrt(HEAD_DIM)
    scores = low_back(jnp.einsum('gqhd,gkhd->ghqk', queries, key_vecs, precision=highest) * score_scale)
    scores = jnp.where(valid_mask[:, None, None, :], scores, negative_big)
    probability = low(jax.nn.softmax(scores, axis=-1))
    context = jnp.einsum('ghqk,gkhd->gqhd', probability, value_vecs, precision=highest)
    context = low_back(low(context)).reshape(SEQ_GRP, LEN, D)
    attn_out = low_back(project(context, w_out))
    resid_three = resid_two + attn_out
    ffn_in = low(norm(resid_three, gain_ffn))
    ffn_hidden = low(jax.nn.silu(low_back(project(ffn_in, w_in))))
    return resid_three + project(ffn_hidden, w_back)

def reference(inputs, lengths, gain_glu, w_value, w_gate, gain_branch, w_left, w_right, gain_mid, w_depth, w_point, gain_attn, w_qkv, w_out, gain_ffn, w_in, w_back, cotangent):
    weights = tuple((argument.astype(jnp.float32) for argument in (gain_glu, w_value, w_gate, gain_branch, w_left, w_right, gain_mid, w_depth, w_point, gain_attn, w_qkv, w_out, gain_ffn, w_in, w_back)))
    blocks = SEQS // SEQ_GRP
    block_in = inputs.astype(jnp.float32).reshape(blocks, SEQ_GRP, LEN, D)
    block_cot = cotangent.astype(jnp.float32).reshape(blocks, SEQ_GRP, LEN, D)
    block_len = lengths.astype(jnp.int32).reshape(blocks, SEQ_GRP)

    def scan_step(totals, pieces):
        values, lens_here, cot_here = pieces
        valid_mask = lax.broadcasted_iota(jnp.int32, (SEQ_GRP, LEN), 1) < lens_here[:, None]

        def forward(params, activations):
            return layer(params, activations, valid_mask)
        result, pullback = jax.vjp(forward, weights, values)
        grad_weights, grad_acts = pullback(cot_here)
        totals = jax.tree.map(lambda earlier, later: earlier + later, totals, grad_weights)
        return (totals, (result.astype(jnp.bfloat16), grad_acts.astype(jnp.bfloat16)))
    initial = jax.tree.map(jnp.zeros_like, weights)
    totals, (results, grad_acts) = lax.scan(scan_step, initial, (block_in, block_len, block_cot))
    outputs = results.reshape(SEQS, LEN, D)
    grad_inputs = grad_acts.reshape(SEQS, LEN, D)
    return (outputs, grad_inputs, totals[0], totals[1], totals[2], totals[3], totals[4], totals[5], totals[6], totals[7], totals[8], totals[9], totals[10], totals[11], totals[12], totals[13], totals[14])
```

```python
import math

import jax
import jax.numpy as jnp
from jax import lax
from jax.sharding import PartitionSpec as P

FF = 2048
HEAD_DIM = 64
EDGE = 16


epsilon = 1e-06
negative_big = -1e30


def matmul(left_side, right_side):
    return jnp.dot(left_side, right_side, preferred_element_type=jnp.float32)


def contract_rows(left_side, right_side):
    return lax.dot_general(
        left_side, right_side, (((0,), (0,)), ((), ())), preferred_element_type=jnp.float32
    )


def contract_cols(left_side, right_side):
    return lax.dot_general(
        left_side, right_side, (((1,), (1,)), ((), ())), preferred_element_type=jnp.float32
    )


def spread_rows(pieces):
    return lax.all_gather(pieces, "mp", axis=1, tiled=True)


def collect_rows(partial_value):
    return lax.psum_scatter(
        partial_value.astype(jnp.bfloat16), "mp", scatter_dimension=1, tiled=True
    ).astype(jnp.float32)


def channel_sums(former, latter):
    return lax.psum((jnp.sum(former, axis=-1), jnp.sum(latter, axis=-1)), "mp")


def normalize(values, gain_vec):
    centre = values - jnp.mean(values, axis=-1, keepdims=True)
    scale_inv = lax.rsqrt(jnp.mean(centre * centre, axis=-1, keepdims=True) + epsilon)
    unit_rows = centre * scale_inv
    return (unit_rows * gain_vec, unit_rows, scale_inv)


def normalize_back(grad_out, unit_rows, scale_inv, gain_vec):
    scaled = grad_out * gain_vec
    mean_one = jnp.mean(scaled, axis=-1, keepdims=True)
    mean_two = jnp.mean(scaled * unit_rows, axis=-1, keepdims=True)
    grad_in = scale_inv * (scaled - mean_one - unit_rows * mean_two)
    return (grad_in, jnp.sum(grad_out * unit_rows, axis=(0, 1)))


def silu_slope(values):
    sigmoid_part = jax.nn.sigmoid(values)
    return sigmoid_part * (1.0 + values * (1.0 - sigmoid_part))


def shifted(values, offset):
    if offset == 0:
        return values
    margin = abs(offset)
    seq_len = values.shape[1]
    filler = jnp.zeros(values.shape[:1] + (margin,) + values.shape[2:], values.dtype)
    padded = jnp.concatenate([filler, values, filler], axis=1)
    return lax.slice_in_dim(padded, margin + offset, margin + offset + seq_len, axis=1)


def place_right(right_vals, stride):
    filler = jnp.zeros(right_vals.shape + (stride - 1,), right_vals.dtype)
    joined = jnp.concatenate([right_vals[..., None], filler], axis=-1)
    return joined.reshape(right_vals.shape[:-1] + (right_vals.shape[-1] * stride,))


def attend_forward(queries, key_vecs, value_vecs, key_valid, block_rows, score_scale):
    contexts = []
    log_parts = []
    for row_start in range(0, queries.shape[0], block_rows):
        query_rows = queries[row_start : row_start + block_rows]
        scores = (
            jnp.einsum("qhd,khd->hqk", query_rows, key_vecs, preferred_element_type=jnp.float32)
            * score_scale
        )
        scores = jnp.where(key_valid[None, None, :], scores, negative_big)
        row_max = jnp.max(scores, axis=-1, keepdims=True)
        weights_exp = jnp.exp(scores - row_max)
        row_total = jnp.sum(weights_exp, axis=-1, keepdims=True)
        probability = (weights_exp / row_total).astype(jnp.bfloat16)
        contexts.append(
            jnp.einsum("hqk,khd->qhd", probability, value_vecs, preferred_element_type=jnp.float32)
        )
        log_parts.append((row_max + jnp.log(row_total))[..., 0])
    return (jnp.concatenate(contexts, axis=0), jnp.concatenate(log_parts, axis=1))


def attend_back(
    queries, key_vecs, value_vecs, key_valid, log_sums, grad_context, block_rows, score_scale
):
    grad_queries = []
    grad_keys = jnp.zeros(key_vecs.shape, jnp.float32)
    grad_values = jnp.zeros(value_vecs.shape, jnp.float32)
    for row_start in range(0, queries.shape[0], block_rows):
        query_rows = queries[row_start : row_start + block_rows]
        grad_rows = grad_context[row_start : row_start + block_rows]
        log_rows = log_sums[:, row_start : row_start + block_rows]
        scores = (
            jnp.einsum("qhd,khd->hqk", query_rows, key_vecs, preferred_element_type=jnp.float32)
            * score_scale
        )
        scores = jnp.where(key_valid[None, None, :], scores, negative_big)
        probability = jnp.exp(scores - log_rows[..., None])
        grad_prob = jnp.einsum(
            "qhd,khd->hqk", grad_rows, value_vecs, preferred_element_type=jnp.float32
        )
        row_dot = jnp.sum(probability * grad_prob, axis=-1, keepdims=True)
        grad_scores = (probability * (grad_prob - row_dot)).astype(jnp.bfloat16)
        grad_queries.append(
            jnp.einsum("hqk,khd->qhd", grad_scores, key_vecs, preferred_element_type=jnp.float32)
            * score_scale
        )
        grad_keys = (
            grad_keys
            + jnp.einsum(
                "hqk,qhd->khd", grad_scores, query_rows, preferred_element_type=jnp.float32
            )
            * score_scale
        )
        grad_values = grad_values + jnp.einsum(
            "hqk,qhd->khd",
            probability.astype(jnp.bfloat16),
            grad_rows,
            preferred_element_type=jnp.float32,
        )
    grad_query_all = jnp.concatenate(grad_queries, axis=0)
    return (grad_query_all.astype(jnp.bfloat16), grad_keys, grad_values)


def split_pass(
    inputs,
    lengths,
    gain_glu,
    w_value,
    w_gate,
    gain_branch,
    w_left,
    w_right,
    gain_mid,
    w_depth,
    w_point,
    gain_attn,
    w_qkv,
    w_out,
    gain_ffn,
    w_in,
    w_back,
    cotangent,
):
    seqs_here, local_len, model_width = inputs.shape
    group_size = lax.axis_size("mp")
    member = lax.axis_index("mp")
    seq_len = local_len * group_size
    group_rows = seqs_here * seq_len
    positions = lax.broadcasted_iota(jnp.int32, (seqs_here, seq_len), 1)
    key_valid = positions < lengths[:, None]
    valid_full = key_valid.astype(jnp.float32)
    valid_own = lax.dynamic_slice_in_dim(valid_full, member * local_len, local_len, axis=1)
    inner_cols = w_left.shape[1]
    right_cols = w_right.shape[2]
    stride = inner_cols // right_cols
    conv_taps = w_right.shape[0]
    sep_taps = w_depth.shape[0]
    sep_width = w_point.shape[1]
    head_cols = w_qkv.shape[2]
    heads_here = head_cols // HEAD_DIM
    score_scale = 1.0 / math.sqrt(HEAD_DIM)
    block_rows = min(512, seq_len)
    group_shape = (seqs_here, seq_len, model_width)
    depth_taps = w_depth.astype(jnp.float32)
    gain_mid_f = gain_mid.astype(jnp.float32)

    def branch_inner(gathered):
        flat_rows = gathered.reshape(group_rows, model_width)
        left_pre = matmul(flat_rows, w_left).reshape(seqs_here, seq_len, inner_cols)
        right_pre = jnp.zeros((group_rows, right_cols), jnp.float32)
        for tap_index in range(conv_taps):
            moved = shifted(gathered, tap_index - conv_taps // 2).reshape(group_rows, model_width)
            right_pre = right_pre + matmul(moved, w_right[tap_index])
        right_pre = right_pre.reshape(seqs_here, seq_len, right_cols)
        mid = jax.nn.silu(left_pre) + place_right(jax.nn.silu(right_pre), stride)
        return (left_pre, right_pre, mid)

    def depth_mix(depth_in):
        depth = jnp.zeros(depth_in.shape, jnp.float32)
        for tap_index in range(sep_taps):
            depth = depth + shifted(depth_in, tap_index - sep_taps // 2) * depth_taps[tap_index]
        return depth.astype(jnp.bfloat16)

    def project_qkv(gathered):
        flat_rows = gathered.reshape(group_rows, model_width)
        joined = jnp.einsum("td,kdc->ktc", flat_rows, w_qkv, preferred_element_type=jnp.float32)
        return joined.astype(jnp.bfloat16).reshape(3, seqs_here, seq_len, heads_here, HEAD_DIM)

    def forward_one(pieces):
        return attend_forward(pieces[0], pieces[1], pieces[2], pieces[3], block_rows, score_scale)

    def backward_one(pieces):
        return attend_back(
            pieces[0],
            pieces[1],
            pieces[2],
            pieces[3],
            pieces[4],
            pieces[5],
            block_rows,
            score_scale,
        )

    resid_in = inputs.astype(jnp.float32)
    normed_glu, unit_glu, inv_glu = normalize(resid_in, gain_glu)
    gathered_glu = spread_rows(normed_glu.astype(jnp.bfloat16))
    flat_glu = gathered_glu.reshape(group_rows, model_width)
    value_pre = matmul(flat_glu, w_value)
    gate_sig = jax.nn.sigmoid(matmul(flat_glu, w_gate))
    glu_local = (value_pre * gate_sig).astype(jnp.bfloat16).reshape(seqs_here, seq_len, -1)
    glu_rows = lax.all_to_all(glu_local, "mp", split_axis=1, concat_axis=2, tiled=True)
    resid_one = resid_in + glu_rows.astype(jnp.float32)
    normed_branch, unit_branch, inv_branch = normalize(resid_one, gain_branch)
    gathered_branch = spread_rows((valid_own[..., None] * normed_branch).astype(jnp.bfloat16))
    left_pre, right_pre, mid = branch_inner(gathered_branch)
    mid_sum, mid_square = channel_sums(mid, mid * mid)
    mid_mean = mid_sum / FF
    inv_mid = lax.rsqrt(mid_square / FF - mid_mean * mid_mean + epsilon)
    unit_mid = (mid - mid_mean[..., None]) * inv_mid[..., None]
    depth_in = valid_full[..., None] * unit_mid * gain_mid_f
    depth_low = depth_mix(depth_in)
    sep_part = matmul(depth_low.reshape(group_rows, inner_cols), w_point).reshape(
        seqs_here, seq_len, sep_width
    )
    sep_rows = collect_rows(sep_part)
    resid_two = resid_one + jnp.pad(sep_rows, ((0, 0), (0, 0), (0, model_width - sep_width)))
    normed_attn, unit_attn, inv_attn = normalize(resid_two, gain_attn)
    gathered_attn = spread_rows(normed_attn.astype(jnp.bfloat16))
    qkv_heads = project_qkv(gathered_attn)
    context, log_sums = lax.map(forward_one, (qkv_heads[0], qkv_heads[1], qkv_heads[2], key_valid))
    context_low = context.astype(jnp.bfloat16).reshape(group_rows, head_cols)
    attn_rows = collect_rows(matmul(context_low, w_out).reshape(group_shape))
    resid_three = resid_two + attn_rows
    normed_ffn, unit_ffn, inv_ffn = normalize(resid_three, gain_ffn)
    gathered_ffn = spread_rows(normed_ffn.astype(jnp.bfloat16))
    ffn_flat = gathered_ffn.reshape(group_rows, model_width)
    ffn_pre = matmul(ffn_flat, w_in)
    ffn_hidden = jax.nn.silu(ffn_pre).astype(jnp.bfloat16)
    final_rows = resid_three + collect_rows(matmul(ffn_hidden, w_back).reshape(group_shape))
    outputs = final_rows.astype(jnp.bfloat16)
    cot_full = spread_rows(cotangent).reshape(group_rows, model_width)
    ffn_flat = spread_rows(normed_ffn.astype(jnp.bfloat16)).reshape(group_rows, model_width)
    ffn_pre = matmul(ffn_flat, w_in)
    ffn_hidden = jax.nn.silu(ffn_pre).astype(jnp.bfloat16)
    grad_hidden = contract_cols(cot_full, w_back)
    grad_ffn_pre = (grad_hidden * silu_slope(ffn_pre)).astype(jnp.bfloat16)
    grad_w_back = contract_rows(ffn_hidden, cot_full)
    grad_w_in = contract_rows(ffn_flat, grad_ffn_pre)
    grad_normed_ffn = collect_rows(contract_cols(grad_ffn_pre, w_in).reshape(group_shape))
    grad_resid, grad_gain_ffn = normalize_back(grad_normed_ffn, unit_ffn, inv_ffn, gain_ffn)
    grad_three = cotangent.astype(jnp.float32) + grad_resid
    grad_attn = spread_rows(grad_three.astype(jnp.bfloat16)).reshape(group_rows, model_width)
    gathered_attn = spread_rows(normed_attn.astype(jnp.bfloat16))
    qkv_heads = project_qkv(gathered_attn)
    attn_flat = gathered_attn.reshape(group_rows, model_width)
    grad_w_out = contract_rows(context_low, grad_attn)
    grad_context = contract_cols(grad_attn, w_out).astype(jnp.bfloat16)
    grad_context = grad_context.reshape(seqs_here, seq_len, heads_here, HEAD_DIM)
    grad_q, grad_k, grad_v = lax.map(
        backward_one, (qkv_heads[0], qkv_heads[1], qkv_heads[2], key_valid, log_sums, grad_context)
    )
    grad_qkv = jnp.stack(
        [grad_q, grad_k.astype(jnp.bfloat16), grad_v.astype(jnp.bfloat16)]
    ).reshape(3, group_rows, head_cols)
    grad_w_qkv = jnp.einsum("td,ktc->kdc", attn_flat, grad_qkv, preferred_element_type=jnp.float32)
    grad_attn_in = jnp.einsum("ktc,kdc->td", grad_qkv, w_qkv, preferred_element_type=jnp.float32)
    grad_normed_attn = collect_rows(grad_attn_in.reshape(group_shape))
    grad_resid, grad_gain_attn = normalize_back(grad_normed_attn, unit_attn, inv_attn, gain_attn)
    grad_two = grad_three + grad_resid
    grad_sep = spread_rows(grad_two[..., :sep_width].astype(jnp.bfloat16)).reshape(
        group_rows, sep_width
    )
    gathered_branch = spread_rows((valid_own[..., None] * normed_branch).astype(jnp.bfloat16))
    left_pre, right_pre, mid = branch_inner(gathered_branch)
    unit_mid = (mid - mid_mean[..., None]) * inv_mid[..., None]
    depth_in = valid_full[..., None] * unit_mid * gain_mid_f
    depth_low = depth_mix(depth_in)
    grad_w_point = contract_rows(depth_low.reshape(group_rows, inner_cols), grad_sep)
    grad_depth = contract_cols(grad_sep, w_point).reshape(seqs_here, seq_len, inner_cols)
    grad_depth_in = jnp.zeros(grad_depth.shape, jnp.float32)
    depth_rows = []
    for tap_index in range(sep_taps):
        offset = tap_index - sep_taps // 2
        grad_depth_in = grad_depth_in + shifted(grad_depth, -offset) * depth_taps[tap_index]
        depth_rows.append(jnp.sum(shifted(depth_in, offset) * grad_depth, axis=(0, 1)))
    grad_w_depth = jnp.stack(depth_rows)
    grad_unit = grad_depth_in * valid_full[..., None]
    grad_gain_mid = jnp.sum(grad_unit * unit_mid, axis=(0, 1))
    scaled = grad_unit * gain_mid_f
    sum_one, sum_two = channel_sums(scaled, scaled * unit_mid)
    grad_mid = inv_mid[..., None] * (
        scaled - (sum_one / FF)[..., None] - unit_mid * (sum_two / FF)[..., None]
    )
    grad_left = (
        (grad_mid * silu_slope(left_pre)).astype(jnp.bfloat16).reshape(group_rows, inner_cols)
    )
    grad_right_act = grad_mid.reshape(seqs_here, seq_len, right_cols, stride)[..., 0]
    grad_right = (
        (grad_right_act * silu_slope(right_pre))
        .astype(jnp.bfloat16)
        .reshape(group_rows, right_cols)
    )
    branch_flat = gathered_branch.reshape(group_rows, model_width)
    grad_w_left = contract_rows(branch_flat, grad_left)
    grad_branch_in = contract_cols(grad_left, w_left).reshape(group_shape)
    right_rows = []
    for tap_index in range(conv_taps):
        offset = tap_index - conv_taps // 2
        moved = shifted(gathered_branch, offset).reshape(group_rows, model_width)
        right_rows.append(contract_rows(moved, grad_right))
        grad_branch_in = grad_branch_in + shifted(
            contract_cols(grad_right, w_right[tap_index]).reshape(group_shape), -offset
        )
    grad_w_right = jnp.stack(right_rows)
    grad_normed_branch = collect_rows(grad_branch_in) * valid_own[..., None]
    grad_resid, grad_gain_branch = normalize_back(
        grad_normed_branch, unit_branch, inv_branch, gain_branch
    )
    grad_one = grad_two + grad_resid
    grad_glu = lax.all_to_all(
        grad_one.astype(jnp.bfloat16), "mp", split_axis=2, concat_axis=1, tiled=True
    )
    grad_glu_flat = grad_glu.reshape(group_rows, -1).astype(jnp.float32)
    flat_glu = spread_rows(normed_glu.astype(jnp.bfloat16)).reshape(group_rows, model_width)
    value_pre = matmul(flat_glu, w_value)
    gate_sig = jax.nn.sigmoid(matmul(flat_glu, w_gate))
    grad_value = (grad_glu_flat * gate_sig).astype(jnp.bfloat16)
    grad_gate = (grad_glu_flat * value_pre * gate_sig * (1.0 - gate_sig)).astype(jnp.bfloat16)
    grad_w_value = contract_rows(flat_glu, grad_value)
    grad_w_gate = contract_rows(flat_glu, grad_gate)
    grad_glu_in = contract_cols(grad_value, w_value) + contract_cols(grad_gate, w_gate)
    grad_normed_glu = collect_rows(grad_glu_in.reshape(group_shape))
    grad_resid, grad_gain_glu = normalize_back(grad_normed_glu, unit_glu, inv_glu, gain_glu)
    grad_inputs = (grad_one + grad_resid).astype(jnp.bfloat16)
    gains = (grad_gain_glu, grad_gain_branch, grad_gain_attn, grad_gain_ffn)
    shards = (
        grad_w_value,
        grad_w_gate,
        grad_w_left,
        grad_w_right,
        grad_gain_mid,
        grad_w_depth,
        grad_w_point,
        grad_w_qkv,
        grad_w_out,
        grad_w_in,
        grad_w_back,
    )
    return (outputs, grad_inputs, gains, shards)


def local(
    inputs,
    lengths,
    gain_glu,
    w_value,
    w_gate,
    gain_branch,
    w_left,
    w_right,
    gain_mid,
    w_depth,
    w_point,
    gain_attn,
    w_qkv,
    w_out,
    gain_ffn,
    w_in,
    w_back,
    cotangent,
):
    outputs, grad_inputs, gains, shards = split_pass(
        inputs,
        lengths,
        gain_glu,
        w_value,
        w_gate,
        gain_branch,
        w_left,
        w_right,
        gain_mid,
        w_depth,
        w_point,
        gain_attn,
        w_qkv,
        w_out,
        gain_ffn,
        w_in,
        w_back,
        cotangent,
    )
    gain_totals = lax.psum((gains[0], gains[1], gains[2], gains[3]), ("dp", "mp"))
    weight_totals = (
        lax.psum(shards[0].astype(jnp.bfloat16), "dp").astype(jnp.float32),
        lax.psum(shards[1].astype(jnp.bfloat16), "dp").astype(jnp.float32),
        lax.psum(shards[2].astype(jnp.bfloat16), "dp").astype(jnp.float32),
        lax.psum(shards[3].astype(jnp.bfloat16), "dp").astype(jnp.float32),
        lax.psum(shards[4].astype(jnp.bfloat16), "dp").astype(jnp.float32),
        lax.psum(shards[5].astype(jnp.bfloat16), "dp").astype(jnp.float32),
        lax.psum(shards[6].astype(jnp.bfloat16), "dp").astype(jnp.float32),
        lax.psum(shards[7].astype(jnp.bfloat16), "dp").astype(jnp.float32),
        lax.psum(shards[8].astype(jnp.bfloat16), "dp").astype(jnp.float32),
        lax.psum(shards[9].astype(jnp.bfloat16), "dp").astype(jnp.float32),
        lax.psum(shards[10].astype(jnp.bfloat16), "dp").astype(jnp.float32),
    )
    return (
        outputs,
        grad_inputs,
        gain_totals[0],
        weight_totals[0],
        weight_totals[1],
        gain_totals[1],
        weight_totals[2],
        weight_totals[3],
        weight_totals[4],
        weight_totals[5],
        weight_totals[6],
        gain_totals[2],
        weight_totals[7],
        weight_totals[8],
        gain_totals[3],
        weight_totals[9],
        weight_totals[10],
    )


def other_core(dp_size):
    return [(index, index ^ 1) for index in range(dp_size)]


def over_mp(values):
    return lax.ppermute(values, "mp", [(0, 1), (1, 0)])


def over_core(values):
    return lax.ppermute(values, "dp", other_core(lax.axis_size("dp")))


def flat_pairs(dp_size, rule):
    pairs = []
    for dp_index in range(dp_size):
        for member in range(2):
            pair, core = dp_index // 2, dp_index % 2
            new_core, new_member = rule(core, member)
            pairs.append((dp_index * 2 + member, (pair * 2 + new_core) * 2 + new_member))
    return pairs


def swap_blocks(values, member, core):
    pairs = flat_pairs(lax.axis_size("dp"), lambda c, m: (m, c))
    pairs = [pair for pair in pairs if pair[0] != pair[1]]
    moved = lax.ppermute(values, ("dp", "mp"), pairs)
    return jnp.where(member == core, values, moved)


def edge_rows(values, member, core):
    rows = values.shape[0]
    edge = jnp.where(member == 0, values[rows - EDGE :], values[:EDGE])
    pairs = flat_pairs(lax.axis_size("dp"), lambda c, m: (1 - m, c))
    return lax.ppermute(edge, ("dp", "mp"), pairs)


def with_edges(values, edge, core):
    blank = jnp.zeros_like(edge)
    before = jnp.where(core == 1, edge, blank)
    after = jnp.where(core == 1, blank, edge)
    return jnp.concatenate([before, values, after], axis=0)


def partner_half(weight, core):
    half = weight.shape[0] // 2
    got = over_mp(lax.dynamic_slice_in_dim(weight, core * half, half, axis=0))
    part = over_core(got)
    return jnp.where(
        core == 0, jnp.concatenate([got, part], axis=0), jnp.concatenate([part, got], axis=0)
    )


def norm_rows(values, gain_vec):
    centre = values - jnp.mean(values, axis=-1, keepdims=True)
    scale_inv = lax.rsqrt(jnp.mean(centre * centre, axis=-1, keepdims=True) + epsilon)
    unit_rows = centre * scale_inv
    return (unit_rows * gain_vec, unit_rows, scale_inv)


def norm_rows_back(grad_out, unit_rows, scale_inv, gain_vec):
    scaled = grad_out * gain_vec
    mean_one = jnp.mean(scaled, axis=-1, keepdims=True)
    mean_two = jnp.mean(scaled * unit_rows, axis=-1, keepdims=True)
    grad_in = scale_inv * (scaled - mean_one - unit_rows * mean_two)
    return (grad_in, jnp.sum(grad_out * unit_rows, axis=0))


def roll_rows(values, offset):
    if offset == 0:
        return values
    return jnp.roll(values, -offset, axis=0)


def paired(
    inputs, lengths, gain_glu, w_value, w_gate, gain_branch, w_left, w_right, gain_mid, w_depth,
    w_point, gain_attn, w_qkv, w_out, gain_ffn, w_in, w_back, cotangent,
):
    low = jnp.bfloat16
    member = lax.axis_index("mp")
    core = lax.axis_index("dp") % 2
    rows, width = inputs.shape[1:]
    own = slice(EDGE, EDGE + rows)

    length = swap_blocks(lengths, member, core)[0]
    edge = edge_rows(inputs[0], member, core)
    block = swap_blocks(inputs[0], member, core)
    cot = swap_blocks(cotangent[0], member, core)

    def both(weight, axis):
        return jnp.concatenate([weight, partner_half(weight, core)], axis=axis)

    def ordered(weight, axis):
        other = partner_half(weight, core)
        return jnp.where(
            member == 0,
            jnp.concatenate([weight, other], axis=axis),
            jnp.concatenate([other, weight], axis=axis),
        )

    value_w = ordered(w_value, 1)
    gate_w = ordered(w_gate, 1)
    left_w = both(w_left, 1)
    right_w = jnp.concatenate(
        [w_right, partner_half(w_right.reshape(-1, w_right.shape[2]), core).reshape(w_right.shape)],
        axis=2,
    )
    mid_gain = jnp.concatenate([gain_mid, over_mp(gain_mid)]).astype(jnp.float32)
    taps = jnp.concatenate([w_depth, over_mp(w_depth)], axis=1).astype(jnp.float32)
    point_w = both(w_point, 0)
    qkv_w = jnp.concatenate(
        [w_qkv, partner_half(w_qkv.reshape(-1, w_qkv.shape[2]), core).reshape(w_qkv.shape)], axis=2
    )
    out_w = both(w_out, 0)
    in_w = both(w_in, 1)
    back_w = both(w_back, 0)
    inner = left_w.shape[1]
    right_cols = right_w.shape[2]
    stride = inner // right_cols
    sep_width = point_w.shape[1]
    sep_taps = taps.shape[0]
    conv_taps = right_w.shape[0]
    heads = qkv_w.shape[2] // HEAD_DIM
    score_scale = 1.0 / math.sqrt(HEAD_DIM)

    positions = core * rows - EDGE + jnp.arange(rows + 2 * EDGE)
    valid = ((positions >= 0) & (positions < length)).astype(jnp.float32)[:, None]

    resid_in = with_edges(block, edge, core).astype(jnp.float32)
    normed, unit_glu, inv_glu = norm_rows(resid_in, gain_glu)
    glu_in = normed.astype(low)
    value_pre = matmul(glu_in, value_w)
    gate_sig = jax.nn.sigmoid(matmul(glu_in, gate_w))
    glu_out = (value_pre * gate_sig).astype(low)
    resid_one = resid_in + glu_out.astype(jnp.float32)
    normed, unit_branch, inv_branch = norm_rows(resid_one, gain_branch)
    branch_in = (valid * normed).astype(low)
    left_pre = matmul(branch_in, left_w)
    right_pre = sum(
        matmul(roll_rows(branch_in, tap - conv_taps // 2), right_w[tap]) for tap in range(conv_taps)
    )
    spread = (
        jnp.arange(inner)[None, :] == stride * jnp.arange(right_cols)[:, None]
    ).astype(low)
    mid = jax.nn.silu(left_pre) + matmul(jax.nn.silu(right_pre).astype(low), spread)
    mid_mean = jnp.mean(mid, axis=-1, keepdims=True)
    inv_mid = lax.rsqrt(jnp.mean((mid - mid_mean) ** 2, axis=-1, keepdims=True) + epsilon)
    unit_mid = (mid - mid_mean) * inv_mid
    depth_in = valid * unit_mid * mid_gain
    depth = sum(
        roll_rows(depth_in, tap - sep_taps // 2)[own] * taps[tap] for tap in range(sep_taps)
    ).astype(low)
    sep_rows = matmul(depth, point_w)
    resid_two = resid_one[own] + jnp.pad(sep_rows, ((0, 0), (0, width - sep_width)))
    normed, unit_attn, inv_attn = norm_rows(resid_two, gain_attn)
    attn_in = normed.astype(low)
    qkv = [matmul(attn_in, qkv_w[index]).astype(low) for index in range(3)]
    kv_own = jnp.concatenate(qkv[1:], axis=1)
    kv_far = over_core(kv_own)
    kv_all = jnp.where(
        core == 0,
        jnp.concatenate([kv_own, kv_far], axis=0),
        jnp.concatenate([kv_far, kv_own], axis=0),
    )
    key_valid = jnp.arange(2 * rows) < length
    queries = qkv[0].reshape(rows, heads, HEAD_DIM)
    keys = kv_all[:, : heads * HEAD_DIM].reshape(2 * rows, heads, HEAD_DIM)
    vals = kv_all[:, heads * HEAD_DIM :].reshape(2 * rows, heads, HEAD_DIM)
    context, log_sums = attend_forward(queries, keys, vals, key_valid, rows, score_scale)
    context_low = context.astype(low).reshape(rows, heads * HEAD_DIM)
    resid_three = resid_two + matmul(context_low, out_w)
    normed, unit_ffn, inv_ffn = norm_rows(resid_three, gain_ffn)
    ffn_in = normed.astype(low)
    ffn_pre = matmul(ffn_in, in_w)
    ffn_hidden = jax.nn.silu(ffn_pre).astype(low)
    outputs = (resid_three + matmul(ffn_hidden, back_w)).astype(low)
    outputs = swap_blocks(outputs, member, core)

    grad_hidden = contract_cols(cot, back_w)
    grad_ffn_pre = (grad_hidden * silu_slope(ffn_pre)).astype(low)
    grad_w_back = contract_rows(ffn_hidden, cot)
    grad_w_in = contract_rows(ffn_in, grad_ffn_pre)
    grad_resid, grad_gain_ffn = norm_rows_back(
        contract_cols(grad_ffn_pre, in_w), unit_ffn, inv_ffn, gain_ffn
    )
    grad_three = cot.astype(jnp.float32) + grad_resid
    grad_attn = grad_three.astype(low)
    grad_w_out = contract_rows(context_low, grad_attn)
    grad_context = contract_cols(grad_attn, out_w).astype(low).reshape(queries.shape)
    grad_q, grad_k, grad_v = attend_back(
        queries, keys, vals, key_valid, log_sums, grad_context, rows, score_scale
    )
    grad_kv = jnp.concatenate([grad_k.reshape(2 * rows, -1), grad_v.reshape(2 * rows, -1)], axis=1)
    kept = lax.dynamic_slice_in_dim(grad_kv, core * rows, rows, axis=0)
    sent = lax.dynamic_slice_in_dim(grad_kv, (1 - core) * rows, rows, axis=0)
    grad_kv = (kept + over_core(sent.astype(low)).astype(jnp.float32)).astype(low)
    grad_qkv = jnp.stack(
        [
            grad_q.reshape(rows, -1),
            grad_kv[:, : heads * HEAD_DIM],
            grad_kv[:, heads * HEAD_DIM :],
        ]
    )
    grad_w_qkv = jnp.stack([contract_rows(attn_in, grad_qkv[index]) for index in range(3)])
    grad_attn_in = sum(contract_cols(grad_qkv[index], qkv_w[index]) for index in range(3))
    grad_resid, grad_gain_attn = norm_rows_back(grad_attn_in, unit_attn, inv_attn, gain_attn)
    grad_two = grad_three + grad_resid
    grad_sep = grad_two[:, :sep_width].astype(low)
    sep_edge = over_core(jnp.where(core == 0, grad_sep[rows - EDGE :], grad_sep[:EDGE]))
    grad_sep_all = with_edges(grad_sep, sep_edge, core)
    grad_w_point = contract_rows(depth, grad_sep)
    grad_depth = contract_cols(grad_sep_all, point_w)
    grad_depth_in = sum(
        roll_rows(grad_depth, sep_taps // 2 - tap) * taps[tap] for tap in range(sep_taps)
    )
    grad_w_depth = jnp.stack(
        [
            jnp.sum(roll_rows(depth_in, tap - sep_taps // 2)[own] * grad_depth[own], axis=0)
            for tap in range(sep_taps)
        ]
    )
    grad_unit = grad_depth_in * valid
    grad_gain_mid = jnp.sum((grad_unit * unit_mid)[own], axis=0)
    scaled = grad_unit * mid_gain
    grad_mid = inv_mid * (
        scaled
        - jnp.mean(scaled, axis=-1, keepdims=True)
        - unit_mid * jnp.mean(scaled * unit_mid, axis=-1, keepdims=True)
    )
    grad_left = (grad_mid * silu_slope(left_pre)).astype(low)
    grad_right = (contract_cols(grad_mid.astype(low), spread) * silu_slope(right_pre)).astype(low)
    grad_w_left = contract_rows(branch_in[own], grad_left[own])
    grad_branch_in = contract_cols(grad_left[own], left_w)
    right_rows = []
    for tap in range(conv_taps):
        offset = tap - conv_taps // 2
        right_rows.append(contract_rows(roll_rows(branch_in, offset)[own], grad_right[own]))
        grad_branch_in = grad_branch_in + contract_cols(
            roll_rows(grad_right, -offset)[own], right_w[tap]
        )
    grad_w_right = jnp.stack(right_rows)
    grad_resid, grad_gain_branch = norm_rows_back(
        grad_branch_in * valid[own], unit_branch[own], inv_branch[own], gain_branch
    )
    grad_one = grad_two + grad_resid
    grad_glu = grad_one.astype(low).astype(jnp.float32)
    sig = gate_sig[own]
    grad_value = (grad_glu * sig).astype(low)
    grad_gate = (grad_glu * value_pre[own] * sig * (1.0 - sig)).astype(low)
    grad_w_value = contract_rows(glu_in[own], grad_value)
    grad_w_gate = contract_rows(glu_in[own], grad_gate)
    grad_resid, grad_gain_glu = norm_rows_back(
        contract_cols(grad_value, value_w) + contract_cols(grad_gate, gate_w),
        unit_glu[own], inv_glu[own], gain_glu,
    )
    grad_inputs = swap_blocks((grad_one + grad_resid).astype(low), member, core)

    gain_totals = lax.psum(
        (grad_gain_glu, grad_gain_branch, grad_gain_attn, grad_gain_ffn), ("dp", "mp")
    )

    def total(grad, axis, in_order=False):
        half = grad.shape[axis] // 2
        at = member if in_order else 0
        mine = lax.dynamic_slice_in_dim(grad, at * half, half, axis=axis)
        theirs = lax.dynamic_slice_in_dim(grad, (1 - at) * half, half, axis=axis)
        mine = mine + over_mp(theirs.astype(low)).astype(jnp.float32)
        return lax.psum(mine.astype(low), "dp").astype(jnp.float32)

    return (
        outputs[None],
        grad_inputs[None],
        gain_totals[0],
        total(grad_w_value, 1, True),
        total(grad_w_gate, 1, True),
        gain_totals[1],
        total(grad_w_left, 1),
        total(grad_w_right, 2),
        total(grad_gain_mid, 0),
        total(grad_w_depth, 1),
        total(grad_w_point, 0),
        gain_totals[2],
        total(grad_w_qkv, 2),
        total(grad_w_out, 0),
        gain_totals[3],
        total(grad_w_in, 1),
        total(grad_w_back, 0),
    )


def solution(mesh):
    placed = (
        P("dp", "mp", None),
        P("dp"),
        P(),
        P(None, "mp"),
        P(None, "mp"),
        P(),
        P(None, "mp"),
        P(None, None, "mp"),
        P("mp"),
        P(None, "mp"),
        P("mp", None),
        P(),
        P(None, None, "mp"),
        P("mp", None),
        P(),
        P(None, "mp"),
        P("mp", None),
        P("dp", "mp", None),
    )
    mp_size, dp_size = mesh.shape["mp"], mesh.shape["dp"]
    plan = paired if mp_size == 2 and dp_size % 2 == 0 else local
    return jax.shard_map(
        plan,
        mesh=mesh,
        in_specs=placed,
        out_specs=(
            P("dp", "mp", None),
            P("dp", "mp", None),
            P(),
            P(None, "mp"),
            P(None, "mp"),
            P(),
            P(None, "mp"),
            P(None, None, "mp"),
            P("mp"),
            P(None, "mp"),
            P("mp", None),
            P(),
            P(None, None, "mp"),
            P("mp", None),
            P(),
            P(None, "mp"),
            P("mp", None),
        ),
        check_vma=False,
    )
```

```python
import functools
import math

import jax
import jax.numpy as jnp
from jax import lax
from jax.experimental import pallas as pl
from jax.experimental.pallas import tpu as pltpu
from jax.sharding import PartitionSpec as P

FF = 2048
HEAD_DIM = 64
EDGE = 16


epsilon = 1e-06
negative_big = -1e30


def matmul(left_side, right_side):
    return jnp.dot(left_side, right_side, preferred_element_type=jnp.float32)


def contract_rows(left_side, right_side):
    return lax.dot_general(
        left_side, right_side, (((0,), (0,)), ((), ())), preferred_element_type=jnp.float32
    )


def contract_cols(left_side, right_side):
    return lax.dot_general(
        left_side, right_side, (((1,), (1,)), ((), ())), preferred_element_type=jnp.float32
    )


def spread_rows(pieces):
    return lax.all_gather(pieces, "mp", axis=1, tiled=True)


def collect_rows(partial_value):
    return lax.psum_scatter(
        partial_value.astype(jnp.bfloat16), "mp", scatter_dimension=1, tiled=True
    ).astype(jnp.float32)


def channel_sums(former, latter):
    return lax.psum((jnp.sum(former, axis=-1), jnp.sum(latter, axis=-1)), "mp")


def normalize(values, gain_vec):
    centre = values - jnp.mean(values, axis=-1, keepdims=True)
    scale_inv = lax.rsqrt(jnp.mean(centre * centre, axis=-1, keepdims=True) + epsilon)
    unit_rows = centre * scale_inv
    return (unit_rows * gain_vec, unit_rows, scale_inv)


def normalize_back(grad_out, unit_rows, scale_inv, gain_vec):
    scaled = grad_out * gain_vec
    mean_one = jnp.mean(scaled, axis=-1, keepdims=True)
    mean_two = jnp.mean(scaled * unit_rows, axis=-1, keepdims=True)
    grad_in = scale_inv * (scaled - mean_one - unit_rows * mean_two)
    return (grad_in, jnp.sum(grad_out * unit_rows, axis=(0, 1)))


def silu_slope(values):
    sigmoid_part = jax.nn.sigmoid(values)
    return sigmoid_part * (1.0 + values * (1.0 - sigmoid_part))


def shifted(values, offset):
    if offset == 0:
        return values
    margin = abs(offset)
    seq_len = values.shape[1]
    filler = jnp.zeros(values.shape[:1] + (margin,) + values.shape[2:], values.dtype)
    padded = jnp.concatenate([filler, values, filler], axis=1)
    return lax.slice_in_dim(padded, margin + offset, margin + offset + seq_len, axis=1)


def place_right(right_vals, stride):
    filler = jnp.zeros(right_vals.shape + (stride - 1,), right_vals.dtype)
    joined = jnp.concatenate([right_vals[..., None], filler], axis=-1)
    return joined.reshape(right_vals.shape[:-1] + (right_vals.shape[-1] * stride,))


def attend_forward(queries, key_vecs, value_vecs, key_valid, block_rows, score_scale):
    contexts = []
    log_parts = []
    for row_start in range(0, queries.shape[0], block_rows):
        query_rows = queries[row_start : row_start + block_rows]
        scores = (
            jnp.einsum("qhd,khd->hqk", query_rows, key_vecs, preferred_element_type=jnp.float32)
            * score_scale
        )
        scores = jnp.where(key_valid[None, None, :], scores, negative_big)
        row_max = jnp.max(scores, axis=-1, keepdims=True)
        weights_exp = jnp.exp(scores - row_max)
        row_total = jnp.sum(weights_exp, axis=-1, keepdims=True)
        probability = (weights_exp / row_total).astype(jnp.bfloat16)
        contexts.append(
            jnp.einsum("hqk,khd->qhd", probability, value_vecs, preferred_element_type=jnp.float32)
        )
        log_parts.append((row_max + jnp.log(row_total))[..., 0])
    return (jnp.concatenate(contexts, axis=0), jnp.concatenate(log_parts, axis=1))


def attend_back(
    queries, key_vecs, value_vecs, key_valid, log_sums, grad_context, block_rows, score_scale
):
    grad_queries = []
    grad_keys = jnp.zeros(key_vecs.shape, jnp.float32)
    grad_values = jnp.zeros(value_vecs.shape, jnp.float32)
    for row_start in range(0, queries.shape[0], block_rows):
        query_rows = queries[row_start : row_start + block_rows]
        grad_rows = grad_context[row_start : row_start + block_rows]
        log_rows = log_sums[:, row_start : row_start + block_rows]
        scores = (
            jnp.einsum("qhd,khd->hqk", query_rows, key_vecs, preferred_element_type=jnp.float32)
            * score_scale
        )
        scores = jnp.where(key_valid[None, None, :], scores, negative_big)
        probability = jnp.exp(scores - log_rows[..., None])
        grad_prob = jnp.einsum(
            "qhd,khd->hqk", grad_rows, value_vecs, preferred_element_type=jnp.float32
        )
        row_dot = jnp.sum(probability * grad_prob, axis=-1, keepdims=True)
        grad_scores = (probability * (grad_prob - row_dot)).astype(jnp.bfloat16)
        grad_queries.append(
            jnp.einsum("hqk,khd->qhd", grad_scores, key_vecs, preferred_element_type=jnp.float32)
            * score_scale
        )
        grad_keys = (
            grad_keys
            + jnp.einsum(
                "hqk,qhd->khd", grad_scores, query_rows, preferred_element_type=jnp.float32
            )
            * score_scale
        )
        grad_values = grad_values + jnp.einsum(
            "hqk,qhd->khd",
            probability.astype(jnp.bfloat16),
            grad_rows,
            preferred_element_type=jnp.float32,
        )
    grad_query_all = jnp.concatenate(grad_queries, axis=0)
    return (grad_query_all.astype(jnp.bfloat16), grad_keys, grad_values)


def split_pass(
    inputs,
    lengths,
    gain_glu,
    w_value,
    w_gate,
    gain_branch,
    w_left,
    w_right,
    gain_mid,
    w_depth,
    w_point,
    gain_attn,
    w_qkv,
    w_out,
    gain_ffn,
    w_in,
    w_back,
    cotangent,
):
    seqs_here, local_len, model_width = inputs.shape
    group_size = lax.axis_size("mp")
    member = lax.axis_index("mp")
    seq_len = local_len * group_size
    group_rows = seqs_here * seq_len
    positions = lax.broadcasted_iota(jnp.int32, (seqs_here, seq_len), 1)
    key_valid = positions < lengths[:, None]
    valid_full = key_valid.astype(jnp.float32)
    valid_own = lax.dynamic_slice_in_dim(valid_full, member * local_len, local_len, axis=1)
    inner_cols = w_left.shape[1]
    right_cols = w_right.shape[2]
    stride = inner_cols // right_cols
    conv_taps = w_right.shape[0]
    sep_taps = w_depth.shape[0]
    sep_width = w_point.shape[1]
    head_cols = w_qkv.shape[2]
    heads_here = head_cols // HEAD_DIM
    score_scale = 1.0 / math.sqrt(HEAD_DIM)
    block_rows = min(512, seq_len)
    group_shape = (seqs_here, seq_len, model_width)
    depth_taps = w_depth.astype(jnp.float32)
    gain_mid_f = gain_mid.astype(jnp.float32)

    def branch_inner(gathered):
        flat_rows = gathered.reshape(group_rows, model_width)
        left_pre = matmul(flat_rows, w_left).reshape(seqs_here, seq_len, inner_cols)
        right_pre = jnp.zeros((group_rows, right_cols), jnp.float32)
        for tap_index in range(conv_taps):
            moved = shifted(gathered, tap_index - conv_taps // 2).reshape(group_rows, model_width)
            right_pre = right_pre + matmul(moved, w_right[tap_index])
        right_pre = right_pre.reshape(seqs_here, seq_len, right_cols)
        mid = jax.nn.silu(left_pre) + place_right(jax.nn.silu(right_pre), stride)
        return (left_pre, right_pre, mid)

    def depth_mix(depth_in):
        depth = jnp.zeros(depth_in.shape, jnp.float32)
        for tap_index in range(sep_taps):
            depth = depth + shifted(depth_in, tap_index - sep_taps // 2) * depth_taps[tap_index]
        return depth.astype(jnp.bfloat16)

    def project_qkv(gathered):
        flat_rows = gathered.reshape(group_rows, model_width)
        joined = jnp.einsum("td,kdc->ktc", flat_rows, w_qkv, preferred_element_type=jnp.float32)
        return joined.astype(jnp.bfloat16).reshape(3, seqs_here, seq_len, heads_here, HEAD_DIM)

    def forward_one(pieces):
        return attend_forward(pieces[0], pieces[1], pieces[2], pieces[3], block_rows, score_scale)

    def backward_one(pieces):
        return attend_back(
            pieces[0],
            pieces[1],
            pieces[2],
            pieces[3],
            pieces[4],
            pieces[5],
            block_rows,
            score_scale,
        )

    resid_in = inputs.astype(jnp.float32)
    normed_glu, unit_glu, inv_glu = normalize(resid_in, gain_glu)
    gathered_glu = spread_rows(normed_glu.astype(jnp.bfloat16))
    flat_glu = gathered_glu.reshape(group_rows, model_width)
    value_pre = matmul(flat_glu, w_value)
    gate_sig = jax.nn.sigmoid(matmul(flat_glu, w_gate))
    glu_local = (value_pre * gate_sig).astype(jnp.bfloat16).reshape(seqs_here, seq_len, -1)
    glu_rows = lax.all_to_all(glu_local, "mp", split_axis=1, concat_axis=2, tiled=True)
    resid_one = resid_in + glu_rows.astype(jnp.float32)
    normed_branch, unit_branch, inv_branch = normalize(resid_one, gain_branch)
    gathered_branch = spread_rows((valid_own[..., None] * normed_branch).astype(jnp.bfloat16))
    left_pre, right_pre, mid = branch_inner(gathered_branch)
    mid_sum, mid_square = channel_sums(mid, mid * mid)
    mid_mean = mid_sum / FF
    inv_mid = lax.rsqrt(mid_square / FF - mid_mean * mid_mean + epsilon)
    unit_mid = (mid - mid_mean[..., None]) * inv_mid[..., None]
    depth_in = valid_full[..., None] * unit_mid * gain_mid_f
    depth_low = depth_mix(depth_in)
    sep_part = matmul(depth_low.reshape(group_rows, inner_cols), w_point).reshape(
        seqs_here, seq_len, sep_width
    )
    sep_rows = collect_rows(sep_part)
    resid_two = resid_one + jnp.pad(sep_rows, ((0, 0), (0, 0), (0, model_width - sep_width)))
    normed_attn, unit_attn, inv_attn = normalize(resid_two, gain_attn)
    gathered_attn = spread_rows(normed_attn.astype(jnp.bfloat16))
    qkv_heads = project_qkv(gathered_attn)
    context, log_sums = lax.map(forward_one, (qkv_heads[0], qkv_heads[1], qkv_heads[2], key_valid))
    context_low = context.astype(jnp.bfloat16).reshape(group_rows, head_cols)
    attn_rows = collect_rows(matmul(context_low, w_out).reshape(group_shape))
    resid_three = resid_two + attn_rows
    normed_ffn, unit_ffn, inv_ffn = normalize(resid_three, gain_ffn)
    gathered_ffn = spread_rows(normed_ffn.astype(jnp.bfloat16))
    ffn_flat = gathered_ffn.reshape(group_rows, model_width)
    ffn_pre = matmul(ffn_flat, w_in)
    ffn_hidden = jax.nn.silu(ffn_pre).astype(jnp.bfloat16)
    final_rows = resid_three + collect_rows(matmul(ffn_hidden, w_back).reshape(group_shape))
    outputs = final_rows.astype(jnp.bfloat16)
    cot_full = spread_rows(cotangent).reshape(group_rows, model_width)
    ffn_flat = spread_rows(normed_ffn.astype(jnp.bfloat16)).reshape(group_rows, model_width)
    ffn_pre = matmul(ffn_flat, w_in)
    ffn_hidden = jax.nn.silu(ffn_pre).astype(jnp.bfloat16)
    grad_hidden = contract_cols(cot_full, w_back)
    grad_ffn_pre = (grad_hidden * silu_slope(ffn_pre)).astype(jnp.bfloat16)
    grad_w_back = contract_rows(ffn_hidden, cot_full)
    grad_w_in = contract_rows(ffn_flat, grad_ffn_pre)
    grad_normed_ffn = collect_rows(contract_cols(grad_ffn_pre, w_in).reshape(group_shape))
    grad_resid, grad_gain_ffn = normalize_back(grad_normed_ffn, unit_ffn, inv_ffn, gain_ffn)
    grad_three = cotangent.astype(jnp.float32) + grad_resid
    grad_attn = spread_rows(grad_three.astype(jnp.bfloat16)).reshape(group_rows, model_width)
    gathered_attn = spread_rows(normed_attn.astype(jnp.bfloat16))
    qkv_heads = project_qkv(gathered_attn)
    attn_flat = gathered_attn.reshape(group_rows, model_width)
    grad_w_out = contract_rows(context_low, grad_attn)
    grad_context = contract_cols(grad_attn, w_out).astype(jnp.bfloat16)
    grad_context = grad_context.reshape(seqs_here, seq_len, heads_here, HEAD_DIM)
    grad_q, grad_k, grad_v = lax.map(
        backward_one, (qkv_heads[0], qkv_heads[1], qkv_heads[2], key_valid, log_sums, grad_context)
    )
    grad_qkv = jnp.stack(
        [grad_q, grad_k.astype(jnp.bfloat16), grad_v.astype(jnp.bfloat16)]
    ).reshape(3, group_rows, head_cols)
    grad_w_qkv = jnp.einsum("td,ktc->kdc", attn_flat, grad_qkv, preferred_element_type=jnp.float32)
    grad_attn_in = jnp.einsum("ktc,kdc->td", grad_qkv, w_qkv, preferred_element_type=jnp.float32)
    grad_normed_attn = collect_rows(grad_attn_in.reshape(group_shape))
    grad_resid, grad_gain_attn = normalize_back(grad_normed_attn, unit_attn, inv_attn, gain_attn)
    grad_two = grad_three + grad_resid
    grad_sep = spread_rows(grad_two[..., :sep_width].astype(jnp.bfloat16)).reshape(
        group_rows, sep_width
    )
    gathered_branch = spread_rows((valid_own[..., None] * normed_branch).astype(jnp.bfloat16))
    left_pre, right_pre, mid = branch_inner(gathered_branch)
    unit_mid = (mid - mid_mean[..., None]) * inv_mid[..., None]
    depth_in = valid_full[..., None] * unit_mid * gain_mid_f
    depth_low = depth_mix(depth_in)
    grad_w_point = contract_rows(depth_low.reshape(group_rows, inner_cols), grad_sep)
    grad_depth = contract_cols(grad_sep, w_point).reshape(seqs_here, seq_len, inner_cols)
    grad_depth_in = jnp.zeros(grad_depth.shape, jnp.float32)
    depth_rows = []
    for tap_index in range(sep_taps):
        offset = tap_index - sep_taps // 2
        grad_depth_in = grad_depth_in + shifted(grad_depth, -offset) * depth_taps[tap_index]
        depth_rows.append(jnp.sum(shifted(depth_in, offset) * grad_depth, axis=(0, 1)))
    grad_w_depth = jnp.stack(depth_rows)
    grad_unit = grad_depth_in * valid_full[..., None]
    grad_gain_mid = jnp.sum(grad_unit * unit_mid, axis=(0, 1))
    scaled = grad_unit * gain_mid_f
    sum_one, sum_two = channel_sums(scaled, scaled * unit_mid)
    grad_mid = inv_mid[..., None] * (
        scaled - (sum_one / FF)[..., None] - unit_mid * (sum_two / FF)[..., None]
    )
    grad_left = (
        (grad_mid * silu_slope(left_pre)).astype(jnp.bfloat16).reshape(group_rows, inner_cols)
    )
    grad_right_act = grad_mid.reshape(seqs_here, seq_len, right_cols, stride)[..., 0]
    grad_right = (
        (grad_right_act * silu_slope(right_pre))
        .astype(jnp.bfloat16)
        .reshape(group_rows, right_cols)
    )
    branch_flat = gathered_branch.reshape(group_rows, model_width)
    grad_w_left = contract_rows(branch_flat, grad_left)
    grad_branch_in = contract_cols(grad_left, w_left).reshape(group_shape)
    right_rows = []
    for tap_index in range(conv_taps):
        offset = tap_index - conv_taps // 2
        moved = shifted(gathered_branch, offset).reshape(group_rows, model_width)
        right_rows.append(contract_rows(moved, grad_right))
        grad_branch_in = grad_branch_in + shifted(
            contract_cols(grad_right, w_right[tap_index]).reshape(group_shape), -offset
        )
    grad_w_right = jnp.stack(right_rows)
    grad_normed_branch = collect_rows(grad_branch_in) * valid_own[..., None]
    grad_resid, grad_gain_branch = normalize_back(
        grad_normed_branch, unit_branch, inv_branch, gain_branch
    )
    grad_one = grad_two + grad_resid
    grad_glu = lax.all_to_all(
        grad_one.astype(jnp.bfloat16), "mp", split_axis=2, concat_axis=1, tiled=True
    )
    grad_glu_flat = grad_glu.reshape(group_rows, -1).astype(jnp.float32)
    flat_glu = spread_rows(normed_glu.astype(jnp.bfloat16)).reshape(group_rows, model_width)
    value_pre = matmul(flat_glu, w_value)
    gate_sig = jax.nn.sigmoid(matmul(flat_glu, w_gate))
    grad_value = (grad_glu_flat * gate_sig).astype(jnp.bfloat16)
    grad_gate = (grad_glu_flat * value_pre * gate_sig * (1.0 - gate_sig)).astype(jnp.bfloat16)
    grad_w_value = contract_rows(flat_glu, grad_value)
    grad_w_gate = contract_rows(flat_glu, grad_gate)
    grad_glu_in = contract_cols(grad_value, w_value) + contract_cols(grad_gate, w_gate)
    grad_normed_glu = collect_rows(grad_glu_in.reshape(group_shape))
    grad_resid, grad_gain_glu = normalize_back(grad_normed_glu, unit_glu, inv_glu, gain_glu)
    grad_inputs = (grad_one + grad_resid).astype(jnp.bfloat16)
    gains = (grad_gain_glu, grad_gain_branch, grad_gain_attn, grad_gain_ffn)
    shards = (
        grad_w_value,
        grad_w_gate,
        grad_w_left,
        grad_w_right,
        grad_gain_mid,
        grad_w_depth,
        grad_w_point,
        grad_w_qkv,
        grad_w_out,
        grad_w_in,
        grad_w_back,
    )
    return (outputs, grad_inputs, gains, shards)


def local(
    inputs,
    lengths,
    gain_glu,
    w_value,
    w_gate,
    gain_branch,
    w_left,
    w_right,
    gain_mid,
    w_depth,
    w_point,
    gain_attn,
    w_qkv,
    w_out,
    gain_ffn,
    w_in,
    w_back,
    cotangent,
):
    outputs, grad_inputs, gains, shards = split_pass(
        inputs,
        lengths,
        gain_glu,
        w_value,
        w_gate,
        gain_branch,
        w_left,
        w_right,
        gain_mid,
        w_depth,
        w_point,
        gain_attn,
        w_qkv,
        w_out,
        gain_ffn,
        w_in,
        w_back,
        cotangent,
    )
    gain_totals = lax.psum((gains[0], gains[1], gains[2], gains[3]), ("dp", "mp"))
    weight_totals = (
        lax.psum(shards[0].astype(jnp.bfloat16), "dp").astype(jnp.float32),
        lax.psum(shards[1].astype(jnp.bfloat16), "dp").astype(jnp.float32),
        lax.psum(shards[2].astype(jnp.bfloat16), "dp").astype(jnp.float32),
        lax.psum(shards[3].astype(jnp.bfloat16), "dp").astype(jnp.float32),
        lax.psum(shards[4].astype(jnp.bfloat16), "dp").astype(jnp.float32),
        lax.psum(shards[5].astype(jnp.bfloat16), "dp").astype(jnp.float32),
        lax.psum(shards[6].astype(jnp.bfloat16), "dp").astype(jnp.float32),
        lax.psum(shards[7].astype(jnp.bfloat16), "dp").astype(jnp.float32),
        lax.psum(shards[8].astype(jnp.bfloat16), "dp").astype(jnp.float32),
        lax.psum(shards[9].astype(jnp.bfloat16), "dp").astype(jnp.float32),
        lax.psum(shards[10].astype(jnp.bfloat16), "dp").astype(jnp.float32),
    )
    return (
        outputs,
        grad_inputs,
        gain_totals[0],
        weight_totals[0],
        weight_totals[1],
        gain_totals[1],
        weight_totals[2],
        weight_totals[3],
        weight_totals[4],
        weight_totals[5],
        weight_totals[6],
        gain_totals[2],
        weight_totals[7],
        weight_totals[8],
        gain_totals[3],
        weight_totals[9],
        weight_totals[10],
    )


HALF = 256
LANES = 128


def dot_nn(left_side, right_side):
    return lax.dot_general(
        left_side, right_side, (((1,), (0,)), ((), ())), preferred_element_type=jnp.float32
    )


def dot_nt(left_side, right_side):
    return lax.dot_general(
        left_side, right_side, (((1,), (1,)), ((), ())), preferred_element_type=jnp.float32
    )


def dot_tn(left_side, right_side):
    return lax.dot_general(
        left_side, right_side, (((0,), (0,)), ((), ())), preferred_element_type=jnp.float32
    )


def row_stats(values):
    centre = values - jnp.mean(values, axis=-1, keepdims=True)
    inv = lax.rsqrt(jnp.mean(centre * centre, axis=-1, keepdims=True) + epsilon)
    return centre * inv, inv


def norm_grad(grad_out, unit, inv, gain):
    scaled = grad_out * gain
    mean_one = jnp.mean(scaled, axis=-1, keepdims=True)
    mean_two = jnp.mean(scaled * unit, axis=-1, keepdims=True)
    return inv * (scaled - mean_one - unit * mean_two)


def sigmoid(values):
    return 0.5 * jnp.tanh(0.5 * values) + 0.5


def silu(values):
    return values * sigmoid(values)


def turned(values):
    return jnp.transpose(values.astype(jnp.float32)).astype(jnp.bfloat16)


class Loader:
    def __init__(self, sems):
        self.sems = sems
        self.count = 0
        self.waits = []

    def start(self, source, target):
        copy = pltpu.make_async_copy(source, target, self.sems.at[self.count])
        self.count += 1
        copy.start()
        self.waits.append(copy)

    def either(self, first, second, use_first, target):
        sem = self.sems.at[self.count]
        self.count += 1

        @pl.when(use_first)
        def _():
            pltpu.make_async_copy(first, target, sem).start()

        @pl.when(jnp.logical_not(use_first))
        def _():
            pltpu.make_async_copy(second, target, sem).start()

        self.waits.append(pltpu.make_async_copy(first, target, sem))

    def wait(self):
        for copy in self.waits:
            copy.wait()
        self.waits = []


def load_pair(loader, own, got, part, taker, core, target, slots=(0, 1)):
    loader.start(own, target.at[slots[0]])
    loader.either(got, part, core == taker, target.at[slots[1]])


def load_left(loader, w_left, got, part, core, target):
    blocks = w_left.shape[1] // HALF
    rows = w_left.shape[0]
    for block in range(blocks):
        loader.start(w_left.at[:, pl.ds(block * HALF, HALF)], target.at[block])
        at = pl.ds(block * rows, rows)
        loader.either(got.at[at], part.at[at], core == 0, target.at[blocks + block])


def load_pack(loader, got, part, core, target):
    count, depth = target.shape[:2]
    for block in range(count):
        at = pl.ds(got.shape[0] - (count - block) * depth, depth)
        loader.either(got.at[at], part.at[at], core == 0, target.at[block])


def load_point(loader, w_point, got, part, core, target):
    at = pl.ds(0, w_point.shape[0])
    load_pair(loader, w_point, got.at[at], part.at[at], 1, core, target)


def load_right(loader, w_right, got, part, core, target):
    loader.start(w_right, target.at[0])
    rows = w_right.shape[1]
    for tap in range(w_right.shape[0]):
        at = (pl.ds(2 * rows + (tap // 2) * rows, rows), pl.ds((tap % 2) * LANES, LANES))
        loader.either(got.at[at], part.at[at], core == 1, target.at[1, tap])


def load_qkv(loader, w_qkv, got, part, core, target, which):
    rows = w_qkv.shape[1]
    for slot, index in enumerate(which):
        loader.start(w_qkv.at[index], target.at[0, slot])
        at = pl.ds(index * rows, rows)
        loader.either(got.at[at], part.at[at], core == 0, target.at[1, slot])


def load_out(loader, w_out, got, part, core, target):
    loader.start(w_out, target.at[0])
    rows = w_out.shape[0]
    for block in range(2):
        at = pl.ds(block * rows, rows)
        loader.either(
            got.at[at], part.at[at], core == 1, target.at[1, :, pl.ds(block * HALF, HALF)]
        )


def load_in(loader, w_in, got2, part2, got3, part3, core, target):
    blocks = w_in.shape[1] // HALF
    rows = w_in.shape[0]
    for block in range(blocks):
        loader.start(w_in.at[:, pl.ds(block * HALF, HALF)], target.at[block])
        got, part = (got2, part2) if block < 2 else (got3, part3)
        at = pl.ds(rows + (block % 2) * rows, rows)
        loader.either(got.at[at], part.at[at], core == 1, target.at[blocks + block])


def load_back(loader, w_back, got, part, core, target):
    loader.start(w_back, target.at[0])
    rows = w_back.shape[0]
    half = rows // 2
    near, far = pl.ds(0, HALF), pl.ds(HALF, HALF)
    for at, taker, spot in (
        (pl.ds(0, rows), 0, (pl.ds(0, rows), near)),
        (pl.ds(rows, half), 0, (pl.ds(0, half), far)),
        (pl.ds(0, half), 1, (pl.ds(half, half), far)),
    ):
        loader.either(got.at[at], part.at[at], core == taker, target.at[1].at[spot])


GROUP = 8


def row_spot(rows, own, lanes):
    row = lax.broadcasted_iota(jnp.int32, (rows, lanes), 0)
    spot = (row % GROUP) * (own // GROUP) + row // GROUP
    return jnp.where(row < own, spot, jnp.where(row < own + EDGE, row - own - EDGE, row - EDGE))


def row_mask(core, length, ext, lanes):
    own = ext - 2 * EDGE
    spot = row_spot(ext, own, lanes) + core * own
    return jnp.where((spot >= 0) & (spot < length), 1.0, 0.0)


def lane_tiles(width):
    return [slice(at, at + LANES) for at in range(0, width, LANES)]


def load_tiles(source, tiles):
    for index, lanes in enumerate(lane_tiles(source.shape[1])):
        tiles[index] = source[:, lanes].astype(jnp.float32)


def gather_rows(tiles, target):
    own = tiles.shape[1]
    for tile, lanes in enumerate(lane_tiles(target.shape[1])):
        for index in range(own // GROUP):
            target[index * GROUP : (index + 1) * GROUP, lanes] = tiles[
                tile, pl.ds(index, GROUP, stride=own // GROUP)
            ]


def scatter_rows(source, tiles, target):
    own = tiles.shape[1]
    for tile, lanes in enumerate(lane_tiles(target.shape[1])):
        for index in range(own // GROUP):
            tiles[tile, pl.ds(index, GROUP, stride=own // GROUP)] = source[
                index * GROUP : (index + 1) * GROUP, lanes
            ]
        target[:, lanes] = tiles[tile].astype(target.dtype)


def next_group(first, row):
    sub = lax.broadcasted_iota(jnp.int32, first.shape, 0)
    return jnp.where(sub == GROUP - 1, row, pltpu.roll(first, GROUP - 1, 0))


def previous_group(last, row):
    sub = lax.broadcasted_iota(jnp.int32, last.shape, 0)
    return jnp.where(sub == 0, row, pltpu.roll(last, 1, 0))


def shift_rows(values, offset):
    if offset == 0:
        return values
    ext = values.shape[0]
    own = ext - 2 * EDGE
    mid, before, after = values[:own], values[own : own + EDGE], values[own + EDGE :]
    sub = lax.broadcasted_iota(jnp.int32, before.shape, 0)
    if offset > 0:
        moved = jnp.concatenate([mid[GROUP:], next_group(mid[:GROUP], after[:1])], axis=0)
        before = jnp.where(sub == EDGE - 1, mid[:1], pltpu.roll(before, EDGE - 1, 0))
        after = pltpu.roll(after, EDGE - 1, 0)
    else:
        moved = jnp.concatenate(
            [previous_group(mid[own - GROUP :], before[EDGE - 1 :]), mid[: own - GROUP]], axis=0
        )
        after = jnp.where(sub == 0, mid[own - 1 :], pltpu.roll(after, 1, 0))
        before = pltpu.roll(before, 1, 0)
    return jnp.concatenate([moved, before, after], axis=0)


def fill_window(window, values, own, reach):
    before, after = values[own : own + EDGE], values[own + EDGE :]
    window[reach * GROUP : reach * GROUP + own] = values[:own]
    for step in range(1, reach + 1):
        last = values[own - step * GROUP : own - (step - 1) * GROUP]
        at = (reach - step) * GROUP
        window[at : at + GROUP] = previous_group(last, before[EDGE - step : EDGE - step + 1])
        first = values[(step - 1) * GROUP : step * GROUP]
        at = reach * GROUP + own + (step - 1) * GROUP
        window[at : at + GROUP] = next_group(first, after[step - 1 : step])


def glu_kernel(
    info, block, moved, edge, gain_glu, gain_branch, w_value, w_gate, got, part_w,
    resid_o, branch_o, gluin_o, value_o, sig_o, x_s, n_s, wv_s, wg_s, sems,
):
    core, member, length = info[0], info[1], info[2]
    loader = Loader(sems)
    load_pair(loader, w_value, got, part_w, 0, core, wv_s, (member, 1 - member))
    load_pair(loader, w_gate, got, part_w, 1, core, wg_s, (member, 1 - member))
    ext = x_s.shape[0]
    rows = ext - 2 * EDGE
    edge_f = edge[...].astype(jnp.float32)
    x_s[rows : rows + EDGE] = jnp.where(core == 1, edge_f, 0.0)
    x_s[rows + EDGE :] = jnp.where(core == 1, 0.0, edge_f)

    @pl.when(core == member)
    def _():
        load_tiles(block, n_s)

    @pl.when(core != member)
    def _():
        load_tiles(moved, n_s)

    gather_rows(n_s, x_s)
    loader.wait()
    valid = row_mask(core, length, ext, LANES)[:, :1]
    part = ext // 2
    for start in (0, part):
        at = slice(start, start + part)
        x = x_s[at]
        glu_in = (row_stats(x)[0] * gain_glu[...]).astype(jnp.bfloat16)
        gluin_o[at] = glu_in
        for half in range(2):
            cols = slice(half * HALF, (half + 1) * HALF)
            value = dot_nn(glu_in, wv_s[half])
            sig = sigmoid(dot_nn(glu_in, wg_s[half]))
            value_o[at, cols] = value.astype(jnp.bfloat16)
            sig_o[at, cols] = sig.astype(jnp.bfloat16)
            resid_o[at, cols] = x[:, cols] + (value * sig).astype(jnp.bfloat16).astype(jnp.float32)
        normed = row_stats(resid_o[at])[0] * gain_branch[...]
        branch_o[at] = (valid[at] * normed).astype(jnp.bfloat16)


def spread_block(index, size, stride):
    source = lax.broadcasted_iota(jnp.int32, (size, size), 0)
    channel = lax.broadcasted_iota(jnp.int32, (size, size), 1) + index * size
    return jnp.where(channel == source * stride, 1.0, 0.0).astype(jnp.bfloat16)


def fill_taps(pack_own, pack_oth, taps_s):
    count, cols = pack_own.shape
    taps_s[:count, :cols] = pack_own[...].astype(jnp.float32)
    for block in range(pack_oth.shape[0]):
        at = cols + block * HALF
        taps_s[:, at : at + HALF] = pack_oth[block].astype(jnp.float32)


def branch_kernel(
    info, branch, resid_one, pack_own, w_left, w_right, w_point, got, part,
    resid_two_o, left_o, right_o, stats_o, depth_o,
    wl_s, wr_s, wp_s, po_s, taps_s, mid_s, din_s, sums_s, sep_s, sems,
):
    core, length = info[0], info[2]
    loader = Loader(sems)
    load_right(loader, w_right, got, part, core, wr_s)
    load_left(loader, w_left, got, part, core, wl_s)
    load_point(loader, w_point, got, part, core, wp_s)
    load_pack(loader, got, part, core, po_s)
    ext = branch.shape[0]
    rows = ext - 2 * EDGE
    chunks = wl_s.shape[0]
    per_shard = chunks // 2
    conv_taps = wr_s.shape[1]
    sep_taps = pack_own.shape[0] - 1
    inner = chunks * HALF
    stride = inner // (2 * wr_s.shape[3])
    loader.wait()
    fill_taps(pack_own, po_s, taps_s)
    right_pre = jnp.zeros((ext, 2 * wr_s.shape[3]), jnp.float32)
    for tap in range(conv_taps):
        product = jnp.concatenate(
            [dot_nn(branch[...], wr_s[0, tap]), dot_nn(branch[...], wr_s[1, tap])], axis=1
        )
        right_pre = right_pre + shift_rows(product, tap - conv_taps // 2)
    right_o[...] = right_pre
    right_act = silu(right_pre).astype(jnp.bfloat16)
    sums_s[...] = jnp.zeros_like(sums_s)

    def first(index, carry):
        left_pre = dot_nn(branch[...], wl_s[index])
        left_o[index] = left_pre.astype(jnp.bfloat16)
        mid = silu(left_pre) + dot_nn(right_act, spread_block(index, HALF, stride))
        mid_s[index] = mid
        near, far = mid[:, :LANES], mid[:, LANES:]
        sums_s[0] += near + far
        sums_s[1] += near * near + far * far
        return carry

    lax.fori_loop(0, chunks, first, 0)
    mean = jnp.sum(sums_s[0], axis=-1, keepdims=True) / inner
    inv = lax.rsqrt(
        jnp.sum(sums_s[1], axis=-1, keepdims=True) / inner - mean * mean + epsilon
    )
    lane = lax.broadcasted_iota(jnp.int32, (ext, LANES), 1)
    stats_o[...] = jnp.where(lane == 0, mean, inv)
    sums_s[0] = jnp.broadcast_to(mean, (ext, LANES))
    sums_s[1] = inv * row_mask(core, length, ext, LANES)
    sep_s[...] = jnp.zeros_like(sep_s)

    def second(index, carry):
        cols = pl.ds(pl.multiple_of(index * HALF, HALF), HALF)
        taps = taps_s[:, cols]
        for side in range(2):
            lanes = slice(side * LANES, (side + 1) * LANES)
            depth_in = (
                (mid_s[index, :, lanes] - sums_s[0]) * sums_s[1] * taps[sep_taps : sep_taps + 1, lanes]
            )
            fill_window(din_s.at[:, lanes], depth_in, rows, sep_taps // 2)
        step = 64
        for start in range(0, rows, step):
            for side in range(2):
                lanes = slice(side * LANES, (side + 1) * LANES)
                acc = din_s[start : start + step, lanes] * taps[:1, lanes]
                for tap in range(1, sep_taps):
                    at = start + tap * GROUP
                    acc = acc + din_s[at : at + step, lanes] * taps[tap : tap + 1, lanes]
                depth_o[index, start : start + step, lanes] = acc.astype(jnp.bfloat16)
        shard, chunk = index // per_shard, index % per_shard
        point = wp_s[shard, pl.ds(pl.multiple_of(chunk * HALF, HALF), HALF)]
        sep_s[...] += dot_nn(depth_o[index], point)
        return carry

    lax.fori_loop(0, chunks, second, 0)
    sep_width = sep_s.shape[1]
    resid_two_o[:, :sep_width] = resid_one[:rows, :sep_width] + sep_s[...]
    resid_two_o[:, sep_width:] = resid_one[:rows, sep_width:]


def kv_kernel(info, resid_two, gain, w_qkv, got, part, attn_o, kv_o, w_s, sems):
    loader = Loader(sems)
    load_qkv(loader, w_qkv, got, part, info[0], w_s, (1, 2))
    attn_in = (row_stats(resid_two[...])[0] * gain[...]).astype(jnp.bfloat16)
    attn_o[...] = attn_in
    loader.wait()
    width = w_s.shape[3]
    for shard in range(2):
        for index in range(2):
            at = (2 * index + shard) * width
            kv_o[:, at : at + width] = dot_nn(attn_in, w_s[shard, index]).astype(jnp.bfloat16)


def query_kernel(info, attn_in, w_qkv, got, part, q_o, w_s, sems):
    loader = Loader(sems)
    load_qkv(loader, w_qkv, got, part, info[0], w_s, (0,))
    loader.wait()
    width = w_s.shape[3]
    scale = 1.0 / math.sqrt(HEAD_DIM)
    for shard in range(2):
        query = dot_nn(attn_in[...], w_s[shard, 0]).astype(jnp.bfloat16).astype(jnp.float32)
        q_o[:, shard * width : (shard + 1) * width] = (query * scale).astype(jnp.bfloat16)


def key_bias(core, length, rows):
    row = lax.broadcasted_iota(jnp.int32, (2 * rows, LANES), 0)
    far = jnp.where(row < rows, 0, 1)
    spot = (row % GROUP) * (rows // GROUP) + (row - far * rows) // GROUP
    spot = spot + jnp.where(core == far, 0, 1) * rows
    return jnp.where(spot < length, 0.0, negative_big)


def head_masks(rows, head):
    lane = lax.broadcasted_iota(jnp.int32, (rows, LANES), 1)
    return (lane // HEAD_DIM) == head, lane == HEAD_DIM * (1 - head)


def attend_kernel(info, q, kvo, kvf, ctx0_o, lse0_o, ctx1_o, lse1_o, bias_s):
    core, length = info[0], info[2]
    rows, width = q.shape
    pairs = width // LANES // 2
    bias_s[...] = key_bias(core, length, rows)

    def pair_step(shard, ctx_o, lse_o, local, carry):
        pair = local + shard * pairs
        cols = pl.ds(pl.multiple_of(pair * LANES, LANES), LANES)
        vcols = pl.ds(pl.multiple_of(pair * LANES + width, LANES), LANES)
        here = pl.ds(pl.multiple_of(local * LANES, LANES), LANES)
        keys = jnp.concatenate([kvo[:, cols], kvf[:, cols]], axis=0).astype(jnp.float32)
        vals = jnp.concatenate([kvo[:, vcols], kvf[:, vcols]], axis=0)
        vals_t = turned(vals)
        query = q[:, cols].astype(jnp.float32)
        outs = []
        for head in range(2):
            in_k, extra_k = head_masks(2 * rows, head)
            in_q, extra_q = head_masks(rows, head)
            km = jnp.where(in_k, keys, jnp.where(extra_k, bias_s[...], 0.0)).astype(jnp.bfloat16)
            qm = jnp.where(in_q, query, jnp.where(extra_q, 1.0, 0.0)).astype(jnp.bfloat16)
            pieces = []
            for start in range(0, rows, HALF):
                scores = dot_nt(km, qm[start : start + HALF])
                top = jnp.max(scores, axis=0, keepdims=True)
                weights = jnp.exp(scores - top)
                total = jnp.sum(weights, axis=0, keepdims=True)
                out = dot_nn(
                    vals_t[head * HEAD_DIM : (head + 1) * HEAD_DIM], weights.astype(jnp.bfloat16)
                )
                pieces.append(out / total)
                lse_o[pl.ds(local * 2 + head, 1), start : start + HALF] = top + jnp.log(total)
            outs.append(jnp.concatenate(pieces, axis=1))
        ctx_o[:, here] = jnp.transpose(jnp.concatenate(outs, axis=0)).astype(jnp.bfloat16)
        return carry

    lax.fori_loop(0, pairs, functools.partial(pair_step, 0, ctx0_o, lse0_o), 0)
    lax.fori_loop(0, pairs, functools.partial(pair_step, 1, ctx1_o, lse1_o), 0)


def ffn_kernel(
    info, resid_two, ctx0, ctx1, cot_own, cot_moved, gain, w_out, w_in, w_back, got2, part2,
    got3, part3,
    out_o, grad_three_o, gctx_o, ggain_o, send_o, keep_o,
    wo_s, wi_s, wb_s, fin_s, fint_s, cot_s, acc_s, gacc_s, ctxt_s, n_s, sems,
):
    core, member = info[0], info[1]
    loader = Loader(sems)
    load_out(loader, w_out, got2, part2, core, wo_s)
    load_in(loader, w_in, got2, part2, got3, part3, core, wi_s)
    load_back(loader, w_back, got3, part3, core, wb_s)

    @pl.when(core == member)
    def _():
        load_tiles(cot_own, n_s)

    @pl.when(core != member)
    def _():
        load_tiles(cot_moved, n_s)

    gather_rows(n_s, acc_s)
    cot_s[...] = acc_s[...].astype(jnp.bfloat16)
    loader.wait()
    part = ctx0.shape[1]
    chunks = wi_s.shape[0]
    per_shard = chunks // 2
    resid = resid_two[...] + dot_nn(ctx0[...], wo_s[0]) + dot_nn(ctx1[...], wo_s[1])
    acc_s[...] = resid
    gacc_s[...] = jnp.zeros_like(gacc_s)
    unit, inv = row_stats(resid)
    ffn_in = unit * gain[...]
    fin_s[...] = ffn_in.astype(jnp.bfloat16)
    fint_s[...] = jnp.transpose(fin_s[...].astype(jnp.float32)).astype(jnp.bfloat16)
    keep_rows = pl.ds(pl.multiple_of(core * HALF, HALF), HALF)
    send_rows = pl.ds(pl.multiple_of((1 - core) * HALF, HALF), HALF)

    def chunk_step(index, carry):
        shard, chunk = index // per_shard, index % per_shard
        rows = pl.ds(pl.multiple_of(chunk * HALF, HALF), HALF)
        into, back = wi_s[index], wb_s[shard, rows]
        pre = dot_nn(fin_s[...], into)
        sig = sigmoid(pre)
        hidden = (pre * sig).astype(jnp.bfloat16)
        acc_s[...] += dot_nn(hidden, back)
        grad_hidden = dot_nt(cot_s[...], back)
        grad_pre = (grad_hidden * (sig * (1.0 + pre * (1.0 - sig)))).astype(jnp.bfloat16)
        send_o[shard, rows] = dot_nn(fint_s[send_rows], grad_pre).astype(jnp.bfloat16)
        keep_o[shard, rows] = dot_nn(fint_s[keep_rows], grad_pre).astype(jnp.bfloat16)
        hidden_t = turned(hidden)
        base = per_shard * HALF
        rows = pl.ds(pl.multiple_of(base + chunk * HALF, HALF), HALF)
        send_o[shard, rows] = dot_nn(hidden_t, cot_s[:, send_rows]).astype(jnp.bfloat16)
        keep_o[shard, rows] = dot_nn(hidden_t, cot_s[:, keep_rows]).astype(jnp.bfloat16)
        gacc_s[...] += dot_nt(grad_pre, into)
        return carry

    lax.fori_loop(0, chunks, chunk_step, 0)
    scatter_rows(acc_s, n_s, out_o)
    unit, inv = row_stats(
        resid_two[...] + dot_nn(ctx0[...], wo_s[0]) + dot_nn(ctx1[...], wo_s[1])
    )
    grad_norm = gacc_s[...]
    ggain_o[...] = jnp.sum(grad_norm * unit, axis=0, keepdims=True)
    grad_three = cot_s[...].astype(jnp.float32) + norm_grad(grad_norm, unit, inv, gain[...])
    grad_three_o[...] = grad_three
    fin_s[...] = grad_three.astype(jnp.bfloat16)
    ctxt_s[:part] = turned(ctx0[...])
    ctxt_s[part:] = turned(ctx1[...])
    base = 2 * per_shard * HALF
    for shard in range(2):
        side = slice(shard * part, (shard + 1) * part)
        gctx_o[:, side] = dot_nt(fin_s[...], wo_s[shard]).astype(jnp.bfloat16)
        send_o[shard, base : base + part] = dot_nn(ctxt_s[side], fin_s[:, send_rows]).astype(
            jnp.bfloat16
        )
        keep_o[shard, base : base + part] = dot_nn(ctxt_s[side], fin_s[:, keep_rows]).astype(
            jnp.bfloat16
        )


def attend_back_kernel(
    shard, info, q, kvo, kvf, ctx, gctx, lse, gq_o, gown_o, gfar_o, bias_s, gk_s, gv_s
):
    core, length = info[0], info[2]
    rows, width = q.shape
    pairs = width // LANES // 2
    part = width // 2
    scale = 1.0 / math.sqrt(HEAD_DIM)
    bias_s[...] = key_bias(core, length, rows)

    def pair_step(local, carry):
        pair = local + shard * pairs
        cols = pl.ds(pl.multiple_of(pair * LANES, LANES), LANES)
        vcols = pl.ds(pl.multiple_of(pair * LANES + width, LANES), LANES)
        here = pl.ds(pl.multiple_of(local * LANES, LANES), LANES)
        vhere = pl.ds(pl.multiple_of(local * LANES + part, LANES), LANES)
        keys = jnp.concatenate([kvo[:, cols], kvf[:, cols]], axis=0).astype(jnp.float32)
        vals = jnp.concatenate([kvo[:, vcols], kvf[:, vcols]], axis=0)
        keys_t = jnp.transpose(keys).astype(jnp.bfloat16)
        query = q[:, cols].astype(jnp.float32)
        grad_out = gctx[:, cols].astype(jnp.float32)
        product_t = jnp.transpose(grad_out * ctx[:, here].astype(jnp.float32))
        gk_s[...] = jnp.zeros_like(gk_s)
        gv_s[...] = jnp.zeros_like(gv_s)
        outs = []
        for head in range(2):
            in_k, extra_k = head_masks(2 * rows, head)
            in_q, extra_q = head_masks(rows, head)
            km = jnp.where(in_k, keys, jnp.where(extra_k, bias_s[...], 0.0)).astype(jnp.bfloat16)
            qm = jnp.where(in_q, query, jnp.where(extra_q, 1.0, 0.0)).astype(jnp.bfloat16)
            qz = jnp.where(in_q, query, 0.0).astype(jnp.bfloat16)
            gz = jnp.where(in_q, grad_out, 0.0).astype(jnp.bfloat16)
            span = slice(head * HEAD_DIM, (head + 1) * HEAD_DIM)
            pieces = []
            for start in range(0, rows, HALF):
                at = slice(start, start + HALF)
                level = lse[pl.ds(local * 2 + head, 1), at]
                delta = jnp.sum(product_t[span, at], axis=0, keepdims=True)
                soft = jnp.exp(dot_nt(km, qm[at]) - level)
                gv_s[...] += dot_nn(soft.astype(jnp.bfloat16), gz[at])
                grad_scores = (soft * (dot_nt(vals, gz[at]) - delta)).astype(jnp.bfloat16)
                gk_s[...] += dot_nn(grad_scores, qz[at])
                pieces.append(dot_nn(keys_t[span], grad_scores))
            outs.append(jnp.concatenate(pieces, axis=1))
        gq_o[:, here] = (jnp.transpose(jnp.concatenate(outs, axis=0)) * scale).astype(jnp.bfloat16)
        gown_o[:, here] = gk_s[:rows]
        gown_o[:, vhere] = gv_s[:rows]
        gfar_o[:, here] = gk_s[rows:].astype(jnp.bfloat16)
        gfar_o[:, vhere] = gv_s[rows:].astype(jnp.bfloat16)
        return carry

    lax.fori_loop(0, pairs, pair_step, 0)


def qkv_part(shard, core, gq, gown, gfar, attn_in, w_s, attnt_s, send_o, keep_o):
    attnt_s[...] = turned(attn_in[...])
    width = w_s.shape[3]
    keep_rows = pl.ds(pl.multiple_of(core * HALF, HALF), HALF)
    send_rows = pl.ds(pl.multiple_of((1 - core) * HALF, HALF), HALF)
    both = (gown[...] + gfar[...].astype(jnp.float32)).astype(jnp.bfloat16)
    grad_in = None
    for index, grad in enumerate((gq[...], both[:, :width], both[:, width:])):
        at = slice(index * HALF, (index + 1) * HALF)
        send_o[at] = dot_nn(attnt_s[send_rows], grad).astype(jnp.bfloat16)
        keep_o[at] = dot_nn(attnt_s[keep_rows], grad).astype(jnp.bfloat16)
        term = dot_nt(grad, w_s[shard, index])
        grad_in = term if grad_in is None else grad_in + term
    return grad_in


def qkv_back_first(
    info, gq, gown, gfar, attn_in, w_qkv, got, part, grad_o, send_o, keep_o, w_s, attnt_s, sems
):
    loader = Loader(sems)
    load_qkv(loader, w_qkv, got, part, info[0], w_s, (0, 1, 2))
    loader.wait()
    grad_o[...] = qkv_part(1, info[0], gq, gown, gfar, attn_in, w_s, attnt_s, send_o, keep_o)


def qkv_back_second(
    info, gq, gown, gfar, attn_in, grad_part, resid_two, grad_three, gain, w_qkv, got, part,
    grad_two_o, gsep_o, gedge_o, ggain_o, send_o, keep_o, w_s, attnt_s, n_s, sems,
):
    loader = Loader(sems)
    load_qkv(loader, w_qkv, got, part, info[0], w_s, (0, 1, 2))
    loader.wait()
    grad_in = grad_part[...] + qkv_part(
        0, info[0], gq, gown, gfar, attn_in, w_s, attnt_s, send_o, keep_o
    )
    unit, inv = row_stats(resid_two[...])
    ggain_o[...] = jnp.sum(grad_in * unit, axis=0, keepdims=True)
    grad_two = grad_three[...] + norm_grad(grad_in, unit, inv, gain[...])
    grad_two_o[...] = grad_two
    gsep_o[...] = grad_two[:, : gsep_o.shape[1]].astype(jnp.bfloat16)
    rows = n_s.shape[1]
    for tile, lanes in enumerate(lane_tiles(gsep_o.shape[1])):
        n_s[tile] = grad_two[:, lanes]
        first = n_s[tile, pl.ds(0, EDGE, stride=GROUP)]
        last = n_s[tile, pl.ds(rows - EDGE * GROUP + GROUP - 1, EDGE, stride=GROUP)]
        gedge_o[:, lanes] = jnp.where(info[0] == 0, last, first).astype(jnp.bfloat16)


def point_kernel(info, gsep, depth, send0, keep0, send1, keep1, send_o, keep_o):
    core = info[0]
    grad_sep = gsep[...]
    per_shard = depth.shape[0] // 2
    per_core = per_shard // 2
    base = send0.shape[0]
    for shard, (send, keep) in enumerate(((send0, keep0), (send1, keep1))):
        send_o[shard, :base] = send[...]
        keep_o[shard, :base] = keep[...]
        for chunk in range(per_core):
            at = slice(base + chunk * HALF, base + (chunk + 1) * HALF)
            first = shard * per_shard
            send_o[shard, at] = dot_tn(
                depth[first + (1 - core) * per_core + chunk], grad_sep
            ).astype(jnp.bfloat16)
            keep_o[shard, at] = dot_tn(
                depth[first + core * per_core + chunk], grad_sep
            ).astype(jnp.bfloat16)


def as_f32(values):
    return values.astype(jnp.float32)


def slope_of(values):
    sig = sigmoid(values)
    return sig * (1.0 + values * (1.0 - sig))


def depth_back_kernel(
    info, gsep, gedge, left_pre, right_pre, stats, pack_own, w_point, got, part,
    unit_o, scaled_o, sums_s, small_s,
    wp_s, po_s, taps_s, gse_s, gd_s, din_s, near_s, unit_s, scaled_s, wide_s, sems,
):
    core, length = info[0], info[2]
    loader = Loader(sems)
    load_point(loader, w_point, got, part, core, wp_s)
    load_pack(loader, got, part, core, po_s)
    ext = left_pre.shape[1]
    rows = ext - 2 * EDGE
    chunks = left_pre.shape[0]
    per_shard = chunks // 2
    inner = chunks * HALF
    sep_taps = pack_own.shape[0] - 1
    right_cols = right_pre.shape[1]
    stride = inner // right_cols
    reach = sep_taps // 2
    edge = gedge[...].astype(jnp.float32)
    gse_s[:rows] = gsep[...]
    gse_s[rows : rows + EDGE] = jnp.where(core == 1, edge, 0.0).astype(jnp.bfloat16)
    gse_s[rows + EDGE :] = jnp.where(core == 1, 0.0, edge).astype(jnp.bfloat16)
    wide_s[0] = row_mask(core, length, ext, LANES)
    wide_s[1] = jnp.broadcast_to(stats[:, 0:1], (ext, LANES))
    wide_s[2] = jnp.broadcast_to(stats[:, 1:2], (ext, LANES))
    scaled_s[...] = jnp.zeros_like(scaled_s)
    sums_s[...] = jnp.zeros_like(sums_s)
    small_s[...] = jnp.zeros_like(small_s)
    right_act = silu(right_pre[...]).astype(jnp.bfloat16)
    loader.wait()
    fill_taps(pack_own, po_s, taps_s)

    def first(index, carry):
        cols = pl.ds(pl.multiple_of(index * HALF, HALF), HALF)
        taps = taps_s[:, cols]
        shard, chunk = index // per_shard, index % per_shard
        point = wp_s[shard, pl.ds(pl.multiple_of(chunk * HALF, HALF), HALF)]
        grad_depth = dot_nt(gse_s[...], point)
        for side, lanes in enumerate(lane_tiles(HALF)):
            fill_window(gd_s.at[side], grad_depth[:, lanes], rows, reach)
            near_s[side, :EDGE] = grad_depth[rows : rows + EDGE, lanes]
            near_s[side, 3 * EDGE :] = grad_depth[rows + EDGE :, lanes]
            base = reach * GROUP
            near_s[side, EDGE : 2 * EDGE] = gd_s[side, pl.ds(base, EDGE, stride=GROUP)]
            base = reach * GROUP + rows - EDGE * GROUP + GROUP - 1
            near_s[side, 2 * EDGE : 3 * EDGE] = gd_s[side, pl.ds(base, EDGE, stride=GROUP)]
        mid = silu(left_pre[index].astype(jnp.float32)) + dot_nn(
            right_act, spread_block(index, HALF, stride)
        )
        for side in range(2):
            lanes = slice(side * LANES, (side + 1) * LANES)
            unit = (mid[:, lanes] - wide_s[1]) * wide_s[2]
            unit_s[:, lanes] = unit
            fill_window(
                din_s.at[side],
                unit * wide_s[0] * taps[sep_taps : sep_taps + 1, lanes],
                rows,
                reach,
            )
            for base, target in ((EDGE - GROUP, rows + EDGE - GROUP), (3 * EDGE, rows + EDGE)):
                acc = near_s[side, base + reach : base + reach + GROUP] * taps[:1, lanes]
                for tap in range(1, sep_taps):
                    at = base + reach - tap
                    acc = acc + near_s[side, at : at + GROUP] * taps[tap : tap + 1, lanes]
                at = slice(target, target + GROUP)
                scaled_s[at, lanes] = acc * wide_s[0, at]
        step = 64
        tap_sums = []
        for side in range(2):
            lanes = slice(side * LANES, (side + 1) * LANES)
            sums = [jnp.zeros((GROUP, LANES), jnp.float32) for _ in range(sep_taps)]
            for start in range(0, rows, step):
                at = start + 2 * reach * GROUP
                acc = gd_s[side, at : at + step] * taps[:1, lanes]
                for tap in range(1, sep_taps):
                    at = start + (2 * reach - tap) * GROUP
                    acc = acc + gd_s[side, at : at + step] * taps[tap : tap + 1, lanes]
                scaled_s[start : start + step, lanes] = acc * wide_s[0, start : start + step]
                at = start + reach * GROUP
                grad = gd_s[side, at : at + step]
                for tap in range(sep_taps):
                    at = start + tap * GROUP
                    term = din_s[side, at : at + step] * grad
                    sums[tap] = sums[tap] + jnp.sum(
                        term.reshape(step // GROUP, GROUP, LANES), axis=0
                    )
            tap_sums.append(sums)
        tap_sums = [jnp.concatenate(pair, axis=1) for pair in zip(*tap_sums)]
        tap_rows = [jnp.sum(value, axis=0, keepdims=True) for value in tap_sums]
        gain = taps[sep_taps : sep_taps + 1]
        gain_row = jnp.sum(
            scaled_s[:rows] * unit_s[:rows],
            axis=0,
            keepdims=True,
        )
        filler = jnp.zeros((small_s.shape[0] - sep_taps - 1, HALF), jnp.float32)
        small_s[:, cols] = jnp.concatenate(tap_rows + [gain_row, filler], axis=0)
        scaled = scaled_s[...] * gain
        scaled_o[index] = scaled.astype(jnp.bfloat16)
        unit_o[index] = unit_s[...].astype(jnp.bfloat16)
        near, far = scaled[:, :LANES], scaled[:, LANES:]
        sums_s[0] += near + far
        sums_s[1] += near * unit_s[:, :LANES] + far * unit_s[:, LANES:]
        return carry

    lax.fori_loop(0, chunks, first, 0)


def branch_back_kernel(
    info, unit, scaled, sums, small, left_pre, right_pre, stats, branch, gain_ffn_g, gain_attn_g,
    gleft_o, gright_o, send_o, keep_o,
    wide_s, gra_s, bt_s,
):
    core = info[0]
    ext = left_pre.shape[1]
    rows = ext - 2 * EDGE
    chunks = left_pre.shape[0]
    per_shard = chunks // 2
    inner = chunks * HALF
    right_cols = right_pre.shape[1]
    stride = inner // right_cols
    for index in range(2):
        mean = jnp.sum(sums[index], axis=-1, keepdims=True) / inner
        wide_s[index] = jnp.broadcast_to(mean, (ext, LANES))
    wide_s[2] = jnp.broadcast_to(stats[:, 1:2], (ext, LANES))
    gra_s[...] = jnp.zeros_like(gra_s)
    bt_s[...] = turned(branch[...])
    keep_rows = pl.ds(pl.multiple_of(core * HALF, HALF), HALF)
    send_rows = pl.ds(pl.multiple_of((1 - core) * HALF, HALF), HALF)

    def second(index, carry):
        shard, chunk = index // per_shard, index % per_shard
        sides = []
        for side in range(2):
            lanes = slice(side * LANES, (side + 1) * LANES)
            sides.append(
                wide_s[2]
                * (as_f32(scaled[index, :, lanes]) - wide_s[0] - as_f32(unit[index, :, lanes]) * wide_s[1])
            )
        grad_mid = jnp.concatenate(sides, axis=1)
        grad_left = (
            grad_mid[:rows] * slope_of(left_pre[index, :rows].astype(jnp.float32))
        ).astype(jnp.bfloat16)
        gleft_o[index] = grad_left
        gra_s[...] += dot_nt(grad_mid.astype(jnp.bfloat16), spread_block(index, HALF, stride))
        at = pl.ds(pl.multiple_of(chunk * HALF, HALF), HALF)
        send_o[shard, at] = dot_nn(bt_s[send_rows, :rows], grad_left).astype(
            jnp.bfloat16
        )
        keep_o[shard, at] = dot_nn(bt_s[keep_rows, :rows], grad_left).astype(
            jnp.bfloat16
        )
        return carry

    lax.fori_loop(0, chunks, second, 0)
    grad_right = gra_s[...] * slope_of(right_pre[...])
    gright_o[...] = grad_right.astype(jnp.bfloat16)
    spot = lax.broadcasted_iota(jnp.int32, grad_right.shape, 0)
    own_right = jnp.where(spot < rows, grad_right, 0.0)
    part = right_cols // 2
    base = per_shard * HALF
    for target, picked, side in ((send_o, send_rows, 1 - core), (keep_o, keep_rows, core)):
        taps3 = []
        for tap in range(3):
            moved = shift_rows(own_right, 1 - tap).astype(jnp.bfloat16)
            taps3.append(dot_nn(bt_s[picked, :], moved).astype(jnp.bfloat16))
        for shard in range(2):
            cols = slice(shard * part, (shard + 1) * part)
            target[shard, base : base + HALF, :part] = taps3[0][:, cols]
            target[shard, base : base + HALF, part:] = taps3[1][:, cols]
            target[shard, base + HALF : base + 2 * HALF, :part] = taps3[2][:, cols]
            target[shard, base + HALF : base + 2 * HALF, part:] = jnp.zeros(
                (HALF, part), jnp.bfloat16
            )
            cols_here = inner // 4
            for piece in range(cols_here // LANES):
                lanes = pl.ds(
                    pl.multiple_of(
                        shard * (inner // 2) + side * cols_here + piece * LANES, LANES
                    ),
                    LANES,
                )
                row = base + HALF + piece * 16
                target[shard, row : row + 16, part:] = small[:, lanes].astype(jnp.bfloat16)
            row = base + HALF + 4 * 16
            for piece in range(4):
                lanes = slice(piece * LANES, (piece + 1) * LANES)
                both = jnp.concatenate(
                    [gain_ffn_g[:, lanes], gain_attn_g[:, lanes], jnp.zeros((14, LANES), jnp.float32)],
                    axis=0,
                )
                target[shard, row : row + 16, part:] = both.astype(jnp.bfloat16)
                row += 16


def join_back_kernel(
    info, gleft, gright, resid_one, grad_two, gain_branch, w_left, w_right, got, part_w,
    grad_one_o, ggain_o, wl_s, wr_s, sems,
):
    core, length = info[0], info[2]
    loader = Loader(sems)
    load_left(loader, w_left, got, part_w, core, wl_s)
    load_right(loader, w_right, got, part_w, core, wr_s)
    ext = gright.shape[0]
    rows = ext - 2 * EDGE
    own = slice(0, rows)
    loader.wait()
    grad_in = jnp.zeros((rows, resid_one.shape[1]), jnp.float32)
    for index in range(wl_s.shape[0]):
        grad_in = grad_in + dot_nt(gleft[index], wl_s[index])
    part = wr_s.shape[3]
    for tap in range(wr_s.shape[1]):
        product = dot_nt(gright[:, :part], wr_s[0, tap]) + dot_nt(gright[:, part:], wr_s[1, tap])
        grad_in = grad_in + shift_rows(product, 1 - tap)[own]
    grad_in = grad_in * row_mask(core, length, ext, LANES)[own, :1]
    unit, inv = row_stats(resid_one[own])
    ggain_o[...] = jnp.sum(grad_in * unit, axis=0, keepdims=True)
    grad_one_o[...] = grad_two[...] + norm_grad(grad_in, unit, inv, gain_branch[...])


def glu_back_kernel(
    info, grad_one, gain_branch_row, gain_glu, block, moved, glu_in, value, sig, w_value, w_gate,
    got, part_w,
    gin_o, send_o, keep_o,
    wv_s, wg_s, x_s, n_s, git_s, sems,
):
    core, member = info[0], info[1]
    loader = Loader(sems)
    load_pair(loader, w_value, got, part_w, 0, core, wv_s, (member, 1 - member))
    load_pair(loader, w_gate, got, part_w, 1, core, wg_s, (member, 1 - member))
    rows = grad_one.shape[0]
    own = slice(0, rows)

    @pl.when(core == member)
    def _():
        load_tiles(block, n_s)

    @pl.when(core != member)
    def _():
        load_tiles(moved, n_s)

    gather_rows(n_s, x_s)
    git_s[...] = turned(glu_in[own])
    loader.wait()
    grad_glu = grad_one[...].astype(jnp.bfloat16).astype(jnp.float32)
    keep_rows = pl.ds(pl.multiple_of(core * HALF, HALF), HALF)
    send_rows = pl.ds(pl.multiple_of((1 - core) * HALF, HALF), HALF)
    grad_norm = jnp.zeros(grad_one.shape, jnp.float32)
    for half in range(2):
        cols = slice(half * HALF, (half + 1) * HALF)
        sig_f = sig[own, cols].astype(jnp.float32)
        grad_here = grad_glu[:, cols] * sig_f
        grad_value = grad_here.astype(jnp.bfloat16)
        grad_gate = (grad_here * value[own, cols].astype(jnp.float32) * (1.0 - sig_f)).astype(
            jnp.bfloat16
        )
        slot = jnp.where(member == half, 0, 1)
        send_o[slot, :HALF] = dot_nn(git_s[send_rows], grad_value).astype(jnp.bfloat16)
        keep_o[slot, :HALF] = dot_nn(git_s[keep_rows], grad_value).astype(jnp.bfloat16)
        send_o[slot, HALF : 2 * HALF] = dot_nn(git_s[send_rows], grad_gate).astype(jnp.bfloat16)
        keep_o[slot, HALF : 2 * HALF] = dot_nn(git_s[keep_rows], grad_gate).astype(jnp.bfloat16)
        grad_norm = grad_norm + dot_nt(grad_value, wv_s[half]) + dot_nt(grad_gate, wg_s[half])
    unit, inv = row_stats(x_s[...])
    gain_glu_row = jnp.sum(grad_norm * unit, axis=0, keepdims=True)
    x_s[...] = grad_one[...] + norm_grad(grad_norm, unit, inv, gain_glu[...])
    scatter_rows(x_s, n_s, gin_o)
    tail = send_o.shape[1] - 2 * HALF
    both = jnp.concatenate(
        [gain_glu_row, gain_branch_row[...], jnp.zeros((14, 2 * HALF), jnp.float32)], axis=0
    )
    both = both.astype(jnp.bfloat16)
    for target in (send_o, keep_o):
        for shard in range(2):
            target[shard, 2 * HALF :] = jnp.zeros((tail, HALF), jnp.bfloat16)
            target[shard, 2 * HALF : 2 * HALF + 16] = both[:, :HALF]
            target[shard, 2 * HALF + 16 : 2 * HALF + 32] = both[:, HALF:]


def over_mp(values):
    return lax.ppermute(values, "mp", [(0, 1), (1, 0)])


def flat_pairs(dp_size, rule):
    pairs = []
    for dp_index in range(dp_size):
        for member in range(2):
            pair, core = dp_index // 2, dp_index % 2
            new_core, new_member = rule(core, member)
            pairs.append((dp_index * 2 + member, (pair * 2 + new_core) * 2 + new_member))
    return pairs


def unpack_kernel(layout, halves, info, both, far, *rest):
    outs, packed, sems = rest[:-2], rest[-2], rest[-1]
    core, ybit, zpos = info[0], info[3], info[4]
    ys, zs, step = both.shape[0], 4, both.shape[3]
    loader = Loader(sems)
    for half in range(2):
        for yside in range(ys):
            for zside in range(zs):
                at = (yside ^ ybit, zside // 2 ^ zpos % 2, zside % 2 ^ zpos // 2)
                first, base = 0, 0
                for size in halves:
                    low = max(first, zside * step)
                    top = min(first + size, (zside + 1) * step)
                    if low < top:
                        source = pl.ds(low - zside * step, top - low)
                        target = packed.at[
                            half, pl.ds(base + yside * size + low - first, top - low)
                        ]
                        loader.either(
                            both.at[at].at[source], far.at[at].at[source], core == half, target
                        )
                    first += size
                    base += 2 * size
    loader.wait()
    layout(packed, outs)


def layout_early(packed, outs):
    layout_attn(packed, outs[:2])
    w_in, w_back, w_out = outs[2:]
    blocks = w_in.shape[1] // HALF
    first = 5 * HALF
    base = first + blocks * HALF
    for half in range(2):
        side = slice(half * HALF, (half + 1) * HALF)
        for block in range(blocks):
            at = first + block * HALF
            w_in[side, block * HALF : (block + 1) * HALF] = as_f32(packed[half, at : at + HALF])
        w_back[:, side] = as_f32(packed[half, base : base + w_back.shape[0]])
        last = base + w_back.shape[0]
        w_out[:, side] = as_f32(packed[half, last : last + w_out.shape[0]])


def layout_attn(packed, outs):
    w_qkv, w_point = outs
    for half in range(2):
        for index in range(3):
            w_qkv[index, half * HALF : (half + 1) * HALF] = as_f32(
                packed[half, index * HALF : (index + 1) * HALF]
            )
        w_point[half * 2 * HALF : (half + 1) * 2 * HALF] = as_f32(
            packed[half, 3 * HALF : 5 * HALF]
        )


def layout_branch(packed, outs):
    w_left, w_right, pack, gains = outs
    blocks = w_left.shape[1] // HALF
    base = blocks * HALF
    for half in range(2):
        side = slice(half * HALF, (half + 1) * HALF)
        for block in range(blocks):
            w_left[side, block * HALF : (block + 1) * HALF] = as_f32(
                packed[half, block * HALF : (block + 1) * HALF]
            )
        w_right[0, side] = as_f32(packed[half, base : base + HALF, :LANES])
        w_right[1, side] = as_f32(packed[half, base : base + HALF, LANES:])
        w_right[2, side] = as_f32(packed[half, base + HALF : base + 2 * HALF, :LANES])
        for piece in range(4):
            row = base + HALF + piece * 16
            at = half * 4 * LANES + piece * LANES
            pack[:, at : at + LANES] = as_f32(packed[half, row : row + 16, LANES:])
            row += 4 * 16
            gains[:, piece * LANES : (piece + 1) * LANES] = as_f32(
                packed[half, row : row + 16, LANES:]
            )


def layout_glu(packed, outs):
    w_value, w_gate, gains = outs
    for half in range(2):
        side = slice(half * HALF, (half + 1) * HALF)
        w_value[side] = as_f32(packed[half, :HALF])
        w_gate[side] = as_f32(packed[half, HALF : 2 * HALF])
        gains[:, side] = as_f32(packed[0, 2 * HALF + 16 * half : 2 * HALF + 16 * (half + 1)])


VMEM_LIMIT = 56 * 1024 * 1024


def call(body, name, ins, outs, scratch, flops, copies=0):
    spaces = {"s": pltpu.SMEM, "v": pltpu.VMEM, "h": pl.ANY}
    shapes = [jax.ShapeDtypeStruct(shape, dtype) for shape, dtype in outs]
    scratch = [pltpu.VMEM(shape, dtype) for shape, dtype in scratch]
    if copies:
        scratch.append(pltpu.SemaphoreType.DMA((copies,)))
    return pl.pallas_call(
        body,
        out_shape=shapes,
        in_specs=[pl.BlockSpec(memory_space=spaces[place]) for _, place in ins],
        out_specs=[pl.BlockSpec(memory_space=pltpu.VMEM) for _ in shapes],
        scratch_shapes=scratch,
        name=name,
        compiler_params=pltpu.CompilerParams(vmem_limit_bytes=VMEM_LIMIT),
        cost_estimate=pl.CostEstimate(flops=10**10, bytes_accessed=10**6, transcendentals=0),
    )(*[array for array, _ in ins])


def dp_xor(values, bits):
    size = lax.axis_size("dp")
    return lax.ppermute(values, "dp", [(index, index ^ bits) for index in range(size)])


def over_x_and_y(values):
    pairs = []
    for dp_index in range(lax.axis_size("dp")):
        for member in range(2):
            pairs.append((dp_index * 2 + member, (dp_index ^ 2) * 2 + 1 - member))
    return lax.ppermute(values, ("dp", "mp"), pairs)


def in_blocks(values):
    return [values[:, at : at + HALF] for at in range(0, values.shape[1], HALF)]


def bundle_branch(core, w_left, w_right, w_point, pack):
    depth = 16
    pack = jnp.pad(pack, ((0, depth - pack.shape[0]), (0, 0)))
    first = jnp.concatenate(in_blocks(w_left) + in_blocks(pack), axis=0)
    blank = jnp.zeros_like(w_right[0])
    second = [
        w_point,
        jnp.concatenate([w_right[0], w_right[1]], axis=1),
        jnp.concatenate([w_right[2], blank], axis=1),
        jnp.zeros((first.shape[0] - w_point.shape[0] - 2 * blank.shape[0], HALF), first.dtype),
    ]
    return jnp.where(core == 0, first, jnp.concatenate(second, axis=0))


def bundle_attn(core, w_qkv, w_out, w_in):
    first = w_qkv.reshape(-1, HALF)
    return jnp.where(core == 0, first, jnp.concatenate(in_blocks(w_out) + in_blocks(w_in)[:2], axis=0))


def bundle_ffn(core, w_in, w_back):
    half = w_back.shape[0] // 2
    near, far = in_blocks(w_back)
    first = jnp.concatenate([near, far[:half]], axis=0)
    return jnp.where(core == 0, first, jnp.concatenate([far[half:]] + in_blocks(w_in)[2:], axis=0))


def later(values, *first):
    return lax.optimization_barrier((values, first))[0]


class Sums:
    def __init__(self, send, keep, ybit):
        self.keep, self.ybit = keep, ybit
        self.recv = dp_xor(send, 1)

    def over_xy(self, *first):
        recv, keep = later((self.recv, self.keep), *first)
        half = keep.shape[1] // 2

        def piece(shard, bit):
            at = bit * half
            cut = lambda values: as_f32(lax.dynamic_slice_in_dim(values[shard], at, half, axis=0))
            return (cut(keep) + cut(recv)).astype(jnp.bfloat16)

        self.kept = piece(0, self.ybit)
        gone = [piece(1, self.ybit), piece(0, 1 - self.ybit), piece(1, 1 - self.ybit)]
        self.got = [over_mp(gone[0]), dp_xor(gone[1], 2), over_x_and_y(gone[2])]
        return gone

    def quarter(self, *first):
        got, kept = later((self.got, self.kept), *first)
        total = as_f32(kept) + as_f32(got[1]) + (as_f32(got[0]) + as_f32(got[2]))
        return total.astype(jnp.bfloat16)


class Rest:
    def __init__(self, quarters, zpos):
        self.quarters, self.zpos = quarters, zpos

    def over_z1(self, *first):
        mine = jnp.concatenate(later(self.quarters, *first), axis=0)
        return self.halve(mine, self.zpos % 2, 4)

    def over_z2(self, *first):
        got, kept = later((self.got, self.kept), *first)
        mine = (as_f32(kept) + as_f32(got)).astype(jnp.bfloat16)
        return self.halve(mine, self.zpos // 2, 8)

    def halve(self, mine, bit, across):
        half = mine.shape[0] // 2
        self.kept = lax.dynamic_slice_in_dim(mine, bit * half, half, axis=0)
        gone = lax.dynamic_slice_in_dim(mine, (1 - bit) * half, half, axis=0)
        self.got = dp_xor(gone, across)
        return [gone]

    def back_z2(self, *first):
        got, kept = later((self.got, self.kept), *first)
        self.mine = (as_f32(kept) + as_f32(got)).astype(jnp.bfloat16)
        self.got = dp_xor(self.mine, 8)
        return [self.mine]

    def back_z1(self, *first):
        return self.double(4, *first)

    def double(self, across, *first):
        got, mine = later((self.got, self.mine), *first)
        self.mine = jnp.stack([mine, got])
        self.got = dp_xor(self.mine, across)
        return [self.mine]

    def back_y(self, *first):
        return self.double(2, *first)

    def back_core(self, *first):
        self.got, mine = later((self.got, self.mine), *first)
        self.both = jnp.stack([mine, self.got])
        self.far = dp_xor(self.both, 1)
        return [self.both]


def unpack(layout, info, sums, outs):
    ys, zs, part, cols = 2, 4, *sums.both.shape[3:]
    halves = [quarter.shape[0] for quarter in sums.quarters]
    return call(
        functools.partial(unpack_kernel, layout, halves),
        "unpack_" + layout.__name__,
        [(info, "s"), (sums.both, "h"), (sums.far, "h")],
        [(shape, jnp.float32) for shape in outs],
        [((2, ys * zs * part, cols), jnp.bfloat16)],
        1e6,
        2 * ys * (zs + len(halves)),
    )


def paired(
    inputs, lengths, gain_glu, w_value, w_gate, gain_branch, w_left, w_right, gain_mid, w_depth,
    w_point, gain_attn, w_qkv, w_out, gain_ffn, w_in, w_back, cotangent,
):
    low, full = jnp.bfloat16, jnp.float32
    member = lax.axis_index("mp")
    place = lax.axis_index("dp")
    core, ybit, zpos = place % 2, (place // 2) % 2, place // 4
    rows, width = inputs.shape[1:]
    ext = rows + 2 * EDGE
    inner = 2 * w_left.shape[1]
    chunks = inner // HALF
    right_cols = 2 * w_right.shape[2]
    sep_width = w_point.shape[1]
    heads = 2 * w_qkv.shape[2] // HEAD_DIM
    row = lambda gain: gain.reshape(1, -1)

    block = inputs[0]
    edge = jnp.where(member == 0, block[rows - EDGE :], block[:EDGE])
    size_code = jnp.stack([lengths[0] // 32, lengths[0] % 32]).astype(low)
    code_rows = jnp.broadcast_to(jnp.repeat(size_code, EDGE // 2)[:, None], (EDGE, width))
    edge = jnp.concatenate([edge, code_rows], axis=0)
    edge = lax.ppermute(
        edge, ("dp", "mp"), flat_pairs(lax.axis_size("dp"), lambda c, m: (1 - m, c))
    )
    code = as_f32(edge[EDGE:, 0])
    length = (code[0] * 32 + code[EDGE // 2]).astype(jnp.int32)
    edge = edge[:EDGE]
    swap = [p for p in flat_pairs(lax.axis_size("dp"), lambda c, m: (m, c)) if p[0] != p[1]]
    moved = lax.ppermute(block, ("dp", "mp"), swap)
    info = jnp.stack([core, member, length, ybit, zpos]).astype(jnp.int32)

    pack = jnp.concatenate([w_depth, gain_mid[None]], axis=0)
    got0 = over_mp(jnp.where(core == 0, w_value, w_gate))
    bundle = later(
        bundle_branch(core, w_left, w_right, w_point, pack), edge
    )
    got1 = over_mp(bundle)
    part0 = dp_xor(later(got0, bundle), 1)
    got2 = over_mp(later(bundle_attn(core, w_qkv, w_out, w_in), got0, moved))
    cot = cotangent[0]
    cot_moved = lax.ppermute(later(cot, got0, moved), ("dp", "mp"), swap)

    v = lambda *arrays: [(array, "v") for array in arrays]
    h = lambda *arrays: [(array, "h") for array in arrays]
    where = [(info, "s")]
    macs = 2.0 * rows * width
    resid_one, branch_in, glu_in, value, sig = call(
        glu_kernel, "glu",
        where + v(block, moved, edge, row(gain_glu), row(gain_branch))
        + h(w_value, w_gate, got0, part0),
        [((ext, width), full)] + [((ext, width), low)] * 4,
        [((ext, width), full), ((width // LANES, rows, LANES), full)]
        + [((2,) + w_value.shape, low)] * 2,
        macs * width * 2, 8,
    )
    got1 = later(got1, glu_in)
    part1 = dp_xor(got1, 1)
    got2 = later(got2, got1)
    part2 = dp_xor(got2, 1)
    got3 = over_mp(later(bundle_ffn(core, w_in, w_back), got1))
    resid_two, left_pre, right_pre, stats, depth = call(
        branch_kernel, "branch",
        where + v(branch_in, resid_one, pack) + h(w_left, w_right, w_point, got1, part1),
        [
            ((rows, width), full), ((chunks, ext, HALF), low), ((ext, right_cols), full),
            ((ext, LANES), full), ((chunks, rows, HALF), low),
        ],
        [
            ((chunks, width, HALF), low), ((2,) + w_right.shape, low), ((2,) + w_point.shape, low),
            ((4, 16, HALF), low), ((16, inner), full), ((chunks, ext, HALF), full),
            ((rows + 64, HALF), full),
            ((2, ext, LANES), full), ((rows, sep_width), full),
        ],
        macs * 8000, 20,
    )
    attn_in, kv_own = call(
        kv_kernel, "keys_values",
        where + v(resid_two, row(gain_attn)) + h(w_qkv, got2, part2),
        [((rows, width), low), ((rows, 2 * width), low)],
        [((2, 2) + w_qkv.shape[1:], low)],
        macs * width * 2, 8,
    )
    (queries,) = call(
        query_kernel, "queries",
        where + v(attn_in) + h(w_qkv, got2, part2),
        [((rows, width), low)],
        [((2, 1) + w_qkv.shape[1:], low)],
        macs * width, 4,
    )
    kv_far = dp_xor(kv_own, 1)
    context0, lse0, context1, lse1 = call(
        attend_kernel, "attend",
        [(later(info, cot_moved), "s")] + v(queries, kv_own, kv_far),
        [((rows, width // 2), low), ((heads // 2, rows), full)] * 2,
        [((2 * rows, LANES), full)],
        macs * 8000,
    )
    part3 = dp_xor(later(got3, lse1), 1)
    r_ffn = 2 * w_in.shape[1] + w_out.shape[0]
    out_rows, grad_three, grad_ctx, ggain_ffn, send, keep = call(
        ffn_kernel, "ffn",
        where + v(resid_two, context0, context1, cot, cot_moved, row(gain_ffn))
        + h(w_out, w_in, w_back, got2, part2, got3, part3),
        [
            ((rows, width), low), ((rows, width), full), ((rows, width), low), ((1, width), full),
            ((2, r_ffn, HALF), low), ((2, r_ffn, HALF), low),
        ],
        [
            ((2,) + w_out.shape, low), ((chunks, width, HALF), low), ((2,) + w_back.shape, low),
            ((rows, width), low), ((width, rows), low), ((rows, width), low), ((rows, width), full),
            ((rows, width), full), ((width, rows), low), ((width // LANES, rows, LANES), full),
        ],
        macs * 16000, 24,
    )
    ffn_sums = Sums(send, keep, ybit)
    swapped_out = lax.ppermute(out_rows, ("dp", "mp"), swap)

    def attend_back(shard, info, context, lse):
        return call(
            functools.partial(attend_back_kernel, shard), "attend_back",
            [(info, "s")] + v(queries, kv_own, kv_far, context, grad_ctx, lse),
            [((rows, width // 2), low), ((rows, width), full), ((rows, width), low)],
            [((2 * rows, LANES), full)] * 3,
            macs * 10000,
        )

    grad_q1, grad_own1, grad_far1 = attend_back(1, info, context1, lse1)
    recv1 = dp_xor(grad_far1, 1)
    sent = ffn_sums.over_xy(grad_q1)
    grad_q0, grad_own0, grad_far0 = attend_back(0, later(info, *sent), context0, lse0)
    recv0 = dp_xor(grad_far0, 1)
    parts = [((3 * HALF, HALF), low)] * 2
    scratch = [((2,) + w_qkv.shape, low), ((width, rows), low)]
    grad_part, send1, keep1 = call(
        qkv_back_first, "qkv_back_first",
        where + v(grad_q1, grad_own1, recv1, attn_in) + h(w_qkv, got2, part2),
        [((rows, width), full)] + parts, scratch, macs * 3000, 12,
    )
    grad_two, grad_sep, sep_edge, ggain_attn, send0, keep0 = call(
        qkv_back_second, "qkv_back_second",
        where
        + v(
            grad_q0, grad_own0, recv0, attn_in, grad_part, resid_two, grad_three, row(gain_attn)
        )
        + h(w_qkv, got2, part2),
        [
            ((rows, width), full), ((rows, sep_width), low), ((EDGE, sep_width), low),
            ((1, width), full),
        ]
        + parts,
        scratch + [((sep_width // LANES, rows, LANES), full)], macs * 3000, 12,
    )
    sep_edge = dp_xor(sep_edge, 1)
    send, keep = call(
        point_kernel, "point_back",
        where + v(grad_sep, depth, send0, keep0, send1, keep1),
        [((2, 5 * HALF, HALF), low)] * 2, [], macs * 1000,
    )
    attn_sums = Sums(send, keep, ybit)
    ffn_quarter = ffn_sums.quarter(send)
    sent = [ffn_quarter]
    unit, scaled, mid_sums, small = call(
        depth_back_kernel, "depth_back",
        [(later(info, *sent), "s")]
        + v(grad_sep, sep_edge, left_pre, right_pre, stats, pack)
        + h(w_point, got1, part1),
        [
            ((chunks, ext, HALF), low), ((chunks, ext, HALF), low), ((2, ext, LANES), full),
            ((16, inner), full),
        ],
        [
            ((2,) + w_point.shape, low), ((4, 16, HALF), low), ((16, inner), full),
            ((ext, sep_width), low),
            ((2, rows + 64, LANES), full), ((2, rows + 64, LANES), full),
            ((2, 4 * EDGE, LANES), full), ((ext, HALF), full), ((ext, HALF), full),
            ((3, ext, LANES), full),
        ],
        macs * 8000, 8,
    )
    sent = attn_sums.over_xy(mid_sums)
    r_branch = inner // 2 + 2 * HALF
    grad_left, grad_right, send, keep = call(
        branch_back_kernel, "branch_back",
        [(later(info, *sent), "s")]
        + v(
            unit, scaled, mid_sums, small, left_pre, right_pre, stats, branch_in, ggain_ffn,
            ggain_attn,
        ),
        [
            ((chunks, rows, HALF), low), ((ext, right_cols), low),
            ((2, r_branch, HALF), low), ((2, r_branch, HALF), low),
        ],
        [((3, ext, LANES), full), ((ext, right_cols), full), ((width, ext), low)],
        macs * 4000,
    )
    branch_sums = Sums(send, keep, ybit)
    early = Rest([attn_sums.quarter(grad_left), ffn_quarter], zpos)
    sent = early.over_z1(grad_left)
    grad_one, ggain_branch = call(
        join_back_kernel, "join_back",
        [(later(info, *sent), "s")]
        + v(grad_left, grad_right, resid_one, grad_two, row(gain_branch))
        + h(w_left, w_right, got1, part1),
        [((rows, width), full), ((1, width), full)],
        [((chunks, width, HALF), low), ((2,) + w_right.shape, low)],
        macs * 4000, 12,
    )
    sent = branch_sums.over_xy(grad_one)
    grad_in, send, keep = call(
        glu_back_kernel, "glu_back",
        [(later(info, *sent), "s")]
        + v(grad_one, ggain_branch, row(gain_glu), block, moved, glu_in, value, sig)
        + h(w_value, w_gate, got0, part0),
        [((rows, width), low), ((2, 640, HALF), low), ((2, 640, HALF), low)],
        [
            ((2,) + w_value.shape, low), ((2,) + w_gate.shape, low), ((rows, width), full),
            ((width // LANES, rows, LANES), full), ((width, rows), low),
        ],
        macs * 3000, 4,
    )
    glu_sums = Sums(send, keep, ybit)
    swapped_in = lax.ppermute(grad_in, ("dp", "mp"), swap)
    sent = early.over_z2(grad_in)
    sent = glu_sums.over_xy(*sent)
    branch_rest = Rest([branch_sums.quarter(*sent)], zpos)
    sent = branch_rest.over_z1(*sent)
    glu_rest = Rest([glu_sums.quarter(*sent)], zpos)
    sent = glu_rest.over_z1(*sent)
    sent = early.back_z2(*sent)
    sent = branch_rest.over_z2(*sent)
    sent = glu_rest.over_z2(*sent)
    sent = early.back_z1(*sent)
    sent = branch_rest.back_z2(*sent)
    sent = glu_rest.back_z2(*sent)
    sent = early.back_y(*sent)
    sent = branch_rest.back_z1(*sent)
    sent = glu_rest.back_z1(*sent)
    sent = early.back_core(*sent)
    sent = branch_rest.back_y(*sent)
    sent = glu_rest.back_y(*sent)
    outputs = jnp.where(member == core, out_rows, swapped_out)
    grad_inputs = jnp.where(member == core, grad_in, swapped_in)
    g_qkv, g_point, g_in, g_back, g_out = unpack(
        layout_early, later(info, *sent), early,
        [w_qkv.shape, w_point.shape, w_in.shape, w_back.shape, w_out.shape],
    )
    sent = branch_rest.back_core(g_qkv)
    sent = glu_rest.back_core(*sent)
    g_left, g_right, g_pack, g_late = unpack(
        layout_branch, later(info, *sent), branch_rest,
        [w_left.shape, w_right.shape, (16, inner // 2), (16, width)],
    )
    g_value, g_gate, g_last = unpack(
        layout_glu, info, glu_rest, [w_value.shape, w_gate.shape, (16, width)]
    )
    taps = w_depth.shape[0]
    return (
        outputs[None],
        grad_inputs[None],
        g_last[0],
        g_value,
        g_gate,
        g_last[1],
        g_left,
        g_right,
        g_pack[taps],
        g_pack[:taps],
        g_point,
        g_late[1],
        g_qkv,
        g_out,
        g_late[0],
        g_in,
        g_back,
    )


def solution(mesh):
    placed = (
        P("dp", "mp", None),
        P("dp"),
        P(),
        P(None, "mp"),
        P(None, "mp"),
        P(),
        P(None, "mp"),
        P(None, None, "mp"),
        P("mp"),
        P(None, "mp"),
        P("mp", None),
        P(),
        P(None, None, "mp"),
        P("mp", None),
        P(),
        P(None, "mp"),
        P("mp", None),
        P("dp", "mp", None),
    )
    fast = mesh.shape["mp"] == 2 and mesh.shape["dp"] == 16
    return jax.shard_map(
        paired if fast else local,
        mesh=mesh,
        in_specs=placed,
        out_specs=(
            P("dp", "mp", None),
            P("dp", "mp", None),
            P(),
            P(None, "mp"),
            P(None, "mp"),
            P(),
            P(None, "mp"),
            P(None, None, "mp"),
            P("mp"),
            P(None, "mp"),
            P("mp", None),
            P(),
            P(None, None, "mp"),
            P("mp", None),
            P(),
            P(None, "mp"),
            P("mp", None),
        ),
        check_vma=False,
    )
```

```python
import functools
import math

import jax
import jax.numpy as jnp
from jax import lax
from jax.experimental import pallas as pl
from jax.experimental.pallas import tpu as pltpu
from jax.sharding import PartitionSpec as P

FF = 2048
HEAD_DIM = 64
EDGE = 16


epsilon = 1e-06
negative_big = -1e30


def matmul(left_side, right_side):
    return jnp.dot(left_side, right_side, preferred_element_type=jnp.float32)


def contract_rows(left_side, right_side):
    return lax.dot_general(
        left_side, right_side, (((0,), (0,)), ((), ())), preferred_element_type=jnp.float32
    )


def contract_cols(left_side, right_side):
    return lax.dot_general(
        left_side, right_side, (((1,), (1,)), ((), ())), preferred_element_type=jnp.float32
    )


def spread_rows(pieces):
    return lax.all_gather(pieces, "mp", axis=1, tiled=True)


def collect_rows(partial_value):
    return lax.psum_scatter(
        partial_value.astype(jnp.bfloat16), "mp", scatter_dimension=1, tiled=True
    ).astype(jnp.float32)


def channel_sums(former, latter):
    return lax.psum((jnp.sum(former, axis=-1), jnp.sum(latter, axis=-1)), "mp")


def normalize(values, gain_vec):
    centre = values - jnp.mean(values, axis=-1, keepdims=True)
    scale_inv = lax.rsqrt(jnp.mean(centre * centre, axis=-1, keepdims=True) + epsilon)
    unit_rows = centre * scale_inv
    return (unit_rows * gain_vec, unit_rows, scale_inv)


def normalize_back(grad_out, unit_rows, scale_inv, gain_vec):
    scaled = grad_out * gain_vec
    mean_one = jnp.mean(scaled, axis=-1, keepdims=True)
    mean_two = jnp.mean(scaled * unit_rows, axis=-1, keepdims=True)
    grad_in = scale_inv * (scaled - mean_one - unit_rows * mean_two)
    return (grad_in, jnp.sum(grad_out * unit_rows, axis=(0, 1)))


def silu_slope(values):
    sigmoid_part = jax.nn.sigmoid(values)
    return sigmoid_part * (1.0 + values * (1.0 - sigmoid_part))


def shifted(values, offset):
    if offset == 0:
        return values
    margin = abs(offset)
    seq_len = values.shape[1]
    filler = jnp.zeros(values.shape[:1] + (margin,) + values.shape[2:], values.dtype)
    padded = jnp.concatenate([filler, values, filler], axis=1)
    return lax.slice_in_dim(padded, margin + offset, margin + offset + seq_len, axis=1)


def place_right(right_vals, stride):
    filler = jnp.zeros(right_vals.shape + (stride - 1,), right_vals.dtype)
    joined = jnp.concatenate([right_vals[..., None], filler], axis=-1)
    return joined.reshape(right_vals.shape[:-1] + (right_vals.shape[-1] * stride,))


def attend_forward(queries, key_vecs, value_vecs, key_valid, block_rows, score_scale):
    contexts = []
    log_parts = []
    for row_start in range(0, queries.shape[0], block_rows):
        query_rows = queries[row_start : row_start + block_rows]
        scores = (
            jnp.einsum("qhd,khd->hqk", query_rows, key_vecs, preferred_element_type=jnp.float32)
            * score_scale
        )
        scores = jnp.where(key_valid[None, None, :], scores, negative_big)
        row_max = jnp.max(scores, axis=-1, keepdims=True)
        weights_exp = jnp.exp(scores - row_max)
        row_total = jnp.sum(weights_exp, axis=-1, keepdims=True)
        probability = (weights_exp / row_total).astype(jnp.bfloat16)
        contexts.append(
            jnp.einsum("hqk,khd->qhd", probability, value_vecs, preferred_element_type=jnp.float32)
        )
        log_parts.append((row_max + jnp.log(row_total))[..., 0])
    return (jnp.concatenate(contexts, axis=0), jnp.concatenate(log_parts, axis=1))


def attend_back(
    queries, key_vecs, value_vecs, key_valid, log_sums, grad_context, block_rows, score_scale
):
    grad_queries = []
    grad_keys = jnp.zeros(key_vecs.shape, jnp.float32)
    grad_values = jnp.zeros(value_vecs.shape, jnp.float32)
    for row_start in range(0, queries.shape[0], block_rows):
        query_rows = queries[row_start : row_start + block_rows]
        grad_rows = grad_context[row_start : row_start + block_rows]
        log_rows = log_sums[:, row_start : row_start + block_rows]
        scores = (
            jnp.einsum("qhd,khd->hqk", query_rows, key_vecs, preferred_element_type=jnp.float32)
            * score_scale
        )
        scores = jnp.where(key_valid[None, None, :], scores, negative_big)
        probability = jnp.exp(scores - log_rows[..., None])
        grad_prob = jnp.einsum(
            "qhd,khd->hqk", grad_rows, value_vecs, preferred_element_type=jnp.float32
        )
        row_dot = jnp.sum(probability * grad_prob, axis=-1, keepdims=True)
        grad_scores = (probability * (grad_prob - row_dot)).astype(jnp.bfloat16)
        grad_queries.append(
            jnp.einsum("hqk,khd->qhd", grad_scores, key_vecs, preferred_element_type=jnp.float32)
            * score_scale
        )
        grad_keys = (
            grad_keys
            + jnp.einsum(
                "hqk,qhd->khd", grad_scores, query_rows, preferred_element_type=jnp.float32
            )
            * score_scale
        )
        grad_values = grad_values + jnp.einsum(
            "hqk,qhd->khd",
            probability.astype(jnp.bfloat16),
            grad_rows,
            preferred_element_type=jnp.float32,
        )
    grad_query_all = jnp.concatenate(grad_queries, axis=0)
    return (grad_query_all.astype(jnp.bfloat16), grad_keys, grad_values)


def split_pass(
    inputs,
    lengths,
    gain_glu,
    w_value,
    w_gate,
    gain_branch,
    w_left,
    w_right,
    gain_mid,
    w_depth,
    w_point,
    gain_attn,
    w_qkv,
    w_out,
    gain_ffn,
    w_in,
    w_back,
    cotangent,
):
    seqs_here, local_len, model_width = inputs.shape
    group_size = lax.axis_size("mp")
    member = lax.axis_index("mp")
    seq_len = local_len * group_size
    group_rows = seqs_here * seq_len
    positions = lax.broadcasted_iota(jnp.int32, (seqs_here, seq_len), 1)
    key_valid = positions < lengths[:, None]
    valid_full = key_valid.astype(jnp.float32)
    valid_own = lax.dynamic_slice_in_dim(valid_full, member * local_len, local_len, axis=1)
    inner_cols = w_left.shape[1]
    right_cols = w_right.shape[2]
    stride = inner_cols // right_cols
    conv_taps = w_right.shape[0]
    sep_taps = w_depth.shape[0]
    sep_width = w_point.shape[1]
    head_cols = w_qkv.shape[2]
    heads_here = head_cols // HEAD_DIM
    score_scale = 1.0 / math.sqrt(HEAD_DIM)
    block_rows = min(512, seq_len)
    group_shape = (seqs_here, seq_len, model_width)
    depth_taps = w_depth.astype(jnp.float32)
    gain_mid_f = gain_mid.astype(jnp.float32)

    def branch_inner(gathered):
        flat_rows = gathered.reshape(group_rows, model_width)
        left_pre = matmul(flat_rows, w_left).reshape(seqs_here, seq_len, inner_cols)
        right_pre = jnp.zeros((group_rows, right_cols), jnp.float32)
        for tap_index in range(conv_taps):
            moved = shifted(gathered, tap_index - conv_taps // 2).reshape(group_rows, model_width)
            right_pre = right_pre + matmul(moved, w_right[tap_index])
        right_pre = right_pre.reshape(seqs_here, seq_len, right_cols)
        mid = jax.nn.silu(left_pre) + place_right(jax.nn.silu(right_pre), stride)
        return (left_pre, right_pre, mid)

    def depth_mix(depth_in):
        depth = jnp.zeros(depth_in.shape, jnp.float32)
        for tap_index in range(sep_taps):
            depth = depth + shifted(depth_in, tap_index - sep_taps // 2) * depth_taps[tap_index]
        return depth.astype(jnp.bfloat16)

    def project_qkv(gathered):
        flat_rows = gathered.reshape(group_rows, model_width)
        joined = jnp.einsum("td,kdc->ktc", flat_rows, w_qkv, preferred_element_type=jnp.float32)
        return joined.astype(jnp.bfloat16).reshape(3, seqs_here, seq_len, heads_here, HEAD_DIM)

    def forward_one(pieces):
        return attend_forward(pieces[0], pieces[1], pieces[2], pieces[3], block_rows, score_scale)

    def backward_one(pieces):
        return attend_back(
            pieces[0],
            pieces[1],
            pieces[2],
            pieces[3],
            pieces[4],
            pieces[5],
            block_rows,
            score_scale,
        )

    resid_in = inputs.astype(jnp.float32)
    normed_glu, unit_glu, inv_glu = normalize(resid_in, gain_glu)
    gathered_glu = spread_rows(normed_glu.astype(jnp.bfloat16))
    flat_glu = gathered_glu.reshape(group_rows, model_width)
    value_pre = matmul(flat_glu, w_value)
    gate_sig = jax.nn.sigmoid(matmul(flat_glu, w_gate))
    glu_local = (value_pre * gate_sig).astype(jnp.bfloat16).reshape(seqs_here, seq_len, -1)
    glu_rows = lax.all_to_all(glu_local, "mp", split_axis=1, concat_axis=2, tiled=True)
    resid_one = resid_in + glu_rows.astype(jnp.float32)
    normed_branch, unit_branch, inv_branch = normalize(resid_one, gain_branch)
    gathered_branch = spread_rows((valid_own[..., None] * normed_branch).astype(jnp.bfloat16))
    left_pre, right_pre, mid = branch_inner(gathered_branch)
    mid_sum, mid_square = channel_sums(mid, mid * mid)
    mid_mean = mid_sum / FF
    inv_mid = lax.rsqrt(mid_square / FF - mid_mean * mid_mean + epsilon)
    unit_mid = (mid - mid_mean[..., None]) * inv_mid[..., None]
    depth_in = valid_full[..., None] * unit_mid * gain_mid_f
    depth_low = depth_mix(depth_in)
    sep_part = matmul(depth_low.reshape(group_rows, inner_cols), w_point).reshape(
        seqs_here, seq_len, sep_width
    )
    sep_rows = collect_rows(sep_part)
    resid_two = resid_one + jnp.pad(sep_rows, ((0, 0), (0, 0), (0, model_width - sep_width)))
    normed_attn, unit_attn, inv_attn = normalize(resid_two, gain_attn)
    gathered_attn = spread_rows(normed_attn.astype(jnp.bfloat16))
    qkv_heads = project_qkv(gathered_attn)
    context, log_sums = lax.map(forward_one, (qkv_heads[0], qkv_heads[1], qkv_heads[2], key_valid))
    context_low = context.astype(jnp.bfloat16).reshape(group_rows, head_cols)
    attn_rows = collect_rows(matmul(context_low, w_out).reshape(group_shape))
    resid_three = resid_two + attn_rows
    normed_ffn, unit_ffn, inv_ffn = normalize(resid_three, gain_ffn)
    gathered_ffn = spread_rows(normed_ffn.astype(jnp.bfloat16))
    ffn_flat = gathered_ffn.reshape(group_rows, model_width)
    ffn_pre = matmul(ffn_flat, w_in)
    ffn_hidden = jax.nn.silu(ffn_pre).astype(jnp.bfloat16)
    final_rows = resid_three + collect_rows(matmul(ffn_hidden, w_back).reshape(group_shape))
    outputs = final_rows.astype(jnp.bfloat16)
    cot_full = spread_rows(cotangent).reshape(group_rows, model_width)
    ffn_flat = spread_rows(normed_ffn.astype(jnp.bfloat16)).reshape(group_rows, model_width)
    ffn_pre = matmul(ffn_flat, w_in)
    ffn_hidden = jax.nn.silu(ffn_pre).astype(jnp.bfloat16)
    grad_hidden = contract_cols(cot_full, w_back)
    grad_ffn_pre = (grad_hidden * silu_slope(ffn_pre)).astype(jnp.bfloat16)
    grad_w_back = contract_rows(ffn_hidden, cot_full)
    grad_w_in = contract_rows(ffn_flat, grad_ffn_pre)
    grad_normed_ffn = collect_rows(contract_cols(grad_ffn_pre, w_in).reshape(group_shape))
    grad_resid, grad_gain_ffn = normalize_back(grad_normed_ffn, unit_ffn, inv_ffn, gain_ffn)
    grad_three = cotangent.astype(jnp.float32) + grad_resid
    grad_attn = spread_rows(grad_three.astype(jnp.bfloat16)).reshape(group_rows, model_width)
    gathered_attn = spread_rows(normed_attn.astype(jnp.bfloat16))
    qkv_heads = project_qkv(gathered_attn)
    attn_flat = gathered_attn.reshape(group_rows, model_width)
    grad_w_out = contract_rows(context_low, grad_attn)
    grad_context = contract_cols(grad_attn, w_out).astype(jnp.bfloat16)
    grad_context = grad_context.reshape(seqs_here, seq_len, heads_here, HEAD_DIM)
    grad_q, grad_k, grad_v = lax.map(
        backward_one, (qkv_heads[0], qkv_heads[1], qkv_heads[2], key_valid, log_sums, grad_context)
    )
    grad_qkv = jnp.stack(
        [grad_q, grad_k.astype(jnp.bfloat16), grad_v.astype(jnp.bfloat16)]
    ).reshape(3, group_rows, head_cols)
    grad_w_qkv = jnp.einsum("td,ktc->kdc", attn_flat, grad_qkv, preferred_element_type=jnp.float32)
    grad_attn_in = jnp.einsum("ktc,kdc->td", grad_qkv, w_qkv, preferred_element_type=jnp.float32)
    grad_normed_attn = collect_rows(grad_attn_in.reshape(group_shape))
    grad_resid, grad_gain_attn = normalize_back(grad_normed_attn, unit_attn, inv_attn, gain_attn)
    grad_two = grad_three + grad_resid
    grad_sep = spread_rows(grad_two[..., :sep_width].astype(jnp.bfloat16)).reshape(
        group_rows, sep_width
    )
    gathered_branch = spread_rows((valid_own[..., None] * normed_branch).astype(jnp.bfloat16))
    left_pre, right_pre, mid = branch_inner(gathered_branch)
    unit_mid = (mid - mid_mean[..., None]) * inv_mid[..., None]
    depth_in = valid_full[..., None] * unit_mid * gain_mid_f
    depth_low = depth_mix(depth_in)
    grad_w_point = contract_rows(depth_low.reshape(group_rows, inner_cols), grad_sep)
    grad_depth = contract_cols(grad_sep, w_point).reshape(seqs_here, seq_len, inner_cols)
    grad_depth_in = jnp.zeros(grad_depth.shape, jnp.float32)
    depth_rows = []
    for tap_index in range(sep_taps):
        offset = tap_index - sep_taps // 2
        grad_depth_in = grad_depth_in + shifted(grad_depth, -offset) * depth_taps[tap_index]
        depth_rows.append(jnp.sum(shifted(depth_in, offset) * grad_depth, axis=(0, 1)))
    grad_w_depth = jnp.stack(depth_rows)
    grad_unit = grad_depth_in * valid_full[..., None]
    grad_gain_mid = jnp.sum(grad_unit * unit_mid, axis=(0, 1))
    scaled = grad_unit * gain_mid_f
    sum_one, sum_two = channel_sums(scaled, scaled * unit_mid)
    grad_mid = inv_mid[..., None] * (
        scaled - (sum_one / FF)[..., None] - unit_mid * (sum_two / FF)[..., None]
    )
    grad_left = (
        (grad_mid * silu_slope(left_pre)).astype(jnp.bfloat16).reshape(group_rows, inner_cols)
    )
    grad_right_act = grad_mid.reshape(seqs_here, seq_len, right_cols, stride)[..., 0]
    grad_right = (
        (grad_right_act * silu_slope(right_pre))
        .astype(jnp.bfloat16)
        .reshape(group_rows, right_cols)
    )
    branch_flat = gathered_branch.reshape(group_rows, model_width)
    grad_w_left = contract_rows(branch_flat, grad_left)
    grad_branch_in = contract_cols(grad_left, w_left).reshape(group_shape)
    right_rows = []
    for tap_index in range(conv_taps):
        offset = tap_index - conv_taps // 2
        moved = shifted(gathered_branch, offset).reshape(group_rows, model_width)
        right_rows.append(contract_rows(moved, grad_right))
        grad_branch_in = grad_branch_in + shifted(
            contract_cols(grad_right, w_right[tap_index]).reshape(group_shape), -offset
        )
    grad_w_right = jnp.stack(right_rows)
    grad_normed_branch = collect_rows(grad_branch_in) * valid_own[..., None]
    grad_resid, grad_gain_branch = normalize_back(
        grad_normed_branch, unit_branch, inv_branch, gain_branch
    )
    grad_one = grad_two + grad_resid
    grad_glu = lax.all_to_all(
        grad_one.astype(jnp.bfloat16), "mp", split_axis=2, concat_axis=1, tiled=True
    )
    grad_glu_flat = grad_glu.reshape(group_rows, -1).astype(jnp.float32)
    flat_glu = spread_rows(normed_glu.astype(jnp.bfloat16)).reshape(group_rows, model_width)
    value_pre = matmul(flat_glu, w_value)
    gate_sig = jax.nn.sigmoid(matmul(flat_glu, w_gate))
    grad_value = (grad_glu_flat * gate_sig).astype(jnp.bfloat16)
    grad_gate = (grad_glu_flat * value_pre * gate_sig * (1.0 - gate_sig)).astype(jnp.bfloat16)
    grad_w_value = contract_rows(flat_glu, grad_value)
    grad_w_gate = contract_rows(flat_glu, grad_gate)
    grad_glu_in = contract_cols(grad_value, w_value) + contract_cols(grad_gate, w_gate)
    grad_normed_glu = collect_rows(grad_glu_in.reshape(group_shape))
    grad_resid, grad_gain_glu = normalize_back(grad_normed_glu, unit_glu, inv_glu, gain_glu)
    grad_inputs = (grad_one + grad_resid).astype(jnp.bfloat16)
    gains = (grad_gain_glu, grad_gain_branch, grad_gain_attn, grad_gain_ffn)
    shards = (
        grad_w_value,
        grad_w_gate,
        grad_w_left,
        grad_w_right,
        grad_gain_mid,
        grad_w_depth,
        grad_w_point,
        grad_w_qkv,
        grad_w_out,
        grad_w_in,
        grad_w_back,
    )
    return (outputs, grad_inputs, gains, shards)


def local(
    inputs,
    lengths,
    gain_glu,
    w_value,
    w_gate,
    gain_branch,
    w_left,
    w_right,
    gain_mid,
    w_depth,
    w_point,
    gain_attn,
    w_qkv,
    w_out,
    gain_ffn,
    w_in,
    w_back,
    cotangent,
):
    outputs, grad_inputs, gains, shards = split_pass(
        inputs,
        lengths,
        gain_glu,
        w_value,
        w_gate,
        gain_branch,
        w_left,
        w_right,
        gain_mid,
        w_depth,
        w_point,
        gain_attn,
        w_qkv,
        w_out,
        gain_ffn,
        w_in,
        w_back,
        cotangent,
    )
    gain_totals = lax.psum((gains[0], gains[1], gains[2], gains[3]), ("dp", "mp"))
    weight_totals = (
        lax.psum(shards[0].astype(jnp.bfloat16), "dp").astype(jnp.float32),
        lax.psum(shards[1].astype(jnp.bfloat16), "dp").astype(jnp.float32),
        lax.psum(shards[2].astype(jnp.bfloat16), "dp").astype(jnp.float32),
        lax.psum(shards[3].astype(jnp.bfloat16), "dp").astype(jnp.float32),
        lax.psum(shards[4].astype(jnp.bfloat16), "dp").astype(jnp.float32),
        lax.psum(shards[5].astype(jnp.bfloat16), "dp").astype(jnp.float32),
        lax.psum(shards[6].astype(jnp.bfloat16), "dp").astype(jnp.float32),
        lax.psum(shards[7].astype(jnp.bfloat16), "dp").astype(jnp.float32),
        lax.psum(shards[8].astype(jnp.bfloat16), "dp").astype(jnp.float32),
        lax.psum(shards[9].astype(jnp.bfloat16), "dp").astype(jnp.float32),
        lax.psum(shards[10].astype(jnp.bfloat16), "dp").astype(jnp.float32),
    )
    return (
        outputs,
        grad_inputs,
        gain_totals[0],
        weight_totals[0],
        weight_totals[1],
        gain_totals[1],
        weight_totals[2],
        weight_totals[3],
        weight_totals[4],
        weight_totals[5],
        weight_totals[6],
        gain_totals[2],
        weight_totals[7],
        weight_totals[8],
        gain_totals[3],
        weight_totals[9],
        weight_totals[10],
    )


HALF = 256
LANES = 128


def dot_nn(left_side, right_side):
    return lax.dot_general(
        left_side, right_side, (((1,), (0,)), ((), ())), preferred_element_type=jnp.float32
    )


def dot_nt(left_side, right_side):
    return lax.dot_general(
        left_side, right_side, (((1,), (1,)), ((), ())), preferred_element_type=jnp.float32
    )


def dot_tn(left_side, right_side):
    return lax.dot_general(
        left_side, right_side, (((0,), (0,)), ((), ())), preferred_element_type=jnp.float32
    )


def row_stats(values):
    centre = values - jnp.mean(values, axis=-1, keepdims=True)
    inv = lax.rsqrt(jnp.mean(centre * centre, axis=-1, keepdims=True) + epsilon)
    return centre * inv, inv


def norm_grad(grad_out, unit, inv, gain):
    scaled = grad_out * gain
    mean_one = jnp.mean(scaled, axis=-1, keepdims=True)
    mean_two = jnp.mean(scaled * unit, axis=-1, keepdims=True)
    return inv * (scaled - mean_one - unit * mean_two)


def sigmoid(values):
    return 0.5 * jnp.tanh(0.5 * values) + 0.5


def silu(values):
    return values * sigmoid(values)


def turned(values):
    return jnp.transpose(values.astype(jnp.float32)).astype(jnp.bfloat16)


class Loader:
    def __init__(self, sems, first=0):
        self.sems = sems
        self.count = first
        self.waits = []

    def start(self, source, target):
        copy = pltpu.make_async_copy(source, target, self.sems.at[self.count])
        self.count += 1
        copy.start()
        self.waits.append(copy)

    def either(self, first, second, use_first, target):
        sem = self.sems.at[self.count]
        self.count += 1

        @pl.when(use_first)
        def _():
            pltpu.make_async_copy(first, target, sem).start()

        @pl.when(jnp.logical_not(use_first))
        def _():
            pltpu.make_async_copy(second, target, sem).start()

        self.waits.append(pltpu.make_async_copy(first, target, sem))

    def wait(self):
        for copy in self.waits:
            copy.wait()
        self.waits = []


def load_pair(loader, own, got, part, taker, core, target, slots=(0, 1)):
    loader.start(own, target.at[slots[0]])
    loader.either(got, part, core == taker, target.at[slots[1]])


def load_left(loader, w_left, got, part, core, target):
    blocks = w_left.shape[1] // HALF
    rows = w_left.shape[0]
    for block in range(blocks):
        loader.start(w_left.at[:, pl.ds(block * HALF, HALF)], target.at[block])
        at = pl.ds(block * rows, rows)
        loader.either(got.at[at], part.at[at], core == 0, target.at[blocks + block])


def load_pack(loader, got, part, core, target):
    count, depth = target.shape[:2]
    for block in range(count):
        at = pl.ds(got.shape[0] - (count - block) * depth, depth)
        loader.either(got.at[at], part.at[at], core == 0, target.at[block])


def load_point(loader, w_point, got, part, core, target):
    at = pl.ds(0, w_point.shape[0])
    load_pair(loader, w_point, got.at[at], part.at[at], 1, core, target)


def load_right(loader, w_right, got, part, core, target):
    loader.start(w_right, target.at[0])
    rows = w_right.shape[1]
    for tap in range(w_right.shape[0]):
        at = (pl.ds(2 * rows + (tap // 2) * rows, rows), pl.ds((tap % 2) * LANES, LANES))
        loader.either(got.at[at], part.at[at], core == 1, target.at[1, tap])


def load_qkv(loader, w_qkv, got, part, core, target, which):
    rows = w_qkv.shape[1]
    for slot, index in enumerate(which):
        loader.start(w_qkv.at[index], target.at[0, slot])
        at = pl.ds(index * rows, rows)
        loader.either(got.at[at], part.at[at], core == 0, target.at[1, slot])


def load_out(loader, w_out, got, part, core, target):
    loader.start(w_out, target.at[0])
    rows = w_out.shape[0]
    for block in range(2):
        at = pl.ds(block * rows, rows)
        loader.either(
            got.at[at], part.at[at], core == 1, target.at[1, :, pl.ds(block * HALF, HALF)]
        )


def load_in(loader, w_in, got2, part2, got3, part3, core, target):
    blocks = w_in.shape[1] // HALF
    rows = w_in.shape[0]
    for block in range(blocks):
        loader.start(w_in.at[:, pl.ds(block * HALF, HALF)], target.at[block])
        got, part = (got2, part2) if block < 2 else (got3, part3)
        at = pl.ds(rows + (block % 2) * rows, rows)
        loader.either(got.at[at], part.at[at], core == 1, target.at[blocks + block])


def load_back(loader, w_back, got, part, core, target):
    loader.start(w_back, target.at[0])
    rows = w_back.shape[0]
    half = rows // 2
    near, far = pl.ds(0, HALF), pl.ds(HALF, HALF)
    for at, taker, spot in (
        (pl.ds(0, rows), 0, (pl.ds(0, rows), near)),
        (pl.ds(rows, half), 0, (pl.ds(0, half), far)),
        (pl.ds(0, half), 1, (pl.ds(half, half), far)),
    ):
        loader.either(got.at[at], part.at[at], core == taker, target.at[1].at[spot])


GROUP = 8


def bundle_kernel(
    info, w_left, w_right, w_point, w_depth, gain_mid, w_qkv, w_out, w_in, w_back,
    one_o, two_o, three_o, sems,
):
    core = info[0]

    def copies(pieces):
        at = {id(one_o): 0, id(two_o): 0, id(three_o): 0}
        started = []
        for target, source in pieces:
            base = at[id(target)]
            at[id(target)] = base + source.shape[0]
            spot = target.at[pl.ds(base, source.shape[0]), pl.ds(0, source.shape[1])]
            copy = pltpu.make_async_copy(source, spot, sems.at[len(started)])
            copy.start()
            started.append(copy)
        for copy in started:
            copy.wait()

    def blocks(values):
        return [values.at[:, pl.ds(at, HALF)] for at in range(0, values.shape[1], HALF)]

    near, far = blocks(w_back)
    half = w_back.shape[0] // 2

    @pl.when(core == 0)
    def _():
        base = w_left.shape[0] * (w_left.shape[1] // HALF)
        taps = jnp.concatenate(
            [
                w_depth[...].astype(jnp.float32),
                gain_mid[...].astype(jnp.float32),
                jnp.zeros((15 - w_depth.shape[0], w_depth.shape[1]), jnp.float32),
            ],
            axis=0,
        ).astype(jnp.bfloat16)
        for block in range(w_depth.shape[1] // HALF):
            at = slice(base + block * 16, base + (block + 1) * 16)
            one_o[at] = taps[:, block * HALF : (block + 1) * HALF]
        copies(
            [(one_o, piece) for piece in blocks(w_left)]
            + [(two_o, w_qkv.at[index]) for index in range(3)]
            + [(three_o, near), (three_o, far.at[pl.ds(0, half)])]
        )

    @pl.when(core == 1)
    def _():
        pieces = [(one_o, w_point)]
        pieces += [(two_o, piece) for piece in blocks(w_out) + blocks(w_in)[:2]]
        pieces += [(three_o, far.at[pl.ds(half, half)])]
        pieces += [(three_o, piece) for piece in blocks(w_in)[2:]]
        rows, base = w_right.shape[1], w_point.shape[0]
        started = []
        for tap in range(w_right.shape[0]):
            spot = one_o.at[
                pl.ds(base + (tap // 2) * rows, rows), pl.ds((tap % 2) * LANES, LANES)
            ]
            copy = pltpu.make_async_copy(w_right.at[tap], spot, sems.at[len(pieces) + tap])
            copy.start()
            started.append(copy)
        copies(pieces)
        for copy in started:
            copy.wait()


def row_spot(rows, own, lanes):
    row = lax.broadcasted_iota(jnp.int32, (rows, lanes), 0)
    spot = (row % GROUP) * (own // GROUP) + row // GROUP
    return jnp.where(row < own, spot, jnp.where(row < own + EDGE, row - own - EDGE, row - EDGE))


def row_mask(core, length, ext, lanes):
    own = ext - 2 * EDGE
    spot = row_spot(ext, own, lanes) + core * own
    return jnp.where((spot >= 0) & (spot < length), 1.0, 0.0)


def lane_tiles(width):
    return [slice(at, at + LANES) for at in range(0, width, LANES)]


def load_tiles(source, tiles):
    for index, lanes in enumerate(lane_tiles(source.shape[1])):
        tiles[index] = source[:, lanes].astype(jnp.float32)


def gather_rows(tiles, target):
    own = tiles.shape[1]
    for tile, lanes in enumerate(lane_tiles(target.shape[1])):
        for index in range(own // GROUP):
            target[index * GROUP : (index + 1) * GROUP, lanes] = tiles[
                tile, pl.ds(index, GROUP, stride=own // GROUP)
            ]


def scatter_rows(source, tiles, target):
    own = tiles.shape[1]
    for tile, lanes in enumerate(lane_tiles(target.shape[1])):
        for index in range(own // GROUP):
            tiles[tile, pl.ds(index, GROUP, stride=own // GROUP)] = source[
                index * GROUP : (index + 1) * GROUP, lanes
            ]
        target[:, lanes] = tiles[tile].astype(target.dtype)


def next_group(first, row):
    sub = lax.broadcasted_iota(jnp.int32, first.shape, 0)
    return jnp.where(sub == GROUP - 1, row, pltpu.roll(first, GROUP - 1, 0))


def previous_group(last, row):
    sub = lax.broadcasted_iota(jnp.int32, last.shape, 0)
    return jnp.where(sub == 0, row, pltpu.roll(last, 1, 0))


def shift_rows(values, offset):
    if offset == 0:
        return values
    ext = values.shape[0]
    own = ext - 2 * EDGE
    mid, before, after = values[:own], values[own : own + EDGE], values[own + EDGE :]
    sub = lax.broadcasted_iota(jnp.int32, before.shape, 0)
    if offset > 0:
        moved = jnp.concatenate([mid[GROUP:], next_group(mid[:GROUP], after[:1])], axis=0)
        before = jnp.where(sub == EDGE - 1, mid[:1], pltpu.roll(before, EDGE - 1, 0))
        after = pltpu.roll(after, EDGE - 1, 0)
    else:
        moved = jnp.concatenate(
            [previous_group(mid[own - GROUP :], before[EDGE - 1 :]), mid[: own - GROUP]], axis=0
        )
        after = jnp.where(sub == 0, mid[own - 1 :], pltpu.roll(after, 1, 0))
        before = pltpu.roll(before, 1, 0)
    return jnp.concatenate([moved, before, after], axis=0)


def fill_window(window, values, own, reach):
    before, after = values[own : own + EDGE], values[own + EDGE :]
    window[reach * GROUP : reach * GROUP + own] = values[:own]
    for step in range(1, reach + 1):
        last = values[own - step * GROUP : own - (step - 1) * GROUP]
        at = (reach - step) * GROUP
        window[at : at + GROUP] = previous_group(last, before[EDGE - step : EDGE - step + 1])
        first = values[(step - 1) * GROUP : step * GROUP]
        at = reach * GROUP + own + (step - 1) * GROUP
        window[at : at + GROUP] = next_group(first, after[step - 1 : step])


def glu_kernel(
    info, block, moved, cot_own, cot_moved, edge, gain_glu, gain_branch, w_value, w_gate, got, part_w,
    cot_o, resid_o, branch_o, gluin_o, value_o, sig_o, x_s, c_s, n_s, wv_s, wg_s, sems,
):
    core, member, length = info[0], info[1], info[2]
    loader = Loader(sems)
    load_pair(loader, w_value, got, part_w, 0, core, wv_s, (member, 1 - member))
    load_pair(loader, w_gate, got, part_w, 1, core, wg_s, (member, 1 - member))
    ext = x_s.shape[0]
    rows = ext - 2 * EDGE
    edge_f = edge[...].astype(jnp.float32)
    x_s[rows : rows + EDGE] = jnp.where(core == 1, edge_f, 0.0)
    x_s[rows + EDGE :] = jnp.where(core == 1, 0.0, edge_f)

    @pl.when(core == member)
    def _():
        load_tiles(block, n_s)

    @pl.when(core != member)
    def _():
        load_tiles(moved, n_s)

    gather_rows(n_s, x_s)

    @pl.when(core == member)
    def _():
        load_tiles(cot_own, n_s)

    @pl.when(core != member)
    def _():
        load_tiles(cot_moved, n_s)

    gather_rows(n_s, c_s)
    cot_o[...] = c_s[...].astype(jnp.bfloat16)
    loader.wait()
    valid = row_mask(core, length, ext, LANES)[:, :1]
    part = ext // 2
    for start in (0, part):
        at = slice(start, start + part)
        x = x_s[at]
        glu_in = (row_stats(x)[0] * gain_glu[...]).astype(jnp.bfloat16)
        gluin_o[at] = glu_in
        for half in range(2):
            cols = slice(half * HALF, (half + 1) * HALF)
            value = dot_nn(glu_in, wv_s[half])
            sig = sigmoid(dot_nn(glu_in, wg_s[half]))
            value_o[at, cols] = value.astype(jnp.bfloat16)
            sig_o[at, cols] = sig.astype(jnp.bfloat16)
            resid_o[at, cols] = x[:, cols] + (value * sig).astype(jnp.bfloat16).astype(jnp.float32)
        normed = row_stats(resid_o[at])[0] * gain_branch[...]
        branch_o[at] = (valid[at] * normed).astype(jnp.bfloat16)


def spread_block(index, rights, stride):
    source = lax.broadcasted_iota(jnp.int32, (rights, HALF), 0)
    channel = lax.broadcasted_iota(jnp.int32, (rights, HALF), 1) + index * HALF
    return jnp.where(channel == source * stride, 1.0, 0.0).astype(jnp.bfloat16)


def conv_rows(branch, weights):
    taps = weights.shape[0]
    total = dot_nn(branch, weights[taps // 2])
    for tap in range(taps):
        if tap != taps // 2:
            total = total + shift_rows(dot_nn(branch, weights[tap]), tap - taps // 2)
    return total


def mid_step(branch, into, right_act, index, stride, left_o, mid_o, sums, at):
    left_pre = dot_nn(branch[...], into[index])
    left_o[at] = left_pre.astype(jnp.bfloat16)
    mid = silu(left_pre) + dot_nn(right_act, spread_block(index, right_act.shape[1], stride))
    mid_o[at] = mid
    near, far = mid[:, :LANES], mid[:, LANES:]
    sums[0] += near + far
    sums[1] += near * near + far * far


def branch_own_kernel(
    info, branch, w_left, w_right, left_o, right_o, mid_o, sums_o, wl_s, sems
):
    loader = Loader(sems)
    blocks = wl_s.shape[0]
    for block in range(blocks):
        loader.start(w_left.at[:, pl.ds(block * HALF, HALF)], wl_s.at[block])
    right_pre = conv_rows(branch[...], w_right)
    right_o[...] = right_pre
    right_act = silu(right_pre).astype(jnp.bfloat16)
    stride = blocks * HALF // right_pre.shape[1]
    sums_o[...] = jnp.zeros_like(sums_o)
    loader.wait()

    def step(index, carry):
        mid_step(branch, wl_s, right_act, index, stride, left_o, mid_o, sums_o, index)
        return carry

    lax.fori_loop(0, blocks, step, 0, unroll=2)


def fill_taps(pack_own, pack_oth, taps_s):
    count, cols = pack_own.shape
    taps_s[:count, :cols] = pack_own[...].astype(jnp.float32)
    for block in range(pack_oth.shape[0]):
        at = cols + block * HALF
        taps_s[:, at : at + HALF] = pack_oth[block].astype(jnp.float32)


def branch_kernel(
    info, branch, resid_one, pack_own, left_own, right_own, mid_own, sums_own, w_point, got, part,
    resid_two_o, left_o, right_o, stats_o, depth_o,
    wl_s, wr_s, wp_s, po_s, taps_s, mid_s, din_s, sums_s, sep_s, sems,
):
    core, length = info[0], info[2]
    loader = Loader(sems)
    taps_conv, depth_in_rows = wr_s.shape[0], wr_s.shape[1]
    for tap in range(taps_conv):
        at = (
            pl.ds(w_point.shape[0] + (tap // 2) * depth_in_rows, depth_in_rows),
            pl.ds((tap % 2) * LANES, LANES),
        )
        loader.either(got.at[at], part.at[at], core == 1, wr_s.at[tap])
    blocks = wl_s.shape[0]
    for block in range(blocks):
        at = pl.ds(block * depth_in_rows, depth_in_rows)
        loader.either(got.at[at], part.at[at], core == 0, wl_s.at[block])
    load_point(loader, w_point, got, part, core, wp_s)
    load_pack(loader, got, part, core, po_s)
    ext = branch.shape[0]
    rows = ext - 2 * EDGE
    chunks = 2 * blocks
    per_shard = blocks
    sep_taps = pack_own.shape[0] - 1
    inner = chunks * HALF
    rights = right_own.shape[1]
    stride = blocks * HALF // rights
    left_o[:blocks] = left_own[...]
    mid_s[:blocks] = mid_own[...]
    sums_s[...] = sums_own[...]
    right_o[:, :rights] = right_own[...]
    loader.wait()
    fill_taps(pack_own, po_s, taps_s)
    right_pre = conv_rows(branch[...], wr_s)
    right_o[:, rights:] = right_pre
    right_act = silu(right_pre).astype(jnp.bfloat16)

    def first(index, carry):
        mid_step(branch, wl_s, right_act, index, stride, left_o, mid_s, sums_s, index + blocks)
        return carry

    lax.fori_loop(0, blocks, first, 0, unroll=2)
    mean = jnp.sum(sums_s[0], axis=-1, keepdims=True) / inner
    inv = lax.rsqrt(
        jnp.sum(sums_s[1], axis=-1, keepdims=True) / inner - mean * mean + epsilon
    )
    lane = lax.broadcasted_iota(jnp.int32, (ext, LANES), 1)
    stats_o[...] = jnp.where(lane == 0, mean, inv)
    sums_s[0] = jnp.broadcast_to(mean, (ext, LANES))
    sums_s[1] = inv * row_mask(core, length, ext, LANES)
    sep_s[...] = jnp.zeros_like(sep_s)

    def second(index, carry):
        cols = pl.ds(pl.multiple_of(index * HALF, HALF), HALF)
        taps = taps_s[:, cols]
        for side in range(2):
            lanes = slice(side * LANES, (side + 1) * LANES)
            depth_in = (
                (mid_s[index, :, lanes] - sums_s[0]) * sums_s[1] * taps[sep_taps : sep_taps + 1, lanes]
            )
            fill_window(din_s.at[:, lanes], depth_in, rows, sep_taps // 2)
        step = 64
        for start in range(0, rows, step):
            for side in range(2):
                lanes = slice(side * LANES, (side + 1) * LANES)
                acc = din_s[start : start + step, lanes] * taps[:1, lanes]
                for tap in range(1, sep_taps):
                    at = start + tap * GROUP
                    acc = acc + din_s[at : at + step, lanes] * taps[tap : tap + 1, lanes]
                depth_o[index, start : start + step, lanes] = acc.astype(jnp.bfloat16)
        shard, chunk = index // per_shard, index % per_shard
        point = wp_s[shard, pl.ds(pl.multiple_of(chunk * HALF, HALF), HALF)]
        sep_s[...] += dot_nn(depth_o[index], point)
        return carry

    lax.fori_loop(0, chunks, second, 0, unroll=2)
    sep_width = sep_s.shape[1]
    resid_two_o[:, :sep_width] = resid_one[:rows, :sep_width] + sep_s[...]
    resid_two_o[:, sep_width:] = resid_one[:rows, sep_width:]


def kv_kernel(info, resid_two, gain, w_qkv, got, part, attn_o, kv_o, w_s, sems):
    loader = Loader(sems)
    load_qkv(loader, w_qkv, got, part, info[0], w_s, (1, 2))
    attn_in = (row_stats(resid_two[...])[0] * gain[...]).astype(jnp.bfloat16)
    attn_o[...] = attn_in
    loader.wait()
    width = w_s.shape[3]
    for shard in range(2):
        for index in range(2):
            at = (2 * index + shard) * width
            kv_o[:, at : at + width] = dot_nn(attn_in, w_s[shard, index]).astype(jnp.bfloat16)


def query_kernel(info, attn_in, w_qkv, got, part, q_o, w_s, sems):
    loader = Loader(sems)
    load_qkv(loader, w_qkv, got, part, info[0], w_s, (0,))
    loader.wait()
    width = w_s.shape[3]
    scale = 1.0 / math.sqrt(HEAD_DIM)
    for shard in range(2):
        query = dot_nn(attn_in[...], w_s[shard, 0]).astype(jnp.bfloat16).astype(jnp.float32)
        q_o[:, shard * width : (shard + 1) * width] = (query * scale).astype(jnp.bfloat16)


def key_bias(core, length, rows):
    spot = row_spot(rows, rows, LANES) + core * rows
    return jnp.where(spot < length, 0.0, negative_big)


def head_masks(rows, head):
    lane = lax.broadcasted_iota(jnp.int32, (rows, LANES), 1)
    return (lane // HEAD_DIM) == head, lane == HEAD_DIM * (1 - head)


def attend_kernel(info, q, kvo, kvf, ctx0_o, lse0_o, ctx1_o, lse1_o, bias_s):
    core, length = info[0], info[2]
    rows, width = q.shape
    pairs = width // LANES // 2
    bias_s[:rows] = key_bias(core, length, rows)
    bias_s[rows:] = key_bias(1 - core, length, rows)

    def pair_step(shard, ctx_o, lse_o, local, carry):
        pair = local + shard * pairs
        cols = pl.ds(pl.multiple_of(pair * LANES, LANES), LANES)
        vcols = pl.ds(pl.multiple_of(pair * LANES + width, LANES), LANES)
        here = pl.ds(pl.multiple_of(local * LANES, LANES), LANES)
        keys = jnp.concatenate([kvo[:, cols], kvf[:, cols]], axis=0).astype(jnp.float32)
        vals = jnp.concatenate([kvo[:, vcols], kvf[:, vcols]], axis=0)
        vals_t = turned(vals)
        query = q[:, cols].astype(jnp.float32)
        outs = []
        for head in range(2):
            in_k, extra_k = head_masks(2 * rows, head)
            in_q, extra_q = head_masks(rows, head)
            km = jnp.where(in_k, keys, jnp.where(extra_k, bias_s[...], 0.0)).astype(jnp.bfloat16)
            qm = jnp.where(in_q, query, jnp.where(extra_q, 1.0, 0.0)).astype(jnp.bfloat16)
            pieces = []
            for start in range(0, rows, HALF):
                scores = dot_nt(km, qm[start : start + HALF])
                top = jnp.max(scores, axis=0, keepdims=True)
                weights = jnp.exp(scores - top)
                total = jnp.sum(weights, axis=0, keepdims=True)
                out = dot_nn(
                    vals_t[head * HEAD_DIM : (head + 1) * HEAD_DIM], weights.astype(jnp.bfloat16)
                )
                pieces.append(out / total)
                lse_o[pl.ds(local * 2 + head, 1), start : start + HALF] = top + jnp.log(total)
            outs.append(jnp.concatenate(pieces, axis=1))
        ctx_o[:, here] = jnp.transpose(jnp.concatenate(outs, axis=0)).astype(jnp.bfloat16)
        return carry

    lax.fori_loop(0, pairs, functools.partial(pair_step, 0, ctx0_o, lse0_o), 0)
    lax.fori_loop(0, pairs, functools.partial(pair_step, 1, ctx1_o, lse1_o), 0)


def ffn_kernel(
    info, resid_two, ctx0, ctx1, cot, gain, w_out, w_in, w_back, got2, part2,
    got3, part3,
    out_o, grad_three_o, gctx_o, ggain_o, send_o, keep_o,
    wo_s, wi_s, wb_s, fin_s, fint_s, cot_s, acc_s, gacc_s, ctxt_s, n_s, sems,
):
    core = info[0]
    loader = Loader(sems)
    load_out(loader, w_out, got2, part2, core, wo_s)
    late = Loader(sems, loader.count)
    load_in(late, w_in, got2, part2, got3, part3, core, wi_s)
    load_back(late, w_back, got3, part3, core, wb_s)

    cot_s[...] = cot[...]
    loader.wait()
    part = ctx0.shape[1]
    chunks = wi_s.shape[0]
    per_shard = chunks // 2
    resid = resid_two[...] + dot_nn(ctx0[...], wo_s[0]) + dot_nn(ctx1[...], wo_s[1])
    acc_s[...] = resid
    gacc_s[...] = jnp.zeros_like(gacc_s)
    unit, inv = row_stats(resid)
    ffn_in = unit * gain[...]
    fin_s[...] = ffn_in.astype(jnp.bfloat16)
    fint_s[...] = jnp.transpose(fin_s[...].astype(jnp.float32)).astype(jnp.bfloat16)
    keep_rows = pl.ds(pl.multiple_of(core * HALF, HALF), HALF)
    send_rows = pl.ds(pl.multiple_of((1 - core) * HALF, HALF), HALF)

    def chunk_step(index, carry):
        shard, chunk = index // per_shard, index % per_shard
        rows = pl.ds(pl.multiple_of(chunk * HALF, HALF), HALF)
        into, back = wi_s[index], wb_s[shard, rows]
        pre = dot_nn(fin_s[...], into)
        sig = sigmoid(pre)
        hidden = (pre * sig).astype(jnp.bfloat16)
        acc_s[...] += dot_nn(hidden, back)
        grad_hidden = dot_nt(cot_s[...], back)
        grad_pre = (grad_hidden * (sig * (1.0 + pre * (1.0 - sig)))).astype(jnp.bfloat16)
        send_o[shard, rows] = dot_nn(fint_s[send_rows], grad_pre).astype(jnp.bfloat16)
        keep_o[shard, rows] = dot_nn(fint_s[keep_rows], grad_pre).astype(jnp.bfloat16)
        hidden_t = turned(hidden)
        base = per_shard * HALF
        rows = pl.ds(pl.multiple_of(base + chunk * HALF, HALF), HALF)
        send_o[shard, rows] = dot_nn(hidden_t, cot_s[:, send_rows]).astype(jnp.bfloat16)
        keep_o[shard, rows] = dot_nn(hidden_t, cot_s[:, keep_rows]).astype(jnp.bfloat16)
        gacc_s[...] += dot_nt(grad_pre, into)
        return carry

    late.wait()
    lax.fori_loop(0, chunks, chunk_step, 0, unroll=2)
    scatter_rows(acc_s, n_s, out_o)
    unit, inv = row_stats(
        resid_two[...] + dot_nn(ctx0[...], wo_s[0]) + dot_nn(ctx1[...], wo_s[1])
    )
    grad_norm = gacc_s[...]
    ggain_o[...] = jnp.sum(grad_norm * unit, axis=0, keepdims=True)
    grad_three = cot_s[...].astype(jnp.float32) + norm_grad(grad_norm, unit, inv, gain[...])
    grad_three_o[...] = grad_three
    fin_s[...] = grad_three.astype(jnp.bfloat16)
    ctxt_s[:part] = turned(ctx0[...])
    ctxt_s[part:] = turned(ctx1[...])
    base = 2 * per_shard * HALF
    for shard in range(2):
        side = slice(shard * part, (shard + 1) * part)
        gctx_o[:, side] = dot_nt(fin_s[...], wo_s[shard]).astype(jnp.bfloat16)
        send_o[shard, base : base + part] = dot_nn(ctxt_s[side], fin_s[:, send_rows]).astype(
            jnp.bfloat16
        )
        keep_o[shard, base : base + part] = dot_nn(ctxt_s[side], fin_s[:, keep_rows]).astype(
            jnp.bfloat16
        )


def attend_back_kernel(side, info, q, kv, ctx0, ctx1, gctx, lse0, lse1, *rest):
    if side:
        gq_o, gkv_o, bias_s, gk_s, gv_s = rest
    else:
        gq_part, gq_o, gkv_o, bias_s, gk_s, gv_s = rest
    core, length = info[0], info[2]
    rows, width = q.shape
    pairs = width // LANES // 2
    scale = 1.0 / math.sqrt(HEAD_DIM)
    bias_s[...] = key_bias(core ^ side, length, rows)

    def pair_step(shard, ctx, lse, local, carry):
        pair = local + shard * pairs
        cols = pl.ds(pl.multiple_of(pair * LANES, LANES), LANES)
        vcols = pl.ds(pl.multiple_of(pair * LANES + width, LANES), LANES)
        here = pl.ds(pl.multiple_of(local * LANES, LANES), LANES)
        keys = kv[:, cols].astype(jnp.float32)
        vals = kv[:, vcols]
        keys_t = jnp.transpose(keys).astype(jnp.bfloat16)
        query = q[:, cols].astype(jnp.float32)
        grad_out = gctx[:, cols].astype(jnp.float32)
        product_t = jnp.transpose(grad_out * ctx[:, here].astype(jnp.float32))
        gk_s[...] = jnp.zeros_like(gk_s)
        gv_s[...] = jnp.zeros_like(gv_s)
        outs = []
        for head in range(2):
            in_q, extra_q = head_masks(rows, head)
            km = jnp.where(in_q, keys, jnp.where(extra_q, bias_s[...], 0.0)).astype(jnp.bfloat16)
            qm = jnp.where(in_q, query, jnp.where(extra_q, 1.0, 0.0)).astype(jnp.bfloat16)
            qz = jnp.where(in_q, query, 0.0).astype(jnp.bfloat16)
            gz = jnp.where(in_q, grad_out, 0.0).astype(jnp.bfloat16)
            span = slice(head * HEAD_DIM, (head + 1) * HEAD_DIM)
            pieces = []
            for start in range(0, rows, HALF):
                at = slice(start, start + HALF)
                level = lse[pl.ds(local * 2 + head, 1), at]
                delta = jnp.sum(product_t[span, at], axis=0, keepdims=True)
                soft = jnp.exp(dot_nt(km, qm[at]) - level)
                gv_s[...] += dot_nn(soft.astype(jnp.bfloat16), gz[at])
                grad_scores = (soft * (dot_nt(vals, gz[at]) - delta)).astype(jnp.bfloat16)
                gk_s[...] += dot_nn(grad_scores, qz[at])
                pieces.append(dot_nn(keys_t[span], grad_scores))
            outs.append(jnp.concatenate(pieces, axis=1))
        grad_q = jnp.transpose(jnp.concatenate(outs, axis=0))
        if not side:
            grad_q = (grad_q + gq_part[:, cols]) * scale
        gq_o[:, cols] = grad_q.astype(gq_o.dtype)
        gkv_o[:, cols] = gk_s[...].astype(gkv_o.dtype)
        gkv_o[:, vcols] = gv_s[...].astype(gkv_o.dtype)
        return carry

    for shard, ctx, lse in ((0, ctx0, lse0), (1, ctx1, lse1)):
        lax.fori_loop(0, pairs, functools.partial(pair_step, shard, ctx, lse), 0)


def qkv_back_kernel(
    info, gq, gown, gfar, attn_in, resid_two, grad_three, gain, w_qkv, got, part,
    grad_two_o, gsep_o, gedge_o, ggain_o, send_o, keep_o, w_s, attnt_s, n_s, sems,
):
    core = info[0]
    loader = Loader(sems)
    load_qkv(loader, w_qkv, got, part, core, w_s, (0, 1, 2))
    attnt_s[...] = turned(attn_in[...])
    width = w_s.shape[3]
    keep_rows = pl.ds(pl.multiple_of(core * HALF, HALF), HALF)
    send_rows = pl.ds(pl.multiple_of((1 - core) * HALF, HALF), HALF)
    loader.wait()
    grad_in = jnp.zeros(resid_two.shape, jnp.float32)
    for index in range(3):
        if index == 0:
            whole = gq[...]
        else:
            cols = slice((index - 1) * 2 * width, index * 2 * width)
            whole = (gown[:, cols] + gfar[:, cols].astype(jnp.float32)).astype(jnp.bfloat16)
        for shard in range(2):
            grad = whole[:, shard * width : (shard + 1) * width]
            at = slice(index * HALF, (index + 1) * HALF)
            send_o[shard, at] = dot_nn(attnt_s[send_rows], grad).astype(jnp.bfloat16)
            keep_o[shard, at] = dot_nn(attnt_s[keep_rows], grad).astype(jnp.bfloat16)
            grad_in = grad_in + dot_nt(grad, w_s[shard, index])
    unit, inv = row_stats(resid_two[...])
    ggain_o[...] = jnp.sum(grad_in * unit, axis=0, keepdims=True)
    grad_two = grad_three[...] + norm_grad(grad_in, unit, inv, gain[...])
    grad_two_o[...] = grad_two
    gsep_o[...] = grad_two[:, : gsep_o.shape[1]].astype(jnp.bfloat16)
    rows = n_s.shape[1]
    for tile, lanes in enumerate(lane_tiles(gsep_o.shape[1])):
        n_s[tile] = grad_two[:, lanes]
        first = n_s[tile, pl.ds(0, EDGE, stride=GROUP)]
        last = n_s[tile, pl.ds(rows - EDGE * GROUP + GROUP - 1, EDGE, stride=GROUP)]
        gedge_o[:, lanes] = jnp.where(core == 0, last, first).astype(jnp.bfloat16)


def point_kernel(info, gsep, depth, send, keep, send_o, keep_o):
    core = info[0]
    grad_sep = gsep[...]
    per_shard = depth.shape[0] // 2
    per_core = per_shard // 2
    base = send.shape[1]
    send_o[:, :base] = send[...]
    keep_o[:, :base] = keep[...]
    for shard in range(2):
        for chunk in range(per_core):
            at = slice(base + chunk * HALF, base + (chunk + 1) * HALF)
            first = shard * per_shard
            send_o[shard, at] = dot_tn(
                depth[first + (1 - core) * per_core + chunk], grad_sep
            ).astype(jnp.bfloat16)
            keep_o[shard, at] = dot_tn(
                depth[first + core * per_core + chunk], grad_sep
            ).astype(jnp.bfloat16)


def as_f32(values):
    return values.astype(jnp.float32)


def slope_of(values):
    sig = sigmoid(values)
    return sig * (1.0 + values * (1.0 - sig))


def depth_back_kernel(
    info, gsep, gedge, left_pre, right_pre, stats, pack_own, w_point, got, part,
    unit_o, scaled_o, sums_s, small_s,
    wp_s, po_s, taps_s, gse_s, gd_s, din_s, near_s, unit_s, scaled_s, wide_s, sems,
):
    core, length = info[0], info[2]
    loader = Loader(sems)
    load_point(loader, w_point, got, part, core, wp_s)
    load_pack(loader, got, part, core, po_s)
    ext = left_pre.shape[1]
    rows = ext - 2 * EDGE
    chunks = left_pre.shape[0]
    per_shard = chunks // 2
    inner = chunks * HALF
    sep_taps = pack_own.shape[0] - 1
    right_cols = right_pre.shape[1]
    stride = inner // right_cols
    reach = sep_taps // 2
    edge = gedge[...].astype(jnp.float32)
    gse_s[:rows] = gsep[...]
    gse_s[rows : rows + EDGE] = jnp.where(core == 1, edge, 0.0).astype(jnp.bfloat16)
    gse_s[rows + EDGE :] = jnp.where(core == 1, 0.0, edge).astype(jnp.bfloat16)
    wide_s[0] = row_mask(core, length, ext, LANES)
    wide_s[1] = jnp.broadcast_to(stats[:, 0:1], (ext, LANES))
    wide_s[2] = jnp.broadcast_to(stats[:, 1:2], (ext, LANES))
    scaled_s[...] = jnp.zeros_like(scaled_s)
    sums_s[...] = jnp.zeros_like(sums_s)
    small_s[...] = jnp.zeros_like(small_s)
    right_act = silu(right_pre[...]).astype(jnp.bfloat16)
    loader.wait()
    fill_taps(pack_own, po_s, taps_s)

    def first(index, carry):
        cols = pl.ds(pl.multiple_of(index * HALF, HALF), HALF)
        taps = taps_s[:, cols]
        shard, chunk = index // per_shard, index % per_shard
        point = wp_s[shard, pl.ds(pl.multiple_of(chunk * HALF, HALF), HALF)]
        grad_depth = dot_nt(gse_s[...], point)
        for side, lanes in enumerate(lane_tiles(HALF)):
            fill_window(gd_s.at[side], grad_depth[:, lanes], rows, reach)
            near_s[side, :EDGE] = grad_depth[rows : rows + EDGE, lanes]
            near_s[side, 3 * EDGE :] = grad_depth[rows + EDGE :, lanes]
            base = reach * GROUP
            near_s[side, EDGE : 2 * EDGE] = gd_s[side, pl.ds(base, EDGE, stride=GROUP)]
            base = reach * GROUP + rows - EDGE * GROUP + GROUP - 1
            near_s[side, 2 * EDGE : 3 * EDGE] = gd_s[side, pl.ds(base, EDGE, stride=GROUP)]
        mid = silu(left_pre[index].astype(jnp.float32)) + dot_nn(
            right_act, spread_block(index, right_cols, stride)
        )
        for side in range(2):
            lanes = slice(side * LANES, (side + 1) * LANES)
            unit = (mid[:, lanes] - wide_s[1]) * wide_s[2]
            unit_s[:, lanes] = unit
            fill_window(
                din_s.at[side],
                unit * wide_s[0] * taps[sep_taps : sep_taps + 1, lanes],
                rows,
                reach,
            )
            for base, target in ((EDGE - GROUP, rows + EDGE - GROUP), (3 * EDGE, rows + EDGE)):
                acc = near_s[side, base + reach : base + reach + GROUP] * taps[:1, lanes]
                for tap in range(1, sep_taps):
                    at = base + reach - tap
                    acc = acc + near_s[side, at : at + GROUP] * taps[tap : tap + 1, lanes]
                at = slice(target, target + GROUP)
                scaled_s[at, lanes] = acc * wide_s[0, at]
        step = 64
        tap_sums = []
        for side in range(2):
            lanes = slice(side * LANES, (side + 1) * LANES)
            sums = [jnp.zeros((GROUP, LANES), jnp.float32) for _ in range(sep_taps)]
            for start in range(0, rows, step):
                at = start + 2 * reach * GROUP
                acc = gd_s[side, at : at + step] * taps[:1, lanes]
                for tap in range(1, sep_taps):
                    at = start + (2 * reach - tap) * GROUP
                    acc = acc + gd_s[side, at : at + step] * taps[tap : tap + 1, lanes]
                scaled_s[start : start + step, lanes] = acc * wide_s[0, start : start + step]
                at = start + reach * GROUP
                grad = gd_s[side, at : at + step]
                for tap in range(sep_taps):
                    at = start + tap * GROUP
                    term = din_s[side, at : at + step] * grad
                    sums[tap] = sums[tap] + jnp.sum(
                        term.reshape(step // GROUP, GROUP, LANES), axis=0
                    )
            tap_sums.append(sums)
        tap_sums = [jnp.concatenate(pair, axis=1) for pair in zip(*tap_sums)]
        tap_rows = [jnp.sum(value, axis=0, keepdims=True) for value in tap_sums]
        gain = taps[sep_taps : sep_taps + 1]
        gain_row = jnp.sum(
            scaled_s[:rows] * unit_s[:rows],
            axis=0,
            keepdims=True,
        )
        filler = jnp.zeros((small_s.shape[0] - sep_taps - 1, HALF), jnp.float32)
        small_s[:, cols] = jnp.concatenate(tap_rows + [gain_row, filler], axis=0)
        scaled = scaled_s[...] * gain
        scaled_o[index] = scaled.astype(jnp.bfloat16)
        unit_o[index] = unit_s[...].astype(jnp.bfloat16)
        near, far = scaled[:, :LANES], scaled[:, LANES:]
        sums_s[0] += near + far
        sums_s[1] += near * unit_s[:, :LANES] + far * unit_s[:, LANES:]
        return carry

    lax.fori_loop(0, chunks, first, 0)


def branch_back_kernel(
    info, unit, scaled, sums, small, left_pre, right_pre, stats, branch, gain_ffn_g, gain_attn_g,
    gleft_o, gright_o, send_o, keep_o,
    wide_s, gra_s, bt_s,
):
    core = info[0]
    ext = left_pre.shape[1]
    rows = ext - 2 * EDGE
    chunks = left_pre.shape[0]
    per_shard = chunks // 2
    inner = chunks * HALF
    right_cols = right_pre.shape[1]
    stride = inner // right_cols
    for index in range(2):
        mean = jnp.sum(sums[index], axis=-1, keepdims=True) / inner
        wide_s[index] = jnp.broadcast_to(mean, (ext, LANES))
    wide_s[2] = jnp.broadcast_to(stats[:, 1:2], (ext, LANES))
    gra_s[...] = jnp.zeros_like(gra_s)
    bt_s[...] = turned(branch[...])
    keep_rows = pl.ds(pl.multiple_of(core * HALF, HALF), HALF)
    send_rows = pl.ds(pl.multiple_of((1 - core) * HALF, HALF), HALF)

    def second(index, carry):
        shard, chunk = index // per_shard, index % per_shard
        sides = []
        for side in range(2):
            lanes = slice(side * LANES, (side + 1) * LANES)
            sides.append(
                wide_s[2]
                * (as_f32(scaled[index, :, lanes]) - wide_s[0] - as_f32(unit[index, :, lanes]) * wide_s[1])
            )
        grad_mid = jnp.concatenate(sides, axis=1)
        grad_left = (
            grad_mid[:rows] * slope_of(left_pre[index, :rows].astype(jnp.float32))
        ).astype(jnp.bfloat16)
        gleft_o[index] = grad_left
        gra_s[...] += dot_nt(
            grad_mid.astype(jnp.bfloat16), spread_block(index, right_cols, stride)
        )
        at = pl.ds(pl.multiple_of(chunk * HALF, HALF), HALF)
        send_o[shard, at] = dot_nn(bt_s[send_rows, :rows], grad_left).astype(
            jnp.bfloat16
        )
        keep_o[shard, at] = dot_nn(bt_s[keep_rows, :rows], grad_left).astype(
            jnp.bfloat16
        )
        return carry

    lax.fori_loop(0, chunks, second, 0, unroll=2)
    grad_right = gra_s[...] * slope_of(right_pre[...])
    gright_o[...] = grad_right.astype(jnp.bfloat16)
    spot = lax.broadcasted_iota(jnp.int32, grad_right.shape, 0)
    own_right = jnp.where(spot < rows, grad_right, 0.0)
    part = right_cols // 2
    base = per_shard * HALF
    for target, picked, side in ((send_o, send_rows, 1 - core), (keep_o, keep_rows, core)):
        taps3 = []
        for tap in range(3):
            moved = shift_rows(own_right, 1 - tap).astype(jnp.bfloat16)
            taps3.append(dot_nn(bt_s[picked, :], moved).astype(jnp.bfloat16))
        for shard in range(2):
            cols = slice(shard * part, (shard + 1) * part)
            target[shard, base : base + HALF, :part] = taps3[0][:, cols]
            target[shard, base : base + HALF, part:] = taps3[1][:, cols]
            target[shard, base + HALF : base + 2 * HALF, :part] = taps3[2][:, cols]
            target[shard, base + HALF : base + 2 * HALF, part:] = jnp.zeros(
                (HALF, part), jnp.bfloat16
            )
            cols_here = inner // 4
            for piece in range(cols_here // LANES):
                lanes = pl.ds(
                    pl.multiple_of(
                        shard * (inner // 2) + side * cols_here + piece * LANES, LANES
                    ),
                    LANES,
                )
                row = base + HALF + piece * 16
                target[shard, row : row + 16, part:] = small[:, lanes].astype(jnp.bfloat16)
            row = base + HALF + 4 * 16
            for piece in range(4):
                lanes = slice(piece * LANES, (piece + 1) * LANES)
                both = jnp.concatenate(
                    [gain_ffn_g[:, lanes], gain_attn_g[:, lanes], jnp.zeros((14, LANES), jnp.float32)],
                    axis=0,
                )
                target[shard, row : row + 16, part:] = both.astype(jnp.bfloat16)
                row += 16


def join_back_kernel(
    info, gleft, gright, resid_one, grad_two, gain_branch, w_left, w_right, got, part_w,
    grad_one_o, ggain_o, wl_s, wr_s, sems,
):
    core, length = info[0], info[2]
    loader = Loader(sems)
    load_left(loader, w_left, got, part_w, core, wl_s)
    load_right(loader, w_right, got, part_w, core, wr_s)
    ext = gright.shape[0]
    rows = ext - 2 * EDGE
    own = slice(0, rows)
    loader.wait()
    grad_in = jnp.zeros((rows, resid_one.shape[1]), jnp.float32)
    for index in range(wl_s.shape[0]):
        grad_in = grad_in + dot_nt(gleft[index], wl_s[index])
    part = wr_s.shape[3]
    for tap in range(wr_s.shape[1]):
        product = dot_nt(gright[:, :part], wr_s[0, tap]) + dot_nt(gright[:, part:], wr_s[1, tap])
        grad_in = grad_in + shift_rows(product, 1 - tap)[own]
    grad_in = grad_in * row_mask(core, length, ext, LANES)[own, :1]
    unit, inv = row_stats(resid_one[own])
    ggain_o[...] = jnp.sum(grad_in * unit, axis=0, keepdims=True)
    grad_one_o[...] = grad_two[...] + norm_grad(grad_in, unit, inv, gain_branch[...])


def glu_back_kernel(
    info, grad_one, gain_branch_row, gain_glu, block, moved, glu_in, value, sig, w_value, w_gate,
    got, part_w,
    gin_o, send_o, keep_o,
    wv_s, wg_s, x_s, n_s, git_s, sems,
):
    core, member = info[0], info[1]
    loader = Loader(sems)
    load_pair(loader, w_value, got, part_w, 0, core, wv_s, (member, 1 - member))
    load_pair(loader, w_gate, got, part_w, 1, core, wg_s, (member, 1 - member))
    rows = grad_one.shape[0]
    own = slice(0, rows)

    @pl.when(core == member)
    def _():
        load_tiles(block, n_s)

    @pl.when(core != member)
    def _():
        load_tiles(moved, n_s)

    gather_rows(n_s, x_s)
    git_s[...] = turned(glu_in[own])
    loader.wait()
    grad_glu = grad_one[...].astype(jnp.bfloat16).astype(jnp.float32)
    keep_rows = pl.ds(pl.multiple_of(core * HALF, HALF), HALF)
    send_rows = pl.ds(pl.multiple_of((1 - core) * HALF, HALF), HALF)
    grad_norm = jnp.zeros(grad_one.shape, jnp.float32)
    for half in range(2):
        cols = slice(half * HALF, (half + 1) * HALF)
        sig_f = sig[own, cols].astype(jnp.float32)
        grad_here = grad_glu[:, cols] * sig_f
        grad_value = grad_here.astype(jnp.bfloat16)
        grad_gate = (grad_here * value[own, cols].astype(jnp.float32) * (1.0 - sig_f)).astype(
            jnp.bfloat16
        )
        slot = jnp.where(member == half, 0, 1)
        send_o[slot, :HALF] = dot_nn(git_s[send_rows], grad_value).astype(jnp.bfloat16)
        keep_o[slot, :HALF] = dot_nn(git_s[keep_rows], grad_value).astype(jnp.bfloat16)
        send_o[slot, HALF : 2 * HALF] = dot_nn(git_s[send_rows], grad_gate).astype(jnp.bfloat16)
        keep_o[slot, HALF : 2 * HALF] = dot_nn(git_s[keep_rows], grad_gate).astype(jnp.bfloat16)
        grad_norm = grad_norm + dot_nt(grad_value, wv_s[half]) + dot_nt(grad_gate, wg_s[half])
    unit, inv = row_stats(x_s[...])
    gain_glu_row = jnp.sum(grad_norm * unit, axis=0, keepdims=True)
    x_s[...] = grad_one[...] + norm_grad(grad_norm, unit, inv, gain_glu[...])
    scatter_rows(x_s, n_s, gin_o)
    tail = send_o.shape[1] - 2 * HALF
    both = jnp.concatenate(
        [gain_glu_row, gain_branch_row[...], jnp.zeros((14, 2 * HALF), jnp.float32)], axis=0
    )
    both = both.astype(jnp.bfloat16)
    for target in (send_o, keep_o):
        for shard in range(2):
            target[shard, 2 * HALF :] = jnp.zeros((tail, HALF), jnp.bfloat16)
            target[shard, 2 * HALF : 2 * HALF + 16] = both[:, :HALF]
            target[shard, 2 * HALF + 16 : 2 * HALF + 32] = both[:, HALF:]


def over_mp(values):
    return lax.ppermute(values, "mp", [(0, 1), (1, 0)])


def flat_pairs(dp_size, rule):
    pairs = []
    for dp_index in range(dp_size):
        for member in range(2):
            pair, core = dp_index // 2, dp_index % 2
            new_core, new_member = rule(core, member)
            pairs.append((dp_index * 2 + member, (pair * 2 + new_core) * 2 + new_member))
    return pairs


def unpack_kernel(layout, sizes, info, both, far, *rest):
    outs, packed, sems = rest[:-2], rest[-2], rest[-1]
    core, ybit, zpos = info[0], info[3], info[4]
    ys = both.shape[0]
    zs, step = (4, both.shape[3]) if len(both.shape) > 3 else (1, both.shape[1])
    loader = Loader(sems)
    for half in range(2):
        for yside in range(ys):
            for zside in range(zs):
                near, far_bit = zside // 2, zside % 2
                at = (yside ^ ybit, near ^ zpos % 2, far_bit ^ zpos // 2)
                if zs == 1:
                    spot = packed.at[half, pl.ds(yside * step, step)]
                    loader.either(both.at[at[0]], far.at[at[0]], core == half, spot)
                    continue
                first, base = 0, 0
                for size in sizes:
                    low = max(first, far_bit * step)
                    top = min(first + size // 2, (far_bit + 1) * step)
                    if low < top:
                        source = pl.ds(low - far_bit * step, top - low)
                        spot = base + yside * size + near * (size // 2) + low - first
                        loader.either(
                            both.at[at].at[source],
                            far.at[at].at[source],
                            core == half,
                            packed.at[half, pl.ds(spot, top - low)],
                        )
                    first += size // 2
                    base += 2 * size
    loader.wait()
    layout(packed, outs)


def layout_ffn(packed, outs):
    w_in, w_back, w_out = outs
    blocks = w_in.shape[1] // HALF
    base = blocks * HALF
    for half in range(2):
        side = slice(half * HALF, (half + 1) * HALF)
        for block in range(blocks):
            at = block * HALF
            w_in[side, block * HALF : (block + 1) * HALF] = as_f32(packed[half, at : at + HALF])
        w_back[:, side] = as_f32(packed[half, base : base + w_back.shape[0]])
        last = base + w_back.shape[0]
        w_out[:, side] = as_f32(packed[half, last : last + w_out.shape[0]])


def layout_attn(packed, outs):
    w_qkv, w_point = outs
    for half in range(2):
        for index in range(3):
            at = index * HALF
            w_qkv[index, half * HALF : (half + 1) * HALF] = as_f32(packed[half, at : at + HALF])
        at = 3 * HALF
        w_point[half * 2 * HALF : (half + 1) * 2 * HALF] = as_f32(packed[half, at : at + 2 * HALF])


def layout_branch(packed, outs):
    w_left, w_right, taps, gain, late_ffn, late_attn = outs
    count = taps.shape[0]
    blocks = w_left.shape[1] // HALF
    base = blocks * HALF
    for half in range(2):
        side = slice(half * HALF, (half + 1) * HALF)
        for block in range(blocks):
            w_left[side, block * HALF : (block + 1) * HALF] = as_f32(
                packed[half, block * HALF : (block + 1) * HALF]
            )
        w_right[0, side] = as_f32(packed[half, base : base + HALF, :LANES])
        w_right[1, side] = as_f32(packed[half, base : base + HALF, LANES:])
        w_right[2, side] = as_f32(packed[half, base + HALF : base + 2 * HALF, :LANES])
        for piece in range(4):
            row = base + HALF + piece * 16
            at = half * 4 * LANES + piece * LANES
            rows = as_f32(packed[half, row : row + 16, LANES:])
            taps[:, at : at + LANES] = rows[:count]
            gain[:, at : at + LANES] = rows[count : count + 1]
            row += 4 * 16
            rows = as_f32(packed[half, row : row + 16, LANES:])
            late_ffn[:, piece * LANES : (piece + 1) * LANES] = rows[:1]
            late_attn[:, piece * LANES : (piece + 1) * LANES] = rows[1:2]


def layout_glu(packed, outs):
    w_value, w_gate, late_glu, late_branch = outs
    for half in range(2):
        side = slice(half * HALF, (half + 1) * HALF)
        w_value[side] = as_f32(packed[half, :HALF])
        w_gate[side] = as_f32(packed[half, HALF : 2 * HALF])
        rows = as_f32(packed[0, 2 * HALF + 16 * half : 2 * HALF + 16 * (half + 1)])
        late_glu[:, side] = rows[:1]
        late_branch[:, side] = rows[1:2]


MEGA = 1024 * 1024
SPARE = 8
ALL_VMEM = 62 * MEGA


def call(body, name, ins, outs, scratch, flops, copies=0, room=None, cost=10**11):
    spaces = {"s": pltpu.SMEM, "v": pltpu.VMEM, "h": pltpu.HBM}
    shapes = [jax.ShapeDtypeStruct(shape, dtype) for shape, dtype in outs]
    held = [(a.shape, a.dtype) for a, place in ins if place == "v"] + outs + scratch
    held = sum(math.prod(shape) * jnp.dtype(dtype).itemsize for shape, dtype in held)
    scratch = [pltpu.VMEM(shape, dtype) for shape, dtype in scratch]
    if copies:
        scratch.append(pltpu.SemaphoreType.DMA((copies,)))
    return pl.pallas_call(
        body,
        out_shape=shapes,
        in_specs=[pl.BlockSpec(memory_space=spaces[place]) for _, place in ins],
        out_specs=[pl.BlockSpec(memory_space=pltpu.VMEM) for _ in shapes],
        scratch_shapes=scratch,
        name=name,
        compiler_params=pltpu.CompilerParams(vmem_limit_bytes=room or held + SPARE * MEGA),
        cost_estimate=pl.CostEstimate(flops=cost, bytes_accessed=10**6, transcendentals=0),
    )(*[array for array, _ in ins])


def dp_xor(values, bits):
    size = lax.axis_size("dp")
    return lax.ppermute(values, "dp", [(index, index ^ bits) for index in range(size)])


def over_x_and_y(values):
    pairs = []
    for dp_index in range(lax.axis_size("dp")):
        for member in range(2):
            pairs.append((dp_index * 2 + member, (dp_index ^ 2) * 2 + 1 - member))
    return lax.ppermute(values, ("dp", "mp"), pairs)


def later(values, *first):
    return lax.optimization_barrier((values, first))[0]


class Sums:
    def __init__(self, send, keep, ybit):
        self.keep, self.ybit = keep, ybit
        self.recv = dp_xor(send, 1)

    def over_xy(self, *first):
        recv, keep = later((self.recv, self.keep), *first)
        half = keep.shape[1] // 2

        def piece(shard, bit):
            at = bit * half
            cut = lambda values: as_f32(lax.dynamic_slice_in_dim(values[shard], at, half, axis=0))
            return (cut(keep) + cut(recv)).astype(jnp.bfloat16)

        self.kept = piece(0, self.ybit)
        gone = [piece(1, self.ybit), piece(0, 1 - self.ybit), piece(1, 1 - self.ybit)]
        self.got = [over_mp(gone[0]), dp_xor(gone[1], 2), over_x_and_y(gone[2])]
        return gone

    def over_x(self, *first):
        recv, keep = later((self.recv, self.keep), *first)
        other = (as_f32(keep[1]) + as_f32(recv[1])).astype(jnp.bfloat16)
        self.kept = as_f32(keep[0]) + as_f32(recv[0])
        self.got = over_mp(other)
        return [other]

    def over_y(self, *first):
        got, kept = later((self.got, self.kept), *first)
        mine = (kept + as_f32(got)).astype(jnp.bfloat16)
        half = mine.shape[0] // 2
        gone = lax.dynamic_slice_in_dim(mine, (1 - self.ybit) * half, half, axis=0)
        self.kept = lax.dynamic_slice_in_dim(mine, self.ybit * half, half, axis=0)
        self.got = dp_xor(gone, 2)
        return [gone]

    def last_quarter(self, *first):
        got, kept = later((self.got, self.kept), *first)
        return (as_f32(kept) + as_f32(got)).astype(jnp.bfloat16)

    def quarter(self, *first):
        got, kept = later((self.got, self.kept), *first)
        total = as_f32(kept) + as_f32(got[1]) + (as_f32(got[0]) + as_f32(got[2]))
        return total.astype(jnp.bfloat16)


def halve(mine, bit, across):
    half = mine.shape[0] // 2
    kept = lax.dynamic_slice_in_dim(mine, bit * half, half, axis=0)
    gone = lax.dynamic_slice_in_dim(mine, (1 - bit) * half, half, axis=0)
    return gone, (kept, dp_xor(gone, across))


class Rest:
    def __init__(self, zpos):
        self.zpos, self.pairs, self.sizes = zpos, [], []

    def over_z1(self, quarter):
        gone, pair = halve(quarter, self.zpos % 2, 4)
        self.pairs.append(pair)
        self.sizes.append(quarter.shape[0])
        return [gone]

    def over_z2(self, *first):
        pairs = later(self.pairs, *first)
        mine = [(as_f32(kept) + as_f32(got)).astype(jnp.bfloat16) for kept, got in pairs]
        gone, (self.kept, self.got) = halve(jnp.concatenate(mine, axis=0), self.zpos // 2, 8)
        return [gone]

    def back_z2(self, *first):
        got, kept = later((self.got, self.kept), *first)
        self.mine = (as_f32(kept) + as_f32(got)).astype(jnp.bfloat16)
        self.got = dp_xor(self.mine, 8)
        return [self.mine]

    def back_z1(self, *first):
        return self.double(4, *first)

    def double(self, across, *first):
        got, mine = later((self.got, self.mine), *first)
        self.mine = jnp.stack([mine, got])
        self.got = dp_xor(self.mine, across)
        return [self.mine]

    def back_y(self, *first):
        return self.double(2, *first)

    def back_core(self, *first):
        self.got, mine = later((self.got, self.mine), *first)
        self.both = jnp.stack([mine, self.got])
        self.far = dp_xor(self.both, 1)
        return [self.both]


class Short(Rest):
    def along_z1(self, quarter):
        self.sizes.append(quarter.shape[0])
        self.mine, self.got = quarter, dp_xor(quarter, 4)
        return [quarter]

    def along_z2(self, *first):
        got, mine = later((self.got, self.mine), *first)
        self.mine = (as_f32(mine) + as_f32(got)).astype(jnp.bfloat16)
        self.got = dp_xor(self.mine, 8)
        return [self.mine]

    def back_y(self, *first):
        got, mine = later((self.got, self.mine), *first)
        self.mine = (as_f32(mine) + as_f32(got)).astype(jnp.bfloat16)
        self.got = dp_xor(self.mine, 2)
        return [self.mine]


def unpack(layout, info, sums, outs):
    ys, cols = 2, sums.both.shape[-1]
    zs, part = (4, sums.both.shape[3]) if sums.both.ndim > 3 else (1, sums.both.shape[1])
    return call(
        functools.partial(unpack_kernel, layout, sums.sizes),
        "unpack_" + layout.__name__,
        [(info, "s"), (sums.both, "h"), (sums.far, "h")],
        [(shape, jnp.float32) for shape in outs],
        [((2, ys * zs * part, cols), jnp.bfloat16)],
        1e6,
        4 * ys * (zs + len(sums.sizes)),
    )


def paired(
    inputs, lengths, gain_glu, w_value, w_gate, gain_branch, w_left, w_right, gain_mid, w_depth,
    w_point, gain_attn, w_qkv, w_out, gain_ffn, w_in, w_back, cotangent,
):
    low, full = jnp.bfloat16, jnp.float32
    member = lax.axis_index("mp")
    place = lax.axis_index("dp")
    core, ybit, zpos = place % 2, (place // 2) % 2, place // 4
    rows, width = inputs.shape[1:]
    ext = rows + 2 * EDGE
    inner = 2 * w_left.shape[1]
    chunks = inner // HALF
    right_cols = 2 * w_right.shape[2]
    sep_width = w_point.shape[1]
    heads = 2 * w_qkv.shape[2] // HEAD_DIM
    row = lambda gain: gain.reshape(1, -1)

    block = inputs[0]
    edge = jnp.where(member == 0, block[rows - EDGE :], block[:EDGE])
    size_code = jnp.stack([lengths[0] // 32, lengths[0] % 32]).astype(low)
    code_rows = jnp.broadcast_to(jnp.repeat(size_code, EDGE // 2)[:, None], (EDGE, width))
    edge = jnp.concatenate([edge, code_rows], axis=0)
    edge = lax.ppermute(
        edge, ("dp", "mp"), flat_pairs(lax.axis_size("dp"), lambda c, m: (1 - m, c))
    )
    code = as_f32(edge[EDGE:, 0])
    length = (code[0] * 32 + code[EDGE // 2]).astype(jnp.int32)
    edge = edge[:EDGE]
    swap = [p for p in flat_pairs(lax.axis_size("dp"), lambda c, m: (m, c)) if p[0] != p[1]]
    moved = lax.ppermute(block, ("dp", "mp"), swap)
    info = jnp.stack([core, member, length, ybit, zpos]).astype(jnp.int32)

    v = lambda *arrays: [(array, "v") for array in arrays]
    h = lambda *arrays: [(array, "h") for array in arrays]
    pack = jnp.concatenate([w_depth, gain_mid[None]], axis=0)
    got0 = over_mp(jnp.where(core == 0, w_value, w_gate))
    blocks = w_left.shape[1] // HALF
    bundle1, bundle2, bundle3 = call(
        bundle_kernel, "bundle",
        [(jnp.stack([core, member]).astype(jnp.int32), "s")]
        + h(w_left, w_right, w_point) + v(w_depth, row(gain_mid)) + h(w_qkv, w_out, w_in, w_back),
        [((blocks * (width + 16), HALF), low)] + [((3 * width, HALF), low)] * 2,
        [], 1, 16, ALL_VMEM,
    )
    got1 = over_mp(bundle1)
    part0 = dp_xor(got0, 1)
    cot = cotangent[0]
    cot_moved = lax.ppermute(cot, ("dp", "mp"), swap)

    where = [(info, "s")]
    macs = 2.0 * rows * width
    cot, resid_one, branch_in, glu_in, value, sig = call(
        glu_kernel, "glu",
        where + v(block, moved, cot, cot_moved, edge, row(gain_glu), row(gain_branch))
        + h(w_value, w_gate, got0, part0),
        [((rows, width), low), ((ext, width), full)] + [((ext, width), low)] * 4,
        [((ext, width), full), ((rows, width), full), ((width // LANES, rows, LANES), full)]
        + [((2,) + w_value.shape, low)] * 2,
        macs * width * 2, 8,
    )
    left_own, right_own, mid_own, sums_own = call(
        branch_own_kernel, "branch_own",
        where + v(branch_in) + h(w_left) + v(w_right),
        [
            ((chunks // 2, ext, HALF), low), ((ext, right_cols // 2), full),
            ((chunks // 2, ext, HALF), full), ((2, ext, LANES), full),
        ],
        [((chunks // 2, width, HALF), low)],
        1, chunks // 2,
    )
    got1 = later(got1, sums_own)
    part1 = dp_xor(got1, 1)
    got2 = over_mp(later(bundle2, got1))
    got3 = over_mp(later(bundle3, got1))
    resid_two, left_pre, right_pre, stats, depth = call(
        branch_kernel, "branch",
        where
        + v(branch_in, resid_one, pack, left_own, right_own, mid_own, sums_own)
        + h(w_point, got1, part1),
        [
            ((rows, width), full), ((chunks, ext, HALF), low), ((ext, right_cols), full),
            ((ext, LANES), full), ((chunks, rows, HALF), low),
        ],
        [
            ((chunks // 2, width, HALF), low), (w_right.shape, low), ((2,) + w_point.shape, low),
            ((4, 16, HALF), low), ((16, inner), full), ((chunks, ext, HALF), full),
            ((rows + 64, HALF), full), ((2, ext, LANES), full), ((rows, sep_width), full),
        ],
        1, 20,
    )
    got2 = later(got2, resid_two)
    part2 = dp_xor(got2, 1)
    attn_in, kv_own = call(
        kv_kernel, "keys_values",
        where + v(resid_two, row(gain_attn)) + h(w_qkv, got2, part2),
        [((rows, width), low), ((rows, 2 * width), low)],
        [((2, 2) + w_qkv.shape[1:], low)],
        macs * width * 2, 8,
    )
    (queries,) = call(
        query_kernel, "queries",
        where + v(attn_in) + h(w_qkv, got2, part2),
        [((rows, width), low)],
        [((2, 1) + w_qkv.shape[1:], low)],
        macs * width, 4,
    )
    kv_far = dp_xor(kv_own, 1)
    context0, lse0, context1, lse1 = call(
        attend_kernel, "attend",
        where + v(queries, kv_own, kv_far),
        [((rows, width // 2), low), ((heads // 2, rows), full)] * 2,
        [((2 * rows, LANES), full)],
        macs * 8000,
    )
    part3 = dp_xor(later(got3, lse1), 1)
    r_ffn = 2 * w_in.shape[1] + w_out.shape[0]
    out_rows, grad_three, grad_ctx, ggain_ffn, send, keep = call(
        ffn_kernel, "ffn",
        where + v(resid_two, context0, context1, cot, row(gain_ffn))
        + h(w_out, w_in, w_back, got2, part2, got3, part3),
        [
            ((rows, width), low), ((rows, width), full), ((rows, width), low), ((1, width), full),
            ((2, r_ffn, HALF), low), ((2, r_ffn, HALF), low),
        ],
        [
            ((2,) + w_out.shape, low), ((chunks, width, HALF), low), ((2,) + w_back.shape, low),
            ((rows, width), low), ((width, rows), low), ((rows, width), low), ((rows, width), full),
            ((rows, width), full), ((width, rows), low), ((width // LANES, rows, LANES), full),
        ],
        macs * 16000, 24, ALL_VMEM,
    )
    ffn_sums = Sums(send, keep, ybit)
    swapped_out = lax.ppermute(out_rows, ("dp", "mp"), swap)

    seen = v(context0, context1, grad_ctx, lse0, lse1)
    grad_q, grad_far = call(
        functools.partial(attend_back_kernel, 1), "attend_back_far",
        where + v(queries, kv_far) + seen,
        [((rows, width), full), ((rows, 2 * width), low)],
        [((rows, LANES), full)] * 3, 1,
    )
    recv = dp_xor(grad_far, 1)
    sent = ffn_sums.over_xy(grad_q)
    out_rows, swapped_out = later((out_rows, swapped_out), *sent)
    outputs = jnp.where(member == core, out_rows, swapped_out)
    sent.append(outputs)
    grad_q, grad_own = call(
        functools.partial(attend_back_kernel, 0), "attend_back_own",
        [(later(info, *sent), "s")] + v(queries, kv_own) + seen + v(grad_q),
        [((rows, width), low), ((rows, 2 * width), full)],
        [((rows, LANES), full)] * 3, 1,
    )
    grad_two, grad_sep, sep_edge, ggain_attn, send, keep = call(
        qkv_back_kernel, "qkv_back",
        where
        + v(grad_q, grad_own, recv, attn_in, resid_two, grad_three, row(gain_attn))
        + h(w_qkv, got2, part2),
        [
            ((rows, width), full), ((rows, sep_width), low), ((EDGE, sep_width), low),
            ((1, width), full),
        ]
        + [((2, 3 * HALF, HALF), low)] * 2,
        [
            ((2,) + w_qkv.shape, low), ((width, rows), low),
            ((sep_width // LANES, rows, LANES), full),
        ],
        1, 12,
    )
    sep_edge = dp_xor(sep_edge, 1)
    send, keep = call(
        point_kernel, "point_back",
        where + v(grad_sep, depth, send, keep),
        [((2, 5 * HALF, HALF), low)] * 2, [], macs * 1000,
    )
    attn_sums = Sums(send, keep, ybit)
    unit, scaled, mid_sums, small = call(
        depth_back_kernel, "depth_back",
        where
        + v(grad_sep, sep_edge, left_pre, right_pre, stats, pack)
        + h(w_point, got1, part1),
        [
            ((chunks, ext, HALF), low), ((chunks, ext, HALF), low), ((2, ext, LANES), full),
            ((16, inner), full),
        ],
        [
            ((2,) + w_point.shape, low), ((4, 16, HALF), low), ((16, inner), full),
            ((ext, sep_width), low),
            ((2, rows + 64, LANES), full), ((2, rows + 64, LANES), full),
            ((2, 4 * EDGE, LANES), full), ((ext, HALF), full), ((ext, HALF), full),
            ((3, ext, LANES), full),
        ],
        macs * 8000, 8,
    )
    ffn_rest = Rest(zpos)
    sent = ffn_rest.over_z1(ffn_sums.quarter(mid_sums))
    sent += attn_sums.over_x(*sent)
    r_branch = inner // 2 + 2 * HALF
    grad_left, grad_right, send, keep = call(
        branch_back_kernel, "branch_back",
        [(later(info, *sent), "s")]
        + v(
            unit, scaled, mid_sums, small, left_pre, right_pre, stats, branch_in, ggain_ffn,
            ggain_attn,
        ),
        [
            ((chunks, rows, HALF), low), ((ext, right_cols), low),
            ((2, r_branch, HALF), low), ((2, r_branch, HALF), low),
        ],
        [((3, ext, LANES), full), ((ext, right_cols), full), ((width, ext), low)],
        macs * 4000,
    )
    branch_sums = Sums(send, keep, ybit)
    sent = ffn_rest.over_z2(grad_left)
    sent += attn_sums.over_y(*sent)
    grad_one, ggain_branch = call(
        join_back_kernel, "join_back",
        [(later(info, *sent), "s")]
        + v(grad_left, grad_right, resid_one, grad_two, row(gain_branch))
        + h(w_left, w_right, got1, part1),
        [((rows, width), full), ((1, width), full)],
        [((chunks, width, HALF), low), ((2,) + w_right.shape, low)],
        macs * 4000, 12,
    )
    sent = ffn_rest.back_z2(grad_one)
    sent += branch_sums.over_xy(*sent)
    attn_rest = Rest(zpos)
    grad_in, send, keep = call(
        glu_back_kernel, "glu_back",
        [(later(info, *sent), "s")]
        + v(grad_one, ggain_branch, row(gain_glu), block, moved, glu_in, value, sig)
        + h(w_value, w_gate, got0, part0),
        [((rows, width), low), ((2, 640, HALF), low), ((2, 640, HALF), low)],
        [
            ((2,) + w_value.shape, low), ((2,) + w_gate.shape, low), ((rows, width), full),
            ((width // LANES, rows, LANES), full), ((width, rows), low),
        ],
        macs * 3000, 4,
    )
    glu_sums = Sums(send, keep, ybit)
    swapped_in = lax.ppermute(grad_in, ("dp", "mp"), swap)
    branch_rest, glu_rest = Rest(zpos), Short(zpos)
    sent = attn_rest.over_z1(attn_sums.last_quarter(grad_in))
    sent = ffn_rest.back_z1(*sent)
    sent = branch_rest.over_z1(branch_sums.quarter(*sent))
    sent = glu_sums.over_x(*sent)
    sent = attn_rest.over_z2(*sent)
    sent = ffn_rest.back_y(*sent)
    sent = branch_rest.over_z2(*sent)
    sent = glu_sums.over_y(*sent)
    sent = attn_rest.back_z2(*sent)
    sent = branch_rest.back_z2(*sent)
    sent = glu_rest.along_z1(glu_sums.last_quarter(*sent))
    grad_in, swapped_in = later((grad_in, swapped_in), *sent)
    grad_inputs = jnp.where(member == core, grad_in, swapped_in)
    sent = ffn_rest.back_core(grad_inputs)
    sent = glu_rest.along_z2(*sent)
    sent = branch_rest.back_z1(*sent)
    sent = attn_rest.back_z1(*sent)
    sent = branch_rest.back_y(*sent)
    sent = glu_rest.back_y(*sent)
    sent = attn_rest.back_y(*sent)
    g_in, g_back, g_out = unpack(
        layout_ffn, later(info, *sent), ffn_rest, [w_in.shape, w_back.shape, w_out.shape]
    )
    sent = branch_rest.back_core(g_in)
    sent = glu_rest.back_core(*sent)
    g_value, g_gate, g_glu_gain, g_branch_gain = unpack(
        layout_glu, later(info, *sent), glu_rest,
        [w_value.shape, w_gate.shape, (1, width), (1, width)],
    )
    g_left, g_right, g_taps, g_mid, g_ffn_gain, g_attn_gain = unpack(
        layout_branch, later(info, g_value), branch_rest,
        [
            w_left.shape, w_right.shape, w_depth.shape, (1, inner // 2), (1, width), (1, width),
        ],
    )
    sent = attn_rest.back_core(g_left)
    g_qkv, g_point = unpack(
        layout_attn, later(info, *sent), attn_rest, [w_qkv.shape, w_point.shape]
    )
    flat = lambda gain: gain.reshape(-1)
    return (
        outputs[None],
        grad_inputs[None],
        flat(g_glu_gain),
        g_value,
        g_gate,
        flat(g_branch_gain),
        g_left,
        g_right,
        flat(g_mid),
        g_taps,
        g_point,
        flat(g_attn_gain),
        g_qkv,
        g_out,
        flat(g_ffn_gain),
        g_in,
        g_back,
    )


def solution(mesh):
    placed = (
        P("dp", "mp", None),
        P("dp"),
        P(),
        P(None, "mp"),
        P(None, "mp"),
        P(),
        P(None, "mp"),
        P(None, None, "mp"),
        P("mp"),
        P(None, "mp"),
        P("mp", None),
        P(),
        P(None, None, "mp"),
        P("mp", None),
        P(),
        P(None, "mp"),
        P("mp", None),
        P("dp", "mp", None),
    )
    fast = mesh.shape["mp"] == 2 and mesh.shape["dp"] == 16
    return jax.shard_map(
        paired if fast else local,
        mesh=mesh,
        in_specs=placed,
        out_specs=(
            P("dp", "mp", None),
            P("dp", "mp", None),
            P(),
            P(None, "mp"),
            P(None, "mp"),
            P(),
            P(None, "mp"),
            P(None, None, "mp"),
            P("mp"),
            P(None, "mp"),
            P("mp", None),
            P(),
            P(None, None, "mp"),
            P("mp", None),
            P(),
            P(None, "mp"),
            P("mp", None),
        ),
        check_vma=False,
    )
```

```python
import functools
import math

import jax
import jax.numpy as jnp
from jax import lax
from jax.experimental import pallas as pl
from jax.experimental.pallas import tpu as pltpu
from jax.sharding import PartitionSpec as P

FF = 2048
HEAD_DIM = 64
EDGE = 16


epsilon = 1e-06
negative_big = -1e30


def matmul(left_side, right_side):
    return jnp.dot(left_side, right_side, preferred_element_type=jnp.float32)


def contract_rows(left_side, right_side):
    return lax.dot_general(
        left_side, right_side, (((0,), (0,)), ((), ())), preferred_element_type=jnp.float32
    )


def contract_cols(left_side, right_side):
    return lax.dot_general(
        left_side, right_side, (((1,), (1,)), ((), ())), preferred_element_type=jnp.float32
    )


def spread_rows(pieces):
    return lax.all_gather(pieces, "mp", axis=1, tiled=True)


def collect_rows(partial_value):
    return lax.psum_scatter(
        partial_value.astype(jnp.bfloat16), "mp", scatter_dimension=1, tiled=True
    ).astype(jnp.float32)


def channel_sums(former, latter):
    return lax.psum((jnp.sum(former, axis=-1), jnp.sum(latter, axis=-1)), "mp")


def normalize(values, gain_vec):
    centre = values - jnp.mean(values, axis=-1, keepdims=True)
    scale_inv = lax.rsqrt(jnp.mean(centre * centre, axis=-1, keepdims=True) + epsilon)
    unit_rows = centre * scale_inv
    return (unit_rows * gain_vec, unit_rows, scale_inv)


def normalize_back(grad_out, unit_rows, scale_inv, gain_vec):
    scaled = grad_out * gain_vec
    mean_one = jnp.mean(scaled, axis=-1, keepdims=True)
    mean_two = jnp.mean(scaled * unit_rows, axis=-1, keepdims=True)
    grad_in = scale_inv * (scaled - mean_one - unit_rows * mean_two)
    return (grad_in, jnp.sum(grad_out * unit_rows, axis=(0, 1)))


def silu_slope(values):
    sigmoid_part = jax.nn.sigmoid(values)
    return sigmoid_part * (1.0 + values * (1.0 - sigmoid_part))


def shifted(values, offset):
    if offset == 0:
        return values
    margin = abs(offset)
    seq_len = values.shape[1]
    filler = jnp.zeros(values.shape[:1] + (margin,) + values.shape[2:], values.dtype)
    padded = jnp.concatenate([filler, values, filler], axis=1)
    return lax.slice_in_dim(padded, margin + offset, margin + offset + seq_len, axis=1)


def place_right(right_vals, stride):
    filler = jnp.zeros(right_vals.shape + (stride - 1,), right_vals.dtype)
    joined = jnp.concatenate([right_vals[..., None], filler], axis=-1)
    return joined.reshape(right_vals.shape[:-1] + (right_vals.shape[-1] * stride,))


def attend_forward(queries, key_vecs, value_vecs, key_valid, block_rows, score_scale):
    contexts = []
    log_parts = []
    for row_start in range(0, queries.shape[0], block_rows):
        query_rows = queries[row_start : row_start + block_rows]
        scores = (
            jnp.einsum("qhd,khd->hqk", query_rows, key_vecs, preferred_element_type=jnp.float32)
            * score_scale
        )
        scores = jnp.where(key_valid[None, None, :], scores, negative_big)
        row_max = jnp.max(scores, axis=-1, keepdims=True)
        weights_exp = jnp.exp(scores - row_max)
        row_total = jnp.sum(weights_exp, axis=-1, keepdims=True)
        probability = (weights_exp / row_total).astype(jnp.bfloat16)
        contexts.append(
            jnp.einsum("hqk,khd->qhd", probability, value_vecs, preferred_element_type=jnp.float32)
        )
        log_parts.append((row_max + jnp.log(row_total))[..., 0])
    return (jnp.concatenate(contexts, axis=0), jnp.concatenate(log_parts, axis=1))


def attend_back(
    queries, key_vecs, value_vecs, key_valid, log_sums, grad_context, block_rows, score_scale
):
    grad_queries = []
    grad_keys = jnp.zeros(key_vecs.shape, jnp.float32)
    grad_values = jnp.zeros(value_vecs.shape, jnp.float32)
    for row_start in range(0, queries.shape[0], block_rows):
        query_rows = queries[row_start : row_start + block_rows]
        grad_rows = grad_context[row_start : row_start + block_rows]
        log_rows = log_sums[:, row_start : row_start + block_rows]
        scores = (
            jnp.einsum("qhd,khd->hqk", query_rows, key_vecs, preferred_element_type=jnp.float32)
            * score_scale
        )
        scores = jnp.where(key_valid[None, None, :], scores, negative_big)
        probability = jnp.exp(scores - log_rows[..., None])
        grad_prob = jnp.einsum(
            "qhd,khd->hqk", grad_rows, value_vecs, preferred_element_type=jnp.float32
        )
        row_dot = jnp.sum(probability * grad_prob, axis=-1, keepdims=True)
        grad_scores = (probability * (grad_prob - row_dot)).astype(jnp.bfloat16)
        grad_queries.append(
            jnp.einsum("hqk,khd->qhd", grad_scores, key_vecs, preferred_element_type=jnp.float32)
            * score_scale
        )
        grad_keys = (
            grad_keys
            + jnp.einsum(
                "hqk,qhd->khd", grad_scores, query_rows, preferred_element_type=jnp.float32
            )
            * score_scale
        )
        grad_values = grad_values + jnp.einsum(
            "hqk,qhd->khd",
            probability.astype(jnp.bfloat16),
            grad_rows,
            preferred_element_type=jnp.float32,
        )
    grad_query_all = jnp.concatenate(grad_queries, axis=0)
    return (grad_query_all.astype(jnp.bfloat16), grad_keys, grad_values)


def split_pass(
    inputs,
    lengths,
    gain_glu,
    w_value,
    w_gate,
    gain_branch,
    w_left,
    w_right,
    gain_mid,
    w_depth,
    w_point,
    gain_attn,
    w_qkv,
    w_out,
    gain_ffn,
    w_in,
    w_back,
    cotangent,
):
    seqs_here, local_len, model_width = inputs.shape
    group_size = lax.axis_size("mp")
    member = lax.axis_index("mp")
    seq_len = local_len * group_size
    group_rows = seqs_here * seq_len
    positions = lax.broadcasted_iota(jnp.int32, (seqs_here, seq_len), 1)
    key_valid = positions < lengths[:, None]
    valid_full = key_valid.astype(jnp.float32)
    valid_own = lax.dynamic_slice_in_dim(valid_full, member * local_len, local_len, axis=1)
    inner_cols = w_left.shape[1]
    right_cols = w_right.shape[2]
    stride = inner_cols // right_cols
    conv_taps = w_right.shape[0]
    sep_taps = w_depth.shape[0]
    sep_width = w_point.shape[1]
    head_cols = w_qkv.shape[2]
    heads_here = head_cols // HEAD_DIM
    score_scale = 1.0 / math.sqrt(HEAD_DIM)
    block_rows = min(512, seq_len)
    group_shape = (seqs_here, seq_len, model_width)
    depth_taps = w_depth.astype(jnp.float32)
    gain_mid_f = gain_mid.astype(jnp.float32)

    def branch_inner(gathered):
        flat_rows = gathered.reshape(group_rows, model_width)
        left_pre = matmul(flat_rows, w_left).reshape(seqs_here, seq_len, inner_cols)
        right_pre = jnp.zeros((group_rows, right_cols), jnp.float32)
        for tap_index in range(conv_taps):
            moved = shifted(gathered, tap_index - conv_taps // 2).reshape(group_rows, model_width)
            right_pre = right_pre + matmul(moved, w_right[tap_index])
        right_pre = right_pre.reshape(seqs_here, seq_len, right_cols)
        mid = jax.nn.silu(left_pre) + place_right(jax.nn.silu(right_pre), stride)
        return (left_pre, right_pre, mid)

    def depth_mix(depth_in):
        depth = jnp.zeros(depth_in.shape, jnp.float32)
        for tap_index in range(sep_taps):
            depth = depth + shifted(depth_in, tap_index - sep_taps // 2) * depth_taps[tap_index]
        return depth.astype(jnp.bfloat16)

    def project_qkv(gathered):
        flat_rows = gathered.reshape(group_rows, model_width)
        joined = jnp.einsum("td,kdc->ktc", flat_rows, w_qkv, preferred_element_type=jnp.float32)
        return joined.astype(jnp.bfloat16).reshape(3, seqs_here, seq_len, heads_here, HEAD_DIM)

    def forward_one(pieces):
        return attend_forward(pieces[0], pieces[1], pieces[2], pieces[3], block_rows, score_scale)

    def backward_one(pieces):
        return attend_back(
            pieces[0],
            pieces[1],
            pieces[2],
            pieces[3],
            pieces[4],
            pieces[5],
            block_rows,
            score_scale,
        )

    resid_in = inputs.astype(jnp.float32)
    normed_glu, unit_glu, inv_glu = normalize(resid_in, gain_glu)
    gathered_glu = spread_rows(normed_glu.astype(jnp.bfloat16))
    flat_glu = gathered_glu.reshape(group_rows, model_width)
    value_pre = matmul(flat_glu, w_value)
    gate_sig = jax.nn.sigmoid(matmul(flat_glu, w_gate))
    glu_local = (value_pre * gate_sig).astype(jnp.bfloat16).reshape(seqs_here, seq_len, -1)
    glu_rows = lax.all_to_all(glu_local, "mp", split_axis=1, concat_axis=2, tiled=True)
    resid_one = resid_in + glu_rows.astype(jnp.float32)
    normed_branch, unit_branch, inv_branch = normalize(resid_one, gain_branch)
    gathered_branch = spread_rows((valid_own[..., None] * normed_branch).astype(jnp.bfloat16))
    left_pre, right_pre, mid = branch_inner(gathered_branch)
    mid_sum, mid_square = channel_sums(mid, mid * mid)
    mid_mean = mid_sum / FF
    inv_mid = lax.rsqrt(mid_square / FF - mid_mean * mid_mean + epsilon)
    unit_mid = (mid - mid_mean[..., None]) * inv_mid[..., None]
    depth_in = valid_full[..., None] * unit_mid * gain_mid_f
    depth_low = depth_mix(depth_in)
    sep_part = matmul(depth_low.reshape(group_rows, inner_cols), w_point).reshape(
        seqs_here, seq_len, sep_width
    )
    sep_rows = collect_rows(sep_part)
    resid_two = resid_one + jnp.pad(sep_rows, ((0, 0), (0, 0), (0, model_width - sep_width)))
    normed_attn, unit_attn, inv_attn = normalize(resid_two, gain_attn)
    gathered_attn = spread_rows(normed_attn.astype(jnp.bfloat16))
    qkv_heads = project_qkv(gathered_attn)
    context, log_sums = lax.map(forward_one, (qkv_heads[0], qkv_heads[1], qkv_heads[2], key_valid))
    context_low = context.astype(jnp.bfloat16).reshape(group_rows, head_cols)
    attn_rows = collect_rows(matmul(context_low, w_out).reshape(group_shape))
    resid_three = resid_two + attn_rows
    normed_ffn, unit_ffn, inv_ffn = normalize(resid_three, gain_ffn)
    gathered_ffn = spread_rows(normed_ffn.astype(jnp.bfloat16))
    ffn_flat = gathered_ffn.reshape(group_rows, model_width)
    ffn_pre = matmul(ffn_flat, w_in)
    ffn_hidden = jax.nn.silu(ffn_pre).astype(jnp.bfloat16)
    final_rows = resid_three + collect_rows(matmul(ffn_hidden, w_back).reshape(group_shape))
    outputs = final_rows.astype(jnp.bfloat16)
    cot_full = spread_rows(cotangent).reshape(group_rows, model_width)
    ffn_flat = spread_rows(normed_ffn.astype(jnp.bfloat16)).reshape(group_rows, model_width)
    ffn_pre = matmul(ffn_flat, w_in)
    ffn_hidden = jax.nn.silu(ffn_pre).astype(jnp.bfloat16)
    grad_hidden = contract_cols(cot_full, w_back)
    grad_ffn_pre = (grad_hidden * silu_slope(ffn_pre)).astype(jnp.bfloat16)
    grad_w_back = contract_rows(ffn_hidden, cot_full)
    grad_w_in = contract_rows(ffn_flat, grad_ffn_pre)
    grad_normed_ffn = collect_rows(contract_cols(grad_ffn_pre, w_in).reshape(group_shape))
    grad_resid, grad_gain_ffn = normalize_back(grad_normed_ffn, unit_ffn, inv_ffn, gain_ffn)
    grad_three = cotangent.astype(jnp.float32) + grad_resid
    grad_attn = spread_rows(grad_three.astype(jnp.bfloat16)).reshape(group_rows, model_width)
    gathered_attn = spread_rows(normed_attn.astype(jnp.bfloat16))
    qkv_heads = project_qkv(gathered_attn)
    attn_flat = gathered_attn.reshape(group_rows, model_width)
    grad_w_out = contract_rows(context_low, grad_attn)
    grad_context = contract_cols(grad_attn, w_out).astype(jnp.bfloat16)
    grad_context = grad_context.reshape(seqs_here, seq_len, heads_here, HEAD_DIM)
    grad_q, grad_k, grad_v = lax.map(
        backward_one, (qkv_heads[0], qkv_heads[1], qkv_heads[2], key_valid, log_sums, grad_context)
    )
    grad_qkv = jnp.stack(
        [grad_q, grad_k.astype(jnp.bfloat16), grad_v.astype(jnp.bfloat16)]
    ).reshape(3, group_rows, head_cols)
    grad_w_qkv = jnp.einsum("td,ktc->kdc", attn_flat, grad_qkv, preferred_element_type=jnp.float32)
    grad_attn_in = jnp.einsum("ktc,kdc->td", grad_qkv, w_qkv, preferred_element_type=jnp.float32)
    grad_normed_attn = collect_rows(grad_attn_in.reshape(group_shape))
    grad_resid, grad_gain_attn = normalize_back(grad_normed_attn, unit_attn, inv_attn, gain_attn)
    grad_two = grad_three + grad_resid
    grad_sep = spread_rows(grad_two[..., :sep_width].astype(jnp.bfloat16)).reshape(
        group_rows, sep_width
    )
    gathered_branch = spread_rows((valid_own[..., None] * normed_branch).astype(jnp.bfloat16))
    left_pre, right_pre, mid = branch_inner(gathered_branch)
    unit_mid = (mid - mid_mean[..., None]) * inv_mid[..., None]
    depth_in = valid_full[..., None] * unit_mid * gain_mid_f
    depth_low = depth_mix(depth_in)
    grad_w_point = contract_rows(depth_low.reshape(group_rows, inner_cols), grad_sep)
    grad_depth = contract_cols(grad_sep, w_point).reshape(seqs_here, seq_len, inner_cols)
    grad_depth_in = jnp.zeros(grad_depth.shape, jnp.float32)
    depth_rows = []
    for tap_index in range(sep_taps):
        offset = tap_index - sep_taps // 2
        grad_depth_in = grad_depth_in + shifted(grad_depth, -offset) * depth_taps[tap_index]
        depth_rows.append(jnp.sum(shifted(depth_in, offset) * grad_depth, axis=(0, 1)))
    grad_w_depth = jnp.stack(depth_rows)
    grad_unit = grad_depth_in * valid_full[..., None]
    grad_gain_mid = jnp.sum(grad_unit * unit_mid, axis=(0, 1))
    scaled = grad_unit * gain_mid_f
    sum_one, sum_two = channel_sums(scaled, scaled * unit_mid)
    grad_mid = inv_mid[..., None] * (
        scaled - (sum_one / FF)[..., None] - unit_mid * (sum_two / FF)[..., None]
    )
    grad_left = (
        (grad_mid * silu_slope(left_pre)).astype(jnp.bfloat16).reshape(group_rows, inner_cols)
    )
    grad_right_act = grad_mid.reshape(seqs_here, seq_len, right_cols, stride)[..., 0]
    grad_right = (
        (grad_right_act * silu_slope(right_pre))
        .astype(jnp.bfloat16)
        .reshape(group_rows, right_cols)
    )
    branch_flat = gathered_branch.reshape(group_rows, model_width)
    grad_w_left = contract_rows(branch_flat, grad_left)
    grad_branch_in = contract_cols(grad_left, w_left).reshape(group_shape)
    right_rows = []
    for tap_index in range(conv_taps):
        offset = tap_index - conv_taps // 2
        moved = shifted(gathered_branch, offset).reshape(group_rows, model_width)
        right_rows.append(contract_rows(moved, grad_right))
        grad_branch_in = grad_branch_in + shifted(
            contract_cols(grad_right, w_right[tap_index]).reshape(group_shape), -offset
        )
    grad_w_right = jnp.stack(right_rows)
    grad_normed_branch = collect_rows(grad_branch_in) * valid_own[..., None]
    grad_resid, grad_gain_branch = normalize_back(
        grad_normed_branch, unit_branch, inv_branch, gain_branch
    )
    grad_one = grad_two + grad_resid
    grad_glu = lax.all_to_all(
        grad_one.astype(jnp.bfloat16), "mp", split_axis=2, concat_axis=1, tiled=True
    )
    grad_glu_flat = grad_glu.reshape(group_rows, -1).astype(jnp.float32)
    flat_glu = spread_rows(normed_glu.astype(jnp.bfloat16)).reshape(group_rows, model_width)
    value_pre = matmul(flat_glu, w_value)
    gate_sig = jax.nn.sigmoid(matmul(flat_glu, w_gate))
    grad_value = (grad_glu_flat * gate_sig).astype(jnp.bfloat16)
    grad_gate = (grad_glu_flat * value_pre * gate_sig * (1.0 - gate_sig)).astype(jnp.bfloat16)
    grad_w_value = contract_rows(flat_glu, grad_value)
    grad_w_gate = contract_rows(flat_glu, grad_gate)
    grad_glu_in = contract_cols(grad_value, w_value) + contract_cols(grad_gate, w_gate)
    grad_normed_glu = collect_rows(grad_glu_in.reshape(group_shape))
    grad_resid, grad_gain_glu = normalize_back(grad_normed_glu, unit_glu, inv_glu, gain_glu)
    grad_inputs = (grad_one + grad_resid).astype(jnp.bfloat16)
    gains = (grad_gain_glu, grad_gain_branch, grad_gain_attn, grad_gain_ffn)
    shards = (
        grad_w_value,
        grad_w_gate,
        grad_w_left,
        grad_w_right,
        grad_gain_mid,
        grad_w_depth,
        grad_w_point,
        grad_w_qkv,
        grad_w_out,
        grad_w_in,
        grad_w_back,
    )
    return (outputs, grad_inputs, gains, shards)


def local(
    inputs,
    lengths,
    gain_glu,
    w_value,
    w_gate,
    gain_branch,
    w_left,
    w_right,
    gain_mid,
    w_depth,
    w_point,
    gain_attn,
    w_qkv,
    w_out,
    gain_ffn,
    w_in,
    w_back,
    cotangent,
):
    outputs, grad_inputs, gains, shards = split_pass(
        inputs,
        lengths,
        gain_glu,
        w_value,
        w_gate,
        gain_branch,
        w_left,
        w_right,
        gain_mid,
        w_depth,
        w_point,
        gain_attn,
        w_qkv,
        w_out,
        gain_ffn,
        w_in,
        w_back,
        cotangent,
    )
    gain_totals = lax.psum((gains[0], gains[1], gains[2], gains[3]), ("dp", "mp"))
    weight_totals = (
        lax.psum(shards[0].astype(jnp.bfloat16), "dp").astype(jnp.float32),
        lax.psum(shards[1].astype(jnp.bfloat16), "dp").astype(jnp.float32),
        lax.psum(shards[2].astype(jnp.bfloat16), "dp").astype(jnp.float32),
        lax.psum(shards[3].astype(jnp.bfloat16), "dp").astype(jnp.float32),
        lax.psum(shards[4].astype(jnp.bfloat16), "dp").astype(jnp.float32),
        lax.psum(shards[5].astype(jnp.bfloat16), "dp").astype(jnp.float32),
        lax.psum(shards[6].astype(jnp.bfloat16), "dp").astype(jnp.float32),
        lax.psum(shards[7].astype(jnp.bfloat16), "dp").astype(jnp.float32),
        lax.psum(shards[8].astype(jnp.bfloat16), "dp").astype(jnp.float32),
        lax.psum(shards[9].astype(jnp.bfloat16), "dp").astype(jnp.float32),
        lax.psum(shards[10].astype(jnp.bfloat16), "dp").astype(jnp.float32),
    )
    return (
        outputs,
        grad_inputs,
        gain_totals[0],
        weight_totals[0],
        weight_totals[1],
        gain_totals[1],
        weight_totals[2],
        weight_totals[3],
        weight_totals[4],
        weight_totals[5],
        weight_totals[6],
        gain_totals[2],
        weight_totals[7],
        weight_totals[8],
        gain_totals[3],
        weight_totals[9],
        weight_totals[10],
    )


HALF = 256
LANES = 128


def dot_nn(left_side, right_side):
    return lax.dot_general(
        left_side, right_side, (((1,), (0,)), ((), ())), preferred_element_type=jnp.float32
    )


def dot_nt(left_side, right_side):
    return lax.dot_general(
        left_side, right_side, (((1,), (1,)), ((), ())), preferred_element_type=jnp.float32
    )


def dot_tn(left_side, right_side):
    return lax.dot_general(
        left_side, right_side, (((0,), (0,)), ((), ())), preferred_element_type=jnp.float32
    )


def row_stats(values):
    centre = values - jnp.mean(values, axis=-1, keepdims=True)
    inv = lax.rsqrt(jnp.mean(centre * centre, axis=-1, keepdims=True) + epsilon)
    return centre * inv, inv


def norm_grad(grad_out, unit, inv, gain):
    scaled = grad_out * gain
    mean_one = jnp.mean(scaled, axis=-1, keepdims=True)
    mean_two = jnp.mean(scaled * unit, axis=-1, keepdims=True)
    return inv * (scaled - mean_one - unit * mean_two)


def sigmoid(values):
    return 0.5 * jnp.tanh(0.5 * values) + 0.5


def silu(values):
    return values * sigmoid(values)


def turned(values):
    return jnp.transpose(values.astype(jnp.float32)).astype(jnp.bfloat16)


class Loader:
    def __init__(self, sems, first=0):
        self.sems = sems
        self.count = first
        self.waits = []
        self.plain = []
        self.by_core = ([], [])

    def copy(self, source, target, at):
        return pltpu.make_async_copy(source, target, self.sems.at[at])

    def start(self, source, target):
        self.plain.append(self.copy(source, target, self.count))
        self.waits.append(self.plain[-1])
        self.count += 1

    def either(self, got, part, taker, target):
        for core in range(2):
            source = got if core == taker else part
            self.by_core[core].append(self.copy(source, target, self.count))
        self.waits.append(self.by_core[0][-1])
        self.count += 1

    def go(self, core):
        for copy in self.plain:
            copy.start()
        for number, copies in enumerate(self.by_core):
            if copies:

                @pl.when(core == number)
                def _(copies=copies):
                    for copy in copies:
                        copy.start()

    def wait(self):
        for copy in self.waits:
            copy.wait()


def load_pair(loader, own, got, part, taker, core, target, slots=(0, 1)):
    loader.start(own, target.at[slots[0]])
    loader.either(got, part, taker, target.at[slots[1]])


def load_left(loader, w_left, got, part, core, target):
    blocks = w_left.shape[1] // HALF
    rows = w_left.shape[0]
    for block in range(blocks):
        loader.start(w_left.at[:, pl.ds(block * HALF, HALF)], target.at[block])
        at = pl.ds(block * rows, rows)
        loader.either(got.at[at], part.at[at], 0, target.at[blocks + block])


def load_pack(loader, got, part, core, target):
    count, depth = target.shape[:2]
    for block in range(count):
        at = pl.ds(got.shape[0] - (count - block) * depth, depth)
        loader.either(got.at[at], part.at[at], 0, target.at[block])


def load_point(loader, w_point, got, part, core, target):
    at = pl.ds(0, w_point.shape[0])
    load_pair(loader, w_point, got.at[at], part.at[at], 1, core, target)


def load_right(loader, w_right, got, part, core, target):
    loader.start(w_right, target.at[0])
    rows = w_right.shape[1]
    for tap in range(w_right.shape[0]):
        at = (pl.ds(2 * rows + (tap // 2) * rows, rows), pl.ds((tap % 2) * LANES, LANES))
        loader.either(got.at[at], part.at[at], 1, target.at[1, tap])


def load_qkv(loader, w_qkv, got, part, core, target, which):
    rows = w_qkv.shape[1]
    for slot, index in enumerate(which):
        loader.start(w_qkv.at[index], target.at[0, slot])
        at = pl.ds(index * rows, rows)
        loader.either(got.at[at], part.at[at], 0, target.at[1, slot])


def load_out(loader, w_out, got, part, core, target):
    loader.start(w_out, target.at[0])
    rows = w_out.shape[0]
    for block in range(2):
        at = pl.ds(block * rows, rows)
        loader.either(
            got.at[at], part.at[at], 1, target.at[1, :, pl.ds(block * HALF, HALF)]
        )


def load_in(loader, w_in, got2, part2, got3, part3, core, target):
    blocks = w_in.shape[1] // HALF
    rows = w_in.shape[0]
    for block in range(blocks):
        loader.start(w_in.at[:, pl.ds(block * HALF, HALF)], target.at[block])
        got, part = (got2, part2) if block < 2 else (got3, part3)
        at = pl.ds(rows + (block % 2) * rows, rows)
        loader.either(got.at[at], part.at[at], 1, target.at[blocks + block])


def load_back(loader, w_back, got, part, core, target):
    loader.start(w_back, target.at[0])
    rows = w_back.shape[0]
    half = rows // 2
    near, far = pl.ds(0, HALF), pl.ds(HALF, HALF)
    for at, taker, spot in (
        (pl.ds(0, rows), 0, (pl.ds(0, rows), near)),
        (pl.ds(rows, half), 0, (pl.ds(0, half), far)),
        (pl.ds(0, half), 1, (pl.ds(half, half), far)),
    ):
        loader.either(got.at[at], part.at[at], taker, target.at[1].at[spot])


GROUP = 8


def bundle_kernel(
    info, w_left, w_right, w_point, w_depth, gain_mid, w_qkv, w_out, w_in, w_back,
    one_o, two_o, three_o, sems,
):
    core = info[0]

    def copies(pieces):
        at = {id(one_o): 0, id(two_o): 0, id(three_o): 0}
        started = []
        for target, source in pieces:
            base = at[id(target)]
            at[id(target)] = base + source.shape[0]
            spot = target.at[pl.ds(base, source.shape[0]), pl.ds(0, source.shape[1])]
            copy = pltpu.make_async_copy(source, spot, sems.at[len(started)])
            copy.start()
            started.append(copy)
        for copy in started:
            copy.wait()

    def blocks(values):
        return [values.at[:, pl.ds(at, HALF)] for at in range(0, values.shape[1], HALF)]

    near, far = blocks(w_back)
    half = w_back.shape[0] // 2

    @pl.when(core == 0)
    def _():
        base = w_left.shape[0] * (w_left.shape[1] // HALF)
        taps = jnp.concatenate(
            [
                w_depth[...].astype(jnp.float32),
                gain_mid[...].astype(jnp.float32),
                jnp.zeros((15 - w_depth.shape[0], w_depth.shape[1]), jnp.float32),
            ],
            axis=0,
        ).astype(jnp.bfloat16)
        for block in range(w_depth.shape[1] // HALF):
            at = slice(base + block * 16, base + (block + 1) * 16)
            one_o[at] = taps[:, block * HALF : (block + 1) * HALF]
        copies(
            [(one_o, piece) for piece in blocks(w_left)]
            + [(two_o, w_qkv.at[index]) for index in range(3)]
            + [(three_o, near), (three_o, far.at[pl.ds(0, half)])]
        )

    @pl.when(core == 1)
    def _():
        pieces = [(one_o, w_point)]
        pieces += [(two_o, piece) for piece in blocks(w_out) + blocks(w_in)[:2]]
        pieces += [(three_o, far.at[pl.ds(half, half)])]
        pieces += [(three_o, piece) for piece in blocks(w_in)[2:]]
        rows, base = w_right.shape[1], w_point.shape[0]
        started = []
        for tap in range(w_right.shape[0]):
            spot = one_o.at[
                pl.ds(base + (tap // 2) * rows, rows), pl.ds((tap % 2) * LANES, LANES)
            ]
            copy = pltpu.make_async_copy(w_right.at[tap], spot, sems.at[len(pieces) + tap])
            copy.start()
            started.append(copy)
        copies(pieces)
        for copy in started:
            copy.wait()


def row_spot(rows, own, lanes):
    row = lax.broadcasted_iota(jnp.int32, (rows, lanes), 0)
    spot = (row % GROUP) * (own // GROUP) + row // GROUP
    return jnp.where(row < own, spot, jnp.where(row < own + EDGE, row - own - EDGE, row - EDGE))


def row_mask(core, length, ext, lanes):
    own = ext - 2 * EDGE
    spot = row_spot(ext, own, lanes) + core * own
    return jnp.where((spot >= 0) & (spot < length), 1.0, 0.0)


def lane_tiles(width):
    return [slice(at, at + LANES) for at in range(0, width, LANES)]


def load_tiles(source, tiles):
    for index, lanes in enumerate(lane_tiles(source.shape[1])):
        tiles[index] = source[:, lanes].astype(jnp.float32)


def gather_rows(tiles, target):
    own = tiles.shape[1]
    for tile, lanes in enumerate(lane_tiles(target.shape[1])):
        for index in range(own // GROUP):
            target[index * GROUP : (index + 1) * GROUP, lanes] = tiles[
                tile, pl.ds(index, GROUP, stride=own // GROUP)
            ]


def scatter_rows(source, tiles, target):
    own = tiles.shape[1]
    for tile, lanes in enumerate(lane_tiles(target.shape[1])):
        for index in range(own // GROUP):
            tiles[tile, pl.ds(index, GROUP, stride=own // GROUP)] = source[
                index * GROUP : (index + 1) * GROUP, lanes
            ]
        target[:, lanes] = tiles[tile].astype(target.dtype)


def next_group(first, row):
    sub = lax.broadcasted_iota(jnp.int32, first.shape, 0)
    return jnp.where(sub == GROUP - 1, row, pltpu.roll(first, GROUP - 1, 0))


def previous_group(last, row):
    sub = lax.broadcasted_iota(jnp.int32, last.shape, 0)
    return jnp.where(sub == 0, row, pltpu.roll(last, 1, 0))


def shift_rows(values, offset):
    if offset == 0:
        return values
    ext = values.shape[0]
    own = ext - 2 * EDGE
    mid, before, after = values[:own], values[own : own + EDGE], values[own + EDGE :]
    sub = lax.broadcasted_iota(jnp.int32, before.shape, 0)
    if offset > 0:
        moved = jnp.concatenate([mid[GROUP:], next_group(mid[:GROUP], after[:1])], axis=0)
        before = jnp.where(sub == EDGE - 1, mid[:1], pltpu.roll(before, EDGE - 1, 0))
        after = pltpu.roll(after, EDGE - 1, 0)
    else:
        moved = jnp.concatenate(
            [previous_group(mid[own - GROUP :], before[EDGE - 1 :]), mid[: own - GROUP]], axis=0
        )
        after = jnp.where(sub == 0, mid[own - 1 :], pltpu.roll(after, 1, 0))
        before = pltpu.roll(before, 1, 0)
    return jnp.concatenate([moved, before, after], axis=0)


def fill_window(window, values, own, reach):
    before, after = values[own : own + EDGE], values[own + EDGE :]
    window[reach * GROUP : reach * GROUP + own] = values[:own]
    for step in range(1, reach + 1):
        last = values[own - step * GROUP : own - (step - 1) * GROUP]
        at = (reach - step) * GROUP
        window[at : at + GROUP] = previous_group(last, before[EDGE - step : EDGE - step + 1])
        first = values[(step - 1) * GROUP : step * GROUP]
        at = reach * GROUP + own + (step - 1) * GROUP
        window[at : at + GROUP] = next_group(first, after[step - 1 : step])


def glu_kernel(
    info, block, moved, cot_own, cot_moved, edge, gain_glu, gain_branch, w_value, w_gate, got, part_w,
    cot_o, resid_o, branch_o, gluin_o, value_o, sig_o, x_s, c_s, n_s, wv_s, wg_s, sems,
):
    core, member, length = info[0], info[1], info[2]
    loader = Loader(sems)
    load_pair(loader, w_value, got, part_w, 0, core, wv_s, (member, 1 - member))
    load_pair(loader, w_gate, got, part_w, 1, core, wg_s, (member, 1 - member))
    loader.go(core)
    ext = x_s.shape[0]
    rows = ext - 2 * EDGE
    edge_f = edge[...].astype(jnp.float32)
    x_s[rows : rows + EDGE] = jnp.where(core == 1, edge_f, 0.0)
    x_s[rows + EDGE :] = jnp.where(core == 1, 0.0, edge_f)

    @pl.when(core == member)
    def _():
        load_tiles(block, n_s)

    @pl.when(core != member)
    def _():
        load_tiles(moved, n_s)

    gather_rows(n_s, x_s)

    @pl.when(core == member)
    def _():
        load_tiles(cot_own, n_s)

    @pl.when(core != member)
    def _():
        load_tiles(cot_moved, n_s)

    gather_rows(n_s, c_s)
    cot_o[...] = c_s[...].astype(jnp.bfloat16)
    loader.wait()
    valid = row_mask(core, length, ext, LANES)[:, :1]
    part = ext // 2
    for start in (0, part):
        at = slice(start, start + part)
        x = x_s[at]
        glu_in = (row_stats(x)[0] * gain_glu[...]).astype(jnp.bfloat16)
        gluin_o[at] = glu_in
        for half in range(2):
            cols = slice(half * HALF, (half + 1) * HALF)
            value = dot_nn(glu_in, wv_s[half])
            sig = sigmoid(dot_nn(glu_in, wg_s[half]))
            value_o[at, cols] = value.astype(jnp.bfloat16)
            sig_o[at, cols] = sig.astype(jnp.bfloat16)
            resid_o[at, cols] = x[:, cols] + (value * sig).astype(jnp.bfloat16).astype(jnp.float32)
        normed = row_stats(resid_o[at])[0] * gain_branch[...]
        branch_o[at] = (valid[at] * normed).astype(jnp.bfloat16)


def spread_block(index, rights, stride):
    source = lax.broadcasted_iota(jnp.int32, (rights, HALF), 0)
    channel = lax.broadcasted_iota(jnp.int32, (rights, HALF), 1) + index * HALF
    return jnp.where(channel == source * stride, 1.0, 0.0).astype(jnp.bfloat16)


def conv_rows(branch, weights):
    taps = weights.shape[0]
    total = dot_nn(branch, weights[taps // 2])
    for tap in range(taps):
        if tap != taps // 2:
            total = total + shift_rows(dot_nn(branch, weights[tap]), tap - taps // 2)
    return total


def mid_step(branch, into, right_act, index, stride, left_o, mid_o, sums, at):
    left_pre = dot_nn(branch[...], into[index])
    left_o[at] = left_pre.astype(jnp.bfloat16)
    mid = silu(left_pre) + dot_nn(right_act, spread_block(index, right_act.shape[1], stride))
    mid_o[at] = mid
    near, far = mid[:, :LANES], mid[:, LANES:]
    sums[0] += near + far
    sums[1] += near * near + far * far


def branch_own_kernel(
    info, branch, w_left, w_right, left_o, right_o, mid_o, sums_o, wl_s, sems
):
    loader = Loader(sems)
    blocks = wl_s.shape[0]
    for block in range(blocks):
        loader.start(w_left.at[:, pl.ds(block * HALF, HALF)], wl_s.at[block])
    loader.go(info[0])
    right_pre = conv_rows(branch[...], w_right)
    right_o[...] = right_pre
    right_act = silu(right_pre).astype(jnp.bfloat16)
    stride = blocks * HALF // right_pre.shape[1]
    sums_o[...] = jnp.zeros_like(sums_o)
    loader.wait()

    def step(index, carry):
        mid_step(branch, wl_s, right_act, index, stride, left_o, mid_o, sums_o, index)
        return carry

    lax.fori_loop(0, blocks, step, 0, unroll=2)


def fill_taps(pack_own, pack_oth, taps_s):
    count, cols = pack_own.shape
    taps_s[:count, :cols] = pack_own[...].astype(jnp.float32)
    for block in range(pack_oth.shape[0]):
        at = cols + block * HALF
        taps_s[:, at : at + HALF] = pack_oth[block].astype(jnp.float32)


def branch_kernel(
    info, branch, resid_one, pack_own, left_own, right_own, mid_own, sums_own, w_point, got, part,
    resid_two_o, left_o, right_o, stats_o, depth_o,
    wl_s, wr_s, wp_s, po_s, taps_s, mid_s, din_s, sums_s, sep_s, sems,
):
    core, length = info[0], info[2]
    loader = Loader(sems)
    taps_conv, depth_in_rows = wr_s.shape[0], wr_s.shape[1]
    for tap in range(taps_conv):
        at = (
            pl.ds(w_point.shape[0] + (tap // 2) * depth_in_rows, depth_in_rows),
            pl.ds((tap % 2) * LANES, LANES),
        )
        loader.either(got.at[at], part.at[at], 1, wr_s.at[tap])
    blocks = wl_s.shape[0]
    for block in range(blocks):
        at = pl.ds(block * depth_in_rows, depth_in_rows)
        loader.either(got.at[at], part.at[at], 0, wl_s.at[block])
    load_point(loader, w_point, got, part, core, wp_s)
    load_pack(loader, got, part, core, po_s)
    loader.go(core)
    ext = branch.shape[0]
    rows = ext - 2 * EDGE
    chunks = 2 * blocks
    per_shard = blocks
    sep_taps = pack_own.shape[0] - 1
    inner = chunks * HALF
    rights = right_own.shape[1]
    stride = blocks * HALF // rights
    left_o[:blocks] = left_own[...]
    mid_s[:blocks] = mid_own[...]
    sums_s[...] = sums_own[...]
    right_o[:, :rights] = right_own[...]
    loader.wait()
    fill_taps(pack_own, po_s, taps_s)
    right_pre = conv_rows(branch[...], wr_s)
    right_o[:, rights:] = right_pre
    right_act = silu(right_pre).astype(jnp.bfloat16)

    def first(index, carry):
        mid_step(branch, wl_s, right_act, index, stride, left_o, mid_s, sums_s, index + blocks)
        return carry

    lax.fori_loop(0, blocks, first, 0, unroll=2)
    mean = jnp.sum(sums_s[0], axis=-1, keepdims=True) / inner
    inv = lax.rsqrt(
        jnp.sum(sums_s[1], axis=-1, keepdims=True) / inner - mean * mean + epsilon
    )
    lane = lax.broadcasted_iota(jnp.int32, (ext, LANES), 1)
    stats_o[...] = jnp.where(lane == 0, mean, inv)
    sums_s[0] = jnp.broadcast_to(mean, (ext, LANES))
    sums_s[1] = inv * row_mask(core, length, ext, LANES)
    sep_s[...] = jnp.zeros_like(sep_s)

    def second(index, carry):
        cols = pl.ds(pl.multiple_of(index * HALF, HALF), HALF)
        taps = taps_s[:, cols]
        for side in range(2):
            lanes = slice(side * LANES, (side + 1) * LANES)
            depth_in = (
                (mid_s[index, :, lanes] - sums_s[0]) * sums_s[1] * taps[sep_taps : sep_taps + 1, lanes]
            )
            fill_window(din_s.at[:, lanes], depth_in, rows, sep_taps // 2)
        step = 64
        for start in range(0, rows, step):
            for side in range(2):
                lanes = slice(side * LANES, (side + 1) * LANES)
                acc = din_s[start : start + step, lanes] * taps[:1, lanes]
                for tap in range(1, sep_taps):
                    at = start + tap * GROUP
                    acc = acc + din_s[at : at + step, lanes] * taps[tap : tap + 1, lanes]
                depth_o[index, start : start + step, lanes] = acc.astype(jnp.bfloat16)
        shard, chunk = index // per_shard, index % per_shard
        point = wp_s[shard, pl.ds(pl.multiple_of(chunk * HALF, HALF), HALF)]
        sep_s[...] += dot_nn(depth_o[index], point)
        return carry

    lax.fori_loop(0, chunks, second, 0, unroll=2)
    sep_width = sep_s.shape[1]
    resid_two_o[:, :sep_width] = resid_one[:rows, :sep_width] + sep_s[...]
    resid_two_o[:, sep_width:] = resid_one[:rows, sep_width:]


def kv_kernel(info, resid_two, gain, w_qkv, got, part, attn_o, kv_o, w_s, sems):
    loader = Loader(sems)
    load_qkv(loader, w_qkv, got, part, info[0], w_s, (1, 2))
    loader.go(info[0])
    attn_in = (row_stats(resid_two[...])[0] * gain[...]).astype(jnp.bfloat16)
    attn_o[...] = attn_in
    loader.wait()
    width = w_s.shape[3]
    for shard in range(2):
        for index in range(2):
            at = (2 * index + shard) * width
            kv_o[:, at : at + width] = dot_nn(attn_in, w_s[shard, index]).astype(jnp.bfloat16)


def query_kernel(info, attn_in, w_qkv, got, part, q_o, w_s, sems):
    loader = Loader(sems)
    load_qkv(loader, w_qkv, got, part, info[0], w_s, (0,))
    loader.go(info[0])
    loader.wait()
    width = w_s.shape[3]
    scale = 1.0 / math.sqrt(HEAD_DIM)
    for shard in range(2):
        query = dot_nn(attn_in[...], w_s[shard, 0]).astype(jnp.bfloat16).astype(jnp.float32)
        q_o[:, shard * width : (shard + 1) * width] = (query * scale).astype(jnp.bfloat16)


def key_bias(core, length, rows):
    spot = row_spot(rows, rows, LANES) + core * rows
    return jnp.where(spot < length, 0.0, negative_big)


def head_masks(rows, head):
    lane = lax.broadcasted_iota(jnp.int32, (rows, LANES), 1)
    return (lane // HEAD_DIM) == head, lane == HEAD_DIM * (1 - head)


def attend_kernel(info, q, kvo, kvf, ctx0_o, lse0_o, ctx1_o, lse1_o, bias_s):
    core, length = info[0], info[2]
    rows, width = q.shape
    pairs = width // LANES // 2
    bias_s[:rows] = key_bias(core, length, rows)
    bias_s[rows:] = key_bias(1 - core, length, rows)

    def pair_step(shard, ctx_o, lse_o, local, carry):
        pair = local + shard * pairs
        cols = pl.ds(pl.multiple_of(pair * LANES, LANES), LANES)
        vcols = pl.ds(pl.multiple_of(pair * LANES + width, LANES), LANES)
        here = pl.ds(pl.multiple_of(local * LANES, LANES), LANES)
        keys = jnp.concatenate([kvo[:, cols], kvf[:, cols]], axis=0).astype(jnp.float32)
        vals = jnp.concatenate([kvo[:, vcols], kvf[:, vcols]], axis=0)
        vals_t = turned(vals)
        query = q[:, cols].astype(jnp.float32)
        outs = []
        for head in range(2):
            in_k, extra_k = head_masks(2 * rows, head)
            in_q, extra_q = head_masks(rows, head)
            km = jnp.where(in_k, keys, jnp.where(extra_k, bias_s[...], 0.0)).astype(jnp.bfloat16)
            qm = jnp.where(in_q, query, jnp.where(extra_q, 1.0, 0.0)).astype(jnp.bfloat16)
            pieces = []
            for start in range(0, rows, HALF):
                scores = dot_nt(km, qm[start : start + HALF])
                top = jnp.max(scores, axis=0, keepdims=True)
                weights = jnp.exp(scores - top)
                total = jnp.sum(weights, axis=0, keepdims=True)
                out = dot_nn(
                    vals_t[head * HEAD_DIM : (head + 1) * HEAD_DIM], weights.astype(jnp.bfloat16)
                )
                pieces.append(out / total)
                lse_o[pl.ds(local * 2 + head, 1), start : start + HALF] = top + jnp.log(total)
            outs.append(jnp.concatenate(pieces, axis=1))
        ctx_o[:, here] = jnp.transpose(jnp.concatenate(outs, axis=0)).astype(jnp.bfloat16)
        return carry

    lax.fori_loop(0, pairs, functools.partial(pair_step, 0, ctx0_o, lse0_o), 0, unroll=2)
    lax.fori_loop(0, pairs, functools.partial(pair_step, 1, ctx1_o, lse1_o), 0, unroll=2)


def ffn_kernel(
    info, resid_two, ctx0, ctx1, cot, gain, w_out, w_in, w_back, got2, part2,
    got3, part3,
    out_o, grad_three_o, gctx_o, ggain_o, send_o, keep_o,
    wo_s, wi_s, wb_s, fin_s, fint_s, cot_s, acc_s, gacc_s, ctxt_s, n_s, sems,
):
    core = info[0]
    loader = Loader(sems)
    load_out(loader, w_out, got2, part2, core, wo_s)
    late = Loader(sems, loader.count)
    load_in(late, w_in, got2, part2, got3, part3, core, wi_s)
    load_back(late, w_back, got3, part3, core, wb_s)

    loader.go(core)
    late.go(core)
    cot_s[...] = cot[...]
    loader.wait()
    part = ctx0.shape[1]
    chunks = wi_s.shape[0]
    per_shard = chunks // 2
    resid = resid_two[...] + dot_nn(ctx0[...], wo_s[0]) + dot_nn(ctx1[...], wo_s[1])
    acc_s[...] = resid
    gacc_s[...] = jnp.zeros_like(gacc_s)
    unit, inv = row_stats(resid)
    ffn_in = unit * gain[...]
    fin_s[...] = ffn_in.astype(jnp.bfloat16)
    fint_s[...] = jnp.transpose(fin_s[...].astype(jnp.float32)).astype(jnp.bfloat16)
    keep_rows = pl.ds(pl.multiple_of(core * HALF, HALF), HALF)
    send_rows = pl.ds(pl.multiple_of((1 - core) * HALF, HALF), HALF)

    def chunk_step(index, carry):
        shard, chunk = index // per_shard, index % per_shard
        rows = pl.ds(pl.multiple_of(chunk * HALF, HALF), HALF)
        into, back = wi_s[index], wb_s[shard, rows]
        pre = dot_nn(fin_s[...], into)
        sig = sigmoid(pre)
        hidden = (pre * sig).astype(jnp.bfloat16)
        acc_s[...] += dot_nn(hidden, back)
        grad_hidden = dot_nt(cot_s[...], back)
        grad_pre = (grad_hidden * (sig * (1.0 + pre * (1.0 - sig)))).astype(jnp.bfloat16)
        send_o[shard, rows] = dot_nn(fint_s[send_rows], grad_pre).astype(jnp.bfloat16)
        keep_o[shard, rows] = dot_nn(fint_s[keep_rows], grad_pre).astype(jnp.bfloat16)
        hidden_t = turned(hidden)
        base = per_shard * HALF
        rows = pl.ds(pl.multiple_of(base + chunk * HALF, HALF), HALF)
        send_o[shard, rows] = dot_nn(hidden_t, cot_s[:, send_rows]).astype(jnp.bfloat16)
        keep_o[shard, rows] = dot_nn(hidden_t, cot_s[:, keep_rows]).astype(jnp.bfloat16)
        gacc_s[...] += dot_nt(grad_pre, into)
        return carry

    late.wait()
    lax.fori_loop(0, chunks, chunk_step, 0, unroll=4)
    scatter_rows(acc_s, n_s, out_o)
    unit, inv = row_stats(
        resid_two[...] + dot_nn(ctx0[...], wo_s[0]) + dot_nn(ctx1[...], wo_s[1])
    )
    grad_norm = gacc_s[...]
    ggain_o[...] = jnp.sum(grad_norm * unit, axis=0, keepdims=True)
    grad_three = cot_s[...].astype(jnp.float32) + norm_grad(grad_norm, unit, inv, gain[...])
    grad_three_o[...] = grad_three
    fin_s[...] = grad_three.astype(jnp.bfloat16)
    ctxt_s[:part] = turned(ctx0[...])
    ctxt_s[part:] = turned(ctx1[...])
    base = 2 * per_shard * HALF
    for shard in range(2):
        side = slice(shard * part, (shard + 1) * part)
        gctx_o[:, side] = dot_nt(fin_s[...], wo_s[shard]).astype(jnp.bfloat16)
        send_o[shard, base : base + part] = dot_nn(ctxt_s[side], fin_s[:, send_rows]).astype(
            jnp.bfloat16
        )
        keep_o[shard, base : base + part] = dot_nn(ctxt_s[side], fin_s[:, keep_rows]).astype(
            jnp.bfloat16
        )


def attend_back_kernel(side, info, q, kv, ctx0, ctx1, gctx, lse0, lse1, *rest):
    if side:
        gq_o, gkv_o, bias_s, gk_s, gv_s = rest
    else:
        gq_part, gq_o, gkv_o, bias_s, gk_s, gv_s = rest
    core, length = info[0], info[2]
    rows, width = q.shape
    pairs = width // LANES // 2
    scale = 1.0 / math.sqrt(HEAD_DIM)
    bias_s[...] = key_bias(core ^ side, length, rows)

    def pair_step(shard, ctx, lse, local, carry):
        pair = local + shard * pairs
        cols = pl.ds(pl.multiple_of(pair * LANES, LANES), LANES)
        vcols = pl.ds(pl.multiple_of(pair * LANES + width, LANES), LANES)
        here = pl.ds(pl.multiple_of(local * LANES, LANES), LANES)
        keys = kv[:, cols].astype(jnp.float32)
        vals = kv[:, vcols]
        keys_t = jnp.transpose(keys).astype(jnp.bfloat16)
        query = q[:, cols].astype(jnp.float32)
        grad_out = gctx[:, cols].astype(jnp.float32)
        product_t = jnp.transpose(grad_out * ctx[:, here].astype(jnp.float32))
        gk_s[...] = jnp.zeros_like(gk_s)
        gv_s[...] = jnp.zeros_like(gv_s)
        outs = []
        for head in range(2):
            in_q, extra_q = head_masks(rows, head)
            km = jnp.where(in_q, keys, jnp.where(extra_q, bias_s[...], 0.0)).astype(jnp.bfloat16)
            qm = jnp.where(in_q, query, jnp.where(extra_q, 1.0, 0.0)).astype(jnp.bfloat16)
            qz = jnp.where(in_q, query, 0.0).astype(jnp.bfloat16)
            gz = jnp.where(in_q, grad_out, 0.0).astype(jnp.bfloat16)
            span = slice(head * HEAD_DIM, (head + 1) * HEAD_DIM)
            pieces = []
            for start in range(0, rows, HALF):
                at = slice(start, start + HALF)
                level = lse[pl.ds(local * 2 + head, 1), at]
                delta = jnp.sum(product_t[span, at], axis=0, keepdims=True)
                soft = jnp.exp(dot_nt(km, qm[at]) - level)
                gv_s[...] += dot_nn(soft.astype(jnp.bfloat16), gz[at])
                grad_scores = (soft * (dot_nt(vals, gz[at]) - delta)).astype(jnp.bfloat16)
                gk_s[...] += dot_nn(grad_scores, qz[at])
                pieces.append(dot_nn(keys_t[span], grad_scores))
            outs.append(jnp.concatenate(pieces, axis=1))
        grad_q = jnp.transpose(jnp.concatenate(outs, axis=0))
        if not side:
            grad_q = (grad_q + gq_part[:, cols]) * scale
        gq_o[:, cols] = grad_q.astype(gq_o.dtype)
        gkv_o[:, cols] = gk_s[...].astype(gkv_o.dtype)
        gkv_o[:, vcols] = gv_s[...].astype(gkv_o.dtype)
        return carry

    for shard, ctx, lse in ((0, ctx0, lse0), (1, ctx1, lse1)):
        lax.fori_loop(0, pairs, functools.partial(pair_step, shard, ctx, lse), 0, unroll=2)


def qkv_back_kernel(
    info, gq, gown, gfar, attn_in, resid_two, grad_three, gain, w_qkv, got, part,
    grad_two_o, gsep_o, gedge_o, ggain_o, send_o, keep_o, w_s, attnt_s, n_s, sems,
):
    core = info[0]
    loader = Loader(sems)
    load_qkv(loader, w_qkv, got, part, core, w_s, (0, 1, 2))
    loader.go(core)
    attnt_s[...] = turned(attn_in[...])
    width = w_s.shape[3]
    keep_rows = pl.ds(pl.multiple_of(core * HALF, HALF), HALF)
    send_rows = pl.ds(pl.multiple_of((1 - core) * HALF, HALF), HALF)
    loader.wait()
    grad_in = jnp.zeros(resid_two.shape, jnp.float32)
    for index in range(3):
        if index == 0:
            whole = gq[...]
        else:
            cols = slice((index - 1) * 2 * width, index * 2 * width)
            whole = (gown[:, cols] + gfar[:, cols].astype(jnp.float32)).astype(jnp.bfloat16)
        for shard in range(2):
            grad = whole[:, shard * width : (shard + 1) * width]
            at = slice(index * HALF, (index + 1) * HALF)
            send_o[shard, at] = dot_nn(attnt_s[send_rows], grad).astype(jnp.bfloat16)
            keep_o[shard, at] = dot_nn(attnt_s[keep_rows], grad).astype(jnp.bfloat16)
            grad_in = grad_in + dot_nt(grad, w_s[shard, index])
    unit, inv = row_stats(resid_two[...])
    ggain_o[...] = jnp.sum(grad_in * unit, axis=0, keepdims=True)
    grad_two = grad_three[...] + norm_grad(grad_in, unit, inv, gain[...])
    grad_two_o[...] = grad_two
    gsep_o[...] = grad_two[:, : gsep_o.shape[1]].astype(jnp.bfloat16)
    rows = n_s.shape[1]
    for tile, lanes in enumerate(lane_tiles(gsep_o.shape[1])):
        n_s[tile] = grad_two[:, lanes]
        first = n_s[tile, pl.ds(0, EDGE, stride=GROUP)]
        last = n_s[tile, pl.ds(rows - EDGE * GROUP + GROUP - 1, EDGE, stride=GROUP)]
        gedge_o[:, lanes] = jnp.where(core == 0, last, first).astype(jnp.bfloat16)


def point_kernel(info, gsep, depth, send, keep, send_o, keep_o):
    core = info[0]
    grad_sep = gsep[...]
    per_shard = depth.shape[0] // 2
    per_core = per_shard // 2
    base = send.shape[1]
    send_o[:, :base] = send[...]
    keep_o[:, :base] = keep[...]
    for shard in range(2):
        for chunk in range(per_core):
            at = slice(base + chunk * HALF, base + (chunk + 1) * HALF)
            first = shard * per_shard
            send_o[shard, at] = dot_tn(
                depth[first + (1 - core) * per_core + chunk], grad_sep
            ).astype(jnp.bfloat16)
            keep_o[shard, at] = dot_tn(
                depth[first + core * per_core + chunk], grad_sep
            ).astype(jnp.bfloat16)


def as_f32(values):
    return values.astype(jnp.float32)


def slope_of(values):
    sig = sigmoid(values)
    return sig * (1.0 + values * (1.0 - sig))


def depth_back_kernel(
    info, gsep, gedge, left_pre, right_pre, stats, pack_own, w_point, got, part,
    unit_o, scaled_o, sums_s, small_s,
    wp_s, po_s, taps_s, gse_s, gd_s, din_s, near_s, unit_s, scaled_s, wide_s, sems,
):
    core, length = info[0], info[2]
    loader = Loader(sems)
    load_point(loader, w_point, got, part, core, wp_s)
    load_pack(loader, got, part, core, po_s)
    loader.go(core)
    ext = left_pre.shape[1]
    rows = ext - 2 * EDGE
    chunks = left_pre.shape[0]
    per_shard = chunks // 2
    inner = chunks * HALF
    sep_taps = pack_own.shape[0] - 1
    right_cols = right_pre.shape[1]
    stride = inner // right_cols
    reach = sep_taps // 2
    edge = gedge[...].astype(jnp.float32)
    gse_s[:rows] = gsep[...]
    gse_s[rows : rows + EDGE] = jnp.where(core == 1, edge, 0.0).astype(jnp.bfloat16)
    gse_s[rows + EDGE :] = jnp.where(core == 1, 0.0, edge).astype(jnp.bfloat16)
    wide_s[0] = row_mask(core, length, ext, LANES)
    wide_s[1] = jnp.broadcast_to(stats[:, 0:1], (ext, LANES))
    wide_s[2] = jnp.broadcast_to(stats[:, 1:2], (ext, LANES))
    scaled_s[...] = jnp.zeros_like(scaled_s)
    sums_s[...] = jnp.zeros_like(sums_s)
    small_s[...] = jnp.zeros_like(small_s)
    right_act = silu(right_pre[...]).astype(jnp.bfloat16)
    loader.wait()
    fill_taps(pack_own, po_s, taps_s)

    def first(index, carry):
        cols = pl.ds(pl.multiple_of(index * HALF, HALF), HALF)
        taps = taps_s[:, cols]
        shard, chunk = index // per_shard, index % per_shard
        point = wp_s[shard, pl.ds(pl.multiple_of(chunk * HALF, HALF), HALF)]
        grad_depth = dot_nt(gse_s[...], point)
        for side, lanes in enumerate(lane_tiles(HALF)):
            fill_window(gd_s.at[side], grad_depth[:, lanes], rows, reach)
            near_s[side, :EDGE] = grad_depth[rows : rows + EDGE, lanes]
            near_s[side, 3 * EDGE :] = grad_depth[rows + EDGE :, lanes]
            base = reach * GROUP
            near_s[side, EDGE : 2 * EDGE] = gd_s[side, pl.ds(base, EDGE, stride=GROUP)]
            base = reach * GROUP + rows - EDGE * GROUP + GROUP - 1
            near_s[side, 2 * EDGE : 3 * EDGE] = gd_s[side, pl.ds(base, EDGE, stride=GROUP)]
        mid = silu(left_pre[index].astype(jnp.float32)) + dot_nn(
            right_act, spread_block(index, right_cols, stride)
        )
        for side in range(2):
            lanes = slice(side * LANES, (side + 1) * LANES)
            unit = (mid[:, lanes] - wide_s[1]) * wide_s[2]
            unit_s[:, lanes] = unit
            fill_window(
                din_s.at[side],
                unit * wide_s[0] * taps[sep_taps : sep_taps + 1, lanes],
                rows,
                reach,
            )
            for base, target in ((EDGE - GROUP, rows + EDGE - GROUP), (3 * EDGE, rows + EDGE)):
                acc = near_s[side, base + reach : base + reach + GROUP] * taps[:1, lanes]
                for tap in range(1, sep_taps):
                    at = base + reach - tap
                    acc = acc + near_s[side, at : at + GROUP] * taps[tap : tap + 1, lanes]
                at = slice(target, target + GROUP)
                scaled_s[at, lanes] = acc * wide_s[0, at]
        step = 64
        tap_sums = []
        for side in range(2):
            lanes = slice(side * LANES, (side + 1) * LANES)
            sums = [jnp.zeros((GROUP, LANES), jnp.float32) for _ in range(sep_taps)]
            for start in range(0, rows, step):
                at = start + 2 * reach * GROUP
                acc = gd_s[side, at : at + step] * taps[:1, lanes]
                for tap in range(1, sep_taps):
                    at = start + (2 * reach - tap) * GROUP
                    acc = acc + gd_s[side, at : at + step] * taps[tap : tap + 1, lanes]
                scaled_s[start : start + step, lanes] = acc * wide_s[0, start : start + step]
                at = start + reach * GROUP
                grad = gd_s[side, at : at + step]
                for tap in range(sep_taps):
                    at = start + tap * GROUP
                    term = din_s[side, at : at + step] * grad
                    sums[tap] = sums[tap] + jnp.sum(
                        term.reshape(step // GROUP, GROUP, LANES), axis=0
                    )
            tap_sums.append(sums)
        tap_sums = [jnp.concatenate(pair, axis=1) for pair in zip(*tap_sums)]
        tap_rows = [jnp.sum(value, axis=0, keepdims=True) for value in tap_sums]
        gain = taps[sep_taps : sep_taps + 1]
        gain_row = jnp.sum(
            scaled_s[:rows] * unit_s[:rows],
            axis=0,
            keepdims=True,
        )
        filler = jnp.zeros((small_s.shape[0] - sep_taps - 1, HALF), jnp.float32)
        small_s[:, cols] = jnp.concatenate(tap_rows + [gain_row, filler], axis=0)
        scaled = scaled_s[...] * gain
        scaled_o[index] = scaled.astype(jnp.bfloat16)
        unit_o[index] = unit_s[...].astype(jnp.bfloat16)
        near, far = scaled[:, :LANES], scaled[:, LANES:]
        sums_s[0] += near + far
        sums_s[1] += near * unit_s[:, :LANES] + far * unit_s[:, LANES:]
        return carry

    lax.fori_loop(0, chunks, first, 0, unroll=2)


def branch_back_kernel(
    info, unit, scaled, sums, small, left_pre, right_pre, stats, branch, gain_ffn_g, gain_attn_g,
    gleft_o, gright_o, send_o, keep_o,
    wide_s, gra_s, bt_s,
):
    core = info[0]
    ext = left_pre.shape[1]
    rows = ext - 2 * EDGE
    chunks = left_pre.shape[0]
    per_shard = chunks // 2
    inner = chunks * HALF
    right_cols = right_pre.shape[1]
    stride = inner // right_cols
    for index in range(2):
        mean = jnp.sum(sums[index], axis=-1, keepdims=True) / inner
        wide_s[index] = jnp.broadcast_to(mean, (ext, LANES))
    wide_s[2] = jnp.broadcast_to(stats[:, 1:2], (ext, LANES))
    gra_s[...] = jnp.zeros_like(gra_s)
    bt_s[...] = turned(branch[...])
    keep_rows = pl.ds(pl.multiple_of(core * HALF, HALF), HALF)
    send_rows = pl.ds(pl.multiple_of((1 - core) * HALF, HALF), HALF)

    def second(index, carry):
        shard, chunk = index // per_shard, index % per_shard
        sides = []
        for side in range(2):
            lanes = slice(side * LANES, (side + 1) * LANES)
            sides.append(
                wide_s[2]
                * (as_f32(scaled[index, :, lanes]) - wide_s[0] - as_f32(unit[index, :, lanes]) * wide_s[1])
            )
        grad_mid = jnp.concatenate(sides, axis=1)
        grad_left = (
            grad_mid[:rows] * slope_of(left_pre[index, :rows].astype(jnp.float32))
        ).astype(jnp.bfloat16)
        gleft_o[index] = grad_left
        gra_s[...] += dot_nt(
            grad_mid.astype(jnp.bfloat16), spread_block(index, right_cols, stride)
        )
        at = pl.ds(pl.multiple_of(chunk * HALF, HALF), HALF)
        send_o[shard, at] = dot_nn(bt_s[send_rows, :rows], grad_left).astype(
            jnp.bfloat16
        )
        keep_o[shard, at] = dot_nn(bt_s[keep_rows, :rows], grad_left).astype(
            jnp.bfloat16
        )
        return carry

    lax.fori_loop(0, chunks, second, 0, unroll=2)
    grad_right = gra_s[...] * slope_of(right_pre[...])
    gright_o[...] = grad_right.astype(jnp.bfloat16)
    spot = lax.broadcasted_iota(jnp.int32, grad_right.shape, 0)
    own_right = jnp.where(spot < rows, grad_right, 0.0)
    part = right_cols // 2
    base = per_shard * HALF
    for target, picked, side in ((send_o, send_rows, 1 - core), (keep_o, keep_rows, core)):
        taps3 = []
        for tap in range(3):
            moved = shift_rows(own_right, 1 - tap).astype(jnp.bfloat16)
            taps3.append(dot_nn(bt_s[picked, :], moved).astype(jnp.bfloat16))
        for shard in range(2):
            cols = slice(shard * part, (shard + 1) * part)
            target[shard, base : base + HALF, :part] = taps3[0][:, cols]
            target[shard, base : base + HALF, part:] = taps3[1][:, cols]
            target[shard, base + HALF : base + 2 * HALF, :part] = taps3[2][:, cols]
            target[shard, base + HALF : base + 2 * HALF, part:] = jnp.zeros(
                (HALF, part), jnp.bfloat16
            )
            cols_here = inner // 4
            for piece in range(cols_here // LANES):
                lanes = pl.ds(
                    pl.multiple_of(
                        shard * (inner // 2) + side * cols_here + piece * LANES, LANES
                    ),
                    LANES,
                )
                row = base + HALF + piece * 16
                target[shard, row : row + 16, part:] = small[:, lanes].astype(jnp.bfloat16)
            row = base + HALF + 4 * 16
            for piece in range(4):
                lanes = slice(piece * LANES, (piece + 1) * LANES)
                both = jnp.concatenate(
                    [gain_ffn_g[:, lanes], gain_attn_g[:, lanes], jnp.zeros((14, LANES), jnp.float32)],
                    axis=0,
                )
                target[shard, row : row + 16, part:] = both.astype(jnp.bfloat16)
                row += 16


def join_back_kernel(
    info, gleft, gright, resid_one, grad_two, gain_branch, w_left, w_right, got, part_w,
    grad_one_o, ggain_o, wl_s, wr_s, sems,
):
    core, length = info[0], info[2]
    loader = Loader(sems)
    load_left(loader, w_left, got, part_w, core, wl_s)
    load_right(loader, w_right, got, part_w, core, wr_s)
    loader.go(core)
    ext = gright.shape[0]
    rows = ext - 2 * EDGE
    own = slice(0, rows)
    loader.wait()
    grad_in = jnp.zeros((rows, resid_one.shape[1]), jnp.float32)
    for index in range(wl_s.shape[0]):
        grad_in = grad_in + dot_nt(gleft[index], wl_s[index])
    part = wr_s.shape[3]
    for tap in range(wr_s.shape[1]):
        product = dot_nt(gright[:, :part], wr_s[0, tap]) + dot_nt(gright[:, part:], wr_s[1, tap])
        grad_in = grad_in + shift_rows(product, 1 - tap)[own]
    grad_in = grad_in * row_mask(core, length, ext, LANES)[own, :1]
    unit, inv = row_stats(resid_one[own])
    ggain_o[...] = jnp.sum(grad_in * unit, axis=0, keepdims=True)
    grad_one_o[...] = grad_two[...] + norm_grad(grad_in, unit, inv, gain_branch[...])


def glu_back_kernel(
    info, grad_one, gain_branch_row, gain_glu, block, moved, glu_in, value, sig, w_value, w_gate,
    got, part_w,
    gin_o, send_o, keep_o,
    wv_s, wg_s, x_s, n_s, git_s, sems,
):
    core, member = info[0], info[1]
    loader = Loader(sems)
    load_pair(loader, w_value, got, part_w, 0, core, wv_s, (member, 1 - member))
    load_pair(loader, w_gate, got, part_w, 1, core, wg_s, (member, 1 - member))
    loader.go(core)
    rows = grad_one.shape[0]
    own = slice(0, rows)

    @pl.when(core == member)
    def _():
        load_tiles(block, n_s)

    @pl.when(core != member)
    def _():
        load_tiles(moved, n_s)

    gather_rows(n_s, x_s)
    git_s[...] = turned(glu_in[own])
    loader.wait()
    grad_glu = grad_one[...].astype(jnp.bfloat16).astype(jnp.float32)
    keep_rows = pl.ds(pl.multiple_of(core * HALF, HALF), HALF)
    send_rows = pl.ds(pl.multiple_of((1 - core) * HALF, HALF), HALF)
    grad_norm = jnp.zeros(grad_one.shape, jnp.float32)
    for half in range(2):
        cols = slice(half * HALF, (half + 1) * HALF)
        sig_f = sig[own, cols].astype(jnp.float32)
        grad_here = grad_glu[:, cols] * sig_f
        grad_value = grad_here.astype(jnp.bfloat16)
        grad_gate = (grad_here * value[own, cols].astype(jnp.float32) * (1.0 - sig_f)).astype(
            jnp.bfloat16
        )
        slot = jnp.where(member == half, 0, 1)
        send_o[slot, :HALF] = dot_nn(git_s[send_rows], grad_value).astype(jnp.bfloat16)
        keep_o[slot, :HALF] = dot_nn(git_s[keep_rows], grad_value).astype(jnp.bfloat16)
        send_o[slot, HALF : 2 * HALF] = dot_nn(git_s[send_rows], grad_gate).astype(jnp.bfloat16)
        keep_o[slot, HALF : 2 * HALF] = dot_nn(git_s[keep_rows], grad_gate).astype(jnp.bfloat16)
        grad_norm = grad_norm + dot_nt(grad_value, wv_s[half]) + dot_nt(grad_gate, wg_s[half])
    unit, inv = row_stats(x_s[...])
    gain_glu_row = jnp.sum(grad_norm * unit, axis=0, keepdims=True)
    x_s[...] = grad_one[...] + norm_grad(grad_norm, unit, inv, gain_glu[...])
    scatter_rows(x_s, n_s, gin_o)
    tail = send_o.shape[1] - 2 * HALF
    both = jnp.concatenate(
        [gain_glu_row, gain_branch_row[...], jnp.zeros((14, 2 * HALF), jnp.float32)], axis=0
    )
    both = both.astype(jnp.bfloat16)
    for target in (send_o, keep_o):
        for shard in range(2):
            target[shard, 2 * HALF :] = jnp.zeros((tail, HALF), jnp.bfloat16)
            target[shard, 2 * HALF : 2 * HALF + 16] = both[:, :HALF]
            target[shard, 2 * HALF + 16 : 2 * HALF + 32] = both[:, HALF:]


def over_mp(values):
    return lax.ppermute(values, "mp", [(0, 1), (1, 0)])


def flat_pairs(dp_size, rule):
    pairs = []
    for dp_index in range(dp_size):
        for member in range(2):
            pair, core = dp_index // 2, dp_index % 2
            new_core, new_member = rule(core, member)
            pairs.append((dp_index * 2 + member, (pair * 2 + new_core) * 2 + new_member))
    return pairs


def unpack_kernel(layout, sizes, info, both, far, *rest):
    outs, packed, sems = rest[:-2], rest[-2], rest[-1]
    core, ybit, zpos = info[0], info[3], info[4]
    ys = both.shape[0]
    zs, step = (4, both.shape[3]) if len(both.shape) > 3 else (1, both.shape[1])
    loader = Loader(sems)
    for half in range(2):
        for yside in range(ys):
            for zside in range(zs):
                near, far_bit = zside // 2, zside % 2
                at = (yside ^ ybit, near ^ zpos % 2, far_bit ^ zpos // 2)
                if zs == 1:
                    spot = packed.at[half, pl.ds(yside * step, step)]
                    loader.either(both.at[at[0]], far.at[at[0]], half, spot)
                    continue
                first, base = 0, 0
                for size in sizes:
                    low = max(first, far_bit * step)
                    top = min(first + size // 2, (far_bit + 1) * step)
                    if low < top:
                        source = pl.ds(low - far_bit * step, top - low)
                        spot = base + yside * size + near * (size // 2) + low - first
                        loader.either(
                            both.at[at].at[source],
                            far.at[at].at[source],
                            half,
                            packed.at[half, pl.ds(spot, top - low)],
                        )
                    first += size // 2
                    base += 2 * size
    loader.go(core)
    loader.wait()
    layout(packed, outs)


def layout_ffn(packed, outs):
    w_in, w_back, w_out = outs
    blocks = w_in.shape[1] // HALF
    base = blocks * HALF
    for half in range(2):
        side = slice(half * HALF, (half + 1) * HALF)
        for block in range(blocks):
            at = block * HALF
            w_in[side, block * HALF : (block + 1) * HALF] = as_f32(packed[half, at : at + HALF])
        w_back[:, side] = as_f32(packed[half, base : base + w_back.shape[0]])
        last = base + w_back.shape[0]
        w_out[:, side] = as_f32(packed[half, last : last + w_out.shape[0]])


def layout_attn(packed, outs):
    w_qkv, w_point = outs
    for half in range(2):
        for index in range(3):
            at = index * HALF
            w_qkv[index, half * HALF : (half + 1) * HALF] = as_f32(packed[half, at : at + HALF])
        at = 3 * HALF
        w_point[half * 2 * HALF : (half + 1) * 2 * HALF] = as_f32(packed[half, at : at + 2 * HALF])


def layout_branch(packed, outs):
    w_left, w_right, taps, gain, late_ffn, late_attn = outs
    count = taps.shape[0]
    blocks = w_left.shape[1] // HALF
    base = blocks * HALF
    for half in range(2):
        side = slice(half * HALF, (half + 1) * HALF)
        for block in range(blocks):
            w_left[side, block * HALF : (block + 1) * HALF] = as_f32(
                packed[half, block * HALF : (block + 1) * HALF]
            )
        w_right[0, side] = as_f32(packed[half, base : base + HALF, :LANES])
        w_right[1, side] = as_f32(packed[half, base : base + HALF, LANES:])
        w_right[2, side] = as_f32(packed[half, base + HALF : base + 2 * HALF, :LANES])
        for piece in range(4):
            row = base + HALF + piece * 16
            at = half * 4 * LANES + piece * LANES
            rows = as_f32(packed[half, row : row + 16, LANES:])
            taps[:, at : at + LANES] = rows[:count]
            gain[:, at : at + LANES] = rows[count : count + 1]
            row += 4 * 16
            rows = as_f32(packed[half, row : row + 16, LANES:])
            late_ffn[:, piece * LANES : (piece + 1) * LANES] = rows[:1]
            late_attn[:, piece * LANES : (piece + 1) * LANES] = rows[1:2]


def layout_glu(packed, outs):
    w_value, w_gate, late_glu, late_branch = outs
    for half in range(2):
        side = slice(half * HALF, (half + 1) * HALF)
        w_value[side] = as_f32(packed[half, :HALF])
        w_gate[side] = as_f32(packed[half, HALF : 2 * HALF])
        rows = as_f32(packed[0, 2 * HALF + 16 * half : 2 * HALF + 16 * (half + 1)])
        late_glu[:, side] = rows[:1]
        late_branch[:, side] = rows[1:2]


MEGA = 1024 * 1024
SPARE = 8
ALL_VMEM = 62 * MEGA


def call(body, name, ins, outs, scratch, flops, copies=0, room=None, cost=10**11):
    spaces = {"s": pltpu.SMEM, "v": pltpu.VMEM, "h": pltpu.HBM}
    shapes = [jax.ShapeDtypeStruct(shape, dtype) for shape, dtype in outs]
    held = [(a.shape, a.dtype) for a, place in ins if place == "v"] + outs + scratch
    held = sum(math.prod(shape) * jnp.dtype(dtype).itemsize for shape, dtype in held)
    scratch = [pltpu.VMEM(shape, dtype) for shape, dtype in scratch]
    if copies:
        scratch.append(pltpu.SemaphoreType.DMA((copies,)))
    return pl.pallas_call(
        body,
        out_shape=shapes,
        in_specs=[pl.BlockSpec(memory_space=spaces[place]) for _, place in ins],
        out_specs=[pl.BlockSpec(memory_space=pltpu.VMEM) for _ in shapes],
        scratch_shapes=scratch,
        name=name,
        compiler_params=pltpu.CompilerParams(vmem_limit_bytes=room or held + SPARE * MEGA),
        cost_estimate=pl.CostEstimate(flops=cost, bytes_accessed=10**6, transcendentals=0),
    )(*[array for array, _ in ins])


def dp_xor(values, bits):
    size = lax.axis_size("dp")
    return lax.ppermute(values, "dp", [(index, index ^ bits) for index in range(size)])


def over_x_and_y(values):
    pairs = []
    for dp_index in range(lax.axis_size("dp")):
        for member in range(2):
            pairs.append((dp_index * 2 + member, (dp_index ^ 2) * 2 + 1 - member))
    return lax.ppermute(values, ("dp", "mp"), pairs)


def later(values, *first):
    return lax.optimization_barrier((values, first))[0]


class Sums:
    def __init__(self, send, keep, ybit):
        self.keep, self.ybit = keep, ybit
        self.recv = dp_xor(send, 1)

    def over_xy(self, *first):
        recv, keep = later((self.recv, self.keep), *first)
        half = keep.shape[1] // 2

        def piece(shard, bit):
            at = bit * half
            cut = lambda values: as_f32(lax.dynamic_slice_in_dim(values[shard], at, half, axis=0))
            return (cut(keep) + cut(recv)).astype(jnp.bfloat16)

        self.kept = piece(0, self.ybit)
        gone = [piece(1, self.ybit), piece(0, 1 - self.ybit), piece(1, 1 - self.ybit)]
        self.got = [over_mp(gone[0]), dp_xor(gone[1], 2), over_x_and_y(gone[2])]
        return gone

    def over_x(self, *first):
        recv, keep = later((self.recv, self.keep), *first)
        other = (as_f32(keep[1]) + as_f32(recv[1])).astype(jnp.bfloat16)
        self.kept = as_f32(keep[0]) + as_f32(recv[0])
        self.got = over_mp(other)
        return [other]

    def over_y(self, *first):
        got, kept = later((self.got, self.kept), *first)
        mine = (kept + as_f32(got)).astype(jnp.bfloat16)
        half = mine.shape[0] // 2
        gone = lax.dynamic_slice_in_dim(mine, (1 - self.ybit) * half, half, axis=0)
        self.kept = lax.dynamic_slice_in_dim(mine, self.ybit * half, half, axis=0)
        self.got = dp_xor(gone, 2)
        return [gone]

    def last_quarter(self, *first):
        got, kept = later((self.got, self.kept), *first)
        return (as_f32(kept) + as_f32(got)).astype(jnp.bfloat16)

    def quarter(self, *first):
        got, kept = later((self.got, self.kept), *first)
        total = as_f32(kept) + as_f32(got[1]) + (as_f32(got[0]) + as_f32(got[2]))
        return total.astype(jnp.bfloat16)


def halve(mine, bit, across):
    half = mine.shape[0] // 2
    kept = lax.dynamic_slice_in_dim(mine, bit * half, half, axis=0)
    gone = lax.dynamic_slice_in_dim(mine, (1 - bit) * half, half, axis=0)
    return gone, (kept, dp_xor(gone, across))


class Rest:
    def __init__(self, zpos):
        self.zpos, self.pairs, self.sizes = zpos, [], []

    def over_z1(self, quarter):
        gone, pair = halve(quarter, self.zpos % 2, 4)
        self.pairs.append(pair)
        self.sizes.append(quarter.shape[0])
        return [gone]

    def over_z2(self, *first):
        pairs = later(self.pairs, *first)
        mine = [(as_f32(kept) + as_f32(got)).astype(jnp.bfloat16) for kept, got in pairs]
        gone, (self.kept, self.got) = halve(jnp.concatenate(mine, axis=0), self.zpos // 2, 8)
        return [gone]

    def back_z2(self, *first):
        got, kept = later((self.got, self.kept), *first)
        self.mine = (as_f32(kept) + as_f32(got)).astype(jnp.bfloat16)
        self.got = dp_xor(self.mine, 8)
        return [self.mine]

    def back_z1(self, *first):
        return self.double(4, *first)

    def double(self, across, *first):
        got, mine = later((self.got, self.mine), *first)
        self.mine = jnp.stack([mine, got])
        self.got = dp_xor(self.mine, across)
        return [self.mine]

    def back_y(self, *first):
        return self.double(2, *first)

    def back_core(self, *first):
        self.got, mine = later((self.got, self.mine), *first)
        self.both = jnp.stack([mine, self.got])
        self.far = dp_xor(self.both, 1)
        return [self.both]


class Short(Rest):
    def along_z1(self, quarter):
        self.sizes.append(quarter.shape[0])
        self.mine, self.got = quarter, dp_xor(quarter, 4)
        return [quarter]

    def along_z2(self, *first):
        got, mine = later((self.got, self.mine), *first)
        self.mine = (as_f32(mine) + as_f32(got)).astype(jnp.bfloat16)
        self.got = dp_xor(self.mine, 8)
        return [self.mine]

    def back_y(self, *first):
        got, mine = later((self.got, self.mine), *first)
        self.mine = (as_f32(mine) + as_f32(got)).astype(jnp.bfloat16)
        self.got = dp_xor(self.mine, 2)
        return [self.mine]


def unpack(layout, info, sums, outs):
    ys, cols = 2, sums.both.shape[-1]
    zs, part = (4, sums.both.shape[3]) if sums.both.ndim > 3 else (1, sums.both.shape[1])
    return call(
        functools.partial(unpack_kernel, layout, sums.sizes),
        "unpack_" + layout.__name__,
        [(info, "s"), (sums.both, "h"), (sums.far, "h")],
        [(shape, jnp.float32) for shape in outs],
        [((2, ys * zs * part, cols), jnp.bfloat16)],
        1e6,
        4 * ys * (zs + len(sums.sizes)),
    )


def paired(
    inputs, lengths, gain_glu, w_value, w_gate, gain_branch, w_left, w_right, gain_mid, w_depth,
    w_point, gain_attn, w_qkv, w_out, gain_ffn, w_in, w_back, cotangent,
):
    low, full = jnp.bfloat16, jnp.float32
    member = lax.axis_index("mp")
    place = lax.axis_index("dp")
    core, ybit, zpos = place % 2, (place // 2) % 2, place // 4
    rows, width = inputs.shape[1:]
    ext = rows + 2 * EDGE
    inner = 2 * w_left.shape[1]
    chunks = inner // HALF
    right_cols = 2 * w_right.shape[2]
    sep_width = w_point.shape[1]
    heads = 2 * w_qkv.shape[2] // HEAD_DIM
    row = lambda gain: gain.reshape(1, -1)

    block = inputs[0]
    edge = jnp.where(member == 0, block[rows - EDGE :], block[:EDGE])
    size_code = jnp.stack([lengths[0] // 32, lengths[0] % 32]).astype(low)
    code_rows = jnp.broadcast_to(jnp.repeat(size_code, EDGE // 2)[:, None], (EDGE, width))
    edge = jnp.concatenate([edge, code_rows], axis=0)
    edge = lax.ppermute(
        edge, ("dp", "mp"), flat_pairs(lax.axis_size("dp"), lambda c, m: (1 - m, c))
    )
    code = as_f32(edge[EDGE:, 0])
    length = (code[0] * 32 + code[EDGE // 2]).astype(jnp.int32)
    edge = edge[:EDGE]
    swap = [p for p in flat_pairs(lax.axis_size("dp"), lambda c, m: (m, c)) if p[0] != p[1]]
    moved = lax.ppermute(block, ("dp", "mp"), swap)
    info = jnp.stack([core, member, length, ybit, zpos]).astype(jnp.int32)

    v = lambda *arrays: [(array, "v") for array in arrays]
    h = lambda *arrays: [(array, "h") for array in arrays]
    pack = jnp.concatenate([w_depth, gain_mid[None]], axis=0)
    got0 = over_mp(jnp.where(core == 0, w_value, w_gate))
    blocks = w_left.shape[1] // HALF
    bundle1, bundle2, bundle3 = call(
        bundle_kernel, "bundle",
        [(jnp.stack([core, member]).astype(jnp.int32), "s")]
        + h(w_left, w_right, w_point) + v(w_depth, row(gain_mid)) + h(w_qkv, w_out, w_in, w_back),
        [((blocks * (width + 16), HALF), low)] + [((3 * width, HALF), low)] * 2,
        [], 1, 16, ALL_VMEM,
    )
    got1 = over_mp(bundle1)
    part0 = dp_xor(got0, 1)
    cot = cotangent[0]
    cot_moved = lax.ppermute(cot, ("dp", "mp"), swap)

    where = [(info, "s")]
    macs = 2.0 * rows * width
    cot, resid_one, branch_in, glu_in, value, sig = call(
        glu_kernel, "glu",
        where + v(block, moved, cot, cot_moved, edge, row(gain_glu), row(gain_branch))
        + h(w_value, w_gate, got0, part0),
        [((rows, width), low), ((ext, width), full)] + [((ext, width), low)] * 4,
        [((ext, width), full), ((rows, width), full), ((width // LANES, rows, LANES), full)]
        + [((2,) + w_value.shape, low)] * 2,
        macs * width * 2, 8,
    )
    left_own, right_own, mid_own, sums_own = call(
        branch_own_kernel, "branch_own",
        where + v(branch_in) + h(w_left) + v(w_right),
        [
            ((chunks // 2, ext, HALF), low), ((ext, right_cols // 2), full),
            ((chunks // 2, ext, HALF), full), ((2, ext, LANES), full),
        ],
        [((chunks // 2, width, HALF), low)],
        1, chunks // 2,
    )
    got1 = later(got1, sums_own)
    part1 = dp_xor(got1, 1)
    got2 = over_mp(later(bundle2, got1))
    got3 = over_mp(later(bundle3, got1))
    resid_two, left_pre, right_pre, stats, depth = call(
        branch_kernel, "branch",
        where
        + v(branch_in, resid_one, pack, left_own, right_own, mid_own, sums_own)
        + h(w_point, got1, part1),
        [
            ((rows, width), full), ((chunks, ext, HALF), low), ((ext, right_cols), full),
            ((ext, LANES), full), ((chunks, rows, HALF), low),
        ],
        [
            ((chunks // 2, width, HALF), low), (w_right.shape, low), ((2,) + w_point.shape, low),
            ((4, 16, HALF), low), ((16, inner), full), ((chunks, ext, HALF), full),
            ((rows + 64, HALF), full), ((2, ext, LANES), full), ((rows, sep_width), full),
        ],
        1, 20,
    )
    got2 = later(got2, resid_two)
    part2 = dp_xor(got2, 1)
    attn_in, kv_own = call(
        kv_kernel, "keys_values",
        where + v(resid_two, row(gain_attn)) + h(w_qkv, got2, part2),
        [((rows, width), low), ((rows, 2 * width), low)],
        [((2, 2) + w_qkv.shape[1:], low)],
        macs * width * 2, 8,
    )
    (queries,) = call(
        query_kernel, "queries",
        where + v(attn_in) + h(w_qkv, got2, part2),
        [((rows, width), low)],
        [((2, 1) + w_qkv.shape[1:], low)],
        macs * width, 4,
    )
    kv_far = dp_xor(kv_own, 1)
    context0, lse0, context1, lse1 = call(
        attend_kernel, "attend",
        where + v(queries, kv_own, kv_far),
        [((rows, width // 2), low), ((heads // 2, rows), full)] * 2,
        [((2 * rows, LANES), full)],
        macs * 8000,
    )
    part3 = dp_xor(later(got3, lse1), 1)
    r_ffn = 2 * w_in.shape[1] + w_out.shape[0]
    out_rows, grad_three, grad_ctx, ggain_ffn, send, keep = call(
        ffn_kernel, "ffn",
        where + v(resid_two, context0, context1, cot, row(gain_ffn))
        + h(w_out, w_in, w_back, got2, part2, got3, part3),
        [
            ((rows, width), low), ((rows, width), full), ((rows, width), low), ((1, width), full),
            ((2, r_ffn, HALF), low), ((2, r_ffn, HALF), low),
        ],
        [
            ((2,) + w_out.shape, low), ((chunks, width, HALF), low), ((2,) + w_back.shape, low),
            ((rows, width), low), ((width, rows), low), ((rows, width), low), ((rows, width), full),
            ((rows, width), full), ((width, rows), low), ((width // LANES, rows, LANES), full),
        ],
        macs * 16000, 24, 50 * MEGA,
    )
    ffn_sums = Sums(send, keep, ybit)
    swapped_out = lax.ppermute(out_rows, ("dp", "mp"), swap)

    seen = v(context0, context1, grad_ctx, lse0, lse1)
    grad_q, grad_far = call(
        functools.partial(attend_back_kernel, 1), "attend_back_far",
        where + v(queries, kv_far) + seen,
        [((rows, width), full), ((rows, 2 * width), low)],
        [((rows, LANES), full)] * 3, 1,
    )
    recv = dp_xor(grad_far, 1)
    sent = ffn_sums.over_xy(grad_q)
    out_rows, swapped_out = later((out_rows, swapped_out), *sent)
    outputs = jnp.where(member == core, out_rows, swapped_out)
    sent.append(outputs)
    grad_q, grad_own = call(
        functools.partial(attend_back_kernel, 0), "attend_back_own",
        [(later(info, *sent), "s")] + v(queries, kv_own) + seen + v(grad_q),
        [((rows, width), low), ((rows, 2 * width), full)],
        [((rows, LANES), full)] * 3, 1,
    )
    grad_two, grad_sep, sep_edge, ggain_attn, send, keep = call(
        qkv_back_kernel, "qkv_back",
        where
        + v(grad_q, grad_own, recv, attn_in, resid_two, grad_three, row(gain_attn))
        + h(w_qkv, got2, part2),
        [
            ((rows, width), full), ((rows, sep_width), low), ((EDGE, sep_width), low),
            ((1, width), full),
        ]
        + [((2, 3 * HALF, HALF), low)] * 2,
        [
            ((2,) + w_qkv.shape, low), ((width, rows), low),
            ((sep_width // LANES, rows, LANES), full),
        ],
        1, 12,
    )
    sep_edge = dp_xor(sep_edge, 1)
    send, keep = call(
        point_kernel, "point_back",
        where + v(grad_sep, depth, send, keep),
        [((2, 5 * HALF, HALF), low)] * 2, [], macs * 1000,
    )
    attn_sums = Sums(send, keep, ybit)
    unit, scaled, mid_sums, small = call(
        depth_back_kernel, "depth_back",
        where
        + v(grad_sep, sep_edge, left_pre, right_pre, stats, pack)
        + h(w_point, got1, part1),
        [
            ((chunks, ext, HALF), low), ((chunks, ext, HALF), low), ((2, ext, LANES), full),
            ((16, inner), full),
        ],
        [
            ((2,) + w_point.shape, low), ((4, 16, HALF), low), ((16, inner), full),
            ((ext, sep_width), low),
            ((2, rows + 64, LANES), full), ((2, rows + 64, LANES), full),
            ((2, 4 * EDGE, LANES), full), ((ext, HALF), full), ((ext, HALF), full),
            ((3, ext, LANES), full),
        ],
        macs * 8000, 8,
    )
    ffn_rest = Rest(zpos)
    sent = ffn_rest.over_z1(ffn_sums.quarter(mid_sums))
    sent += attn_sums.over_x(*sent)
    r_branch = inner // 2 + 2 * HALF
    grad_left, grad_right, send, keep = call(
        branch_back_kernel, "branch_back",
        [(later(info, *sent), "s")]
        + v(
            unit, scaled, mid_sums, small, left_pre, right_pre, stats, branch_in, ggain_ffn,
            ggain_attn,
        ),
        [
            ((chunks, rows, HALF), low), ((ext, right_cols), low),
            ((2, r_branch, HALF), low), ((2, r_branch, HALF), low),
        ],
        [((3, ext, LANES), full), ((ext, right_cols), full), ((width, ext), low)],
        macs * 4000,
    )
    branch_sums = Sums(send, keep, ybit)
    sent = ffn_rest.over_z2(grad_left)
    sent += attn_sums.over_y(*sent)
    grad_one, ggain_branch = call(
        join_back_kernel, "join_back",
        [(later(info, *sent), "s")]
        + v(grad_left, grad_right, resid_one, grad_two, row(gain_branch))
        + h(w_left, w_right, got1, part1),
        [((rows, width), full), ((1, width), full)],
        [((chunks, width, HALF), low), ((2,) + w_right.shape, low)],
        macs * 4000, 12,
    )
    sent = ffn_rest.back_z2(grad_one)
    sent += branch_sums.over_xy(*sent)
    attn_rest = Rest(zpos)
    grad_in, send, keep = call(
        glu_back_kernel, "glu_back",
        [(later(info, *sent), "s")]
        + v(grad_one, ggain_branch, row(gain_glu), block, moved, glu_in, value, sig)
        + h(w_value, w_gate, got0, part0),
        [((rows, width), low), ((2, 640, HALF), low), ((2, 640, HALF), low)],
        [
            ((2,) + w_value.shape, low), ((2,) + w_gate.shape, low), ((rows, width), full),
            ((width // LANES, rows, LANES), full), ((width, rows), low),
        ],
        macs * 3000, 4,
    )
    glu_sums = Sums(send, keep, ybit)
    swapped_in = lax.ppermute(grad_in, ("dp", "mp"), swap)
    branch_rest, glu_rest = Rest(zpos), Short(zpos)
    sent = attn_rest.over_z1(attn_sums.last_quarter(grad_in))
    sent = ffn_rest.back_z1(*sent)
    sent = branch_rest.over_z1(branch_sums.quarter(*sent))
    sent = glu_sums.over_x(*sent)
    sent = attn_rest.over_z2(*sent)
    sent = branch_rest.over_z2(*sent)
    sent = glu_sums.over_y(*sent)
    sent = ffn_rest.back_y(*sent)
    sent = attn_rest.back_z2(*sent)
    sent = branch_rest.back_z2(*sent)
    sent = glu_rest.along_z1(glu_sums.last_quarter(*sent))
    grad_in, swapped_in = later((grad_in, swapped_in), *sent)
    grad_inputs = jnp.where(member == core, grad_in, swapped_in)
    sent = branch_rest.back_z1(grad_inputs)
    sent = glu_rest.along_z2(*sent)
    sent = ffn_rest.back_core(*sent)
    sent = attn_rest.back_z1(*sent)
    sent = branch_rest.back_y(*sent)
    sent = glu_rest.back_y(*sent)
    sent = attn_rest.back_y(*sent)
    g_in, g_back, g_out = unpack(
        layout_ffn, later(info, *sent), ffn_rest, [w_in.shape, w_back.shape, w_out.shape]
    )
    sent = branch_rest.back_core(g_in)
    sent = glu_rest.back_core(*sent)
    g_value, g_gate, g_glu_gain, g_branch_gain = unpack(
        layout_glu, later(info, *sent), glu_rest,
        [w_value.shape, w_gate.shape, (1, width), (1, width)],
    )
    g_left, g_right, g_taps, g_mid, g_ffn_gain, g_attn_gain = unpack(
        layout_branch, later(info, g_value), branch_rest,
        [
            w_left.shape, w_right.shape, w_depth.shape, (1, inner // 2), (1, width), (1, width),
        ],
    )
    sent = attn_rest.back_core(g_left)
    g_qkv, g_point = unpack(
        layout_attn, later(info, *sent), attn_rest, [w_qkv.shape, w_point.shape]
    )
    flat = lambda gain: gain.reshape(-1)
    return (
        outputs[None],
        grad_inputs[None],
        flat(g_glu_gain),
        g_value,
        g_gate,
        flat(g_branch_gain),
        g_left,
        g_right,
        flat(g_mid),
        g_taps,
        g_point,
        flat(g_attn_gain),
        g_qkv,
        g_out,
        flat(g_ffn_gain),
        g_in,
        g_back,
    )


def solution(mesh):
    placed = (
        P("dp", "mp", None),
        P("dp"),
        P(),
        P(None, "mp"),
        P(None, "mp"),
        P(),
        P(None, "mp"),
        P(None, None, "mp"),
        P("mp"),
        P(None, "mp"),
        P("mp", None),
        P(),
        P(None, None, "mp"),
        P("mp", None),
        P(),
        P(None, "mp"),
        P("mp", None),
        P("dp", "mp", None),
    )
    fast = mesh.shape["mp"] == 2 and mesh.shape["dp"] == 16
    return jax.shard_map(
        paired if fast else local,
        mesh=mesh,
        in_specs=placed,
        out_specs=(
            P("dp", "mp", None),
            P("dp", "mp", None),
            P(),
            P(None, "mp"),
            P(None, "mp"),
            P(),
            P(None, "mp"),
            P(None, None, "mp"),
            P("mp"),
            P(None, "mp"),
            P("mp", None),
            P(),
            P(None, None, "mp"),
            P("mp", None),
            P(),
            P(None, "mp"),
            P("mp", None),
        ),
        check_vma=False,
    )
```

```python
import functools
import math

import jax
import jax.numpy as jnp
from jax import lax
from jax.experimental import pallas as pl
from jax.experimental.pallas import tpu as pltpu
from jax.sharding import PartitionSpec as P

FF = 2048
HEAD_DIM = 64
EDGE = 16


epsilon = 1e-06
negative_big = -1e30


def matmul(left_side, right_side):
    return jnp.dot(left_side, right_side, preferred_element_type=jnp.float32)


def contract_rows(left_side, right_side):
    return lax.dot_general(
        left_side, right_side, (((0,), (0,)), ((), ())), preferred_element_type=jnp.float32
    )


def contract_cols(left_side, right_side):
    return lax.dot_general(
        left_side, right_side, (((1,), (1,)), ((), ())), preferred_element_type=jnp.float32
    )


def spread_rows(pieces):
    return lax.all_gather(pieces, "mp", axis=1, tiled=True)


def collect_rows(partial_value):
    return lax.psum_scatter(
        partial_value.astype(jnp.bfloat16), "mp", scatter_dimension=1, tiled=True
    ).astype(jnp.float32)


def channel_sums(former, latter):
    return lax.psum((jnp.sum(former, axis=-1), jnp.sum(latter, axis=-1)), "mp")


def normalize(values, gain_vec):
    centre = values - jnp.mean(values, axis=-1, keepdims=True)
    scale_inv = lax.rsqrt(jnp.mean(centre * centre, axis=-1, keepdims=True) + epsilon)
    unit_rows = centre * scale_inv
    return (unit_rows * gain_vec, unit_rows, scale_inv)


def normalize_back(grad_out, unit_rows, scale_inv, gain_vec):
    scaled = grad_out * gain_vec
    mean_one = jnp.mean(scaled, axis=-1, keepdims=True)
    mean_two = jnp.mean(scaled * unit_rows, axis=-1, keepdims=True)
    grad_in = scale_inv * (scaled - mean_one - unit_rows * mean_two)
    return (grad_in, jnp.sum(grad_out * unit_rows, axis=(0, 1)))


def silu_slope(values):
    sigmoid_part = jax.nn.sigmoid(values)
    return sigmoid_part * (1.0 + values * (1.0 - sigmoid_part))


def shifted(values, offset):
    if offset == 0:
        return values
    margin = abs(offset)
    seq_len = values.shape[1]
    filler = jnp.zeros(values.shape[:1] + (margin,) + values.shape[2:], values.dtype)
    padded = jnp.concatenate([filler, values, filler], axis=1)
    return lax.slice_in_dim(padded, margin + offset, margin + offset + seq_len, axis=1)


def place_right(right_vals, stride):
    filler = jnp.zeros(right_vals.shape + (stride - 1,), right_vals.dtype)
    joined = jnp.concatenate([right_vals[..., None], filler], axis=-1)
    return joined.reshape(right_vals.shape[:-1] + (right_vals.shape[-1] * stride,))


def attend_forward(queries, key_vecs, value_vecs, key_valid, block_rows, score_scale):
    contexts = []
    log_parts = []
    for row_start in range(0, queries.shape[0], block_rows):
        query_rows = queries[row_start : row_start + block_rows]
        scores = (
            jnp.einsum("qhd,khd->hqk", query_rows, key_vecs, preferred_element_type=jnp.float32)
            * score_scale
        )
        scores = jnp.where(key_valid[None, None, :], scores, negative_big)
        row_max = jnp.max(scores, axis=-1, keepdims=True)
        weights_exp = jnp.exp(scores - row_max)
        row_total = jnp.sum(weights_exp, axis=-1, keepdims=True)
        probability = (weights_exp / row_total).astype(jnp.bfloat16)
        contexts.append(
            jnp.einsum("hqk,khd->qhd", probability, value_vecs, preferred_element_type=jnp.float32)
        )
        log_parts.append((row_max + jnp.log(row_total))[..., 0])
    return (jnp.concatenate(contexts, axis=0), jnp.concatenate(log_parts, axis=1))


def attend_back(
    queries, key_vecs, value_vecs, key_valid, log_sums, grad_context, block_rows, score_scale
):
    grad_queries = []
    grad_keys = jnp.zeros(key_vecs.shape, jnp.float32)
    grad_values = jnp.zeros(value_vecs.shape, jnp.float32)
    for row_start in range(0, queries.shape[0], block_rows):
        query_rows = queries[row_start : row_start + block_rows]
        grad_rows = grad_context[row_start : row_start + block_rows]
        log_rows = log_sums[:, row_start : row_start + block_rows]
        scores = (
            jnp.einsum("qhd,khd->hqk", query_rows, key_vecs, preferred_element_type=jnp.float32)
            * score_scale
        )
        scores = jnp.where(key_valid[None, None, :], scores, negative_big)
        probability = jnp.exp(scores - log_rows[..., None])
        grad_prob = jnp.einsum(
            "qhd,khd->hqk", grad_rows, value_vecs, preferred_element_type=jnp.float32
        )
        row_dot = jnp.sum(probability * grad_prob, axis=-1, keepdims=True)
        grad_scores = (probability * (grad_prob - row_dot)).astype(jnp.bfloat16)
        grad_queries.append(
            jnp.einsum("hqk,khd->qhd", grad_scores, key_vecs, preferred_element_type=jnp.float32)
            * score_scale
        )
        grad_keys = (
            grad_keys
            + jnp.einsum(
                "hqk,qhd->khd", grad_scores, query_rows, preferred_element_type=jnp.float32
            )
            * score_scale
        )
        grad_values = grad_values + jnp.einsum(
            "hqk,qhd->khd",
            probability.astype(jnp.bfloat16),
            grad_rows,
            preferred_element_type=jnp.float32,
        )
    grad_query_all = jnp.concatenate(grad_queries, axis=0)
    return (grad_query_all.astype(jnp.bfloat16), grad_keys, grad_values)


def split_pass(
    inputs,
    lengths,
    gain_glu,
    w_value,
    w_gate,
    gain_branch,
    w_left,
    w_right,
    gain_mid,
    w_depth,
    w_point,
    gain_attn,
    w_qkv,
    w_out,
    gain_ffn,
    w_in,
    w_back,
    cotangent,
):
    seqs_here, local_len, model_width = inputs.shape
    group_size = lax.axis_size("mp")
    member = lax.axis_index("mp")
    seq_len = local_len * group_size
    group_rows = seqs_here * seq_len
    positions = lax.broadcasted_iota(jnp.int32, (seqs_here, seq_len), 1)
    key_valid = positions < lengths[:, None]
    valid_full = key_valid.astype(jnp.float32)
    valid_own = lax.dynamic_slice_in_dim(valid_full, member * local_len, local_len, axis=1)
    inner_cols = w_left.shape[1]
    right_cols = w_right.shape[2]
    stride = inner_cols // right_cols
    conv_taps = w_right.shape[0]
    sep_taps = w_depth.shape[0]
    sep_width = w_point.shape[1]
    head_cols = w_qkv.shape[2]
    heads_here = head_cols // HEAD_DIM
    score_scale = 1.0 / math.sqrt(HEAD_DIM)
    block_rows = min(512, seq_len)
    group_shape = (seqs_here, seq_len, model_width)
    depth_taps = w_depth.astype(jnp.float32)
    gain_mid_f = gain_mid.astype(jnp.float32)

    def branch_inner(gathered):
        flat_rows = gathered.reshape(group_rows, model_width)
        left_pre = matmul(flat_rows, w_left).reshape(seqs_here, seq_len, inner_cols)
        right_pre = jnp.zeros((group_rows, right_cols), jnp.float32)
        for tap_index in range(conv_taps):
            moved = shifted(gathered, tap_index - conv_taps // 2).reshape(group_rows, model_width)
            right_pre = right_pre + matmul(moved, w_right[tap_index])
        right_pre = right_pre.reshape(seqs_here, seq_len, right_cols)
        mid = jax.nn.silu(left_pre) + place_right(jax.nn.silu(right_pre), stride)
        return (left_pre, right_pre, mid)

    def depth_mix(depth_in):
        depth = jnp.zeros(depth_in.shape, jnp.float32)
        for tap_index in range(sep_taps):
            depth = depth + shifted(depth_in, tap_index - sep_taps // 2) * depth_taps[tap_index]
        return depth.astype(jnp.bfloat16)

    def project_qkv(gathered):
        flat_rows = gathered.reshape(group_rows, model_width)
        joined = jnp.einsum("td,kdc->ktc", flat_rows, w_qkv, preferred_element_type=jnp.float32)
        return joined.astype(jnp.bfloat16).reshape(3, seqs_here, seq_len, heads_here, HEAD_DIM)

    def forward_one(pieces):
        return attend_forward(pieces[0], pieces[1], pieces[2], pieces[3], block_rows, score_scale)

    def backward_one(pieces):
        return attend_back(
            pieces[0],
            pieces[1],
            pieces[2],
            pieces[3],
            pieces[4],
            pieces[5],
            block_rows,
            score_scale,
        )

    resid_in = inputs.astype(jnp.float32)
    normed_glu, unit_glu, inv_glu = normalize(resid_in, gain_glu)
    gathered_glu = spread_rows(normed_glu.astype(jnp.bfloat16))
    flat_glu = gathered_glu.reshape(group_rows, model_width)
    value_pre = matmul(flat_glu, w_value)
    gate_sig = jax.nn.sigmoid(matmul(flat_glu, w_gate))
    glu_local = (value_pre * gate_sig).astype(jnp.bfloat16).reshape(seqs_here, seq_len, -1)
    glu_rows = lax.all_to_all(glu_local, "mp", split_axis=1, concat_axis=2, tiled=True)
    resid_one = resid_in + glu_rows.astype(jnp.float32)
    normed_branch, unit_branch, inv_branch = normalize(resid_one, gain_branch)
    gathered_branch = spread_rows((valid_own[..., None] * normed_branch).astype(jnp.bfloat16))
    left_pre, right_pre, mid = branch_inner(gathered_branch)
    mid_sum, mid_square = channel_sums(mid, mid * mid)
    mid_mean = mid_sum / FF
    inv_mid = lax.rsqrt(mid_square / FF - mid_mean * mid_mean + epsilon)
    unit_mid = (mid - mid_mean[..., None]) * inv_mid[..., None]
    depth_in = valid_full[..., None] * unit_mid * gain_mid_f
    depth_low = depth_mix(depth_in)
    sep_part = matmul(depth_low.reshape(group_rows, inner_cols), w_point).reshape(
        seqs_here, seq_len, sep_width
    )
    sep_rows = collect_rows(sep_part)
    resid_two = resid_one + jnp.pad(sep_rows, ((0, 0), (0, 0), (0, model_width - sep_width)))
    normed_attn, unit_attn, inv_attn = normalize(resid_two, gain_attn)
    gathered_attn = spread_rows(normed_attn.astype(jnp.bfloat16))
    qkv_heads = project_qkv(gathered_attn)
    context, log_sums = lax.map(forward_one, (qkv_heads[0], qkv_heads[1], qkv_heads[2], key_valid))
    context_low = context.astype(jnp.bfloat16).reshape(group_rows, head_cols)
    attn_rows = collect_rows(matmul(context_low, w_out).reshape(group_shape))
    resid_three = resid_two + attn_rows
    normed_ffn, unit_ffn, inv_ffn = normalize(resid_three, gain_ffn)
    gathered_ffn = spread_rows(normed_ffn.astype(jnp.bfloat16))
    ffn_flat = gathered_ffn.reshape(group_rows, model_width)
    ffn_pre = matmul(ffn_flat, w_in)
    ffn_hidden = jax.nn.silu(ffn_pre).astype(jnp.bfloat16)
    final_rows = resid_three + collect_rows(matmul(ffn_hidden, w_back).reshape(group_shape))
    outputs = final_rows.astype(jnp.bfloat16)
    cot_full = spread_rows(cotangent).reshape(group_rows, model_width)
    ffn_flat = spread_rows(normed_ffn.astype(jnp.bfloat16)).reshape(group_rows, model_width)
    ffn_pre = matmul(ffn_flat, w_in)
    ffn_hidden = jax.nn.silu(ffn_pre).astype(jnp.bfloat16)
    grad_hidden = contract_cols(cot_full, w_back)
    grad_ffn_pre = (grad_hidden * silu_slope(ffn_pre)).astype(jnp.bfloat16)
    grad_w_back = contract_rows(ffn_hidden, cot_full)
    grad_w_in = contract_rows(ffn_flat, grad_ffn_pre)
    grad_normed_ffn = collect_rows(contract_cols(grad_ffn_pre, w_in).reshape(group_shape))
    grad_resid, grad_gain_ffn = normalize_back(grad_normed_ffn, unit_ffn, inv_ffn, gain_ffn)
    grad_three = cotangent.astype(jnp.float32) + grad_resid
    grad_attn = spread_rows(grad_three.astype(jnp.bfloat16)).reshape(group_rows, model_width)
    gathered_attn = spread_rows(normed_attn.astype(jnp.bfloat16))
    qkv_heads = project_qkv(gathered_attn)
    attn_flat = gathered_attn.reshape(group_rows, model_width)
    grad_w_out = contract_rows(context_low, grad_attn)
    grad_context = contract_cols(grad_attn, w_out).astype(jnp.bfloat16)
    grad_context = grad_context.reshape(seqs_here, seq_len, heads_here, HEAD_DIM)
    grad_q, grad_k, grad_v = lax.map(
        backward_one, (qkv_heads[0], qkv_heads[1], qkv_heads[2], key_valid, log_sums, grad_context)
    )
    grad_qkv = jnp.stack(
        [grad_q, grad_k.astype(jnp.bfloat16), grad_v.astype(jnp.bfloat16)]
    ).reshape(3, group_rows, head_cols)
    grad_w_qkv = jnp.einsum("td,ktc->kdc", attn_flat, grad_qkv, preferred_element_type=jnp.float32)
    grad_attn_in = jnp.einsum("ktc,kdc->td", grad_qkv, w_qkv, preferred_element_type=jnp.float32)
    grad_normed_attn = collect_rows(grad_attn_in.reshape(group_shape))
    grad_resid, grad_gain_attn = normalize_back(grad_normed_attn, unit_attn, inv_attn, gain_attn)
    grad_two = grad_three + grad_resid
    grad_sep = spread_rows(grad_two[..., :sep_width].astype(jnp.bfloat16)).reshape(
        group_rows, sep_width
    )
    gathered_branch = spread_rows((valid_own[..., None] * normed_branch).astype(jnp.bfloat16))
    left_pre, right_pre, mid = branch_inner(gathered_branch)
    unit_mid = (mid - mid_mean[..., None]) * inv_mid[..., None]
    depth_in = valid_full[..., None] * unit_mid * gain_mid_f
    depth_low = depth_mix(depth_in)
    grad_w_point = contract_rows(depth_low.reshape(group_rows, inner_cols), grad_sep)
    grad_depth = contract_cols(grad_sep, w_point).reshape(seqs_here, seq_len, inner_cols)
    grad_depth_in = jnp.zeros(grad_depth.shape, jnp.float32)
    depth_rows = []
    for tap_index in range(sep_taps):
        offset = tap_index - sep_taps // 2
        grad_depth_in = grad_depth_in + shifted(grad_depth, -offset) * depth_taps[tap_index]
        depth_rows.append(jnp.sum(shifted(depth_in, offset) * grad_depth, axis=(0, 1)))
    grad_w_depth = jnp.stack(depth_rows)
    grad_unit = grad_depth_in * valid_full[..., None]
    grad_gain_mid = jnp.sum(grad_unit * unit_mid, axis=(0, 1))
    scaled = grad_unit * gain_mid_f
    sum_one, sum_two = channel_sums(scaled, scaled * unit_mid)
    grad_mid = inv_mid[..., None] * (
        scaled - (sum_one / FF)[..., None] - unit_mid * (sum_two / FF)[..., None]
    )
    grad_left = (
        (grad_mid * silu_slope(left_pre)).astype(jnp.bfloat16).reshape(group_rows, inner_cols)
    )
    grad_right_act = grad_mid.reshape(seqs_here, seq_len, right_cols, stride)[..., 0]
    grad_right = (
        (grad_right_act * silu_slope(right_pre))
        .astype(jnp.bfloat16)
        .reshape(group_rows, right_cols)
    )
    branch_flat = gathered_branch.reshape(group_rows, model_width)
    grad_w_left = contract_rows(branch_flat, grad_left)
    grad_branch_in = contract_cols(grad_left, w_left).reshape(group_shape)
    right_rows = []
    for tap_index in range(conv_taps):
        offset = tap_index - conv_taps // 2
        moved = shifted(gathered_branch, offset).reshape(group_rows, model_width)
        right_rows.append(contract_rows(moved, grad_right))
        grad_branch_in = grad_branch_in + shifted(
            contract_cols(grad_right, w_right[tap_index]).reshape(group_shape), -offset
        )
    grad_w_right = jnp.stack(right_rows)
    grad_normed_branch = collect_rows(grad_branch_in) * valid_own[..., None]
    grad_resid, grad_gain_branch = normalize_back(
        grad_normed_branch, unit_branch, inv_branch, gain_branch
    )
    grad_one = grad_two + grad_resid
    grad_glu = lax.all_to_all(
        grad_one.astype(jnp.bfloat16), "mp", split_axis=2, concat_axis=1, tiled=True
    )
    grad_glu_flat = grad_glu.reshape(group_rows, -1).astype(jnp.float32)
    flat_glu = spread_rows(normed_glu.astype(jnp.bfloat16)).reshape(group_rows, model_width)
    value_pre = matmul(flat_glu, w_value)
    gate_sig = jax.nn.sigmoid(matmul(flat_glu, w_gate))
    grad_value = (grad_glu_flat * gate_sig).astype(jnp.bfloat16)
    grad_gate = (grad_glu_flat * value_pre * gate_sig * (1.0 - gate_sig)).astype(jnp.bfloat16)
    grad_w_value = contract_rows(flat_glu, grad_value)
    grad_w_gate = contract_rows(flat_glu, grad_gate)
    grad_glu_in = contract_cols(grad_value, w_value) + contract_cols(grad_gate, w_gate)
    grad_normed_glu = collect_rows(grad_glu_in.reshape(group_shape))
    grad_resid, grad_gain_glu = normalize_back(grad_normed_glu, unit_glu, inv_glu, gain_glu)
    grad_inputs = (grad_one + grad_resid).astype(jnp.bfloat16)
    gains = (grad_gain_glu, grad_gain_branch, grad_gain_attn, grad_gain_ffn)
    shards = (
        grad_w_value,
        grad_w_gate,
        grad_w_left,
        grad_w_right,
        grad_gain_mid,
        grad_w_depth,
        grad_w_point,
        grad_w_qkv,
        grad_w_out,
        grad_w_in,
        grad_w_back,
    )
    return (outputs, grad_inputs, gains, shards)


def local(
    inputs,
    lengths,
    gain_glu,
    w_value,
    w_gate,
    gain_branch,
    w_left,
    w_right,
    gain_mid,
    w_depth,
    w_point,
    gain_attn,
    w_qkv,
    w_out,
    gain_ffn,
    w_in,
    w_back,
    cotangent,
):
    outputs, grad_inputs, gains, shards = split_pass(
        inputs,
        lengths,
        gain_glu,
        w_value,
        w_gate,
        gain_branch,
        w_left,
        w_right,
        gain_mid,
        w_depth,
        w_point,
        gain_attn,
        w_qkv,
        w_out,
        gain_ffn,
        w_in,
        w_back,
        cotangent,
    )
    gain_totals = lax.psum((gains[0], gains[1], gains[2], gains[3]), ("dp", "mp"))
    weight_totals = (
        lax.psum(shards[0].astype(jnp.bfloat16), "dp").astype(jnp.float32),
        lax.psum(shards[1].astype(jnp.bfloat16), "dp").astype(jnp.float32),
        lax.psum(shards[2].astype(jnp.bfloat16), "dp").astype(jnp.float32),
        lax.psum(shards[3].astype(jnp.bfloat16), "dp").astype(jnp.float32),
        lax.psum(shards[4].astype(jnp.bfloat16), "dp").astype(jnp.float32),
        lax.psum(shards[5].astype(jnp.bfloat16), "dp").astype(jnp.float32),
        lax.psum(shards[6].astype(jnp.bfloat16), "dp").astype(jnp.float32),
        lax.psum(shards[7].astype(jnp.bfloat16), "dp").astype(jnp.float32),
        lax.psum(shards[8].astype(jnp.bfloat16), "dp").astype(jnp.float32),
        lax.psum(shards[9].astype(jnp.bfloat16), "dp").astype(jnp.float32),
        lax.psum(shards[10].astype(jnp.bfloat16), "dp").astype(jnp.float32),
    )
    return (
        outputs,
        grad_inputs,
        gain_totals[0],
        weight_totals[0],
        weight_totals[1],
        gain_totals[1],
        weight_totals[2],
        weight_totals[3],
        weight_totals[4],
        weight_totals[5],
        weight_totals[6],
        gain_totals[2],
        weight_totals[7],
        weight_totals[8],
        gain_totals[3],
        weight_totals[9],
        weight_totals[10],
    )


HALF = 256
LANES = 128


def dot_nn(left_side, right_side):
    return lax.dot_general(
        left_side, right_side, (((1,), (0,)), ((), ())), preferred_element_type=jnp.float32
    )


def dot_nt(left_side, right_side):
    return lax.dot_general(
        left_side, right_side, (((1,), (1,)), ((), ())), preferred_element_type=jnp.float32
    )


def dot_tn(left_side, right_side):
    return lax.dot_general(
        left_side, right_side, (((0,), (0,)), ((), ())), preferred_element_type=jnp.float32
    )


def row_stats(values):
    centre = values - jnp.mean(values, axis=-1, keepdims=True)
    inv = lax.rsqrt(jnp.mean(centre * centre, axis=-1, keepdims=True) + epsilon)
    return centre * inv, inv


def norm_grad(grad_out, unit, inv, gain):
    scaled = grad_out * gain
    mean_one = jnp.mean(scaled, axis=-1, keepdims=True)
    mean_two = jnp.mean(scaled * unit, axis=-1, keepdims=True)
    return inv * (scaled - mean_one - unit * mean_two)


def sigmoid(values):
    return 0.5 * jnp.tanh(0.5 * values) + 0.5


def silu(values):
    return values * sigmoid(values)


def turned(values):
    return jnp.transpose(values.astype(jnp.float32)).astype(jnp.bfloat16)


class Loader:
    def __init__(self, sems, first=0):
        self.sems = sems
        self.count = first
        self.waits = []
        self.plain = []
        self.by_core = ([], [])

    def copy(self, source, target, at):
        return pltpu.make_async_copy(source, target, self.sems.at[at])

    def start(self, source, target):
        self.plain.append(self.copy(source, target, self.count))
        self.waits.append(self.plain[-1])
        self.count += 1

    def either(self, got, part, taker, target):
        for core in range(2):
            source = got if core == taker else part
            self.by_core[core].append(self.copy(source, target, self.count))
        self.waits.append(self.by_core[0][-1])
        self.count += 1

    def go(self, core):
        for copy in self.plain:
            copy.start()
        for number, copies in enumerate(self.by_core):
            if copies:

                @pl.when(core == number)
                def _(copies=copies):
                    for copy in copies:
                        copy.start()

    def wait(self):
        for copy in self.waits:
            copy.wait()


def load_pair(loader, own, got, part, taker, core, target, slots=(0, 1)):
    loader.start(own, target.at[slots[0]])
    loader.either(got, part, taker, target.at[slots[1]])


def load_left(loader, w_left, got, part, core, target):
    blocks = w_left.shape[1] // HALF
    rows = w_left.shape[0]
    for block in range(blocks):
        loader.start(w_left.at[:, pl.ds(block * HALF, HALF)], target.at[block])
        at = pl.ds(block * rows, rows)
        loader.either(got.at[at], part.at[at], 0, target.at[blocks + block])


def load_pack(loader, got, part, core, target):
    count, depth = target.shape[:2]
    for block in range(count):
        at = pl.ds(got.shape[0] - (count - block) * depth, depth)
        loader.either(got.at[at], part.at[at], 0, target.at[block])


def load_point(loader, w_point, got, part, core, target):
    at = pl.ds(0, w_point.shape[0])
    load_pair(loader, w_point, got.at[at], part.at[at], 1, core, target)


def load_right(loader, w_right, got, part, core, target):
    loader.start(w_right, target.at[0])
    rows = w_right.shape[1]
    for tap in range(w_right.shape[0]):
        at = (pl.ds(2 * rows + (tap // 2) * rows, rows), pl.ds((tap % 2) * LANES, LANES))
        loader.either(got.at[at], part.at[at], 1, target.at[1, tap])


def load_qkv(loader, w_qkv, got, part, core, target, which):
    rows = w_qkv.shape[1]
    for slot, index in enumerate(which):
        loader.start(w_qkv.at[index], target.at[0, slot])
        at = pl.ds(index * rows, rows)
        loader.either(got.at[at], part.at[at], 0, target.at[1, slot])


def load_out(loader, w_out, got, part, core, target):
    loader.start(w_out, target.at[0])
    rows = w_out.shape[0]
    for block in range(2):
        at = pl.ds(block * rows, rows)
        loader.either(
            got.at[at], part.at[at], 1, target.at[1, :, pl.ds(block * HALF, HALF)]
        )


def load_in(loader, w_in, got2, part2, got3, part3, core, target):
    blocks = w_in.shape[1] // HALF
    rows = w_in.shape[0]
    for block in range(blocks):
        loader.start(w_in.at[:, pl.ds(block * HALF, HALF)], target.at[block])
        got, part = (got2, part2) if block < 2 else (got3, part3)
        at = pl.ds(rows + (block % 2) * rows, rows)
        loader.either(got.at[at], part.at[at], 1, target.at[blocks + block])


def load_back(loader, w_back, got, part, core, target):
    loader.start(w_back, target.at[0])
    rows = w_back.shape[0]
    half = rows // 2
    near, far = pl.ds(0, HALF), pl.ds(HALF, HALF)
    for at, taker, spot in (
        (pl.ds(0, rows), 0, (pl.ds(0, rows), near)),
        (pl.ds(rows, half), 0, (pl.ds(0, half), far)),
        (pl.ds(0, half), 1, (pl.ds(half, half), far)),
    ):
        loader.either(got.at[at], part.at[at], taker, target.at[1].at[spot])


GROUP = 8


def bundle_kernel(
    info, w_left, w_right, w_point, w_depth, gain_mid, w_qkv, w_out, w_in, w_back,
    one_o, two_o, three_o, sems,
):
    core = info[0]

    def copies(pieces):
        at = {id(one_o): 0, id(two_o): 0, id(three_o): 0}
        started = []
        for target, source in pieces:
            base = at[id(target)]
            at[id(target)] = base + source.shape[0]
            spot = target.at[pl.ds(base, source.shape[0]), pl.ds(0, source.shape[1])]
            copy = pltpu.make_async_copy(source, spot, sems.at[len(started)])
            copy.start()
            started.append(copy)
        for copy in started:
            copy.wait()

    def blocks(values):
        return [values.at[:, pl.ds(at, HALF)] for at in range(0, values.shape[1], HALF)]

    near, far = blocks(w_back)
    half = w_back.shape[0] // 2

    @pl.when(core == 0)
    def _():
        base = w_left.shape[0] * (w_left.shape[1] // HALF)
        taps = jnp.concatenate(
            [
                w_depth[...].astype(jnp.float32),
                gain_mid[...].astype(jnp.float32),
                jnp.zeros((15 - w_depth.shape[0], w_depth.shape[1]), jnp.float32),
            ],
            axis=0,
        ).astype(jnp.bfloat16)
        for block in range(w_depth.shape[1] // HALF):
            at = slice(base + block * 16, base + (block + 1) * 16)
            one_o[at] = taps[:, block * HALF : (block + 1) * HALF]
        copies(
            [(one_o, piece) for piece in blocks(w_left)]
            + [(two_o, w_qkv.at[index]) for index in range(3)]
            + [(three_o, near), (three_o, far.at[pl.ds(0, half)])]
        )

    @pl.when(core == 1)
    def _():
        pieces = [(one_o, w_point)]
        pieces += [(two_o, piece) for piece in blocks(w_out) + blocks(w_in)[:2]]
        pieces += [(three_o, far.at[pl.ds(half, half)])]
        pieces += [(three_o, piece) for piece in blocks(w_in)[2:]]
        rows, base = w_right.shape[1], w_point.shape[0]
        started = []
        for tap in range(w_right.shape[0]):
            spot = one_o.at[
                pl.ds(base + (tap // 2) * rows, rows), pl.ds((tap % 2) * LANES, LANES)
            ]
            copy = pltpu.make_async_copy(w_right.at[tap], spot, sems.at[len(pieces) + tap])
            copy.start()
            started.append(copy)
        copies(pieces)
        for copy in started:
            copy.wait()


def row_spot(rows, own, lanes):
    row = lax.broadcasted_iota(jnp.int32, (rows, lanes), 0)
    spot = (row % GROUP) * (own // GROUP) + row // GROUP
    return jnp.where(row < own, spot, jnp.where(row < own + EDGE, row - own - EDGE, row - EDGE))


def row_mask(core, length, ext, lanes):
    own = ext - 2 * EDGE
    spot = row_spot(ext, own, lanes) + core * own
    return jnp.where((spot >= 0) & (spot < length), 1.0, 0.0)


def lane_tiles(width):
    return [slice(at, at + LANES) for at in range(0, width, LANES)]


def load_tiles(source, tiles):
    for index, lanes in enumerate(lane_tiles(source.shape[1])):
        tiles[index] = source[:, lanes].astype(jnp.float32)


def gather_rows(tiles, target):
    own = tiles.shape[1]
    for tile, lanes in enumerate(lane_tiles(target.shape[1])):
        for index in range(own // GROUP):
            target[index * GROUP : (index + 1) * GROUP, lanes] = tiles[
                tile, pl.ds(index, GROUP, stride=own // GROUP)
            ]


def scatter_rows(source, tiles, target):
    own = tiles.shape[1]
    for tile, lanes in enumerate(lane_tiles(target.shape[1])):
        for index in range(own // GROUP):
            tiles[tile, pl.ds(index, GROUP, stride=own // GROUP)] = source[
                index * GROUP : (index + 1) * GROUP, lanes
            ]
        target[:, lanes] = tiles[tile].astype(target.dtype)


def next_group(first, row):
    sub = lax.broadcasted_iota(jnp.int32, first.shape, 0)
    return jnp.where(sub == GROUP - 1, row, pltpu.roll(first, GROUP - 1, 0))


def previous_group(last, row):
    sub = lax.broadcasted_iota(jnp.int32, last.shape, 0)
    return jnp.where(sub == 0, row, pltpu.roll(last, 1, 0))


def shift_rows(values, offset):
    if offset == 0:
        return values
    ext = values.shape[0]
    own = ext - 2 * EDGE
    mid, before, after = values[:own], values[own : own + EDGE], values[own + EDGE :]
    sub = lax.broadcasted_iota(jnp.int32, before.shape, 0)
    if offset > 0:
        moved = jnp.concatenate([mid[GROUP:], next_group(mid[:GROUP], after[:1])], axis=0)
        before = jnp.where(sub == EDGE - 1, mid[:1], pltpu.roll(before, EDGE - 1, 0))
        after = pltpu.roll(after, EDGE - 1, 0)
    else:
        moved = jnp.concatenate(
            [previous_group(mid[own - GROUP :], before[EDGE - 1 :]), mid[: own - GROUP]], axis=0
        )
        after = jnp.where(sub == 0, mid[own - 1 :], pltpu.roll(after, 1, 0))
        before = pltpu.roll(before, 1, 0)
    return jnp.concatenate([moved, before, after], axis=0)


def fill_window(window, values, own, reach):
    before, after = values[own : own + EDGE], values[own + EDGE :]
    window[reach * GROUP : reach * GROUP + own] = values[:own]
    for step in range(1, reach + 1):
        last = values[own - step * GROUP : own - (step - 1) * GROUP]
        at = (reach - step) * GROUP
        window[at : at + GROUP] = previous_group(last, before[EDGE - step : EDGE - step + 1])
        first = values[(step - 1) * GROUP : step * GROUP]
        at = reach * GROUP + own + (step - 1) * GROUP
        window[at : at + GROUP] = next_group(first, after[step - 1 : step])


def glu_kernel(
    info, block, moved, cot_own, cot_moved, edge, gain_glu, gain_branch, w_value, w_gate, got, part_w,
    cot_o, resid_o, branch_o, gluin_o, value_o, sig_o, x_s, c_s, n_s, wv_s, wg_s, sems,
):
    core, member, length = info[0], info[1], info[2]
    loader = Loader(sems)
    load_pair(loader, w_value, got, part_w, 0, core, wv_s, (member, 1 - member))
    load_pair(loader, w_gate, got, part_w, 1, core, wg_s, (member, 1 - member))
    loader.go(core)
    ext = x_s.shape[0]
    rows = ext - 2 * EDGE
    edge_f = edge[...].astype(jnp.float32)
    x_s[rows : rows + EDGE] = jnp.where(core == 1, edge_f, 0.0)
    x_s[rows + EDGE :] = jnp.where(core == 1, 0.0, edge_f)

    @pl.when(core == member)
    def _():
        load_tiles(block, n_s)

    @pl.when(core != member)
    def _():
        load_tiles(moved, n_s)

    gather_rows(n_s, x_s)

    @pl.when(core == member)
    def _():
        load_tiles(cot_own, n_s)

    @pl.when(core != member)
    def _():
        load_tiles(cot_moved, n_s)

    gather_rows(n_s, c_s)
    cot_o[...] = c_s[...].astype(jnp.bfloat16)
    loader.wait()
    valid = row_mask(core, length, ext, LANES)[:, :1]
    part = ext // 2
    for start in (0, part):
        at = slice(start, start + part)
        x = x_s[at]
        glu_in = (row_stats(x)[0] * gain_glu[...]).astype(jnp.bfloat16)
        gluin_o[at] = glu_in
        for half in range(2):
            cols = slice(half * HALF, (half + 1) * HALF)
            value = dot_nn(glu_in, wv_s[half])
            sig = sigmoid(dot_nn(glu_in, wg_s[half]))
            value_o[at, cols] = value.astype(jnp.bfloat16)
            sig_o[at, cols] = sig.astype(jnp.bfloat16)
            resid_o[at, cols] = x[:, cols] + (value * sig).astype(jnp.bfloat16).astype(jnp.float32)
        normed = row_stats(resid_o[at])[0] * gain_branch[...]
        branch_o[at] = (valid[at] * normed).astype(jnp.bfloat16)


def spread_block(index, rights, stride):
    source = lax.broadcasted_iota(jnp.int32, (rights, HALF), 0)
    channel = lax.broadcasted_iota(jnp.int32, (rights, HALF), 1) + index * HALF
    return jnp.where(channel == source * stride, 1.0, 0.0).astype(jnp.bfloat16)


def conv_rows(branch, weights):
    taps = weights.shape[0]
    total = dot_nn(branch, weights[taps // 2])
    for tap in range(taps):
        if tap != taps // 2:
            total = total + shift_rows(dot_nn(branch, weights[tap]), tap - taps // 2)
    return total


def mid_step(branch, into, right_act, index, stride, left_o, mid_o, sums, at):
    left_pre = dot_nn(branch[...], into[index])
    left_o[at] = left_pre.astype(jnp.bfloat16)
    mid = silu(left_pre) + dot_nn(right_act, spread_block(index, right_act.shape[1], stride))
    mid_o[at] = mid
    near, far = mid[:, :LANES], mid[:, LANES:]
    sums[0] += near + far
    sums[1] += near * near + far * far


def branch_own_kernel(
    info, branch, w_left, w_right, left_o, right_o, mid_o, sums_o, wl_s, sems
):
    loader = Loader(sems)
    blocks = wl_s.shape[0]
    for block in range(blocks):
        loader.start(w_left.at[:, pl.ds(block * HALF, HALF)], wl_s.at[block])
    loader.go(info[0])
    right_pre = conv_rows(branch[...], w_right)
    right_o[...] = right_pre
    right_act = silu(right_pre).astype(jnp.bfloat16)
    stride = blocks * HALF // right_pre.shape[1]
    sums_o[...] = jnp.zeros_like(sums_o)
    loader.wait()

    def step(index, carry):
        mid_step(branch, wl_s, right_act, index, stride, left_o, mid_o, sums_o, index)
        return carry

    lax.fori_loop(0, blocks, step, 0, unroll=2)


def fill_taps(pack_own, pack_oth, taps_s):
    count, cols = pack_own.shape
    taps_s[:count, :cols] = pack_own[...].astype(jnp.float32)
    for block in range(pack_oth.shape[0]):
        at = cols + block * HALF
        taps_s[:, at : at + HALF] = pack_oth[block].astype(jnp.float32)


def branch_kernel(
    info, branch, resid_one, pack_own, left_own, right_own, mid_own, sums_own, w_point, got, part,
    resid_two_o, left_o, right_o, stats_o, depth_o,
    wl_s, wr_s, wp_s, po_s, taps_s, mid_s, din_s, sums_s, sep_s, sems,
):
    core, length = info[0], info[2]
    loader = Loader(sems)
    taps_conv, depth_in_rows = wr_s.shape[0], wr_s.shape[1]
    for tap in range(taps_conv):
        at = (
            pl.ds(w_point.shape[0] + (tap // 2) * depth_in_rows, depth_in_rows),
            pl.ds((tap % 2) * LANES, LANES),
        )
        loader.either(got.at[at], part.at[at], 1, wr_s.at[tap])
    blocks = wl_s.shape[0]
    for block in range(blocks):
        at = pl.ds(block * depth_in_rows, depth_in_rows)
        loader.either(got.at[at], part.at[at], 0, wl_s.at[block])
    load_point(loader, w_point, got, part, core, wp_s)
    load_pack(loader, got, part, core, po_s)
    loader.go(core)
    ext = branch.shape[0]
    rows = ext - 2 * EDGE
    chunks = 2 * blocks
    per_shard = blocks
    sep_taps = pack_own.shape[0] - 1
    inner = chunks * HALF
    rights = right_own.shape[1]
    stride = blocks * HALF // rights
    left_o[:blocks] = left_own[...]
    mid_s[:blocks] = mid_own[...]
    sums_s[...] = sums_own[...]
    right_o[:, :rights] = right_own[...]
    loader.wait()
    fill_taps(pack_own, po_s, taps_s)
    right_pre = conv_rows(branch[...], wr_s)
    right_o[:, rights:] = right_pre
    right_act = silu(right_pre).astype(jnp.bfloat16)

    def first(index, carry):
        mid_step(branch, wl_s, right_act, index, stride, left_o, mid_s, sums_s, index + blocks)
        return carry

    lax.fori_loop(0, blocks, first, 0, unroll=2)
    mean = jnp.sum(sums_s[0], axis=-1, keepdims=True) / inner
    inv = lax.rsqrt(
        jnp.sum(sums_s[1], axis=-1, keepdims=True) / inner - mean * mean + epsilon
    )
    lane = lax.broadcasted_iota(jnp.int32, (ext, LANES), 1)
    stats_o[...] = jnp.where(lane == 0, mean, inv)
    sums_s[0] = jnp.broadcast_to(mean, (ext, LANES))
    sums_s[1] = inv * row_mask(core, length, ext, LANES)
    sep_s[...] = jnp.zeros_like(sep_s)

    def second(index, carry):
        cols = pl.ds(pl.multiple_of(index * HALF, HALF), HALF)
        taps = taps_s[:, cols]
        for side in range(2):
            lanes = slice(side * LANES, (side + 1) * LANES)
            depth_in = (
                (mid_s[index, :, lanes] - sums_s[0]) * sums_s[1] * taps[sep_taps : sep_taps + 1, lanes]
            )
            fill_window(din_s.at[:, lanes], depth_in, rows, sep_taps // 2)
        step = 64
        for start in range(0, rows, step):
            for side in range(2):
                lanes = slice(side * LANES, (side + 1) * LANES)
                acc = din_s[start : start + step, lanes] * taps[:1, lanes]
                for tap in range(1, sep_taps):
                    at = start + tap * GROUP
                    acc = acc + din_s[at : at + step, lanes] * taps[tap : tap + 1, lanes]
                depth_o[index, start : start + step, lanes] = acc.astype(jnp.bfloat16)
        shard, chunk = index // per_shard, index % per_shard
        point = wp_s[shard, pl.ds(pl.multiple_of(chunk * HALF, HALF), HALF)]
        sep_s[...] += dot_nn(depth_o[index], point)
        return carry

    lax.fori_loop(0, chunks, second, 0, unroll=2)
    sep_width = sep_s.shape[1]
    resid_two_o[:, :sep_width] = resid_one[:rows, :sep_width] + sep_s[...]
    resid_two_o[:, sep_width:] = resid_one[:rows, sep_width:]


def kv_kernel(info, resid_two, gain, w_qkv, got, part, attn_o, kv_o, w_s, sems):
    loader = Loader(sems)
    load_qkv(loader, w_qkv, got, part, info[0], w_s, (1, 2))
    loader.go(info[0])
    attn_in = (row_stats(resid_two[...])[0] * gain[...]).astype(jnp.bfloat16)
    attn_o[...] = attn_in
    loader.wait()
    width = w_s.shape[3]
    for shard in range(2):
        for index in range(2):
            at = (2 * index + shard) * width
            kv_o[:, at : at + width] = dot_nn(attn_in, w_s[shard, index]).astype(jnp.bfloat16)


def query_kernel(info, attn_in, w_qkv, got, part, q_o, w_s, sems):
    loader = Loader(sems)
    load_qkv(loader, w_qkv, got, part, info[0], w_s, (0,))
    loader.go(info[0])
    loader.wait()
    width = w_s.shape[3]
    scale = 1.0 / math.sqrt(HEAD_DIM)
    for shard in range(2):
        query = dot_nn(attn_in[...], w_s[shard, 0]).astype(jnp.bfloat16).astype(jnp.float32)
        q_o[:, shard * width : (shard + 1) * width] = (query * scale).astype(jnp.bfloat16)


def key_bias(core, length, rows):
    spot = row_spot(rows, rows, LANES) + core * rows
    return jnp.where(spot < length, 0.0, negative_big)


def head_masks(rows, head):
    lane = lax.broadcasted_iota(jnp.int32, (rows, LANES), 1)
    return (lane // HEAD_DIM) == head, lane == HEAD_DIM * (1 - head)


def attend_kernel(info, q, kvo, kvf, ctx0_o, lse0_o, ctx1_o, lse1_o, bias_s):
    core, length = info[0], info[2]
    rows, width = q.shape
    pairs = width // LANES // 2
    bias_s[:rows] = key_bias(core, length, rows)
    bias_s[rows:] = key_bias(1 - core, length, rows)

    def pair_step(shard, ctx_o, lse_o, local, carry):
        pair = local + shard * pairs
        cols = pl.ds(pl.multiple_of(pair * LANES, LANES), LANES)
        vcols = pl.ds(pl.multiple_of(pair * LANES + width, LANES), LANES)
        here = pl.ds(pl.multiple_of(local * LANES, LANES), LANES)
        keys = jnp.concatenate([kvo[:, cols], kvf[:, cols]], axis=0).astype(jnp.float32)
        vals = jnp.concatenate([kvo[:, vcols], kvf[:, vcols]], axis=0)
        vals_t = turned(vals)
        query = q[:, cols].astype(jnp.float32)
        outs = []
        for head in range(2):
            in_k, extra_k = head_masks(2 * rows, head)
            in_q, extra_q = head_masks(rows, head)
            km = jnp.where(in_k, keys, jnp.where(extra_k, bias_s[...], 0.0)).astype(jnp.bfloat16)
            qm = jnp.where(in_q, query, jnp.where(extra_q, 1.0, 0.0)).astype(jnp.bfloat16)
            pieces = []
            for start in range(0, rows, HALF):
                scores = dot_nt(km, qm[start : start + HALF])
                top = jnp.max(scores, axis=0, keepdims=True)
                weights = jnp.exp(scores - top)
                total = jnp.sum(weights, axis=0, keepdims=True)
                out = dot_nn(
                    vals_t[head * HEAD_DIM : (head + 1) * HEAD_DIM], weights.astype(jnp.bfloat16)
                )
                pieces.append(out / total)
                lse_o[pl.ds(local * 2 + head, 1), start : start + HALF] = top + jnp.log(total)
            outs.append(jnp.concatenate(pieces, axis=1))
        ctx_o[:, here] = jnp.transpose(jnp.concatenate(outs, axis=0)).astype(jnp.bfloat16)
        return carry

    lax.fori_loop(0, pairs, functools.partial(pair_step, 0, ctx0_o, lse0_o), 0, unroll=2)
    lax.fori_loop(0, pairs, functools.partial(pair_step, 1, ctx1_o, lse1_o), 0, unroll=2)


def ffn_kernel(
    info, resid_two, ctx0, ctx1, cot, gain, w_out, w_in, w_back, got2, part2,
    got3, part3,
    out_o, grad_three_o, gctx_o, ggain_o, send_o, keep_o,
    wo_s, wi_s, wb_s, fin_s, fint_s, cot_s, acc_s, gacc_s, ctxt_s, n_s, sems,
):
    core = info[0]
    loader = Loader(sems)
    load_out(loader, w_out, got2, part2, core, wo_s)
    late = Loader(sems, loader.count)
    load_in(late, w_in, got2, part2, got3, part3, core, wi_s)
    load_back(late, w_back, got3, part3, core, wb_s)

    loader.go(core)
    late.go(core)
    cot_s[...] = cot[...]
    loader.wait()
    part = ctx0.shape[1]
    chunks = wi_s.shape[0]
    per_shard = chunks // 2
    resid = resid_two[...] + dot_nn(ctx0[...], wo_s[0]) + dot_nn(ctx1[...], wo_s[1])
    acc_s[...] = resid
    gacc_s[...] = jnp.zeros_like(gacc_s)
    unit, inv = row_stats(resid)
    ffn_in = unit * gain[...]
    fin_s[...] = ffn_in.astype(jnp.bfloat16)
    fint_s[...] = jnp.transpose(fin_s[...].astype(jnp.float32)).astype(jnp.bfloat16)
    keep_rows = pl.ds(pl.multiple_of(core * HALF, HALF), HALF)
    send_rows = pl.ds(pl.multiple_of((1 - core) * HALF, HALF), HALF)

    def chunk_step(index, carry):
        shard, chunk = index // per_shard, index % per_shard
        rows = pl.ds(pl.multiple_of(chunk * HALF, HALF), HALF)
        into, back = wi_s[index], wb_s[shard, rows]
        pre = dot_nn(fin_s[...], into)
        sig = sigmoid(pre)
        hidden = (pre * sig).astype(jnp.bfloat16)
        acc_s[...] += dot_nn(hidden, back)
        grad_hidden = dot_nt(cot_s[...], back)
        grad_pre = (grad_hidden * (sig * (1.0 + pre * (1.0 - sig)))).astype(jnp.bfloat16)
        send_o[shard, rows] = dot_nn(fint_s[send_rows], grad_pre).astype(jnp.bfloat16)
        keep_o[shard, rows] = dot_nn(fint_s[keep_rows], grad_pre).astype(jnp.bfloat16)
        hidden_t = turned(hidden)
        base = per_shard * HALF
        rows = pl.ds(pl.multiple_of(base + chunk * HALF, HALF), HALF)
        send_o[shard, rows] = dot_nn(hidden_t, cot_s[:, send_rows]).astype(jnp.bfloat16)
        keep_o[shard, rows] = dot_nn(hidden_t, cot_s[:, keep_rows]).astype(jnp.bfloat16)
        gacc_s[...] += dot_nt(grad_pre, into)
        return carry

    late.wait()
    lax.fori_loop(0, chunks, chunk_step, 0, unroll=4)
    scatter_rows(acc_s, n_s, out_o)
    unit, inv = row_stats(
        resid_two[...] + dot_nn(ctx0[...], wo_s[0]) + dot_nn(ctx1[...], wo_s[1])
    )
    grad_norm = gacc_s[...]
    ggain_o[...] = jnp.sum(grad_norm * unit, axis=0, keepdims=True)
    grad_three = cot_s[...].astype(jnp.float32) + norm_grad(grad_norm, unit, inv, gain[...])
    grad_three_o[...] = grad_three
    fin_s[...] = grad_three.astype(jnp.bfloat16)
    ctxt_s[:part] = turned(ctx0[...])
    ctxt_s[part:] = turned(ctx1[...])
    base = 2 * per_shard * HALF
    for shard in range(2):
        side = slice(shard * part, (shard + 1) * part)
        gctx_o[:, side] = dot_nt(fin_s[...], wo_s[shard]).astype(jnp.bfloat16)
        send_o[shard, base : base + part] = dot_nn(ctxt_s[side], fin_s[:, send_rows]).astype(
            jnp.bfloat16
        )
        keep_o[shard, base : base + part] = dot_nn(ctxt_s[side], fin_s[:, keep_rows]).astype(
            jnp.bfloat16
        )


def attend_back_kernel(side, info, q, kv, ctx0, ctx1, gctx, lse0, lse1, *rest):
    if side:
        gq_o, gkv_o, bias_s, gk_s, gv_s = rest
    else:
        gq_part, gq_o, gkv_o, bias_s, gk_s, gv_s = rest
    core, length = info[0], info[2]
    rows, width = q.shape
    pairs = width // LANES // 2
    scale = 1.0 / math.sqrt(HEAD_DIM)
    bias_s[...] = key_bias(core ^ side, length, rows)

    def pair_step(shard, ctx, lse, local, carry):
        pair = local + shard * pairs
        cols = pl.ds(pl.multiple_of(pair * LANES, LANES), LANES)
        vcols = pl.ds(pl.multiple_of(pair * LANES + width, LANES), LANES)
        here = pl.ds(pl.multiple_of(local * LANES, LANES), LANES)
        keys = kv[:, cols].astype(jnp.float32)
        vals = kv[:, vcols]
        keys_t = jnp.transpose(keys).astype(jnp.bfloat16)
        query = q[:, cols].astype(jnp.float32)
        grad_out = gctx[:, cols].astype(jnp.float32)
        product_t = jnp.transpose(grad_out * ctx[:, here].astype(jnp.float32))
        gk_s[...] = jnp.zeros_like(gk_s)
        gv_s[...] = jnp.zeros_like(gv_s)
        outs = []
        for head in range(2):
            in_q, extra_q = head_masks(rows, head)
            km = jnp.where(in_q, keys, jnp.where(extra_q, bias_s[...], 0.0)).astype(jnp.bfloat16)
            qm = jnp.where(in_q, query, jnp.where(extra_q, 1.0, 0.0)).astype(jnp.bfloat16)
            qz = jnp.where(in_q, query, 0.0).astype(jnp.bfloat16)
            gz = jnp.where(in_q, grad_out, 0.0).astype(jnp.bfloat16)
            span = slice(head * HEAD_DIM, (head + 1) * HEAD_DIM)
            pieces = []
            for start in range(0, rows, HALF):
                at = slice(start, start + HALF)
                level = lse[pl.ds(local * 2 + head, 1), at]
                delta = jnp.sum(product_t[span, at], axis=0, keepdims=True)
                soft = jnp.exp(dot_nt(km, qm[at]) - level)
                gv_s[...] += dot_nn(soft.astype(jnp.bfloat16), gz[at])
                grad_scores = (soft * (dot_nt(vals, gz[at]) - delta)).astype(jnp.bfloat16)
                gk_s[...] += dot_nn(grad_scores, qz[at])
                pieces.append(dot_nn(keys_t[span], grad_scores))
            outs.append(jnp.concatenate(pieces, axis=1))
        grad_q = jnp.transpose(jnp.concatenate(outs, axis=0))
        if not side:
            grad_q = (grad_q + gq_part[:, cols]) * scale
        gq_o[:, cols] = grad_q.astype(gq_o.dtype)
        gkv_o[:, cols] = gk_s[...].astype(gkv_o.dtype)
        gkv_o[:, vcols] = gv_s[...].astype(gkv_o.dtype)
        return carry

    for shard, ctx, lse in ((0, ctx0, lse0), (1, ctx1, lse1)):
        lax.fori_loop(0, pairs, functools.partial(pair_step, shard, ctx, lse), 0, unroll=2)


def qkv_back_kernel(
    info, gq, gown, gfar, attn_in, resid_two, grad_three, gain, w_qkv, got, part,
    grad_two_o, gsep_o, gedge_o, ggain_o, send_o, keep_o, w_s, attnt_s, n_s, sems,
):
    core = info[0]
    loader = Loader(sems)
    load_qkv(loader, w_qkv, got, part, core, w_s, (0, 1, 2))
    loader.go(core)
    attnt_s[...] = turned(attn_in[...])
    width = w_s.shape[3]
    keep_rows = pl.ds(pl.multiple_of(core * HALF, HALF), HALF)
    send_rows = pl.ds(pl.multiple_of((1 - core) * HALF, HALF), HALF)
    loader.wait()
    grad_in = jnp.zeros(resid_two.shape, jnp.float32)
    for index in range(3):
        if index == 0:
            whole = gq[...]
        else:
            cols = slice((index - 1) * 2 * width, index * 2 * width)
            whole = (gown[:, cols] + gfar[:, cols].astype(jnp.float32)).astype(jnp.bfloat16)
        for shard in range(2):
            grad = whole[:, shard * width : (shard + 1) * width]
            at = slice(index * HALF, (index + 1) * HALF)
            send_o[shard, at] = dot_nn(attnt_s[send_rows], grad).astype(jnp.bfloat16)
            keep_o[shard, at] = dot_nn(attnt_s[keep_rows], grad).astype(jnp.bfloat16)
            grad_in = grad_in + dot_nt(grad, w_s[shard, index])
    unit, inv = row_stats(resid_two[...])
    ggain_o[...] = jnp.sum(grad_in * unit, axis=0, keepdims=True)
    grad_two = grad_three[...] + norm_grad(grad_in, unit, inv, gain[...])
    grad_two_o[...] = grad_two
    gsep_o[...] = grad_two[:, : gsep_o.shape[1]].astype(jnp.bfloat16)
    rows = n_s.shape[1]
    for tile, lanes in enumerate(lane_tiles(gsep_o.shape[1])):
        n_s[tile] = grad_two[:, lanes]
        first = n_s[tile, pl.ds(0, EDGE, stride=GROUP)]
        last = n_s[tile, pl.ds(rows - EDGE * GROUP + GROUP - 1, EDGE, stride=GROUP)]
        gedge_o[:, lanes] = jnp.where(core == 0, last, first).astype(jnp.bfloat16)


def point_kernel(info, gsep, depth, send, keep, send_o, keep_o):
    core = info[0]
    grad_sep = gsep[...]
    per_shard = depth.shape[0] // 2
    per_core = per_shard // 2
    base = send.shape[1]
    send_o[:, :base] = send[...]
    keep_o[:, :base] = keep[...]
    for shard in range(2):
        for chunk in range(per_core):
            at = slice(base + chunk * HALF, base + (chunk + 1) * HALF)
            first = shard * per_shard
            send_o[shard, at] = dot_tn(
                depth[first + (1 - core) * per_core + chunk], grad_sep
            ).astype(jnp.bfloat16)
            keep_o[shard, at] = dot_tn(
                depth[first + core * per_core + chunk], grad_sep
            ).astype(jnp.bfloat16)


def as_f32(values):
    return values.astype(jnp.float32)


def slope_of(values):
    sig = sigmoid(values)
    return sig * (1.0 + values * (1.0 - sig))


def depth_back_kernel(
    info, gsep, gedge, left_pre, right_pre, stats, pack_own, w_point, got, part,
    unit_o, scaled_o, sums_s, small_s,
    wp_s, po_s, taps_s, gse_s, gd_s, din_s, near_s, unit_s, scaled_s, wide_s, sems,
):
    core, length = info[0], info[2]
    loader = Loader(sems)
    load_point(loader, w_point, got, part, core, wp_s)
    load_pack(loader, got, part, core, po_s)
    loader.go(core)
    ext = left_pre.shape[1]
    rows = ext - 2 * EDGE
    chunks = left_pre.shape[0]
    per_shard = chunks // 2
    inner = chunks * HALF
    sep_taps = pack_own.shape[0] - 1
    right_cols = right_pre.shape[1]
    stride = inner // right_cols
    reach = sep_taps // 2
    edge = gedge[...].astype(jnp.float32)
    gse_s[:rows] = gsep[...]
    gse_s[rows : rows + EDGE] = jnp.where(core == 1, edge, 0.0).astype(jnp.bfloat16)
    gse_s[rows + EDGE :] = jnp.where(core == 1, 0.0, edge).astype(jnp.bfloat16)
    wide_s[0] = row_mask(core, length, ext, LANES)
    wide_s[1] = jnp.broadcast_to(stats[:, 0:1], (ext, LANES))
    wide_s[2] = jnp.broadcast_to(stats[:, 1:2], (ext, LANES))
    scaled_s[...] = jnp.zeros_like(scaled_s)
    sums_s[...] = jnp.zeros_like(sums_s)
    small_s[...] = jnp.zeros_like(small_s)
    right_act = silu(right_pre[...]).astype(jnp.bfloat16)
    loader.wait()
    fill_taps(pack_own, po_s, taps_s)

    def first(index, carry):
        cols = pl.ds(pl.multiple_of(index * HALF, HALF), HALF)
        taps = taps_s[:, cols]
        shard, chunk = index // per_shard, index % per_shard
        point = wp_s[shard, pl.ds(pl.multiple_of(chunk * HALF, HALF), HALF)]
        grad_depth = dot_nt(gse_s[...], point)
        for side, lanes in enumerate(lane_tiles(HALF)):
            fill_window(gd_s.at[side], grad_depth[:, lanes], rows, reach)
            near_s[side, :EDGE] = grad_depth[rows : rows + EDGE, lanes]
            near_s[side, 3 * EDGE :] = grad_depth[rows + EDGE :, lanes]
            base = reach * GROUP
            near_s[side, EDGE : 2 * EDGE] = gd_s[side, pl.ds(base, EDGE, stride=GROUP)]
            base = reach * GROUP + rows - EDGE * GROUP + GROUP - 1
            near_s[side, 2 * EDGE : 3 * EDGE] = gd_s[side, pl.ds(base, EDGE, stride=GROUP)]
        mid = silu(left_pre[index].astype(jnp.float32)) + dot_nn(
            right_act, spread_block(index, right_cols, stride)
        )
        for side in range(2):
            lanes = slice(side * LANES, (side + 1) * LANES)
            unit = (mid[:, lanes] - wide_s[1]) * wide_s[2]
            unit_s[:, lanes] = unit
            fill_window(
                din_s.at[side],
                unit * wide_s[0] * taps[sep_taps : sep_taps + 1, lanes],
                rows,
                reach,
            )
            for base, target in ((EDGE - GROUP, rows + EDGE - GROUP), (3 * EDGE, rows + EDGE)):
                acc = near_s[side, base + reach : base + reach + GROUP] * taps[:1, lanes]
                for tap in range(1, sep_taps):
                    at = base + reach - tap
                    acc = acc + near_s[side, at : at + GROUP] * taps[tap : tap + 1, lanes]
                at = slice(target, target + GROUP)
                scaled_s[at, lanes] = acc * wide_s[0, at]
        step = 64
        tap_sums = []
        for side in range(2):
            lanes = slice(side * LANES, (side + 1) * LANES)
            sums = [jnp.zeros((GROUP, LANES), jnp.float32) for _ in range(sep_taps)]
            for start in range(0, rows, step):
                at = start + 2 * reach * GROUP
                acc = gd_s[side, at : at + step] * taps[:1, lanes]
                for tap in range(1, sep_taps):
                    at = start + (2 * reach - tap) * GROUP
                    acc = acc + gd_s[side, at : at + step] * taps[tap : tap + 1, lanes]
                scaled_s[start : start + step, lanes] = acc * wide_s[0, start : start + step]
                at = start + reach * GROUP
                grad = gd_s[side, at : at + step]
                for tap in range(sep_taps):
                    at = start + tap * GROUP
                    term = din_s[side, at : at + step] * grad
                    sums[tap] = sums[tap] + jnp.sum(
                        term.reshape(step // GROUP, GROUP, LANES), axis=0
                    )
            tap_sums.append(sums)
        tap_sums = [jnp.concatenate(pair, axis=1) for pair in zip(*tap_sums)]
        tap_rows = [jnp.sum(value, axis=0, keepdims=True) for value in tap_sums]
        gain = taps[sep_taps : sep_taps + 1]
        gain_row = jnp.sum(
            scaled_s[:rows] * unit_s[:rows],
            axis=0,
            keepdims=True,
        )
        filler = jnp.zeros((small_s.shape[0] - sep_taps - 1, HALF), jnp.float32)
        small_s[:, cols] = jnp.concatenate(tap_rows + [gain_row, filler], axis=0)
        scaled = scaled_s[...] * gain
        scaled_o[index] = scaled.astype(jnp.bfloat16)
        unit_o[index] = unit_s[...].astype(jnp.bfloat16)
        near, far = scaled[:, :LANES], scaled[:, LANES:]
        sums_s[0] += near + far
        sums_s[1] += near * unit_s[:, :LANES] + far * unit_s[:, LANES:]
        return carry

    lax.fori_loop(0, chunks, first, 0, unroll=2)


def branch_back_kernel(
    info, unit, scaled, sums, small, left_pre, right_pre, stats, branch, gain_ffn_g, gain_attn_g,
    gleft_o, gright_o, send_o, keep_o,
    wide_s, gra_s, bt_s,
):
    core = info[0]
    ext = left_pre.shape[1]
    rows = ext - 2 * EDGE
    chunks = left_pre.shape[0]
    per_shard = chunks // 2
    inner = chunks * HALF
    right_cols = right_pre.shape[1]
    stride = inner // right_cols
    for index in range(2):
        mean = jnp.sum(sums[index], axis=-1, keepdims=True) / inner
        wide_s[index] = jnp.broadcast_to(mean, (ext, LANES))
    wide_s[2] = jnp.broadcast_to(stats[:, 1:2], (ext, LANES))
    gra_s[...] = jnp.zeros_like(gra_s)
    bt_s[...] = turned(branch[...])
    keep_rows = pl.ds(pl.multiple_of(core * HALF, HALF), HALF)
    send_rows = pl.ds(pl.multiple_of((1 - core) * HALF, HALF), HALF)

    def second(index, carry):
        shard, chunk = index // per_shard, index % per_shard
        sides = []
        for side in range(2):
            lanes = slice(side * LANES, (side + 1) * LANES)
            sides.append(
                wide_s[2]
                * (as_f32(scaled[index, :, lanes]) - wide_s[0] - as_f32(unit[index, :, lanes]) * wide_s[1])
            )
        grad_mid = jnp.concatenate(sides, axis=1)
        grad_left = (
            grad_mid[:rows] * slope_of(left_pre[index, :rows].astype(jnp.float32))
        ).astype(jnp.bfloat16)
        gleft_o[index] = grad_left
        gra_s[...] += dot_nt(
            grad_mid.astype(jnp.bfloat16), spread_block(index, right_cols, stride)
        )
        at = pl.ds(pl.multiple_of(chunk * HALF, HALF), HALF)
        send_o[shard, at] = dot_nn(bt_s[send_rows, :rows], grad_left).astype(
            jnp.bfloat16
        )
        keep_o[shard, at] = dot_nn(bt_s[keep_rows, :rows], grad_left).astype(
            jnp.bfloat16
        )
        return carry

    lax.fori_loop(0, chunks, second, 0, unroll=2)
    grad_right = gra_s[...] * slope_of(right_pre[...])
    gright_o[...] = grad_right.astype(jnp.bfloat16)
    spot = lax.broadcasted_iota(jnp.int32, grad_right.shape, 0)
    own_right = jnp.where(spot < rows, grad_right, 0.0)
    part = right_cols // 2
    base = per_shard * HALF
    for target, picked, side in ((send_o, send_rows, 1 - core), (keep_o, keep_rows, core)):
        taps3 = []
        for tap in range(3):
            moved = shift_rows(own_right, 1 - tap).astype(jnp.bfloat16)
            taps3.append(dot_nn(bt_s[picked, :], moved).astype(jnp.bfloat16))
        for shard in range(2):
            cols = slice(shard * part, (shard + 1) * part)
            target[shard, base : base + HALF, :part] = taps3[0][:, cols]
            target[shard, base : base + HALF, part:] = taps3[1][:, cols]
            target[shard, base + HALF : base + 2 * HALF, :part] = taps3[2][:, cols]
            target[shard, base + HALF : base + 2 * HALF, part:] = jnp.zeros(
                (HALF, part), jnp.bfloat16
            )
            cols_here = inner // 4
            for piece in range(cols_here // LANES):
                lanes = pl.ds(
                    pl.multiple_of(
                        shard * (inner // 2) + side * cols_here + piece * LANES, LANES
                    ),
                    LANES,
                )
                row = base + HALF + piece * 16
                target[shard, row : row + 16, part:] = small[:, lanes].astype(jnp.bfloat16)
            row = base + HALF + 4 * 16
            for piece in range(4):
                lanes = slice(piece * LANES, (piece + 1) * LANES)
                both = jnp.concatenate(
                    [gain_ffn_g[:, lanes], gain_attn_g[:, lanes], jnp.zeros((14, LANES), jnp.float32)],
                    axis=0,
                )
                target[shard, row : row + 16, part:] = both.astype(jnp.bfloat16)
                row += 16


def join_back_kernel(
    info, gleft, gright, resid_one, grad_two, gain_branch, w_left, w_right, got, part_w,
    grad_one_o, ggain_o, wl_s, wr_s, sems,
):
    core, length = info[0], info[2]
    loader = Loader(sems)
    load_left(loader, w_left, got, part_w, core, wl_s)
    load_right(loader, w_right, got, part_w, core, wr_s)
    loader.go(core)
    ext = gright.shape[0]
    rows = ext - 2 * EDGE
    own = slice(0, rows)
    loader.wait()
    grad_in = jnp.zeros((rows, resid_one.shape[1]), jnp.float32)
    for index in range(wl_s.shape[0]):
        grad_in = grad_in + dot_nt(gleft[index], wl_s[index])
    part = wr_s.shape[3]
    for tap in range(wr_s.shape[1]):
        product = dot_nt(gright[:, :part], wr_s[0, tap]) + dot_nt(gright[:, part:], wr_s[1, tap])
        grad_in = grad_in + shift_rows(product, 1 - tap)[own]
    grad_in = grad_in * row_mask(core, length, ext, LANES)[own, :1]
    unit, inv = row_stats(resid_one[own])
    ggain_o[...] = jnp.sum(grad_in * unit, axis=0, keepdims=True)
    grad_one_o[...] = grad_two[...] + norm_grad(grad_in, unit, inv, gain_branch[...])


def glu_back_kernel(
    info, grad_one, gain_branch_row, gain_glu, block, moved, glu_in, value, sig, w_value, w_gate,
    got, part_w,
    gin_o, send_o, keep_o,
    wv_s, wg_s, x_s, n_s, git_s, sems,
):
    core, member = info[0], info[1]
    loader = Loader(sems)
    load_pair(loader, w_value, got, part_w, 0, core, wv_s, (member, 1 - member))
    load_pair(loader, w_gate, got, part_w, 1, core, wg_s, (member, 1 - member))
    loader.go(core)
    rows = grad_one.shape[0]
    own = slice(0, rows)

    @pl.when(core == member)
    def _():
        load_tiles(block, n_s)

    @pl.when(core != member)
    def _():
        load_tiles(moved, n_s)

    gather_rows(n_s, x_s)
    git_s[...] = turned(glu_in[own])
    loader.wait()
    grad_glu = grad_one[...].astype(jnp.bfloat16).astype(jnp.float32)
    keep_rows = pl.ds(pl.multiple_of(core * HALF, HALF), HALF)
    send_rows = pl.ds(pl.multiple_of((1 - core) * HALF, HALF), HALF)
    grad_norm = jnp.zeros(grad_one.shape, jnp.float32)
    for half in range(2):
        cols = slice(half * HALF, (half + 1) * HALF)
        sig_f = sig[own, cols].astype(jnp.float32)
        grad_here = grad_glu[:, cols] * sig_f
        grad_value = grad_here.astype(jnp.bfloat16)
        grad_gate = (grad_here * value[own, cols].astype(jnp.float32) * (1.0 - sig_f)).astype(
            jnp.bfloat16
        )
        slot = jnp.where(member == half, 0, 1)
        send_o[slot, :HALF] = dot_nn(git_s[send_rows], grad_value).astype(jnp.bfloat16)
        keep_o[slot, :HALF] = dot_nn(git_s[keep_rows], grad_value).astype(jnp.bfloat16)
        send_o[slot, HALF : 2 * HALF] = dot_nn(git_s[send_rows], grad_gate).astype(jnp.bfloat16)
        keep_o[slot, HALF : 2 * HALF] = dot_nn(git_s[keep_rows], grad_gate).astype(jnp.bfloat16)
        grad_norm = grad_norm + dot_nt(grad_value, wv_s[half]) + dot_nt(grad_gate, wg_s[half])
    unit, inv = row_stats(x_s[...])
    gain_glu_row = jnp.sum(grad_norm * unit, axis=0, keepdims=True)
    x_s[...] = grad_one[...] + norm_grad(grad_norm, unit, inv, gain_glu[...])
    scatter_rows(x_s, n_s, gin_o)
    tail = send_o.shape[1] - 2 * HALF
    both = jnp.concatenate(
        [gain_glu_row, gain_branch_row[...], jnp.zeros((14, 2 * HALF), jnp.float32)], axis=0
    )
    both = both.astype(jnp.bfloat16)
    for target in (send_o, keep_o):
        for shard in range(2):
            target[shard, 2 * HALF :] = jnp.zeros((tail, HALF), jnp.bfloat16)
            target[shard, 2 * HALF : 2 * HALF + 16] = both[:, :HALF]
            target[shard, 2 * HALF + 16 : 2 * HALF + 32] = both[:, HALF:]


def over_mp(values):
    return lax.ppermute(values, "mp", [(0, 1), (1, 0)])


def flat_pairs(dp_size, rule):
    pairs = []
    for dp_index in range(dp_size):
        for member in range(2):
            pair, core = dp_index // 2, dp_index % 2
            new_core, new_member = rule(core, member)
            pairs.append((dp_index * 2 + member, (pair * 2 + new_core) * 2 + new_member))
    return pairs


def unpack_kernel(layout, sizes, info, both, far, *rest):
    outs, packed, sems = rest[:-2], rest[-2], rest[-1]
    core, ybit, zpos = info[0], info[3], info[4]
    ys = both.shape[0]
    zs, step = (4, both.shape[3]) if len(both.shape) > 3 else (1, both.shape[1])
    loader = Loader(sems)
    for half in range(2):
        for yside in range(ys):
            for zside in range(zs):
                near, far_bit = zside // 2, zside % 2
                at = (yside ^ ybit, near ^ zpos % 2, far_bit ^ zpos // 2)
                if zs == 1:
                    spot = packed.at[half, pl.ds(yside * step, step)]
                    loader.either(both.at[at[0]], far.at[at[0]], half, spot)
                    continue
                first, base = 0, 0
                for size in sizes:
                    low = max(first, far_bit * step)
                    top = min(first + size // 2, (far_bit + 1) * step)
                    if low < top:
                        source = pl.ds(low - far_bit * step, top - low)
                        spot = base + yside * size + near * (size // 2) + low - first
                        loader.either(
                            both.at[at].at[source],
                            far.at[at].at[source],
                            half,
                            packed.at[half, pl.ds(spot, top - low)],
                        )
                    first += size // 2
                    base += 2 * size
    loader.go(core)
    loader.wait()
    layout(packed, outs)


def layout_ffn(packed, outs):
    w_in, w_back, w_out = outs
    blocks = w_in.shape[1] // HALF
    base = blocks * HALF
    for half in range(2):
        side = slice(half * HALF, (half + 1) * HALF)
        for block in range(blocks):
            at = block * HALF
            w_in[side, block * HALF : (block + 1) * HALF] = as_f32(packed[half, at : at + HALF])
        w_back[:, side] = as_f32(packed[half, base : base + w_back.shape[0]])
        last = base + w_back.shape[0]
        w_out[:, side] = as_f32(packed[half, last : last + w_out.shape[0]])


def layout_attn(packed, outs):
    w_qkv, w_point = outs
    for half in range(2):
        for index in range(3):
            at = index * HALF
            w_qkv[index, half * HALF : (half + 1) * HALF] = as_f32(packed[half, at : at + HALF])
        at = 3 * HALF
        w_point[half * 2 * HALF : (half + 1) * 2 * HALF] = as_f32(packed[half, at : at + 2 * HALF])


def layout_branch(packed, outs):
    w_left, w_right, taps, gain, late_ffn, late_attn = outs
    count = taps.shape[0]
    blocks = w_left.shape[1] // HALF
    base = blocks * HALF
    for half in range(2):
        side = slice(half * HALF, (half + 1) * HALF)
        for block in range(blocks):
            w_left[side, block * HALF : (block + 1) * HALF] = as_f32(
                packed[half, block * HALF : (block + 1) * HALF]
            )
        w_right[0, side] = as_f32(packed[half, base : base + HALF, :LANES])
        w_right[1, side] = as_f32(packed[half, base : base + HALF, LANES:])
        w_right[2, side] = as_f32(packed[half, base + HALF : base + 2 * HALF, :LANES])
        for piece in range(4):
            row = base + HALF + piece * 16
            at = half * 4 * LANES + piece * LANES
            rows = as_f32(packed[half, row : row + 16, LANES:])
            taps[:, at : at + LANES] = rows[:count]
            gain[:, at : at + LANES] = rows[count : count + 1]
            row += 4 * 16
            rows = as_f32(packed[half, row : row + 16, LANES:])
            late_ffn[:, piece * LANES : (piece + 1) * LANES] = rows[:1]
            late_attn[:, piece * LANES : (piece + 1) * LANES] = rows[1:2]


def layout_glu(packed, outs):
    w_value, w_gate, late_glu, late_branch = outs
    for half in range(2):
        side = slice(half * HALF, (half + 1) * HALF)
        w_value[side] = as_f32(packed[half, :HALF])
        w_gate[side] = as_f32(packed[half, HALF : 2 * HALF])
        rows = as_f32(packed[0, 2 * HALF + 16 * half : 2 * HALF + 16 * (half + 1)])
        late_glu[:, side] = rows[:1]
        late_branch[:, side] = rows[1:2]


MEGA = 1024 * 1024
SPARE = 8
ALL_VMEM = 62 * MEGA


def call(body, name, ins, outs, scratch, flops, copies=0, room=None, cost=10**11):
    spaces = {"s": pltpu.SMEM, "v": pltpu.VMEM, "h": pltpu.HBM}
    shapes = [jax.ShapeDtypeStruct(shape, dtype) for shape, dtype in outs]
    held = [(a.shape, a.dtype) for a, place in ins if place == "v"] + outs + scratch
    held = sum(math.prod(shape) * jnp.dtype(dtype).itemsize for shape, dtype in held)
    scratch = [pltpu.VMEM(shape, dtype) for shape, dtype in scratch]
    if copies:
        scratch.append(pltpu.SemaphoreType.DMA((copies,)))
    return pl.pallas_call(
        body,
        out_shape=shapes,
        in_specs=[pl.BlockSpec(memory_space=spaces[place]) for _, place in ins],
        out_specs=[pl.BlockSpec(memory_space=pltpu.VMEM) for _ in shapes],
        scratch_shapes=scratch,
        name=name,
        compiler_params=pltpu.CompilerParams(vmem_limit_bytes=room or held + SPARE * MEGA),
        cost_estimate=pl.CostEstimate(flops=cost, bytes_accessed=10**6, transcendentals=0),
    )(*[array for array, _ in ins])


def dp_xor(values, bits):
    size = lax.axis_size("dp")
    return lax.ppermute(values, "dp", [(index, index ^ bits) for index in range(size)])


def over_x_and_y(values):
    pairs = []
    for dp_index in range(lax.axis_size("dp")):
        for member in range(2):
            pairs.append((dp_index * 2 + member, (dp_index ^ 2) * 2 + 1 - member))
    return lax.ppermute(values, ("dp", "mp"), pairs)


def later(values, *first):
    return lax.optimization_barrier((values, first))[0]


class Sums:
    def __init__(self, send, keep, ybit):
        self.keep, self.ybit = keep, ybit
        self.recv = dp_xor(send, 1)

    def over_xy(self, *first):
        recv, keep = later((self.recv, self.keep), *first)
        half = keep.shape[1] // 2

        def piece(shard, bit):
            at = bit * half
            cut = lambda values: as_f32(lax.dynamic_slice_in_dim(values[shard], at, half, axis=0))
            return (cut(keep) + cut(recv)).astype(jnp.bfloat16)

        self.kept = piece(0, self.ybit)
        gone = [piece(1, self.ybit), piece(0, 1 - self.ybit), piece(1, 1 - self.ybit)]
        self.got = [over_mp(gone[0]), dp_xor(gone[1], 2), over_x_and_y(gone[2])]
        return gone

    def over_x(self, *first):
        recv, keep = later((self.recv, self.keep), *first)
        other = (as_f32(keep[1]) + as_f32(recv[1])).astype(jnp.bfloat16)
        self.kept = as_f32(keep[0]) + as_f32(recv[0])
        self.got = over_mp(other)
        return [other]

    def over_y(self, *first):
        got, kept = later((self.got, self.kept), *first)
        mine = (kept + as_f32(got)).astype(jnp.bfloat16)
        half = mine.shape[0] // 2
        gone = lax.dynamic_slice_in_dim(mine, (1 - self.ybit) * half, half, axis=0)
        self.kept = lax.dynamic_slice_in_dim(mine, self.ybit * half, half, axis=0)
        self.got = dp_xor(gone, 2)
        return [gone]

    def last_quarter(self, *first):
        got, kept = later((self.got, self.kept), *first)
        return (as_f32(kept) + as_f32(got)).astype(jnp.bfloat16)

    def quarter(self, *first):
        got, kept = later((self.got, self.kept), *first)
        total = as_f32(kept) + as_f32(got[1]) + (as_f32(got[0]) + as_f32(got[2]))
        return total.astype(jnp.bfloat16)


def halve(mine, bit, across):
    half = mine.shape[0] // 2
    kept = lax.dynamic_slice_in_dim(mine, bit * half, half, axis=0)
    gone = lax.dynamic_slice_in_dim(mine, (1 - bit) * half, half, axis=0)
    return gone, (kept, dp_xor(gone, across))


class Rest:
    def __init__(self, zpos):
        self.zpos, self.pairs, self.sizes = zpos, [], []

    def over_z1(self, quarter):
        gone, pair = halve(quarter, self.zpos % 2, 4)
        self.pairs.append(pair)
        self.sizes.append(quarter.shape[0])
        return [gone]

    def over_z2(self, *first):
        pairs = later(self.pairs, *first)
        mine = [(as_f32(kept) + as_f32(got)).astype(jnp.bfloat16) for kept, got in pairs]
        gone, (self.kept, self.got) = halve(jnp.concatenate(mine, axis=0), self.zpos // 2, 8)
        return [gone]

    def back_z2(self, *first):
        got, kept = later((self.got, self.kept), *first)
        self.mine = (as_f32(kept) + as_f32(got)).astype(jnp.bfloat16)
        self.got = dp_xor(self.mine, 8)
        return [self.mine]

    def back_z1(self, *first):
        return self.double(4, *first)

    def double(self, across, *first):
        got, mine = later((self.got, self.mine), *first)
        self.mine = jnp.stack([mine, got])
        self.got = dp_xor(self.mine, across)
        return [self.mine]

    def back_y(self, *first):
        return self.double(2, *first)

    def back_core(self, *first):
        self.got, mine = later((self.got, self.mine), *first)
        self.both = jnp.stack([mine, self.got])
        self.far = dp_xor(self.both, 1)
        return [self.both]


class Short(Rest):
    def along_z1(self, quarter):
        self.sizes.append(quarter.shape[0])
        self.mine, self.got = quarter, dp_xor(quarter, 4)
        return [quarter]

    def along_z2(self, *first):
        got, mine = later((self.got, self.mine), *first)
        self.mine = (as_f32(mine) + as_f32(got)).astype(jnp.bfloat16)
        self.got = dp_xor(self.mine, 8)
        return [self.mine]

    def back_y(self, *first):
        got, mine = later((self.got, self.mine), *first)
        self.mine = (as_f32(mine) + as_f32(got)).astype(jnp.bfloat16)
        self.got = dp_xor(self.mine, 2)
        return [self.mine]


def unpack(layout, info, sums, outs):
    ys, cols = 2, sums.both.shape[-1]
    zs, part = (4, sums.both.shape[3]) if sums.both.ndim > 3 else (1, sums.both.shape[1])
    return call(
        functools.partial(unpack_kernel, layout, sums.sizes),
        "unpack_" + layout.__name__,
        [(info, "s"), (sums.both, "h"), (sums.far, "h")],
        [(shape, jnp.float32) for shape in outs],
        [((2, ys * zs * part, cols), jnp.bfloat16)],
        1e6,
        4 * ys * (zs + len(sums.sizes)),
    )


def paired(
    inputs, lengths, gain_glu, w_value, w_gate, gain_branch, w_left, w_right, gain_mid, w_depth,
    w_point, gain_attn, w_qkv, w_out, gain_ffn, w_in, w_back, cotangent,
):
    low, full = jnp.bfloat16, jnp.float32
    member = lax.axis_index("mp")
    place = lax.axis_index("dp")
    core, ybit, zpos = place % 2, (place // 2) % 2, place // 4
    rows, width = inputs.shape[1:]
    ext = rows + 2 * EDGE
    inner = 2 * w_left.shape[1]
    chunks = inner // HALF
    right_cols = 2 * w_right.shape[2]
    sep_width = w_point.shape[1]
    heads = 2 * w_qkv.shape[2] // HEAD_DIM
    row = lambda gain: gain.reshape(1, -1)

    block = inputs[0]
    edge = jnp.where(member == 0, block[rows - EDGE :], block[:EDGE])
    size_code = jnp.stack([lengths[0] // 32, lengths[0] % 32]).astype(low)
    code_rows = jnp.broadcast_to(jnp.repeat(size_code, EDGE // 2)[:, None], (EDGE, width))
    edge = jnp.concatenate([edge, code_rows], axis=0)
    edge = lax.ppermute(
        edge, ("dp", "mp"), flat_pairs(lax.axis_size("dp"), lambda c, m: (1 - m, c))
    )
    code = as_f32(edge[EDGE:, 0])
    length = (code[0] * 32 + code[EDGE // 2]).astype(jnp.int32)
    edge = edge[:EDGE]
    swap = [p for p in flat_pairs(lax.axis_size("dp"), lambda c, m: (m, c)) if p[0] != p[1]]
    moved = lax.ppermute(block, ("dp", "mp"), swap)
    info = jnp.stack([core, member, length, ybit, zpos]).astype(jnp.int32)

    v = lambda *arrays: [(array, "v") for array in arrays]
    h = lambda *arrays: [(array, "h") for array in arrays]
    pack = jnp.concatenate([w_depth, gain_mid[None]], axis=0)
    got0 = over_mp(jnp.where(core == 0, w_value, w_gate))
    blocks = w_left.shape[1] // HALF
    bundle1, bundle2, bundle3 = call(
        bundle_kernel, "bundle",
        [(jnp.stack([core, member]).astype(jnp.int32), "s")]
        + h(w_left, w_right, w_point) + v(w_depth, row(gain_mid)) + h(w_qkv, w_out, w_in, w_back),
        [((blocks * (width + 16), HALF), low)] + [((3 * width, HALF), low)] * 2,
        [], 1, 16, ALL_VMEM,
    )
    got1 = over_mp(bundle1)
    part0 = dp_xor(got0, 1)
    cot = cotangent[0]
    cot_moved = lax.ppermute(cot, ("dp", "mp"), swap)

    where = [(info, "s")]
    macs = 2.0 * rows * width
    cot, resid_one, branch_in, glu_in, value, sig = call(
        glu_kernel, "glu",
        where + v(block, moved, cot, cot_moved, edge, row(gain_glu), row(gain_branch))
        + h(w_value, w_gate, got0, part0),
        [((rows, width), low), ((ext, width), full)] + [((ext, width), low)] * 4,
        [((ext, width), full), ((rows, width), full), ((width // LANES, rows, LANES), full)]
        + [((2,) + w_value.shape, low)] * 2,
        macs * width * 2, 8,
    )
    left_own, right_own, mid_own, sums_own = call(
        branch_own_kernel, "branch_own",
        where + v(branch_in) + h(w_left) + v(w_right),
        [
            ((chunks // 2, ext, HALF), low), ((ext, right_cols // 2), full),
            ((chunks // 2, ext, HALF), full), ((2, ext, LANES), full),
        ],
        [((chunks // 2, width, HALF), low)],
        1, chunks // 2,
    )
    got1 = later(got1, sums_own)
    part1 = dp_xor(got1, 1)
    got2 = over_mp(later(bundle2, got1))
    got3 = over_mp(later(bundle3, got1))
    resid_two, left_pre, right_pre, stats, depth = call(
        branch_kernel, "branch",
        where
        + v(branch_in, resid_one, pack, left_own, right_own, mid_own, sums_own)
        + h(w_point, got1, part1),
        [
            ((rows, width), full), ((chunks, ext, HALF), low), ((ext, right_cols), full),
            ((ext, LANES), full), ((chunks, rows, HALF), low),
        ],
        [
            ((chunks // 2, width, HALF), low), (w_right.shape, low), ((2,) + w_point.shape, low),
            ((4, 16, HALF), low), ((16, inner), full), ((chunks, ext, HALF), full),
            ((rows + 64, HALF), full), ((2, ext, LANES), full), ((rows, sep_width), full),
        ],
        1, 20,
    )
    got2 = later(got2, resid_two)
    part2 = dp_xor(got2, 1)
    attn_in, kv_own = call(
        kv_kernel, "keys_values",
        where + v(resid_two, row(gain_attn)) + h(w_qkv, got2, part2),
        [((rows, width), low), ((rows, 2 * width), low)],
        [((2, 2) + w_qkv.shape[1:], low)],
        macs * width * 2, 8,
    )
    (queries,) = call(
        query_kernel, "queries",
        where + v(attn_in) + h(w_qkv, got2, part2),
        [((rows, width), low)],
        [((2, 1) + w_qkv.shape[1:], low)],
        macs * width, 4,
    )
    kv_far = dp_xor(kv_own, 1)
    context0, lse0, context1, lse1 = call(
        attend_kernel, "attend",
        where + v(queries, kv_own, kv_far),
        [((rows, width // 2), low), ((heads // 2, rows), full)] * 2,
        [((2 * rows, LANES), full)],
        macs * 8000,
    )
    part3 = dp_xor(later(got3, lse1), 1)
    r_ffn = 2 * w_in.shape[1] + w_out.shape[0]
    out_rows, grad_three, grad_ctx, ggain_ffn, send, keep = call(
        ffn_kernel, "ffn",
        where + v(resid_two, context0, context1, cot, row(gain_ffn))
        + h(w_out, w_in, w_back, got2, part2, got3, part3),
        [
            ((rows, width), low), ((rows, width), full), ((rows, width), low), ((1, width), full),
            ((2, r_ffn, HALF), low), ((2, r_ffn, HALF), low),
        ],
        [
            ((2,) + w_out.shape, low), ((chunks, width, HALF), low), ((2,) + w_back.shape, low),
            ((rows, width), low), ((width, rows), low), ((rows, width), low), ((rows, width), full),
            ((rows, width), full), ((width, rows), low), ((width // LANES, rows, LANES), full),
        ],
        macs * 16000, 24, 50 * MEGA,
    )
    ffn_sums = Sums(send, keep, ybit)
    swapped_out = lax.ppermute(out_rows, ("dp", "mp"), swap)

    seen = v(context0, context1, grad_ctx, lse0, lse1)
    grad_q, grad_far = call(
        functools.partial(attend_back_kernel, 1), "attend_back_far",
        where + v(queries, kv_far) + seen,
        [((rows, width), full), ((rows, 2 * width), low)],
        [((rows, LANES), full)] * 3, 1,
    )
    recv = dp_xor(grad_far, 1)
    sent = ffn_sums.over_xy(grad_q)
    out_rows, swapped_out = later((out_rows, swapped_out), *sent)
    outputs = jnp.where(member == core, out_rows, swapped_out)
    sent.append(outputs)
    grad_q, grad_own = call(
        functools.partial(attend_back_kernel, 0), "attend_back_own",
        [(later(info, *sent), "s")] + v(queries, kv_own) + seen + v(grad_q),
        [((rows, width), low), ((rows, 2 * width), full)],
        [((rows, LANES), full)] * 3, 1,
    )
    grad_two, grad_sep, sep_edge, ggain_attn, send, keep = call(
        qkv_back_kernel, "qkv_back",
        where
        + v(grad_q, grad_own, recv, attn_in, resid_two, grad_three, row(gain_attn))
        + h(w_qkv, got2, part2),
        [
            ((rows, width), full), ((rows, sep_width), low), ((EDGE, sep_width), low),
            ((1, width), full),
        ]
        + [((2, 3 * HALF, HALF), low)] * 2,
        [
            ((2,) + w_qkv.shape, low), ((width, rows), low),
            ((sep_width // LANES, rows, LANES), full),
        ],
        1, 12,
    )
    sep_edge = dp_xor(sep_edge, 1)
    send, keep = call(
        point_kernel, "point_back",
        where + v(grad_sep, depth, send, keep),
        [((2, 5 * HALF, HALF), low)] * 2, [], macs * 1000,
    )
    attn_sums = Sums(send, keep, ybit)
    unit, scaled, mid_sums, small = call(
        depth_back_kernel, "depth_back",
        where
        + v(grad_sep, sep_edge, left_pre, right_pre, stats, pack)
        + h(w_point, got1, part1),
        [
            ((chunks, ext, HALF), low), ((chunks, ext, HALF), low), ((2, ext, LANES), full),
            ((16, inner), full),
        ],
        [
            ((2,) + w_point.shape, low), ((4, 16, HALF), low), ((16, inner), full),
            ((ext, sep_width), low),
            ((2, rows + 64, LANES), full), ((2, rows + 64, LANES), full),
            ((2, 4 * EDGE, LANES), full), ((ext, HALF), full), ((ext, HALF), full),
            ((3, ext, LANES), full),
        ],
        macs * 8000, 8,
    )
    ffn_rest = Rest(zpos)
    sent = ffn_rest.over_z1(ffn_sums.quarter(mid_sums))
    sent += attn_sums.over_x(*sent)
    r_branch = inner // 2 + 2 * HALF
    grad_left, grad_right, send, keep = call(
        branch_back_kernel, "branch_back",
        [(later(info, *sent), "s")]
        + v(
            unit, scaled, mid_sums, small, left_pre, right_pre, stats, branch_in, ggain_ffn,
            ggain_attn,
        ),
        [
            ((chunks, rows, HALF), low), ((ext, right_cols), low),
            ((2, r_branch, HALF), low), ((2, r_branch, HALF), low),
        ],
        [((3, ext, LANES), full), ((ext, right_cols), full), ((width, ext), low)],
        macs * 4000,
    )
    branch_sums = Sums(send, keep, ybit)
    sent = ffn_rest.over_z2(grad_left)
    sent += attn_sums.over_y(*sent)
    grad_one, ggain_branch = call(
        join_back_kernel, "join_back",
        [(later(info, *sent), "s")]
        + v(grad_left, grad_right, resid_one, grad_two, row(gain_branch))
        + h(w_left, w_right, got1, part1),
        [((rows, width), full), ((1, width), full)],
        [((chunks, width, HALF), low), ((2,) + w_right.shape, low)],
        macs * 4000, 12,
    )
    sent = ffn_rest.back_z2(grad_one)
    sent += branch_sums.over_xy(*sent)
    attn_rest = Rest(zpos)
    grad_in, send, keep = call(
        glu_back_kernel, "glu_back",
        [(later(info, *sent), "s")]
        + v(grad_one, ggain_branch, row(gain_glu), block, moved, glu_in, value, sig)
        + h(w_value, w_gate, got0, part0),
        [((rows, width), low), ((2, 640, HALF), low), ((2, 640, HALF), low)],
        [
            ((2,) + w_value.shape, low), ((2,) + w_gate.shape, low), ((rows, width), full),
            ((width // LANES, rows, LANES), full), ((width, rows), low),
        ],
        macs * 3000, 4,
    )
    glu_sums = Sums(send, keep, ybit)
    branch_rest, glu_rest = Rest(zpos), Short(zpos)
    sent = attn_rest.over_z1(attn_sums.last_quarter(grad_in))
    sent = ffn_rest.back_z1(*sent)
    sent = branch_rest.over_z1(branch_sums.quarter(*sent))
    sent = glu_sums.over_x(*sent)
    swapped_in = lax.ppermute(later(grad_in, *sent), ("dp", "mp"), swap)
    sent = attn_rest.over_z2(*sent)
    sent = branch_rest.over_z2(*sent)
    sent = glu_sums.over_y(*sent)
    sent = ffn_rest.back_y(*sent)
    sent = attn_rest.back_z2(*sent)
    sent = branch_rest.back_z2(*sent)
    sent = glu_rest.along_z1(glu_sums.last_quarter(*sent))
    grad_in, swapped_in = later((grad_in, swapped_in), *sent)
    grad_inputs = jnp.where(member == core, grad_in, swapped_in)
    sent = branch_rest.back_z1(grad_inputs)
    sent = glu_rest.along_z2(*sent)
    sent = branch_rest.back_y(*sent)
    sent = attn_rest.back_z1(*sent)
    sent = ffn_rest.back_core(*sent)
    sent = glu_rest.back_y(*sent)
    sent = attn_rest.back_y(*sent)
    g_in, g_back, g_out = unpack(
        layout_ffn, later(info, *sent), ffn_rest, [w_in.shape, w_back.shape, w_out.shape]
    )
    sent = branch_rest.back_core(g_in)
    sent = glu_rest.back_core(*sent)
    g_value, g_gate, g_glu_gain, g_branch_gain = unpack(
        layout_glu, later(info, *sent), glu_rest,
        [w_value.shape, w_gate.shape, (1, width), (1, width)],
    )
    g_left, g_right, g_taps, g_mid, g_ffn_gain, g_attn_gain = unpack(
        layout_branch, later(info, g_value), branch_rest,
        [
            w_left.shape, w_right.shape, w_depth.shape, (1, inner // 2), (1, width), (1, width),
        ],
    )
    sent = attn_rest.back_core(g_left)
    g_qkv, g_point = unpack(
        layout_attn, later(info, *sent), attn_rest, [w_qkv.shape, w_point.shape]
    )
    flat = lambda gain: gain.reshape(-1)
    return (
        outputs[None],
        grad_inputs[None],
        flat(g_glu_gain),
        g_value,
        g_gate,
        flat(g_branch_gain),
        g_left,
        g_right,
        flat(g_mid),
        g_taps,
        g_point,
        flat(g_attn_gain),
        g_qkv,
        g_out,
        flat(g_ffn_gain),
        g_in,
        g_back,
    )


def solution(mesh):
    placed = (
        P("dp", "mp", None),
        P("dp"),
        P(),
        P(None, "mp"),
        P(None, "mp"),
        P(),
        P(None, "mp"),
        P(None, None, "mp"),
        P("mp"),
        P(None, "mp"),
        P("mp", None),
        P(),
        P(None, None, "mp"),
        P("mp", None),
        P(),
        P(None, "mp"),
        P("mp", None),
        P("dp", "mp", None),
    )
    fast = mesh.shape["mp"] == 2 and mesh.shape["dp"] == 16
    return jax.shard_map(
        paired if fast else local,
        mesh=mesh,
        in_specs=placed,
        out_specs=(
            P("dp", "mp", None),
            P("dp", "mp", None),
            P(),
            P(None, "mp"),
            P(None, "mp"),
            P(),
            P(None, "mp"),
            P(None, None, "mp"),
            P("mp"),
            P(None, "mp"),
            P("mp", None),
            P(),
            P(None, None, "mp"),
            P("mp", None),
            P(),
            P(None, "mp"),
            P("mp", None),
        ),
        check_vma=False,
    )
```

```python
import functools
import math

import jax
import jax.numpy as jnp
from jax import lax
from jax.experimental import pallas as pl
from jax.experimental.pallas import tpu as pltpu
from jax.sharding import PartitionSpec as P

FF = 2048
HEAD_DIM = 64
EDGE = 16


epsilon = 1e-06
negative_big = -1e30


def matmul(left_side, right_side):
    return jnp.dot(left_side, right_side, preferred_element_type=jnp.float32)


def contract_rows(left_side, right_side):
    return lax.dot_general(
        left_side, right_side, (((0,), (0,)), ((), ())), preferred_element_type=jnp.float32
    )


def contract_cols(left_side, right_side):
    return lax.dot_general(
        left_side, right_side, (((1,), (1,)), ((), ())), preferred_element_type=jnp.float32
    )


def spread_rows(pieces):
    return lax.all_gather(pieces, "mp", axis=1, tiled=True)


def collect_rows(partial_value):
    return lax.psum_scatter(
        partial_value.astype(jnp.bfloat16), "mp", scatter_dimension=1, tiled=True
    ).astype(jnp.float32)


def channel_sums(former, latter):
    return lax.psum((jnp.sum(former, axis=-1), jnp.sum(latter, axis=-1)), "mp")


def normalize(values, gain_vec):
    centre = values - jnp.mean(values, axis=-1, keepdims=True)
    scale_inv = lax.rsqrt(jnp.mean(centre * centre, axis=-1, keepdims=True) + epsilon)
    unit_rows = centre * scale_inv
    return (unit_rows * gain_vec, unit_rows, scale_inv)


def normalize_back(grad_out, unit_rows, scale_inv, gain_vec):
    scaled = grad_out * gain_vec
    mean_one = jnp.mean(scaled, axis=-1, keepdims=True)
    mean_two = jnp.mean(scaled * unit_rows, axis=-1, keepdims=True)
    grad_in = scale_inv * (scaled - mean_one - unit_rows * mean_two)
    return (grad_in, jnp.sum(grad_out * unit_rows, axis=(0, 1)))


def silu_slope(values):
    sigmoid_part = jax.nn.sigmoid(values)
    return sigmoid_part * (1.0 + values * (1.0 - sigmoid_part))


def shifted(values, offset):
    if offset == 0:
        return values
    margin = abs(offset)
    seq_len = values.shape[1]
    filler = jnp.zeros(values.shape[:1] + (margin,) + values.shape[2:], values.dtype)
    padded = jnp.concatenate([filler, values, filler], axis=1)
    return lax.slice_in_dim(padded, margin + offset, margin + offset + seq_len, axis=1)


def place_right(right_vals, stride):
    filler = jnp.zeros(right_vals.shape + (stride - 1,), right_vals.dtype)
    joined = jnp.concatenate([right_vals[..., None], filler], axis=-1)
    return joined.reshape(right_vals.shape[:-1] + (right_vals.shape[-1] * stride,))


def attend_forward(queries, key_vecs, value_vecs, key_valid, block_rows, score_scale):
    contexts = []
    log_parts = []
    for row_start in range(0, queries.shape[0], block_rows):
        query_rows = queries[row_start : row_start + block_rows]
        scores = (
            jnp.einsum("qhd,khd->hqk", query_rows, key_vecs, preferred_element_type=jnp.float32)
            * score_scale
        )
        scores = jnp.where(key_valid[None, None, :], scores, negative_big)
        row_max = jnp.max(scores, axis=-1, keepdims=True)
        weights_exp = jnp.exp(scores - row_max)
        row_total = jnp.sum(weights_exp, axis=-1, keepdims=True)
        probability = (weights_exp / row_total).astype(jnp.bfloat16)
        contexts.append(
            jnp.einsum("hqk,khd->qhd", probability, value_vecs, preferred_element_type=jnp.float32)
        )
        log_parts.append((row_max + jnp.log(row_total))[..., 0])
    return (jnp.concatenate(contexts, axis=0), jnp.concatenate(log_parts, axis=1))


def attend_back(
    queries, key_vecs, value_vecs, key_valid, log_sums, grad_context, block_rows, score_scale
):
    grad_queries = []
    grad_keys = jnp.zeros(key_vecs.shape, jnp.float32)
    grad_values = jnp.zeros(value_vecs.shape, jnp.float32)
    for row_start in range(0, queries.shape[0], block_rows):
        query_rows = queries[row_start : row_start + block_rows]
        grad_rows = grad_context[row_start : row_start + block_rows]
        log_rows = log_sums[:, row_start : row_start + block_rows]
        scores = (
            jnp.einsum("qhd,khd->hqk", query_rows, key_vecs, preferred_element_type=jnp.float32)
            * score_scale
        )
        scores = jnp.where(key_valid[None, None, :], scores, negative_big)
        probability = jnp.exp(scores - log_rows[..., None])
        grad_prob = jnp.einsum(
            "qhd,khd->hqk", grad_rows, value_vecs, preferred_element_type=jnp.float32
        )
        row_dot = jnp.sum(probability * grad_prob, axis=-1, keepdims=True)
        grad_scores = (probability * (grad_prob - row_dot)).astype(jnp.bfloat16)
        grad_queries.append(
            jnp.einsum("hqk,khd->qhd", grad_scores, key_vecs, preferred_element_type=jnp.float32)
            * score_scale
        )
        grad_keys = (
            grad_keys
            + jnp.einsum(
                "hqk,qhd->khd", grad_scores, query_rows, preferred_element_type=jnp.float32
            )
            * score_scale
        )
        grad_values = grad_values + jnp.einsum(
            "hqk,qhd->khd",
            probability.astype(jnp.bfloat16),
            grad_rows,
            preferred_element_type=jnp.float32,
        )
    grad_query_all = jnp.concatenate(grad_queries, axis=0)
    return (grad_query_all.astype(jnp.bfloat16), grad_keys, grad_values)


def split_pass(
    inputs,
    lengths,
    gain_glu,
    w_value,
    w_gate,
    gain_branch,
    w_left,
    w_right,
    gain_mid,
    w_depth,
    w_point,
    gain_attn,
    w_qkv,
    w_out,
    gain_ffn,
    w_in,
    w_back,
    cotangent,
):
    seqs_here, local_len, model_width = inputs.shape
    group_size = lax.axis_size("mp")
    member = lax.axis_index("mp")
    seq_len = local_len * group_size
    group_rows = seqs_here * seq_len
    positions = lax.broadcasted_iota(jnp.int32, (seqs_here, seq_len), 1)
    key_valid = positions < lengths[:, None]
    valid_full = key_valid.astype(jnp.float32)
    valid_own = lax.dynamic_slice_in_dim(valid_full, member * local_len, local_len, axis=1)
    inner_cols = w_left.shape[1]
    right_cols = w_right.shape[2]
    stride = inner_cols // right_cols
    conv_taps = w_right.shape[0]
    sep_taps = w_depth.shape[0]
    sep_width = w_point.shape[1]
    head_cols = w_qkv.shape[2]
    heads_here = head_cols // HEAD_DIM
    score_scale = 1.0 / math.sqrt(HEAD_DIM)
    block_rows = min(512, seq_len)
    group_shape = (seqs_here, seq_len, model_width)
    depth_taps = w_depth.astype(jnp.float32)
    gain_mid_f = gain_mid.astype(jnp.float32)

    def branch_inner(gathered):
        flat_rows = gathered.reshape(group_rows, model_width)
        left_pre = matmul(flat_rows, w_left).reshape(seqs_here, seq_len, inner_cols)
        right_pre = jnp.zeros((group_rows, right_cols), jnp.float32)
        for tap_index in range(conv_taps):
            moved = shifted(gathered, tap_index - conv_taps // 2).reshape(group_rows, model_width)
            right_pre = right_pre + matmul(moved, w_right[tap_index])
        right_pre = right_pre.reshape(seqs_here, seq_len, right_cols)
        mid = jax.nn.silu(left_pre) + place_right(jax.nn.silu(right_pre), stride)
        return (left_pre, right_pre, mid)

    def depth_mix(depth_in):
        depth = jnp.zeros(depth_in.shape, jnp.float32)
        for tap_index in range(sep_taps):
            depth = depth + shifted(depth_in, tap_index - sep_taps // 2) * depth_taps[tap_index]
        return depth.astype(jnp.bfloat16)

    def project_qkv(gathered):
        flat_rows = gathered.reshape(group_rows, model_width)
        joined = jnp.einsum("td,kdc->ktc", flat_rows, w_qkv, preferred_element_type=jnp.float32)
        return joined.astype(jnp.bfloat16).reshape(3, seqs_here, seq_len, heads_here, HEAD_DIM)

    def forward_one(pieces):
        return attend_forward(pieces[0], pieces[1], pieces[2], pieces[3], block_rows, score_scale)

    def backward_one(pieces):
        return attend_back(
            pieces[0],
            pieces[1],
            pieces[2],
            pieces[3],
            pieces[4],
            pieces[5],
            block_rows,
            score_scale,
        )

    resid_in = inputs.astype(jnp.float32)
    normed_glu, unit_glu, inv_glu = normalize(resid_in, gain_glu)
    gathered_glu = spread_rows(normed_glu.astype(jnp.bfloat16))
    flat_glu = gathered_glu.reshape(group_rows, model_width)
    value_pre = matmul(flat_glu, w_value)
    gate_sig = jax.nn.sigmoid(matmul(flat_glu, w_gate))
    glu_local = (value_pre * gate_sig).astype(jnp.bfloat16).reshape(seqs_here, seq_len, -1)
    glu_rows = lax.all_to_all(glu_local, "mp", split_axis=1, concat_axis=2, tiled=True)
    resid_one = resid_in + glu_rows.astype(jnp.float32)
    normed_branch, unit_branch, inv_branch = normalize(resid_one, gain_branch)
    gathered_branch = spread_rows((valid_own[..., None] * normed_branch).astype(jnp.bfloat16))
    left_pre, right_pre, mid = branch_inner(gathered_branch)
    mid_sum, mid_square = channel_sums(mid, mid * mid)
    mid_mean = mid_sum / FF
    inv_mid = lax.rsqrt(mid_square / FF - mid_mean * mid_mean + epsilon)
    unit_mid = (mid - mid_mean[..., None]) * inv_mid[..., None]
    depth_in = valid_full[..., None] * unit_mid * gain_mid_f
    depth_low = depth_mix(depth_in)
    sep_part = matmul(depth_low.reshape(group_rows, inner_cols), w_point).reshape(
        seqs_here, seq_len, sep_width
    )
    sep_rows = collect_rows(sep_part)
    resid_two = resid_one + jnp.pad(sep_rows, ((0, 0), (0, 0), (0, model_width - sep_width)))
    normed_attn, unit_attn, inv_attn = normalize(resid_two, gain_attn)
    gathered_attn = spread_rows(normed_attn.astype(jnp.bfloat16))
    qkv_heads = project_qkv(gathered_attn)
    context, log_sums = lax.map(forward_one, (qkv_heads[0], qkv_heads[1], qkv_heads[2], key_valid))
    context_low = context.astype(jnp.bfloat16).reshape(group_rows, head_cols)
    attn_rows = collect_rows(matmul(context_low, w_out).reshape(group_shape))
    resid_three = resid_two + attn_rows
    normed_ffn, unit_ffn, inv_ffn = normalize(resid_three, gain_ffn)
    gathered_ffn = spread_rows(normed_ffn.astype(jnp.bfloat16))
    ffn_flat = gathered_ffn.reshape(group_rows, model_width)
    ffn_pre = matmul(ffn_flat, w_in)
    ffn_hidden = jax.nn.silu(ffn_pre).astype(jnp.bfloat16)
    final_rows = resid_three + collect_rows(matmul(ffn_hidden, w_back).reshape(group_shape))
    outputs = final_rows.astype(jnp.bfloat16)
    cot_full = spread_rows(cotangent).reshape(group_rows, model_width)
    ffn_flat = spread_rows(normed_ffn.astype(jnp.bfloat16)).reshape(group_rows, model_width)
    ffn_pre = matmul(ffn_flat, w_in)
    ffn_hidden = jax.nn.silu(ffn_pre).astype(jnp.bfloat16)
    grad_hidden = contract_cols(cot_full, w_back)
    grad_ffn_pre = (grad_hidden * silu_slope(ffn_pre)).astype(jnp.bfloat16)
    grad_w_back = contract_rows(ffn_hidden, cot_full)
    grad_w_in = contract_rows(ffn_flat, grad_ffn_pre)
    grad_normed_ffn = collect_rows(contract_cols(grad_ffn_pre, w_in).reshape(group_shape))
    grad_resid, grad_gain_ffn = normalize_back(grad_normed_ffn, unit_ffn, inv_ffn, gain_ffn)
    grad_three = cotangent.astype(jnp.float32) + grad_resid
    grad_attn = spread_rows(grad_three.astype(jnp.bfloat16)).reshape(group_rows, model_width)
    gathered_attn = spread_rows(normed_attn.astype(jnp.bfloat16))
    qkv_heads = project_qkv(gathered_attn)
    attn_flat = gathered_attn.reshape(group_rows, model_width)
    grad_w_out = contract_rows(context_low, grad_attn)
    grad_context = contract_cols(grad_attn, w_out).astype(jnp.bfloat16)
    grad_context = grad_context.reshape(seqs_here, seq_len, heads_here, HEAD_DIM)
    grad_q, grad_k, grad_v = lax.map(
        backward_one, (qkv_heads[0], qkv_heads[1], qkv_heads[2], key_valid, log_sums, grad_context)
    )
    grad_qkv = jnp.stack(
        [grad_q, grad_k.astype(jnp.bfloat16), grad_v.astype(jnp.bfloat16)]
    ).reshape(3, group_rows, head_cols)
    grad_w_qkv = jnp.einsum("td,ktc->kdc", attn_flat, grad_qkv, preferred_element_type=jnp.float32)
    grad_attn_in = jnp.einsum("ktc,kdc->td", grad_qkv, w_qkv, preferred_element_type=jnp.float32)
    grad_normed_attn = collect_rows(grad_attn_in.reshape(group_shape))
    grad_resid, grad_gain_attn = normalize_back(grad_normed_attn, unit_attn, inv_attn, gain_attn)
    grad_two = grad_three + grad_resid
    grad_sep = spread_rows(grad_two[..., :sep_width].astype(jnp.bfloat16)).reshape(
        group_rows, sep_width
    )
    gathered_branch = spread_rows((valid_own[..., None] * normed_branch).astype(jnp.bfloat16))
    left_pre, right_pre, mid = branch_inner(gathered_branch)
    unit_mid = (mid - mid_mean[..., None]) * inv_mid[..., None]
    depth_in = valid_full[..., None] * unit_mid * gain_mid_f
    depth_low = depth_mix(depth_in)
    grad_w_point = contract_rows(depth_low.reshape(group_rows, inner_cols), grad_sep)
    grad_depth = contract_cols(grad_sep, w_point).reshape(seqs_here, seq_len, inner_cols)
    grad_depth_in = jnp.zeros(grad_depth.shape, jnp.float32)
    depth_rows = []
    for tap_index in range(sep_taps):
        offset = tap_index - sep_taps // 2
        grad_depth_in = grad_depth_in + shifted(grad_depth, -offset) * depth_taps[tap_index]
        depth_rows.append(jnp.sum(shifted(depth_in, offset) * grad_depth, axis=(0, 1)))
    grad_w_depth = jnp.stack(depth_rows)
    grad_unit = grad_depth_in * valid_full[..., None]
    grad_gain_mid = jnp.sum(grad_unit * unit_mid, axis=(0, 1))
    scaled = grad_unit * gain_mid_f
    sum_one, sum_two = channel_sums(scaled, scaled * unit_mid)
    grad_mid = inv_mid[..., None] * (
        scaled - (sum_one / FF)[..., None] - unit_mid * (sum_two / FF)[..., None]
    )
    grad_left = (
        (grad_mid * silu_slope(left_pre)).astype(jnp.bfloat16).reshape(group_rows, inner_cols)
    )
    grad_right_act = grad_mid.reshape(seqs_here, seq_len, right_cols, stride)[..., 0]
    grad_right = (
        (grad_right_act * silu_slope(right_pre))
        .astype(jnp.bfloat16)
        .reshape(group_rows, right_cols)
    )
    branch_flat = gathered_branch.reshape(group_rows, model_width)
    grad_w_left = contract_rows(branch_flat, grad_left)
    grad_branch_in = contract_cols(grad_left, w_left).reshape(group_shape)
    right_rows = []
    for tap_index in range(conv_taps):
        offset = tap_index - conv_taps // 2
        moved = shifted(gathered_branch, offset).reshape(group_rows, model_width)
        right_rows.append(contract_rows(moved, grad_right))
        grad_branch_in = grad_branch_in + shifted(
            contract_cols(grad_right, w_right[tap_index]).reshape(group_shape), -offset
        )
    grad_w_right = jnp.stack(right_rows)
    grad_normed_branch = collect_rows(grad_branch_in) * valid_own[..., None]
    grad_resid, grad_gain_branch = normalize_back(
        grad_normed_branch, unit_branch, inv_branch, gain_branch
    )
    grad_one = grad_two + grad_resid
    grad_glu = lax.all_to_all(
        grad_one.astype(jnp.bfloat16), "mp", split_axis=2, concat_axis=1, tiled=True
    )
    grad_glu_flat = grad_glu.reshape(group_rows, -1).astype(jnp.float32)
    flat_glu = spread_rows(normed_glu.astype(jnp.bfloat16)).reshape(group_rows, model_width)
    value_pre = matmul(flat_glu, w_value)
    gate_sig = jax.nn.sigmoid(matmul(flat_glu, w_gate))
    grad_value = (grad_glu_flat * gate_sig).astype(jnp.bfloat16)
    grad_gate = (grad_glu_flat * value_pre * gate_sig * (1.0 - gate_sig)).astype(jnp.bfloat16)
    grad_w_value = contract_rows(flat_glu, grad_value)
    grad_w_gate = contract_rows(flat_glu, grad_gate)
    grad_glu_in = contract_cols(grad_value, w_value) + contract_cols(grad_gate, w_gate)
    grad_normed_glu = collect_rows(grad_glu_in.reshape(group_shape))
    grad_resid, grad_gain_glu = normalize_back(grad_normed_glu, unit_glu, inv_glu, gain_glu)
    grad_inputs = (grad_one + grad_resid).astype(jnp.bfloat16)
    gains = (grad_gain_glu, grad_gain_branch, grad_gain_attn, grad_gain_ffn)
    shards = (
        grad_w_value,
        grad_w_gate,
        grad_w_left,
        grad_w_right,
        grad_gain_mid,
        grad_w_depth,
        grad_w_point,
        grad_w_qkv,
        grad_w_out,
        grad_w_in,
        grad_w_back,
    )
    return (outputs, grad_inputs, gains, shards)


def local(
    inputs,
    lengths,
    gain_glu,
    w_value,
    w_gate,
    gain_branch,
    w_left,
    w_right,
    gain_mid,
    w_depth,
    w_point,
    gain_attn,
    w_qkv,
    w_out,
    gain_ffn,
    w_in,
    w_back,
    cotangent,
):
    outputs, grad_inputs, gains, shards = split_pass(
        inputs,
        lengths,
        gain_glu,
        w_value,
        w_gate,
        gain_branch,
        w_left,
        w_right,
        gain_mid,
        w_depth,
        w_point,
        gain_attn,
        w_qkv,
        w_out,
        gain_ffn,
        w_in,
        w_back,
        cotangent,
    )
    gain_totals = lax.psum((gains[0], gains[1], gains[2], gains[3]), ("dp", "mp"))
    weight_totals = (
        lax.psum(shards[0].astype(jnp.bfloat16), "dp").astype(jnp.float32),
        lax.psum(shards[1].astype(jnp.bfloat16), "dp").astype(jnp.float32),
        lax.psum(shards[2].astype(jnp.bfloat16), "dp").astype(jnp.float32),
        lax.psum(shards[3].astype(jnp.bfloat16), "dp").astype(jnp.float32),
        lax.psum(shards[4].astype(jnp.bfloat16), "dp").astype(jnp.float32),
        lax.psum(shards[5].astype(jnp.bfloat16), "dp").astype(jnp.float32),
        lax.psum(shards[6].astype(jnp.bfloat16), "dp").astype(jnp.float32),
        lax.psum(shards[7].astype(jnp.bfloat16), "dp").astype(jnp.float32),
        lax.psum(shards[8].astype(jnp.bfloat16), "dp").astype(jnp.float32),
        lax.psum(shards[9].astype(jnp.bfloat16), "dp").astype(jnp.float32),
        lax.psum(shards[10].astype(jnp.bfloat16), "dp").astype(jnp.float32),
    )
    return (
        outputs,
        grad_inputs,
        gain_totals[0],
        weight_totals[0],
        weight_totals[1],
        gain_totals[1],
        weight_totals[2],
        weight_totals[3],
        weight_totals[4],
        weight_totals[5],
        weight_totals[6],
        gain_totals[2],
        weight_totals[7],
        weight_totals[8],
        gain_totals[3],
        weight_totals[9],
        weight_totals[10],
    )


HALF = 256
LANES = 128


def dot_nn(left_side, right_side):
    return lax.dot_general(
        left_side, right_side, (((1,), (0,)), ((), ())), preferred_element_type=jnp.float32
    )


def dot_nt(left_side, right_side):
    return lax.dot_general(
        left_side, right_side, (((1,), (1,)), ((), ())), preferred_element_type=jnp.float32
    )


def dot_tn(left_side, right_side):
    return lax.dot_general(
        left_side, right_side, (((0,), (0,)), ((), ())), preferred_element_type=jnp.float32
    )


def row_stats(values):
    centre = values - jnp.mean(values, axis=-1, keepdims=True)
    inv = lax.rsqrt(jnp.mean(centre * centre, axis=-1, keepdims=True) + epsilon)
    return centre * inv, inv


def norm_grad(grad_out, unit, inv, gain):
    scaled = grad_out * gain
    mean_one = jnp.mean(scaled, axis=-1, keepdims=True)
    mean_two = jnp.mean(scaled * unit, axis=-1, keepdims=True)
    return inv * (scaled - mean_one - unit * mean_two)


def sigmoid(values):
    return 0.5 * jnp.tanh(0.5 * values) + 0.5


def silu(values):
    return values * sigmoid(values)


def turned(values):
    return jnp.transpose(values.astype(jnp.float32)).astype(jnp.bfloat16)


class Loader:
    def __init__(self, sems, first=0):
        self.sems = sems
        self.count = first
        self.waits = []
        self.plain = []
        self.by_core = ([], [])

    def copy(self, source, target, at):
        return pltpu.make_async_copy(source, target, self.sems.at[at])

    def start(self, source, target):
        self.plain.append(self.copy(source, target, self.count))
        self.waits.append(self.plain[-1])
        self.count += 1

    def either(self, got, part, taker, target):
        for core in range(2):
            source = got if core == taker else part
            self.by_core[core].append(self.copy(source, target, self.count))
        self.waits.append(self.by_core[0][-1])
        self.count += 1

    def go(self, core):
        for copy in self.plain:
            copy.start()
        for number, copies in enumerate(self.by_core):
            if copies:

                @pl.when(core == number)
                def _(copies=copies):
                    for copy in copies:
                        copy.start()

    def wait(self):
        for copy in self.waits:
            copy.wait()


def load_pair(loader, own, got, part, taker, core, target, slots=(0, 1)):
    loader.start(own, target.at[slots[0]])
    loader.either(got, part, taker, target.at[slots[1]])


def load_left(loader, w_left, got, part, core, target):
    blocks = w_left.shape[1] // HALF
    rows = w_left.shape[0]
    for block in range(blocks):
        loader.start(w_left.at[:, pl.ds(block * HALF, HALF)], target.at[block])
        at = pl.ds(block * rows, rows)
        loader.either(got.at[at], part.at[at], 0, target.at[blocks + block])


def load_pack(loader, got, part, core, target):
    count, depth = target.shape[:2]
    for block in range(count):
        at = pl.ds(got.shape[0] - (count - block) * depth, depth)
        loader.either(got.at[at], part.at[at], 0, target.at[block])


def load_point(loader, w_point, got, part, core, target):
    at = pl.ds(0, w_point.shape[0])
    load_pair(loader, w_point, got.at[at], part.at[at], 1, core, target)


def load_right(loader, w_right, got, part, core, target):
    loader.start(w_right, target.at[0])
    rows = w_right.shape[1]
    for tap in range(w_right.shape[0]):
        at = (pl.ds(2 * rows + (tap // 2) * rows, rows), pl.ds((tap % 2) * LANES, LANES))
        loader.either(got.at[at], part.at[at], 1, target.at[1, tap])


def load_qkv(loader, w_qkv, got, part, core, target, which):
    rows = w_qkv.shape[1]
    for slot, index in enumerate(which):
        loader.start(w_qkv.at[index], target.at[0, slot])
        at = pl.ds(index * rows, rows)
        loader.either(got.at[at], part.at[at], 0, target.at[1, slot])


def load_out(loader, w_out, got, part, core, target):
    loader.start(w_out, target.at[0])
    rows = w_out.shape[0]
    for block in range(2):
        at = pl.ds(block * rows, rows)
        loader.either(
            got.at[at], part.at[at], 1, target.at[1, :, pl.ds(block * HALF, HALF)]
        )


def load_in(loader, w_in, got2, part2, got3, part3, core, target):
    blocks = w_in.shape[1] // HALF
    rows = w_in.shape[0]
    for block in range(blocks):
        loader.start(w_in.at[:, pl.ds(block * HALF, HALF)], target.at[block])
        got, part = (got2, part2) if block < 2 else (got3, part3)
        at = pl.ds(rows + (block % 2) * rows, rows)
        loader.either(got.at[at], part.at[at], 1, target.at[blocks + block])


def load_back(loader, w_back, got, part, core, target):
    loader.start(w_back, target.at[0])
    rows = w_back.shape[0]
    half = rows // 2
    near, far = pl.ds(0, HALF), pl.ds(HALF, HALF)
    for at, taker, spot in (
        (pl.ds(0, rows), 0, (pl.ds(0, rows), near)),
        (pl.ds(rows, half), 0, (pl.ds(0, half), far)),
        (pl.ds(0, half), 1, (pl.ds(half, half), far)),
    ):
        loader.either(got.at[at], part.at[at], taker, target.at[1].at[spot])


GROUP = 8


def bundle_kernel(
    info, w_left, w_right, w_point, w_depth, gain_mid, w_qkv, w_out, w_in, w_back,
    one_o, two_o, three_o, sems,
):
    core = info[0]

    def copies(pieces):
        at = {id(one_o): 0, id(two_o): 0, id(three_o): 0}
        started = []
        for target, source in pieces:
            base = at[id(target)]
            at[id(target)] = base + source.shape[0]
            spot = target.at[pl.ds(base, source.shape[0]), pl.ds(0, source.shape[1])]
            copy = pltpu.make_async_copy(source, spot, sems.at[len(started)])
            copy.start()
            started.append(copy)
        for copy in started:
            copy.wait()

    def blocks(values):
        return [values.at[:, pl.ds(at, HALF)] for at in range(0, values.shape[1], HALF)]

    near, far = blocks(w_back)
    half = w_back.shape[0] // 2

    @pl.when(core == 0)
    def _():
        base = w_left.shape[0] * (w_left.shape[1] // HALF)
        taps = jnp.concatenate(
            [
                w_depth[...].astype(jnp.float32),
                gain_mid[...].astype(jnp.float32),
                jnp.zeros((15 - w_depth.shape[0], w_depth.shape[1]), jnp.float32),
            ],
            axis=0,
        ).astype(jnp.bfloat16)
        for block in range(w_depth.shape[1] // HALF):
            at = slice(base + block * 16, base + (block + 1) * 16)
            one_o[at] = taps[:, block * HALF : (block + 1) * HALF]
        copies(
            [(one_o, piece) for piece in blocks(w_left)]
            + [(two_o, w_qkv.at[index]) for index in range(3)]
            + [(three_o, near), (three_o, far.at[pl.ds(0, half)])]
        )

    @pl.when(core == 1)
    def _():
        pieces = [(one_o, w_point)]
        pieces += [(two_o, piece) for piece in blocks(w_out) + blocks(w_in)[:2]]
        pieces += [(three_o, far.at[pl.ds(half, half)])]
        pieces += [(three_o, piece) for piece in blocks(w_in)[2:]]
        rows, base = w_right.shape[1], w_point.shape[0]
        started = []
        for tap in range(w_right.shape[0]):
            spot = one_o.at[
                pl.ds(base + (tap // 2) * rows, rows), pl.ds((tap % 2) * LANES, LANES)
            ]
            copy = pltpu.make_async_copy(w_right.at[tap], spot, sems.at[len(pieces) + tap])
            copy.start()
            started.append(copy)
        copies(pieces)
        for copy in started:
            copy.wait()


def row_spot(rows, own, lanes):
    row = lax.broadcasted_iota(jnp.int32, (rows, lanes), 0)
    spot = (row % GROUP) * (own // GROUP) + row // GROUP
    return jnp.where(row < own, spot, jnp.where(row < own + EDGE, row - own - EDGE, row - EDGE))


def row_mask(core, length, ext, lanes):
    own = ext - 2 * EDGE
    spot = row_spot(ext, own, lanes) + core * own
    return jnp.where((spot >= 0) & (spot < length), 1.0, 0.0)


def lane_tiles(width):
    return [slice(at, at + LANES) for at in range(0, width, LANES)]


def load_tiles(source, tiles):
    for index, lanes in enumerate(lane_tiles(source.shape[1])):
        tiles[index] = source[:, lanes].astype(jnp.float32)


def gather_rows(tiles, target):
    own = tiles.shape[1]
    for tile, lanes in enumerate(lane_tiles(target.shape[1])):
        for index in range(own // GROUP):
            target[index * GROUP : (index + 1) * GROUP, lanes] = tiles[
                tile, pl.ds(index, GROUP, stride=own // GROUP)
            ]


def scatter_rows(source, tiles, target):
    own = tiles.shape[1]
    for tile, lanes in enumerate(lane_tiles(target.shape[1])):
        for index in range(own // GROUP):
            tiles[tile, pl.ds(index, GROUP, stride=own // GROUP)] = source[
                index * GROUP : (index + 1) * GROUP, lanes
            ]
        target[:, lanes] = tiles[tile].astype(target.dtype)


def next_group(first, row):
    sub = lax.broadcasted_iota(jnp.int32, first.shape, 0)
    return jnp.where(sub == GROUP - 1, row, pltpu.roll(first, GROUP - 1, 0))


def previous_group(last, row):
    sub = lax.broadcasted_iota(jnp.int32, last.shape, 0)
    return jnp.where(sub == 0, row, pltpu.roll(last, 1, 0))


def shift_rows(values, offset):
    if offset == 0:
        return values
    ext = values.shape[0]
    own = ext - 2 * EDGE
    mid, before, after = values[:own], values[own : own + EDGE], values[own + EDGE :]
    sub = lax.broadcasted_iota(jnp.int32, before.shape, 0)
    if offset > 0:
        moved = jnp.concatenate([mid[GROUP:], next_group(mid[:GROUP], after[:1])], axis=0)
        before = jnp.where(sub == EDGE - 1, mid[:1], pltpu.roll(before, EDGE - 1, 0))
        after = pltpu.roll(after, EDGE - 1, 0)
    else:
        moved = jnp.concatenate(
            [previous_group(mid[own - GROUP :], before[EDGE - 1 :]), mid[: own - GROUP]], axis=0
        )
        after = jnp.where(sub == 0, mid[own - 1 :], pltpu.roll(after, 1, 0))
        before = pltpu.roll(before, 1, 0)
    return jnp.concatenate([moved, before, after], axis=0)


def fill_window(window, values, own, reach):
    before, after = values[own : own + EDGE], values[own + EDGE :]
    window[reach * GROUP : reach * GROUP + own] = values[:own]
    for step in range(1, reach + 1):
        last = values[own - step * GROUP : own - (step - 1) * GROUP]
        at = (reach - step) * GROUP
        window[at : at + GROUP] = previous_group(last, before[EDGE - step : EDGE - step + 1])
        first = values[(step - 1) * GROUP : step * GROUP]
        at = reach * GROUP + own + (step - 1) * GROUP
        window[at : at + GROUP] = next_group(first, after[step - 1 : step])


def glu_kernel(
    info, block, moved, cot_own, cot_moved, edge, gain_glu, gain_branch, w_value, w_gate, got, part_w,
    cot_o, resid_o, branch_o, gluin_o, value_o, sig_o, x_s, c_s, n_s, wv_s, wg_s, sems,
):
    core, member, length = info[0], info[1], info[2]
    loader = Loader(sems)
    load_pair(loader, w_value, got, part_w, 0, core, wv_s, (member, 1 - member))
    load_pair(loader, w_gate, got, part_w, 1, core, wg_s, (member, 1 - member))
    loader.go(core)
    ext = x_s.shape[0]
    rows = ext - 2 * EDGE
    edge_f = edge[...].astype(jnp.float32)
    x_s[rows : rows + EDGE] = jnp.where(core == 1, edge_f, 0.0)
    x_s[rows + EDGE :] = jnp.where(core == 1, 0.0, edge_f)

    @pl.when(core == member)
    def _():
        load_tiles(block, n_s)

    @pl.when(core != member)
    def _():
        load_tiles(moved, n_s)

    gather_rows(n_s, x_s)

    @pl.when(core == member)
    def _():
        load_tiles(cot_own, n_s)

    @pl.when(core != member)
    def _():
        load_tiles(cot_moved, n_s)

    gather_rows(n_s, c_s)
    cot_o[...] = c_s[...].astype(jnp.bfloat16)
    loader.wait()
    valid = row_mask(core, length, ext, LANES)[:, :1]
    part = ext // 2
    for start in (0, part):
        at = slice(start, start + part)
        x = x_s[at]
        glu_in = (row_stats(x)[0] * gain_glu[...]).astype(jnp.bfloat16)
        gluin_o[at] = glu_in
        for half in range(2):
            cols = slice(half * HALF, (half + 1) * HALF)
            value = dot_nn(glu_in, wv_s[half])
            sig = sigmoid(dot_nn(glu_in, wg_s[half]))
            value_o[at, cols] = value.astype(jnp.bfloat16)
            sig_o[at, cols] = sig.astype(jnp.bfloat16)
            resid_o[at, cols] = x[:, cols] + (value * sig).astype(jnp.bfloat16).astype(jnp.float32)
        normed = row_stats(resid_o[at])[0] * gain_branch[...]
        branch_o[at] = (valid[at] * normed).astype(jnp.bfloat16)


def spread_block(index, rights, stride):
    source = lax.broadcasted_iota(jnp.int32, (rights, HALF), 0)
    channel = lax.broadcasted_iota(jnp.int32, (rights, HALF), 1) + index * HALF
    return jnp.where(channel == source * stride, 1.0, 0.0).astype(jnp.bfloat16)


def conv_rows(branch, weights):
    taps = weights.shape[0]
    total = dot_nn(branch, weights[taps // 2])
    for tap in range(taps):
        if tap != taps // 2:
            total = total + shift_rows(dot_nn(branch, weights[tap]), tap - taps // 2)
    return total


def mid_step(branch, into, right_act, index, stride, left_o, mid_o, sums, at):
    left_pre = dot_nn(branch[...], into[index])
    left_o[at] = left_pre.astype(jnp.bfloat16)
    mid = silu(left_pre) + dot_nn(right_act, spread_block(index, right_act.shape[1], stride))
    mid_o[at] = mid
    near, far = mid[:, :LANES], mid[:, LANES:]
    sums[0] += near + far
    sums[1] += near * near + far * far


def branch_own_kernel(
    info, branch, w_left, w_right, left_o, right_o, mid_o, sums_o, wl_s, sems
):
    loader = Loader(sems)
    blocks = wl_s.shape[0]
    for block in range(blocks):
        loader.start(w_left.at[:, pl.ds(block * HALF, HALF)], wl_s.at[block])
    loader.go(info[0])
    right_pre = conv_rows(branch[...], w_right)
    right_o[...] = right_pre
    right_act = silu(right_pre).astype(jnp.bfloat16)
    stride = blocks * HALF // right_pre.shape[1]
    sums_o[...] = jnp.zeros_like(sums_o)
    loader.wait()

    def step(index, carry):
        mid_step(branch, wl_s, right_act, index, stride, left_o, mid_o, sums_o, index)
        return carry

    lax.fori_loop(0, blocks, step, 0, unroll=2)


def fill_taps(pack_own, pack_oth, taps_s):
    count, cols = pack_own.shape
    taps_s[:count, :cols] = pack_own[...].astype(jnp.float32)
    for block in range(pack_oth.shape[0]):
        at = cols + block * HALF
        taps_s[:, at : at + HALF] = pack_oth[block].astype(jnp.float32)


def branch_kernel(
    info, branch, resid_one, pack_own, left_own, right_own, mid_own, sums_own, w_point, got, part,
    resid_two_o, left_o, right_o, stats_o, depth_o,
    wl_s, wr_s, wp_s, po_s, taps_s, mid_s, din_s, sums_s, sep_s, sems,
):
    core, length = info[0], info[2]
    loader = Loader(sems)
    taps_conv, depth_in_rows = wr_s.shape[0], wr_s.shape[1]
    for tap in range(taps_conv):
        at = (
            pl.ds(w_point.shape[0] + (tap // 2) * depth_in_rows, depth_in_rows),
            pl.ds((tap % 2) * LANES, LANES),
        )
        loader.either(got.at[at], part.at[at], 1, wr_s.at[tap])
    blocks = wl_s.shape[0]
    for block in range(blocks):
        at = pl.ds(block * depth_in_rows, depth_in_rows)
        loader.either(got.at[at], part.at[at], 0, wl_s.at[block])
    load_point(loader, w_point, got, part, core, wp_s)
    load_pack(loader, got, part, core, po_s)
    loader.go(core)
    ext = branch.shape[0]
    rows = ext - 2 * EDGE
    chunks = 2 * blocks
    per_shard = blocks
    sep_taps = pack_own.shape[0] - 1
    inner = chunks * HALF
    rights = right_own.shape[1]
    stride = blocks * HALF // rights
    left_o[:blocks] = left_own[...]
    mid_s[:blocks] = mid_own[...]
    sums_s[...] = sums_own[...]
    right_o[:, :rights] = right_own[...]
    loader.wait()
    fill_taps(pack_own, po_s, taps_s)
    right_pre = conv_rows(branch[...], wr_s)
    right_o[:, rights:] = right_pre
    right_act = silu(right_pre).astype(jnp.bfloat16)

    def first(index, carry):
        mid_step(branch, wl_s, right_act, index, stride, left_o, mid_s, sums_s, index + blocks)
        return carry

    lax.fori_loop(0, blocks, first, 0, unroll=2)
    mean = jnp.sum(sums_s[0], axis=-1, keepdims=True) / inner
    inv = lax.rsqrt(
        jnp.sum(sums_s[1], axis=-1, keepdims=True) / inner - mean * mean + epsilon
    )
    lane = lax.broadcasted_iota(jnp.int32, (ext, LANES), 1)
    stats_o[...] = jnp.where(lane == 0, mean, inv)
    sums_s[0] = jnp.broadcast_to(mean, (ext, LANES))
    sums_s[1] = inv * row_mask(core, length, ext, LANES)
    sep_s[...] = jnp.zeros_like(sep_s)

    def second(index, carry):
        cols = pl.ds(pl.multiple_of(index * HALF, HALF), HALF)
        taps = taps_s[:, cols]
        for side in range(2):
            lanes = slice(side * LANES, (side + 1) * LANES)
            depth_in = (
                (mid_s[index, :, lanes] - sums_s[0]) * sums_s[1] * taps[sep_taps : sep_taps + 1, lanes]
            )
            fill_window(din_s.at[:, lanes], depth_in, rows, sep_taps // 2)
        step = 64
        for start in range(0, rows, step):
            for side in range(2):
                lanes = slice(side * LANES, (side + 1) * LANES)
                acc = din_s[start : start + step, lanes] * taps[:1, lanes]
                for tap in range(1, sep_taps):
                    at = start + tap * GROUP
                    acc = acc + din_s[at : at + step, lanes] * taps[tap : tap + 1, lanes]
                depth_o[index, start : start + step, lanes] = acc.astype(jnp.bfloat16)
        shard, chunk = index // per_shard, index % per_shard
        point = wp_s[shard, pl.ds(pl.multiple_of(chunk * HALF, HALF), HALF)]
        sep_s[...] += dot_nn(depth_o[index], point)
        return carry

    lax.fori_loop(0, chunks, second, 0, unroll=2)
    sep_width = sep_s.shape[1]
    resid_two_o[:, :sep_width] = resid_one[:rows, :sep_width] + sep_s[...]
    resid_two_o[:, sep_width:] = resid_one[:rows, sep_width:]


def kv_kernel(info, resid_two, gain, w_qkv, got, part, attn_o, kv_o, w_s, sems):
    loader = Loader(sems)
    load_qkv(loader, w_qkv, got, part, info[0], w_s, (1, 2))
    loader.go(info[0])
    attn_in = (row_stats(resid_two[...])[0] * gain[...]).astype(jnp.bfloat16)
    attn_o[...] = attn_in
    loader.wait()
    width = w_s.shape[3]
    for shard in range(2):
        for index in range(2):
            at = (2 * index + shard) * width
            kv_o[:, at : at + width] = dot_nn(attn_in, w_s[shard, index]).astype(jnp.bfloat16)


def query_kernel(info, attn_in, w_qkv, got, part, q_o, w_s, sems):
    loader = Loader(sems)
    load_qkv(loader, w_qkv, got, part, info[0], w_s, (0,))
    loader.go(info[0])
    loader.wait()
    width = w_s.shape[3]
    scale = 1.0 / math.sqrt(HEAD_DIM)
    for shard in range(2):
        query = dot_nn(attn_in[...], w_s[shard, 0]).astype(jnp.bfloat16).astype(jnp.float32)
        q_o[:, shard * width : (shard + 1) * width] = (query * scale).astype(jnp.bfloat16)


def key_bias(core, length, rows):
    spot = row_spot(rows, rows, LANES) + core * rows
    return jnp.where(spot < length, 0.0, negative_big)


def head_masks(rows, head):
    lane = lax.broadcasted_iota(jnp.int32, (rows, LANES), 1)
    return (lane // HEAD_DIM) == head, lane == HEAD_DIM * (1 - head)


def attend_kernel(info, q, kvo, kvf, ctx0_o, lse0_o, ctx1_o, lse1_o, bias_s):
    core, length = info[0], info[2]
    rows, width = q.shape
    pairs = width // LANES // 2
    bias_s[:rows] = key_bias(core, length, rows)
    bias_s[rows:] = key_bias(1 - core, length, rows)

    def pair_step(shard, ctx_o, lse_o, local, carry):
        pair = local + shard * pairs
        cols = pl.ds(pl.multiple_of(pair * LANES, LANES), LANES)
        vcols = pl.ds(pl.multiple_of(pair * LANES + width, LANES), LANES)
        here = pl.ds(pl.multiple_of(local * LANES, LANES), LANES)
        keys = jnp.concatenate([kvo[:, cols], kvf[:, cols]], axis=0).astype(jnp.float32)
        vals = jnp.concatenate([kvo[:, vcols], kvf[:, vcols]], axis=0)
        vals_t = turned(vals)
        query = q[:, cols].astype(jnp.float32)
        outs = []
        for head in range(2):
            in_k, extra_k = head_masks(2 * rows, head)
            in_q, extra_q = head_masks(rows, head)
            km = jnp.where(in_k, keys, jnp.where(extra_k, bias_s[...], 0.0)).astype(jnp.bfloat16)
            qm = jnp.where(in_q, query, jnp.where(extra_q, 1.0, 0.0)).astype(jnp.bfloat16)
            pieces = []
            for start in range(0, rows, HALF):
                scores = dot_nt(km, qm[start : start + HALF])
                top = jnp.max(scores, axis=0, keepdims=True)
                weights = jnp.exp(scores - top)
                total = jnp.sum(weights, axis=0, keepdims=True)
                out = dot_nn(
                    vals_t[head * HEAD_DIM : (head + 1) * HEAD_DIM], weights.astype(jnp.bfloat16)
                )
                pieces.append(out / total)
                lse_o[pl.ds(local * 2 + head, 1), start : start + HALF] = top + jnp.log(total)
            outs.append(jnp.concatenate(pieces, axis=1))
        ctx_o[:, here] = jnp.transpose(jnp.concatenate(outs, axis=0)).astype(jnp.bfloat16)
        return carry

    lax.fori_loop(0, pairs, functools.partial(pair_step, 0, ctx0_o, lse0_o), 0, unroll=2)
    lax.fori_loop(0, pairs, functools.partial(pair_step, 1, ctx1_o, lse1_o), 0, unroll=2)


def ffn_kernel(
    info, resid_two, ctx0, ctx1, cot, gain, w_out, w_in, w_back, got2, part2,
    got3, part3,
    out_o, grad_three_o, gctx_o, ggain_o, send_o, keep_o,
    wo_s, wi_s, wb_s, fin_s, fint_s, cot_s, acc_s, gacc_s, ctxt_s, n_s, sems,
):
    core = info[0]
    loader = Loader(sems)
    load_out(loader, w_out, got2, part2, core, wo_s)
    late = Loader(sems, loader.count)
    load_in(late, w_in, got2, part2, got3, part3, core, wi_s)
    load_back(late, w_back, got3, part3, core, wb_s)

    loader.go(core)
    late.go(core)
    cot_s[...] = cot[...]
    loader.wait()
    part = ctx0.shape[1]
    chunks = wi_s.shape[0]
    per_shard = chunks // 2
    resid = resid_two[...] + dot_nn(ctx0[...], wo_s[0]) + dot_nn(ctx1[...], wo_s[1])
    acc_s[...] = resid
    gacc_s[...] = jnp.zeros_like(gacc_s)
    unit, inv = row_stats(resid)
    ffn_in = unit * gain[...]
    fin_s[...] = ffn_in.astype(jnp.bfloat16)
    fint_s[...] = jnp.transpose(fin_s[...].astype(jnp.float32)).astype(jnp.bfloat16)
    keep_rows = pl.ds(pl.multiple_of(core * HALF, HALF), HALF)
    send_rows = pl.ds(pl.multiple_of((1 - core) * HALF, HALF), HALF)

    def chunk_step(index, carry):
        shard, chunk = index // per_shard, index % per_shard
        rows = pl.ds(pl.multiple_of(chunk * HALF, HALF), HALF)
        into, back = wi_s[index], wb_s[shard, rows]
        pre = dot_nn(fin_s[...], into)
        sig = sigmoid(pre)
        hidden = (pre * sig).astype(jnp.bfloat16)
        acc_s[...] += dot_nn(hidden, back)
        grad_hidden = dot_nt(cot_s[...], back)
        grad_pre = (grad_hidden * (sig * (1.0 + pre * (1.0 - sig)))).astype(jnp.bfloat16)
        send_o[shard, rows] = dot_nn(fint_s[send_rows], grad_pre).astype(jnp.bfloat16)
        keep_o[shard, rows] = dot_nn(fint_s[keep_rows], grad_pre).astype(jnp.bfloat16)
        hidden_t = turned(hidden)
        base = per_shard * HALF
        rows = pl.ds(pl.multiple_of(base + chunk * HALF, HALF), HALF)
        send_o[shard, rows] = dot_nn(hidden_t, cot_s[:, send_rows]).astype(jnp.bfloat16)
        keep_o[shard, rows] = dot_nn(hidden_t, cot_s[:, keep_rows]).astype(jnp.bfloat16)
        gacc_s[...] += dot_nt(grad_pre, into)
        return carry

    late.wait()
    lax.fori_loop(0, chunks, chunk_step, 0, unroll=4)
    scatter_rows(acc_s, n_s, out_o)
    unit, inv = row_stats(
        resid_two[...] + dot_nn(ctx0[...], wo_s[0]) + dot_nn(ctx1[...], wo_s[1])
    )
    grad_norm = gacc_s[...]
    ggain_o[...] = jnp.sum(grad_norm * unit, axis=0, keepdims=True)
    grad_three = cot_s[...].astype(jnp.float32) + norm_grad(grad_norm, unit, inv, gain[...])
    grad_three_o[...] = grad_three
    fin_s[...] = grad_three.astype(jnp.bfloat16)
    ctxt_s[:part] = turned(ctx0[...])
    ctxt_s[part:] = turned(ctx1[...])
    base = 2 * per_shard * HALF
    for shard in range(2):
        side = slice(shard * part, (shard + 1) * part)
        gctx_o[:, side] = dot_nt(fin_s[...], wo_s[shard]).astype(jnp.bfloat16)
        send_o[shard, base : base + part] = dot_nn(ctxt_s[side], fin_s[:, send_rows]).astype(
            jnp.bfloat16
        )
        keep_o[shard, base : base + part] = dot_nn(ctxt_s[side], fin_s[:, keep_rows]).astype(
            jnp.bfloat16
        )


def attend_back_kernel(side, info, q, kv, ctx0, ctx1, gctx, lse0, lse1, *rest):
    if side:
        gq_o, gkv_o, bias_s, gk_s, gv_s = rest
    else:
        gq_part, gq_o, gkv_o, bias_s, gk_s, gv_s = rest
    core, length = info[0], info[2]
    rows, width = q.shape
    pairs = width // LANES // 2
    scale = 1.0 / math.sqrt(HEAD_DIM)
    bias_s[...] = key_bias(core ^ side, length, rows)

    def pair_step(shard, ctx, lse, local, carry):
        pair = local + shard * pairs
        cols = pl.ds(pl.multiple_of(pair * LANES, LANES), LANES)
        vcols = pl.ds(pl.multiple_of(pair * LANES + width, LANES), LANES)
        here = pl.ds(pl.multiple_of(local * LANES, LANES), LANES)
        keys = kv[:, cols].astype(jnp.float32)
        vals = kv[:, vcols]
        keys_t = jnp.transpose(keys).astype(jnp.bfloat16)
        query = q[:, cols].astype(jnp.float32)
        grad_out = gctx[:, cols].astype(jnp.float32)
        product_t = jnp.transpose(grad_out * ctx[:, here].astype(jnp.float32))
        gk_s[...] = jnp.zeros_like(gk_s)
        gv_s[...] = jnp.zeros_like(gv_s)
        outs = []
        for head in range(2):
            in_q, extra_q = head_masks(rows, head)
            km = jnp.where(in_q, keys, jnp.where(extra_q, bias_s[...], 0.0)).astype(jnp.bfloat16)
            qm = jnp.where(in_q, query, jnp.where(extra_q, 1.0, 0.0)).astype(jnp.bfloat16)
            qz = jnp.where(in_q, query, 0.0).astype(jnp.bfloat16)
            gz = jnp.where(in_q, grad_out, 0.0).astype(jnp.bfloat16)
            span = slice(head * HEAD_DIM, (head + 1) * HEAD_DIM)
            pieces = []
            for start in range(0, rows, HALF):
                at = slice(start, start + HALF)
                level = lse[pl.ds(local * 2 + head, 1), at]
                delta = jnp.sum(product_t[span, at], axis=0, keepdims=True)
                soft = jnp.exp(dot_nt(km, qm[at]) - level)
                gv_s[...] += dot_nn(soft.astype(jnp.bfloat16), gz[at])
                grad_scores = (soft * (dot_nt(vals, gz[at]) - delta)).astype(jnp.bfloat16)
                gk_s[...] += dot_nn(grad_scores, qz[at])
                pieces.append(dot_nn(keys_t[span], grad_scores))
            outs.append(jnp.concatenate(pieces, axis=1))
        grad_q = jnp.transpose(jnp.concatenate(outs, axis=0))
        if not side:
            grad_q = (grad_q + gq_part[:, cols]) * scale
        gq_o[:, cols] = grad_q.astype(gq_o.dtype)
        gkv_o[:, cols] = gk_s[...].astype(gkv_o.dtype)
        gkv_o[:, vcols] = gv_s[...].astype(gkv_o.dtype)
        return carry

    for shard, ctx, lse in ((0, ctx0, lse0), (1, ctx1, lse1)):
        lax.fori_loop(0, pairs, functools.partial(pair_step, shard, ctx, lse), 0, unroll=2)


def qkv_back_kernel(
    info, gq, gown, gfar, attn_in, resid_two, grad_three, gain, w_qkv, got, part,
    grad_two_o, gsep_o, gedge_o, ggain_o, send_o, keep_o, w_s, attnt_s, n_s, sems,
):
    core = info[0]
    loader = Loader(sems)
    load_qkv(loader, w_qkv, got, part, core, w_s, (0, 1, 2))
    loader.go(core)
    attnt_s[...] = turned(attn_in[...])
    width = w_s.shape[3]
    keep_rows = pl.ds(pl.multiple_of(core * HALF, HALF), HALF)
    send_rows = pl.ds(pl.multiple_of((1 - core) * HALF, HALF), HALF)
    loader.wait()
    grad_in = jnp.zeros(resid_two.shape, jnp.float32)
    for index in range(3):
        if index == 0:
            whole = gq[...]
        else:
            cols = slice((index - 1) * 2 * width, index * 2 * width)
            whole = (gown[:, cols] + gfar[:, cols].astype(jnp.float32)).astype(jnp.bfloat16)
        for shard in range(2):
            grad = whole[:, shard * width : (shard + 1) * width]
            at = slice(index * HALF, (index + 1) * HALF)
            send_o[shard, at] = dot_nn(attnt_s[send_rows], grad).astype(jnp.bfloat16)
            keep_o[shard, at] = dot_nn(attnt_s[keep_rows], grad).astype(jnp.bfloat16)
            grad_in = grad_in + dot_nt(grad, w_s[shard, index])
    unit, inv = row_stats(resid_two[...])
    ggain_o[...] = jnp.sum(grad_in * unit, axis=0, keepdims=True)
    grad_two = grad_three[...] + norm_grad(grad_in, unit, inv, gain[...])
    grad_two_o[...] = grad_two
    gsep_o[...] = grad_two[:, : gsep_o.shape[1]].astype(jnp.bfloat16)
    rows = n_s.shape[1]
    for tile, lanes in enumerate(lane_tiles(gsep_o.shape[1])):
        n_s[tile] = grad_two[:, lanes]
        first = n_s[tile, pl.ds(0, EDGE, stride=GROUP)]
        last = n_s[tile, pl.ds(rows - EDGE * GROUP + GROUP - 1, EDGE, stride=GROUP)]
        gedge_o[:, lanes] = jnp.where(core == 0, last, first).astype(jnp.bfloat16)


def point_kernel(info, gsep, depth, send, keep, send_o, keep_o):
    core = info[0]
    grad_sep = gsep[...]
    per_shard = depth.shape[0] // 2
    per_core = per_shard // 2
    base = send.shape[1]
    send_o[:, :base] = send[...]
    keep_o[:, :base] = keep[...]
    for shard in range(2):
        for chunk in range(per_core):
            at = slice(base + chunk * HALF, base + (chunk + 1) * HALF)
            first = shard * per_shard
            send_o[shard, at] = dot_tn(
                depth[first + (1 - core) * per_core + chunk], grad_sep
            ).astype(jnp.bfloat16)
            keep_o[shard, at] = dot_tn(
                depth[first + core * per_core + chunk], grad_sep
            ).astype(jnp.bfloat16)


def as_f32(values):
    return values.astype(jnp.float32)


def slope_of(values):
    sig = sigmoid(values)
    return sig * (1.0 + values * (1.0 - sig))


def depth_back_kernel(
    info, gsep, gedge, left_pre, right_pre, stats, pack_own, w_point, got, part,
    unit_o, scaled_o, sums_s, small_s,
    wp_s, po_s, taps_s, gse_s, gd_s, din_s, near_s, unit_s, scaled_s, wide_s, sems,
):
    core, length = info[0], info[2]
    loader = Loader(sems)
    load_point(loader, w_point, got, part, core, wp_s)
    load_pack(loader, got, part, core, po_s)
    loader.go(core)
    ext = left_pre.shape[1]
    rows = ext - 2 * EDGE
    chunks = left_pre.shape[0]
    per_shard = chunks // 2
    inner = chunks * HALF
    sep_taps = pack_own.shape[0] - 1
    right_cols = right_pre.shape[1]
    stride = inner // right_cols
    reach = sep_taps // 2
    edge = gedge[...].astype(jnp.float32)
    gse_s[:rows] = gsep[...]
    gse_s[rows : rows + EDGE] = jnp.where(core == 1, edge, 0.0).astype(jnp.bfloat16)
    gse_s[rows + EDGE :] = jnp.where(core == 1, 0.0, edge).astype(jnp.bfloat16)
    wide_s[0] = row_mask(core, length, ext, LANES)
    wide_s[1] = jnp.broadcast_to(stats[:, 0:1], (ext, LANES))
    wide_s[2] = jnp.broadcast_to(stats[:, 1:2], (ext, LANES))
    scaled_s[...] = jnp.zeros_like(scaled_s)
    sums_s[...] = jnp.zeros_like(sums_s)
    small_s[...] = jnp.zeros_like(small_s)
    right_act = silu(right_pre[...]).astype(jnp.bfloat16)
    loader.wait()
    fill_taps(pack_own, po_s, taps_s)

    def first(index, carry):
        cols = pl.ds(pl.multiple_of(index * HALF, HALF), HALF)
        taps = taps_s[:, cols]
        shard, chunk = index // per_shard, index % per_shard
        point = wp_s[shard, pl.ds(pl.multiple_of(chunk * HALF, HALF), HALF)]
        grad_depth = dot_nt(gse_s[...], point)
        for side, lanes in enumerate(lane_tiles(HALF)):
            fill_window(gd_s.at[side], grad_depth[:, lanes], rows, reach)
            near_s[side, :EDGE] = grad_depth[rows : rows + EDGE, lanes]
            near_s[side, 3 * EDGE :] = grad_depth[rows + EDGE :, lanes]
            base = reach * GROUP
            near_s[side, EDGE : 2 * EDGE] = gd_s[side, pl.ds(base, EDGE, stride=GROUP)]
            base = reach * GROUP + rows - EDGE * GROUP + GROUP - 1
            near_s[side, 2 * EDGE : 3 * EDGE] = gd_s[side, pl.ds(base, EDGE, stride=GROUP)]
        mid = silu(left_pre[index].astype(jnp.float32)) + dot_nn(
            right_act, spread_block(index, right_cols, stride)
        )
        for side in range(2):
            lanes = slice(side * LANES, (side + 1) * LANES)
            unit = (mid[:, lanes] - wide_s[1]) * wide_s[2]
            unit_s[:, lanes] = unit
            fill_window(
                din_s.at[side],
                unit * wide_s[0] * taps[sep_taps : sep_taps + 1, lanes],
                rows,
                reach,
            )
            for base, target in ((EDGE - GROUP, rows + EDGE - GROUP), (3 * EDGE, rows + EDGE)):
                acc = near_s[side, base + reach : base + reach + GROUP] * taps[:1, lanes]
                for tap in range(1, sep_taps):
                    at = base + reach - tap
                    acc = acc + near_s[side, at : at + GROUP] * taps[tap : tap + 1, lanes]
                at = slice(target, target + GROUP)
                scaled_s[at, lanes] = acc * wide_s[0, at]
        step = 64
        tap_sums = []
        for side in range(2):
            lanes = slice(side * LANES, (side + 1) * LANES)
            sums = [jnp.zeros((GROUP, LANES), jnp.float32) for _ in range(sep_taps)]
            for start in range(0, rows, step):
                at = start + 2 * reach * GROUP
                acc = gd_s[side, at : at + step] * taps[:1, lanes]
                for tap in range(1, sep_taps):
                    at = start + (2 * reach - tap) * GROUP
                    acc = acc + gd_s[side, at : at + step] * taps[tap : tap + 1, lanes]
                scaled_s[start : start + step, lanes] = acc * wide_s[0, start : start + step]
                at = start + reach * GROUP
                grad = gd_s[side, at : at + step]
                for tap in range(sep_taps):
                    at = start + tap * GROUP
                    term = din_s[side, at : at + step] * grad
                    sums[tap] = sums[tap] + jnp.sum(
                        term.reshape(step // GROUP, GROUP, LANES), axis=0
                    )
            tap_sums.append(sums)
        tap_sums = [jnp.concatenate(pair, axis=1) for pair in zip(*tap_sums)]
        tap_rows = [jnp.sum(value, axis=0, keepdims=True) for value in tap_sums]
        gain = taps[sep_taps : sep_taps + 1]
        gain_row = jnp.sum(
            scaled_s[:rows] * unit_s[:rows],
            axis=0,
            keepdims=True,
        )
        filler = jnp.zeros((small_s.shape[0] - sep_taps - 1, HALF), jnp.float32)
        small_s[:, cols] = jnp.concatenate(tap_rows + [gain_row, filler], axis=0)
        scaled = scaled_s[...] * gain
        scaled_o[index] = scaled.astype(jnp.bfloat16)
        unit_o[index] = unit_s[...].astype(jnp.bfloat16)
        near, far = scaled[:, :LANES], scaled[:, LANES:]
        sums_s[0] += near + far
        sums_s[1] += near * unit_s[:, :LANES] + far * unit_s[:, LANES:]
        return carry

    lax.fori_loop(0, chunks, first, 0, unroll=2)


def branch_back_kernel(
    info, unit, scaled, sums, small, left_pre, right_pre, stats, branch, gain_ffn_g, gain_attn_g,
    gleft_o, gright_o, send_o, keep_o,
    wide_s, gra_s, bt_s,
):
    core = info[0]
    ext = left_pre.shape[1]
    rows = ext - 2 * EDGE
    chunks = left_pre.shape[0]
    per_shard = chunks // 2
    inner = chunks * HALF
    right_cols = right_pre.shape[1]
    stride = inner // right_cols
    for index in range(2):
        mean = jnp.sum(sums[index], axis=-1, keepdims=True) / inner
        wide_s[index] = jnp.broadcast_to(mean, (ext, LANES))
    wide_s[2] = jnp.broadcast_to(stats[:, 1:2], (ext, LANES))
    gra_s[...] = jnp.zeros_like(gra_s)
    bt_s[...] = turned(branch[...])
    keep_rows = pl.ds(pl.multiple_of(core * HALF, HALF), HALF)
    send_rows = pl.ds(pl.multiple_of((1 - core) * HALF, HALF), HALF)

    def second(index, carry):
        shard, chunk = index // per_shard, index % per_shard
        sides = []
        for side in range(2):
            lanes = slice(side * LANES, (side + 1) * LANES)
            sides.append(
                wide_s[2]
                * (as_f32(scaled[index, :, lanes]) - wide_s[0] - as_f32(unit[index, :, lanes]) * wide_s[1])
            )
        grad_mid = jnp.concatenate(sides, axis=1)
        grad_left = (
            grad_mid[:rows] * slope_of(left_pre[index, :rows].astype(jnp.float32))
        ).astype(jnp.bfloat16)
        gleft_o[index] = grad_left
        gra_s[...] += dot_nt(
            grad_mid.astype(jnp.bfloat16), spread_block(index, right_cols, stride)
        )
        at = pl.ds(pl.multiple_of(chunk * HALF, HALF), HALF)
        send_o[shard, at] = dot_nn(bt_s[send_rows, :rows], grad_left).astype(
            jnp.bfloat16
        )
        keep_o[shard, at] = dot_nn(bt_s[keep_rows, :rows], grad_left).astype(
            jnp.bfloat16
        )
        return carry

    lax.fori_loop(0, chunks, second, 0, unroll=2)
    grad_right = gra_s[...] * slope_of(right_pre[...])
    gright_o[...] = grad_right.astype(jnp.bfloat16)
    spot = lax.broadcasted_iota(jnp.int32, grad_right.shape, 0)
    own_right = jnp.where(spot < rows, grad_right, 0.0)
    part = right_cols // 2
    base = per_shard * HALF
    for target, picked, side in ((send_o, send_rows, 1 - core), (keep_o, keep_rows, core)):
        taps3 = []
        for tap in range(3):
            moved = shift_rows(own_right, 1 - tap).astype(jnp.bfloat16)
            taps3.append(dot_nn(bt_s[picked, :], moved).astype(jnp.bfloat16))
        for shard in range(2):
            cols = slice(shard * part, (shard + 1) * part)
            target[shard, base : base + HALF, :part] = taps3[0][:, cols]
            target[shard, base : base + HALF, part:] = taps3[1][:, cols]
            target[shard, base + HALF : base + 2 * HALF, :part] = taps3[2][:, cols]
            target[shard, base + HALF : base + 2 * HALF, part:] = jnp.zeros(
                (HALF, part), jnp.bfloat16
            )
            cols_here = inner // 4
            for piece in range(cols_here // LANES):
                lanes = pl.ds(
                    pl.multiple_of(
                        shard * (inner // 2) + side * cols_here + piece * LANES, LANES
                    ),
                    LANES,
                )
                row = base + HALF + piece * 16
                target[shard, row : row + 16, part:] = small[:, lanes].astype(jnp.bfloat16)
            row = base + HALF + 4 * 16
            for piece in range(4):
                lanes = slice(piece * LANES, (piece + 1) * LANES)
                both = jnp.concatenate(
                    [gain_ffn_g[:, lanes], gain_attn_g[:, lanes], jnp.zeros((14, LANES), jnp.float32)],
                    axis=0,
                )
                target[shard, row : row + 16, part:] = both.astype(jnp.bfloat16)
                row += 16


def join_back_kernel(
    info, gleft, gright, resid_one, grad_two, gain_branch, w_left, w_right, got, part_w,
    grad_one_o, ggain_o, wl_s, wr_s, sems,
):
    core, length = info[0], info[2]
    loader = Loader(sems)
    load_left(loader, w_left, got, part_w, core, wl_s)
    load_right(loader, w_right, got, part_w, core, wr_s)
    loader.go(core)
    ext = gright.shape[0]
    rows = ext - 2 * EDGE
    own = slice(0, rows)
    loader.wait()
    grad_in = jnp.zeros((rows, resid_one.shape[1]), jnp.float32)
    for index in range(wl_s.shape[0]):
        grad_in = grad_in + dot_nt(gleft[index], wl_s[index])
    part = wr_s.shape[3]
    for tap in range(wr_s.shape[1]):
        product = dot_nt(gright[:, :part], wr_s[0, tap]) + dot_nt(gright[:, part:], wr_s[1, tap])
        grad_in = grad_in + shift_rows(product, 1 - tap)[own]
    grad_in = grad_in * row_mask(core, length, ext, LANES)[own, :1]
    unit, inv = row_stats(resid_one[own])
    ggain_o[...] = jnp.sum(grad_in * unit, axis=0, keepdims=True)
    grad_one_o[...] = grad_two[...] + norm_grad(grad_in, unit, inv, gain_branch[...])


def glu_back_kernel(
    info, grad_one, gain_branch_row, gain_glu, block, moved, glu_in, value, sig, w_value, w_gate,
    got, part_w,
    gin_o, send_o, keep_o,
    wv_s, wg_s, x_s, n_s, git_s, sems,
):
    core, member = info[0], info[1]
    loader = Loader(sems)
    load_pair(loader, w_value, got, part_w, 0, core, wv_s, (member, 1 - member))
    load_pair(loader, w_gate, got, part_w, 1, core, wg_s, (member, 1 - member))
    loader.go(core)
    rows = grad_one.shape[0]
    own = slice(0, rows)

    @pl.when(core == member)
    def _():
        load_tiles(block, n_s)

    @pl.when(core != member)
    def _():
        load_tiles(moved, n_s)

    gather_rows(n_s, x_s)
    git_s[...] = turned(glu_in[own])
    loader.wait()
    grad_glu = grad_one[...].astype(jnp.bfloat16).astype(jnp.float32)
    keep_rows = pl.ds(pl.multiple_of(core * HALF, HALF), HALF)
    send_rows = pl.ds(pl.multiple_of((1 - core) * HALF, HALF), HALF)
    grad_norm = jnp.zeros(grad_one.shape, jnp.float32)
    for half in range(2):
        cols = slice(half * HALF, (half + 1) * HALF)
        sig_f = sig[own, cols].astype(jnp.float32)
        grad_here = grad_glu[:, cols] * sig_f
        grad_value = grad_here.astype(jnp.bfloat16)
        grad_gate = (grad_here * value[own, cols].astype(jnp.float32) * (1.0 - sig_f)).astype(
            jnp.bfloat16
        )
        slot = jnp.where(member == half, 0, 1)
        send_o[slot, :HALF] = dot_nn(git_s[send_rows], grad_value).astype(jnp.bfloat16)
        keep_o[slot, :HALF] = dot_nn(git_s[keep_rows], grad_value).astype(jnp.bfloat16)
        send_o[slot, HALF : 2 * HALF] = dot_nn(git_s[send_rows], grad_gate).astype(jnp.bfloat16)
        keep_o[slot, HALF : 2 * HALF] = dot_nn(git_s[keep_rows], grad_gate).astype(jnp.bfloat16)
        grad_norm = grad_norm + dot_nt(grad_value, wv_s[half]) + dot_nt(grad_gate, wg_s[half])
    unit, inv = row_stats(x_s[...])
    gain_glu_row = jnp.sum(grad_norm * unit, axis=0, keepdims=True)
    x_s[...] = grad_one[...] + norm_grad(grad_norm, unit, inv, gain_glu[...])
    scatter_rows(x_s, n_s, gin_o)
    tail = send_o.shape[1] - 2 * HALF
    both = jnp.concatenate(
        [gain_glu_row, gain_branch_row[...], jnp.zeros((14, 2 * HALF), jnp.float32)], axis=0
    )
    both = both.astype(jnp.bfloat16)
    for target in (send_o, keep_o):
        for shard in range(2):
            target[shard, 2 * HALF :] = jnp.zeros((tail, HALF), jnp.bfloat16)
            target[shard, 2 * HALF : 2 * HALF + 16] = both[:, :HALF]
            target[shard, 2 * HALF + 16 : 2 * HALF + 32] = both[:, HALF:]


def over_mp(values):
    return lax.ppermute(values, "mp", [(0, 1), (1, 0)])


def flat_pairs(dp_size, rule):
    pairs = []
    for dp_index in range(dp_size):
        for member in range(2):
            pair, core = dp_index // 2, dp_index % 2
            new_core, new_member = rule(core, member)
            pairs.append((dp_index * 2 + member, (pair * 2 + new_core) * 2 + new_member))
    return pairs


def unpack_kernel(layout, sizes, info, both, far, *rest):
    outs, packed, sems = rest[:-2], rest[-2], rest[-1]
    core, ybit, zpos = info[0], info[3], info[4]
    ys = both.shape[0]
    zs, step = (4, both.shape[3]) if len(both.shape) > 3 else (1, both.shape[1])
    loader = Loader(sems)
    for half in range(2):
        for yside in range(ys):
            for zside in range(zs):
                near, far_bit = zside // 2, zside % 2
                at = (yside ^ ybit, near ^ zpos % 2, far_bit ^ zpos // 2)
                if zs == 1:
                    spot = packed.at[half, pl.ds(yside * step, step)]
                    loader.either(both.at[at[0]], far.at[at[0]], half, spot)
                    continue
                first, base = 0, 0
                for size in sizes:
                    low = max(first, far_bit * step)
                    top = min(first + size // 2, (far_bit + 1) * step)
                    if low < top:
                        source = pl.ds(low - far_bit * step, top - low)
                        spot = base + yside * size + near * (size // 2) + low - first
                        loader.either(
                            both.at[at].at[source],
                            far.at[at].at[source],
                            half,
                            packed.at[half, pl.ds(spot, top - low)],
                        )
                    first += size // 2
                    base += 2 * size
    loader.go(core)
    loader.wait()
    layout(packed, outs)


def layout_ffn(packed, outs):
    w_in, w_back, w_out = outs
    blocks = w_in.shape[1] // HALF
    base = blocks * HALF
    for half in range(2):
        side = slice(half * HALF, (half + 1) * HALF)
        for block in range(blocks):
            at = block * HALF
            w_in[side, block * HALF : (block + 1) * HALF] = as_f32(packed[half, at : at + HALF])
        w_back[:, side] = as_f32(packed[half, base : base + w_back.shape[0]])
        last = base + w_back.shape[0]
        w_out[:, side] = as_f32(packed[half, last : last + w_out.shape[0]])


def layout_attn(packed, outs):
    w_qkv, w_point = outs
    for half in range(2):
        for index in range(3):
            at = index * HALF
            w_qkv[index, half * HALF : (half + 1) * HALF] = as_f32(packed[half, at : at + HALF])
        at = 3 * HALF
        w_point[half * 2 * HALF : (half + 1) * 2 * HALF] = as_f32(packed[half, at : at + 2 * HALF])


def layout_branch(packed, outs):
    w_left, w_right, taps, gain, late_ffn, late_attn = outs
    count = taps.shape[0]
    blocks = w_left.shape[1] // HALF
    base = blocks * HALF
    for half in range(2):
        side = slice(half * HALF, (half + 1) * HALF)
        for block in range(blocks):
            w_left[side, block * HALF : (block + 1) * HALF] = as_f32(
                packed[half, block * HALF : (block + 1) * HALF]
            )
        w_right[0, side] = as_f32(packed[half, base : base + HALF, :LANES])
        w_right[1, side] = as_f32(packed[half, base : base + HALF, LANES:])
        w_right[2, side] = as_f32(packed[half, base + HALF : base + 2 * HALF, :LANES])
        for piece in range(4):
            row = base + HALF + piece * 16
            at = half * 4 * LANES + piece * LANES
            rows = as_f32(packed[half, row : row + 16, LANES:])
            taps[:, at : at + LANES] = rows[:count]
            gain[:, at : at + LANES] = rows[count : count + 1]
            row += 4 * 16
            rows = as_f32(packed[half, row : row + 16, LANES:])
            late_ffn[:, piece * LANES : (piece + 1) * LANES] = rows[:1]
            late_attn[:, piece * LANES : (piece + 1) * LANES] = rows[1:2]


def layout_glu(packed, outs):
    w_value, w_gate, late_glu, late_branch = outs
    for half in range(2):
        side = slice(half * HALF, (half + 1) * HALF)
        w_value[side] = as_f32(packed[half, :HALF])
        w_gate[side] = as_f32(packed[half, HALF : 2 * HALF])
        rows = as_f32(packed[0, 2 * HALF + 16 * half : 2 * HALF + 16 * (half + 1)])
        late_glu[:, side] = rows[:1]
        late_branch[:, side] = rows[1:2]


MEGA = 1024 * 1024
SPARE = 8
ALL_VMEM = 62 * MEGA


def call(body, name, ins, outs, scratch, flops, copies=0, room=None, cost=10**11):
    spaces = {"s": pltpu.SMEM, "v": pltpu.VMEM, "h": pltpu.HBM}
    shapes = [jax.ShapeDtypeStruct(shape, dtype) for shape, dtype in outs]
    held = [(a.shape, a.dtype) for a, place in ins if place == "v"] + outs + scratch
    held = sum(math.prod(shape) * jnp.dtype(dtype).itemsize for shape, dtype in held)
    scratch = [pltpu.VMEM(shape, dtype) for shape, dtype in scratch]
    if copies:
        scratch.append(pltpu.SemaphoreType.DMA((copies,)))
    return pl.pallas_call(
        body,
        out_shape=shapes,
        in_specs=[pl.BlockSpec(memory_space=spaces[place]) for _, place in ins],
        out_specs=[pl.BlockSpec(memory_space=pltpu.VMEM) for _ in shapes],
        scratch_shapes=scratch,
        name=name,
        compiler_params=pltpu.CompilerParams(vmem_limit_bytes=room or held + SPARE * MEGA),
        cost_estimate=pl.CostEstimate(flops=cost, bytes_accessed=10**6, transcendentals=0),
    )(*[array for array, _ in ins])


def dp_xor(values, bits):
    size = lax.axis_size("dp")
    return lax.ppermute(values, "dp", [(index, index ^ bits) for index in range(size)])


def over_x_and_y(values):
    pairs = []
    for dp_index in range(lax.axis_size("dp")):
        for member in range(2):
            pairs.append((dp_index * 2 + member, (dp_index ^ 2) * 2 + 1 - member))
    return lax.ppermute(values, ("dp", "mp"), pairs)


def later(values, *first):
    return lax.optimization_barrier((values, first))[0]


class Sums:
    def __init__(self, send, keep, ybit):
        self.keep, self.ybit = keep, ybit
        self.recv = dp_xor(send, 1)

    def over_xy(self, *first):
        recv, keep = later((self.recv, self.keep), *first)
        half = keep.shape[1] // 2

        def piece(shard, bit):
            at = bit * half
            cut = lambda values: as_f32(lax.dynamic_slice_in_dim(values[shard], at, half, axis=0))
            return (cut(keep) + cut(recv)).astype(jnp.bfloat16)

        self.kept = piece(0, self.ybit)
        gone = [piece(1, self.ybit), piece(0, 1 - self.ybit), piece(1, 1 - self.ybit)]
        self.got = [over_mp(gone[0]), dp_xor(gone[1], 2), over_x_and_y(gone[2])]
        return gone

    def over_x(self, *first):
        recv, keep = later((self.recv, self.keep), *first)
        other = (as_f32(keep[1]) + as_f32(recv[1])).astype(jnp.bfloat16)
        self.kept = as_f32(keep[0]) + as_f32(recv[0])
        self.got = over_mp(other)
        return [other]

    def over_y(self, *first):
        got, kept = later((self.got, self.kept), *first)
        mine = (kept + as_f32(got)).astype(jnp.bfloat16)
        half = mine.shape[0] // 2
        gone = lax.dynamic_slice_in_dim(mine, (1 - self.ybit) * half, half, axis=0)
        self.kept = lax.dynamic_slice_in_dim(mine, self.ybit * half, half, axis=0)
        self.got = dp_xor(gone, 2)
        return [gone]

    def last_quarter(self, *first):
        got, kept = later((self.got, self.kept), *first)
        return (as_f32(kept) + as_f32(got)).astype(jnp.bfloat16)

    def quarter(self, *first):
        got, kept = later((self.got, self.kept), *first)
        total = as_f32(kept) + as_f32(got[1]) + (as_f32(got[0]) + as_f32(got[2]))
        return total.astype(jnp.bfloat16)


def halve(mine, bit, across):
    half = mine.shape[0] // 2
    kept = lax.dynamic_slice_in_dim(mine, bit * half, half, axis=0)
    gone = lax.dynamic_slice_in_dim(mine, (1 - bit) * half, half, axis=0)
    return gone, (kept, dp_xor(gone, across))


class Rest:
    def __init__(self, zpos):
        self.zpos, self.pairs, self.sizes = zpos, [], []

    def over_z1(self, quarter):
        gone, pair = halve(quarter, self.zpos % 2, 4)
        self.pairs.append(pair)
        self.sizes.append(quarter.shape[0])
        return [gone]

    def over_z2(self, *first):
        pairs = later(self.pairs, *first)
        mine = [(as_f32(kept) + as_f32(got)).astype(jnp.bfloat16) for kept, got in pairs]
        gone, (self.kept, self.got) = halve(jnp.concatenate(mine, axis=0), self.zpos // 2, 8)
        return [gone]

    def back_z2(self, *first):
        got, kept = later((self.got, self.kept), *first)
        self.mine = (as_f32(kept) + as_f32(got)).astype(jnp.bfloat16)
        self.got = dp_xor(self.mine, 8)
        return [self.mine]

    def back_z1(self, *first):
        return self.double(4, *first)

    def double(self, across, *first):
        got, mine = later((self.got, self.mine), *first)
        self.mine = jnp.stack([mine, got])
        self.got = dp_xor(self.mine, across)
        return [self.mine]

    def back_y(self, *first):
        return self.double(2, *first)

    def back_core(self, *first):
        self.got, mine = later((self.got, self.mine), *first)
        self.both = jnp.stack([mine, self.got])
        self.far = dp_xor(self.both, 1)
        return [self.both]


class Short(Rest):
    def along_z1(self, quarter):
        self.sizes.append(quarter.shape[0])
        self.mine, self.got = quarter, dp_xor(quarter, 4)
        return [quarter]

    def along_z2(self, *first):
        got, mine = later((self.got, self.mine), *first)
        self.mine = (as_f32(mine) + as_f32(got)).astype(jnp.bfloat16)
        self.got = dp_xor(self.mine, 8)
        return [self.mine]

    def back_y(self, *first):
        got, mine = later((self.got, self.mine), *first)
        self.mine = (as_f32(mine) + as_f32(got)).astype(jnp.bfloat16)
        self.got = dp_xor(self.mine, 2)
        return [self.mine]


def unpack(layout, info, sums, outs):
    ys, cols = 2, sums.both.shape[-1]
    zs, part = (4, sums.both.shape[3]) if sums.both.ndim > 3 else (1, sums.both.shape[1])
    return call(
        functools.partial(unpack_kernel, layout, sums.sizes),
        "unpack_" + layout.__name__,
        [(info, "s"), (sums.both, "h"), (sums.far, "h")],
        [(shape, jnp.float32) for shape in outs],
        [((2, ys * zs * part, cols), jnp.bfloat16)],
        1e6,
        4 * ys * (zs + len(sums.sizes)),
    )


def paired(
    inputs, lengths, gain_glu, w_value, w_gate, gain_branch, w_left, w_right, gain_mid, w_depth,
    w_point, gain_attn, w_qkv, w_out, gain_ffn, w_in, w_back, cotangent,
):
    low, full = jnp.bfloat16, jnp.float32
    member = lax.axis_index("mp")
    place = lax.axis_index("dp")
    core, ybit, zpos = place % 2, (place // 2) % 2, place // 4
    rows, width = inputs.shape[1:]
    ext = rows + 2 * EDGE
    inner = 2 * w_left.shape[1]
    chunks = inner // HALF
    right_cols = 2 * w_right.shape[2]
    sep_width = w_point.shape[1]
    heads = 2 * w_qkv.shape[2] // HEAD_DIM
    row = lambda gain: gain.reshape(1, -1)

    block = inputs[0]
    edge = jnp.where(member == 0, block[rows - EDGE :], block[:EDGE])
    size_code = jnp.stack([lengths[0] // 32, lengths[0] % 32]).astype(low)
    code_rows = jnp.broadcast_to(jnp.repeat(size_code, EDGE // 2)[:, None], (EDGE, width))
    edge = jnp.concatenate([edge, code_rows], axis=0)
    edge = lax.ppermute(
        edge, ("dp", "mp"), flat_pairs(lax.axis_size("dp"), lambda c, m: (1 - m, c))
    )
    code = as_f32(edge[EDGE:, 0])
    length = (code[0] * 32 + code[EDGE // 2]).astype(jnp.int32)
    edge = edge[:EDGE]
    swap = [p for p in flat_pairs(lax.axis_size("dp"), lambda c, m: (m, c)) if p[0] != p[1]]
    moved = lax.ppermute(block, ("dp", "mp"), swap)
    info = jnp.stack([core, member, length, ybit, zpos]).astype(jnp.int32)

    v = lambda *arrays: [(array, "v") for array in arrays]
    h = lambda *arrays: [(array, "h") for array in arrays]
    pack = jnp.concatenate([w_depth, gain_mid[None]], axis=0)
    got0 = over_mp(jnp.where(core == 0, w_value, w_gate))
    blocks = w_left.shape[1] // HALF
    bundle1, bundle2, bundle3 = call(
        bundle_kernel, "bundle",
        [(jnp.stack([core, member]).astype(jnp.int32), "s")]
        + h(w_left, w_right, w_point) + v(w_depth, row(gain_mid)) + h(w_qkv, w_out, w_in, w_back),
        [((blocks * (width + 16), HALF), low)] + [((3 * width, HALF), low)] * 2,
        [], 1, 16, ALL_VMEM,
    )
    got1 = over_mp(bundle1)
    part0 = dp_xor(got0, 1)
    cot = cotangent[0]
    cot_moved = lax.ppermute(cot, ("dp", "mp"), swap)

    where = [(info, "s")]
    macs = 2.0 * rows * width
    cot, resid_one, branch_in, glu_in, value, sig = call(
        glu_kernel, "glu",
        where + v(block, moved, cot, cot_moved, edge, row(gain_glu), row(gain_branch))
        + h(w_value, w_gate, got0, part0),
        [((rows, width), low), ((ext, width), full)] + [((ext, width), low)] * 4,
        [((ext, width), full), ((rows, width), full), ((width // LANES, rows, LANES), full)]
        + [((2,) + w_value.shape, low)] * 2,
        macs * width * 2, 8,
    )
    left_own, right_own, mid_own, sums_own = call(
        branch_own_kernel, "branch_own",
        where + v(branch_in) + h(w_left) + v(w_right),
        [
            ((chunks // 2, ext, HALF), low), ((ext, right_cols // 2), full),
            ((chunks // 2, ext, HALF), full), ((2, ext, LANES), full),
        ],
        [((chunks // 2, width, HALF), low)],
        1, chunks // 2,
    )
    got1 = later(got1, sums_own)
    part1 = dp_xor(got1, 1)
    got2 = over_mp(later(bundle2, got1))
    got3 = over_mp(later(bundle3, got1))
    resid_two, left_pre, right_pre, stats, depth = call(
        branch_kernel, "branch",
        where
        + v(branch_in, resid_one, pack, left_own, right_own, mid_own, sums_own)
        + h(w_point, got1, part1),
        [
            ((rows, width), full), ((chunks, ext, HALF), low), ((ext, right_cols), full),
            ((ext, LANES), full), ((chunks, rows, HALF), low),
        ],
        [
            ((chunks // 2, width, HALF), low), (w_right.shape, low), ((2,) + w_point.shape, low),
            ((4, 16, HALF), low), ((16, inner), full), ((chunks, ext, HALF), full),
            ((rows + 64, HALF), full), ((2, ext, LANES), full), ((rows, sep_width), full),
        ],
        1, 20,
    )
    got2 = later(got2, resid_two)
    part2 = dp_xor(got2, 1)
    attn_in, kv_own = call(
        kv_kernel, "keys_values",
        where + v(resid_two, row(gain_attn)) + h(w_qkv, got2, part2),
        [((rows, width), low), ((rows, 2 * width), low)],
        [((2, 2) + w_qkv.shape[1:], low)],
        macs * width * 2, 8,
    )
    (queries,) = call(
        query_kernel, "queries",
        where + v(attn_in) + h(w_qkv, got2, part2),
        [((rows, width), low)],
        [((2, 1) + w_qkv.shape[1:], low)],
        macs * width, 4,
    )
    kv_far = dp_xor(kv_own, 1)
    context0, lse0, context1, lse1 = call(
        attend_kernel, "attend",
        where + v(queries, kv_own, kv_far),
        [((rows, width // 2), low), ((heads // 2, rows), full)] * 2,
        [((2 * rows, LANES), full)],
        macs * 8000,
    )
    part3 = dp_xor(later(got3, lse1), 1)
    r_ffn = 2 * w_in.shape[1] + w_out.shape[0]
    out_rows, grad_three, grad_ctx, ggain_ffn, send, keep = call(
        ffn_kernel, "ffn",
        where + v(resid_two, context0, context1, cot, row(gain_ffn))
        + h(w_out, w_in, w_back, got2, part2, got3, part3),
        [
            ((rows, width), low), ((rows, width), full), ((rows, width), low), ((1, width), full),
            ((2, r_ffn, HALF), low), ((2, r_ffn, HALF), low),
        ],
        [
            ((2,) + w_out.shape, low), ((chunks, width, HALF), low), ((2,) + w_back.shape, low),
            ((rows, width), low), ((width, rows), low), ((rows, width), low), ((rows, width), full),
            ((rows, width), full), ((width, rows), low), ((width // LANES, rows, LANES), full),
        ],
        macs * 16000, 24, 38 * MEGA,
    )
    ffn_sums = Sums(send, keep, ybit)
    swapped_out = lax.ppermute(out_rows, ("dp", "mp"), swap)

    seen = v(context0, context1, grad_ctx, lse0, lse1)
    grad_q, grad_far = call(
        functools.partial(attend_back_kernel, 1), "attend_back_far",
        where + v(queries, kv_far) + seen,
        [((rows, width), full), ((rows, 2 * width), low)],
        [((rows, LANES), full)] * 3, 1,
    )
    recv = dp_xor(grad_far, 1)
    sent = ffn_sums.over_xy(grad_q)
    out_rows, swapped_out = later((out_rows, swapped_out), *sent)
    outputs = jnp.where(member == core, out_rows, swapped_out)
    sent.append(outputs)
    grad_q, grad_own = call(
        functools.partial(attend_back_kernel, 0), "attend_back_own",
        [(later(info, *sent), "s")] + v(queries, kv_own) + seen + v(grad_q),
        [((rows, width), low), ((rows, 2 * width), full)],
        [((rows, LANES), full)] * 3, 1,
    )
    grad_two, grad_sep, sep_edge, ggain_attn, send, keep = call(
        qkv_back_kernel, "qkv_back",
        where
        + v(grad_q, grad_own, recv, attn_in, resid_two, grad_three, row(gain_attn))
        + h(w_qkv, got2, part2),
        [
            ((rows, width), full), ((rows, sep_width), low), ((EDGE, sep_width), low),
            ((1, width), full),
        ]
        + [((2, 3 * HALF, HALF), low)] * 2,
        [
            ((2,) + w_qkv.shape, low), ((width, rows), low),
            ((sep_width // LANES, rows, LANES), full),
        ],
        1, 12,
    )
    sep_edge = dp_xor(sep_edge, 1)
    send, keep = call(
        point_kernel, "point_back",
        where + v(grad_sep, depth, send, keep),
        [((2, 5 * HALF, HALF), low)] * 2, [], macs * 1000,
    )
    attn_sums = Sums(send, keep, ybit)
    unit, scaled, mid_sums, small = call(
        depth_back_kernel, "depth_back",
        where
        + v(grad_sep, sep_edge, left_pre, right_pre, stats, pack)
        + h(w_point, got1, part1),
        [
            ((chunks, ext, HALF), low), ((chunks, ext, HALF), low), ((2, ext, LANES), full),
            ((16, inner), full),
        ],
        [
            ((2,) + w_point.shape, low), ((4, 16, HALF), low), ((16, inner), full),
            ((ext, sep_width), low),
            ((2, rows + 64, LANES), full), ((2, rows + 64, LANES), full),
            ((2, 4 * EDGE, LANES), full), ((ext, HALF), full), ((ext, HALF), full),
            ((3, ext, LANES), full),
        ],
        macs * 8000, 8,
    )
    ffn_rest = Rest(zpos)
    sent = ffn_rest.over_z1(ffn_sums.quarter(mid_sums))
    sent += attn_sums.over_x(*sent)
    r_branch = inner // 2 + 2 * HALF
    grad_left, grad_right, send, keep = call(
        branch_back_kernel, "branch_back",
        [(later(info, *sent), "s")]
        + v(
            unit, scaled, mid_sums, small, left_pre, right_pre, stats, branch_in, ggain_ffn,
            ggain_attn,
        ),
        [
            ((chunks, rows, HALF), low), ((ext, right_cols), low),
            ((2, r_branch, HALF), low), ((2, r_branch, HALF), low),
        ],
        [((3, ext, LANES), full), ((ext, right_cols), full), ((width, ext), low)],
        macs * 4000,
    )
    branch_sums = Sums(send, keep, ybit)
    sent = ffn_rest.over_z2(grad_left)
    sent += attn_sums.over_y(*sent)
    grad_one, ggain_branch = call(
        join_back_kernel, "join_back",
        [(later(info, *sent), "s")]
        + v(grad_left, grad_right, resid_one, grad_two, row(gain_branch))
        + h(w_left, w_right, got1, part1),
        [((rows, width), full), ((1, width), full)],
        [((chunks, width, HALF), low), ((2,) + w_right.shape, low)],
        macs * 4000, 12,
    )
    sent = ffn_rest.back_z2(grad_one)
    sent += branch_sums.over_xy(*sent)
    attn_rest = Rest(zpos)
    grad_in, send, keep = call(
        glu_back_kernel, "glu_back",
        [(later(info, *sent), "s")]
        + v(grad_one, ggain_branch, row(gain_glu), block, moved, glu_in, value, sig)
        + h(w_value, w_gate, got0, part0),
        [((rows, width), low), ((2, 640, HALF), low), ((2, 640, HALF), low)],
        [
            ((2,) + w_value.shape, low), ((2,) + w_gate.shape, low), ((rows, width), full),
            ((width // LANES, rows, LANES), full), ((width, rows), low),
        ],
        macs * 3000, 4,
    )
    glu_sums = Sums(send, keep, ybit)
    branch_rest, glu_rest = Rest(zpos), Short(zpos)
    sent = attn_rest.over_z1(attn_sums.last_quarter(grad_in))
    sent = ffn_rest.back_z1(*sent)
    sent = branch_rest.over_z1(branch_sums.quarter(*sent))
    sent = glu_sums.over_x(*sent)
    swapped_in = lax.ppermute(later(grad_in, *sent), ("dp", "mp"), swap)
    sent = attn_rest.over_z2(*sent)
    sent = branch_rest.over_z2(*sent)
    sent = glu_sums.over_y(*sent)
    sent = ffn_rest.back_y(*sent)
    sent = attn_rest.back_z2(*sent)
    sent = branch_rest.back_z2(*sent)
    sent = glu_rest.along_z1(glu_sums.last_quarter(*sent))
    grad_in, swapped_in = later((grad_in, swapped_in), *sent)
    grad_inputs = jnp.where(member == core, grad_in, swapped_in)
    sent = branch_rest.back_z1(grad_inputs)
    sent = glu_rest.along_z2(*sent)
    sent = branch_rest.back_y(*sent)
    sent = attn_rest.back_z1(*sent)
    sent = ffn_rest.back_core(*sent)
    sent = glu_rest.back_y(*sent)
    sent = attn_rest.back_y(*sent)
    sent = branch_rest.back_core(*sent)
    g_left, g_right, g_taps, g_mid, g_ffn_gain, g_attn_gain = unpack(
        layout_branch, later(info, *sent), branch_rest,
        [
            w_left.shape, w_right.shape, w_depth.shape, (1, inner // 2), (1, width), (1, width),
        ],
    )
    sent = glu_rest.back_core(g_left)
    g_in, g_back, g_out = unpack(
        layout_ffn, later(info, *sent), ffn_rest, [w_in.shape, w_back.shape, w_out.shape]
    )
    sent = attn_rest.back_core(g_in)
    g_value, g_gate, g_glu_gain, g_branch_gain = unpack(
        layout_glu, later(info, *sent), glu_rest,
        [w_value.shape, w_gate.shape, (1, width), (1, width)],
    )
    g_qkv, g_point = unpack(
        layout_attn, later(info, g_value), attn_rest, [w_qkv.shape, w_point.shape]
    )
    flat = lambda gain: gain.reshape(-1)
    return (
        outputs[None],
        grad_inputs[None],
        flat(g_glu_gain),
        g_value,
        g_gate,
        flat(g_branch_gain),
        g_left,
        g_right,
        flat(g_mid),
        g_taps,
        g_point,
        flat(g_attn_gain),
        g_qkv,
        g_out,
        flat(g_ffn_gain),
        g_in,
        g_back,
    )


def solution(mesh):
    placed = (
        P("dp", "mp", None),
        P("dp"),
        P(),
        P(None, "mp"),
        P(None, "mp"),
        P(),
        P(None, "mp"),
        P(None, None, "mp"),
        P("mp"),
        P(None, "mp"),
        P("mp", None),
        P(),
        P(None, None, "mp"),
        P("mp", None),
        P(),
        P(None, "mp"),
        P("mp", None),
        P("dp", "mp", None),
    )
    fast = mesh.shape["mp"] == 2 and mesh.shape["dp"] == 16
    return jax.shard_map(
        paired if fast else local,
        mesh=mesh,
        in_specs=placed,
        out_specs=(
            P("dp", "mp", None),
            P("dp", "mp", None),
            P(),
            P(None, "mp"),
            P(None, "mp"),
            P(),
            P(None, "mp"),
            P(None, None, "mp"),
            P("mp"),
            P(None, "mp"),
            P("mp", None),
            P(),
            P(None, None, "mp"),
            P("mp", None),
            P(),
            P(None, "mp"),
            P("mp", None),
        ),
        check_vma=False,
    )
```

```python
import functools
import math

import jax
import jax.numpy as jnp
from jax import lax
from jax.experimental import pallas as pl
from jax.experimental.pallas import tpu as pltpu
from jax.sharding import PartitionSpec as P

FF = 2048
HEAD_DIM = 64
EDGE = 16


epsilon = 1e-06
negative_big = -1e30


def matmul(left_side, right_side):
    return jnp.dot(left_side, right_side, preferred_element_type=jnp.float32)


def contract_rows(left_side, right_side):
    return lax.dot_general(
        left_side, right_side, (((0,), (0,)), ((), ())), preferred_element_type=jnp.float32
    )


def contract_cols(left_side, right_side):
    return lax.dot_general(
        left_side, right_side, (((1,), (1,)), ((), ())), preferred_element_type=jnp.float32
    )


def spread_rows(pieces):
    return lax.all_gather(pieces, "mp", axis=1, tiled=True)


def collect_rows(partial_value):
    return lax.psum_scatter(
        partial_value.astype(jnp.bfloat16), "mp", scatter_dimension=1, tiled=True
    ).astype(jnp.float32)


def channel_sums(former, latter):
    return lax.psum((jnp.sum(former, axis=-1), jnp.sum(latter, axis=-1)), "mp")


def normalize(values, gain_vec):
    centre = values - jnp.mean(values, axis=-1, keepdims=True)
    scale_inv = lax.rsqrt(jnp.mean(centre * centre, axis=-1, keepdims=True) + epsilon)
    unit_rows = centre * scale_inv
    return (unit_rows * gain_vec, unit_rows, scale_inv)


def normalize_back(grad_out, unit_rows, scale_inv, gain_vec):
    scaled = grad_out * gain_vec
    mean_one = jnp.mean(scaled, axis=-1, keepdims=True)
    mean_two = jnp.mean(scaled * unit_rows, axis=-1, keepdims=True)
    grad_in = scale_inv * (scaled - mean_one - unit_rows * mean_two)
    return (grad_in, jnp.sum(grad_out * unit_rows, axis=(0, 1)))


def silu_slope(values):
    sigmoid_part = jax.nn.sigmoid(values)
    return sigmoid_part * (1.0 + values * (1.0 - sigmoid_part))


def shifted(values, offset):
    if offset == 0:
        return values
    margin = abs(offset)
    seq_len = values.shape[1]
    filler = jnp.zeros(values.shape[:1] + (margin,) + values.shape[2:], values.dtype)
    padded = jnp.concatenate([filler, values, filler], axis=1)
    return lax.slice_in_dim(padded, margin + offset, margin + offset + seq_len, axis=1)


def place_right(right_vals, stride):
    filler = jnp.zeros(right_vals.shape + (stride - 1,), right_vals.dtype)
    joined = jnp.concatenate([right_vals[..., None], filler], axis=-1)
    return joined.reshape(right_vals.shape[:-1] + (right_vals.shape[-1] * stride,))


def attend_forward(queries, key_vecs, value_vecs, key_valid, block_rows, score_scale):
    contexts = []
    log_parts = []
    for row_start in range(0, queries.shape[0], block_rows):
        query_rows = queries[row_start : row_start + block_rows]
        scores = (
            jnp.einsum("qhd,khd->hqk", query_rows, key_vecs, preferred_element_type=jnp.float32)
            * score_scale
        )
        scores = jnp.where(key_valid[None, None, :], scores, negative_big)
        row_max = jnp.max(scores, axis=-1, keepdims=True)
        weights_exp = jnp.exp(scores - row_max)
        row_total = jnp.sum(weights_exp, axis=-1, keepdims=True)
        probability = (weights_exp / row_total).astype(jnp.bfloat16)
        contexts.append(
            jnp.einsum("hqk,khd->qhd", probability, value_vecs, preferred_element_type=jnp.float32)
        )
        log_parts.append((row_max + jnp.log(row_total))[..., 0])
    return (jnp.concatenate(contexts, axis=0), jnp.concatenate(log_parts, axis=1))


def attend_back(
    queries, key_vecs, value_vecs, key_valid, log_sums, grad_context, block_rows, score_scale
):
    grad_queries = []
    grad_keys = jnp.zeros(key_vecs.shape, jnp.float32)
    grad_values = jnp.zeros(value_vecs.shape, jnp.float32)
    for row_start in range(0, queries.shape[0], block_rows):
        query_rows = queries[row_start : row_start + block_rows]
        grad_rows = grad_context[row_start : row_start + block_rows]
        log_rows = log_sums[:, row_start : row_start + block_rows]
        scores = (
            jnp.einsum("qhd,khd->hqk", query_rows, key_vecs, preferred_element_type=jnp.float32)
            * score_scale
        )
        scores = jnp.where(key_valid[None, None, :], scores, negative_big)
        probability = jnp.exp(scores - log_rows[..., None])
        grad_prob = jnp.einsum(
            "qhd,khd->hqk", grad_rows, value_vecs, preferred_element_type=jnp.float32
        )
        row_dot = jnp.sum(probability * grad_prob, axis=-1, keepdims=True)
        grad_scores = (probability * (grad_prob - row_dot)).astype(jnp.bfloat16)
        grad_queries.append(
            jnp.einsum("hqk,khd->qhd", grad_scores, key_vecs, preferred_element_type=jnp.float32)
            * score_scale
        )
        grad_keys = (
            grad_keys
            + jnp.einsum(
                "hqk,qhd->khd", grad_scores, query_rows, preferred_element_type=jnp.float32
            )
            * score_scale
        )
        grad_values = grad_values + jnp.einsum(
            "hqk,qhd->khd",
            probability.astype(jnp.bfloat16),
            grad_rows,
            preferred_element_type=jnp.float32,
        )
    grad_query_all = jnp.concatenate(grad_queries, axis=0)
    return (grad_query_all.astype(jnp.bfloat16), grad_keys, grad_values)


def split_pass(
    inputs,
    lengths,
    gain_glu,
    w_value,
    w_gate,
    gain_branch,
    w_left,
    w_right,
    gain_mid,
    w_depth,
    w_point,
    gain_attn,
    w_qkv,
    w_out,
    gain_ffn,
    w_in,
    w_back,
    cotangent,
):
    seqs_here, local_len, model_width = inputs.shape
    group_size = lax.axis_size("mp")
    member = lax.axis_index("mp")
    seq_len = local_len * group_size
    group_rows = seqs_here * seq_len
    positions = lax.broadcasted_iota(jnp.int32, (seqs_here, seq_len), 1)
    key_valid = positions < lengths[:, None]
    valid_full = key_valid.astype(jnp.float32)
    valid_own = lax.dynamic_slice_in_dim(valid_full, member * local_len, local_len, axis=1)
    inner_cols = w_left.shape[1]
    right_cols = w_right.shape[2]
    stride = inner_cols // right_cols
    conv_taps = w_right.shape[0]
    sep_taps = w_depth.shape[0]
    sep_width = w_point.shape[1]
    head_cols = w_qkv.shape[2]
    heads_here = head_cols // HEAD_DIM
    score_scale = 1.0 / math.sqrt(HEAD_DIM)
    block_rows = min(512, seq_len)
    group_shape = (seqs_here, seq_len, model_width)
    depth_taps = w_depth.astype(jnp.float32)
    gain_mid_f = gain_mid.astype(jnp.float32)

    def branch_inner(gathered):
        flat_rows = gathered.reshape(group_rows, model_width)
        left_pre = matmul(flat_rows, w_left).reshape(seqs_here, seq_len, inner_cols)
        right_pre = jnp.zeros((group_rows, right_cols), jnp.float32)
        for tap_index in range(conv_taps):
            moved = shifted(gathered, tap_index - conv_taps // 2).reshape(group_rows, model_width)
            right_pre = right_pre + matmul(moved, w_right[tap_index])
        right_pre = right_pre.reshape(seqs_here, seq_len, right_cols)
        mid = jax.nn.silu(left_pre) + place_right(jax.nn.silu(right_pre), stride)
        return (left_pre, right_pre, mid)

    def depth_mix(depth_in):
        depth = jnp.zeros(depth_in.shape, jnp.float32)
        for tap_index in range(sep_taps):
            depth = depth + shifted(depth_in, tap_index - sep_taps // 2) * depth_taps[tap_index]
        return depth.astype(jnp.bfloat16)

    def project_qkv(gathered):
        flat_rows = gathered.reshape(group_rows, model_width)
        joined = jnp.einsum("td,kdc->ktc", flat_rows, w_qkv, preferred_element_type=jnp.float32)
        return joined.astype(jnp.bfloat16).reshape(3, seqs_here, seq_len, heads_here, HEAD_DIM)

    def forward_one(pieces):
        return attend_forward(pieces[0], pieces[1], pieces[2], pieces[3], block_rows, score_scale)

    def backward_one(pieces):
        return attend_back(
            pieces[0],
            pieces[1],
            pieces[2],
            pieces[3],
            pieces[4],
            pieces[5],
            block_rows,
            score_scale,
        )

    resid_in = inputs.astype(jnp.float32)
    normed_glu, unit_glu, inv_glu = normalize(resid_in, gain_glu)
    gathered_glu = spread_rows(normed_glu.astype(jnp.bfloat16))
    flat_glu = gathered_glu.reshape(group_rows, model_width)
    value_pre = matmul(flat_glu, w_value)
    gate_sig = jax.nn.sigmoid(matmul(flat_glu, w_gate))
    glu_local = (value_pre * gate_sig).astype(jnp.bfloat16).reshape(seqs_here, seq_len, -1)
    glu_rows = lax.all_to_all(glu_local, "mp", split_axis=1, concat_axis=2, tiled=True)
    resid_one = resid_in + glu_rows.astype(jnp.float32)
    normed_branch, unit_branch, inv_branch = normalize(resid_one, gain_branch)
    gathered_branch = spread_rows((valid_own[..., None] * normed_branch).astype(jnp.bfloat16))
    left_pre, right_pre, mid = branch_inner(gathered_branch)
    mid_sum, mid_square = channel_sums(mid, mid * mid)
    mid_mean = mid_sum / FF
    inv_mid = lax.rsqrt(mid_square / FF - mid_mean * mid_mean + epsilon)
    unit_mid = (mid - mid_mean[..., None]) * inv_mid[..., None]
    depth_in = valid_full[..., None] * unit_mid * gain_mid_f
    depth_low = depth_mix(depth_in)
    sep_part = matmul(depth_low.reshape(group_rows, inner_cols), w_point).reshape(
        seqs_here, seq_len, sep_width
    )
    sep_rows = collect_rows(sep_part)
    resid_two = resid_one + jnp.pad(sep_rows, ((0, 0), (0, 0), (0, model_width - sep_width)))
    normed_attn, unit_attn, inv_attn = normalize(resid_two, gain_attn)
    gathered_attn = spread_rows(normed_attn.astype(jnp.bfloat16))
    qkv_heads = project_qkv(gathered_attn)
    context, log_sums = lax.map(forward_one, (qkv_heads[0], qkv_heads[1], qkv_heads[2], key_valid))
    context_low = context.astype(jnp.bfloat16).reshape(group_rows, head_cols)
    attn_rows = collect_rows(matmul(context_low, w_out).reshape(group_shape))
    resid_three = resid_two + attn_rows
    normed_ffn, unit_ffn, inv_ffn = normalize(resid_three, gain_ffn)
    gathered_ffn = spread_rows(normed_ffn.astype(jnp.bfloat16))
    ffn_flat = gathered_ffn.reshape(group_rows, model_width)
    ffn_pre = matmul(ffn_flat, w_in)
    ffn_hidden = jax.nn.silu(ffn_pre).astype(jnp.bfloat16)
    final_rows = resid_three + collect_rows(matmul(ffn_hidden, w_back).reshape(group_shape))
    outputs = final_rows.astype(jnp.bfloat16)
    cot_full = spread_rows(cotangent).reshape(group_rows, model_width)
    ffn_flat = spread_rows(normed_ffn.astype(jnp.bfloat16)).reshape(group_rows, model_width)
    ffn_pre = matmul(ffn_flat, w_in)
    ffn_hidden = jax.nn.silu(ffn_pre).astype(jnp.bfloat16)
    grad_hidden = contract_cols(cot_full, w_back)
    grad_ffn_pre = (grad_hidden * silu_slope(ffn_pre)).astype(jnp.bfloat16)
    grad_w_back = contract_rows(ffn_hidden, cot_full)
    grad_w_in = contract_rows(ffn_flat, grad_ffn_pre)
    grad_normed_ffn = collect_rows(contract_cols(grad_ffn_pre, w_in).reshape(group_shape))
    grad_resid, grad_gain_ffn = normalize_back(grad_normed_ffn, unit_ffn, inv_ffn, gain_ffn)
    grad_three = cotangent.astype(jnp.float32) + grad_resid
    grad_attn = spread_rows(grad_three.astype(jnp.bfloat16)).reshape(group_rows, model_width)
    gathered_attn = spread_rows(normed_attn.astype(jnp.bfloat16))
    qkv_heads = project_qkv(gathered_attn)
    attn_flat = gathered_attn.reshape(group_rows, model_width)
    grad_w_out = contract_rows(context_low, grad_attn)
    grad_context = contract_cols(grad_attn, w_out).astype(jnp.bfloat16)
    grad_context = grad_context.reshape(seqs_here, seq_len, heads_here, HEAD_DIM)
    grad_q, grad_k, grad_v = lax.map(
        backward_one, (qkv_heads[0], qkv_heads[1], qkv_heads[2], key_valid, log_sums, grad_context)
    )
    grad_qkv = jnp.stack(
        [grad_q, grad_k.astype(jnp.bfloat16), grad_v.astype(jnp.bfloat16)]
    ).reshape(3, group_rows, head_cols)
    grad_w_qkv = jnp.einsum("td,ktc->kdc", attn_flat, grad_qkv, preferred_element_type=jnp.float32)
    grad_attn_in = jnp.einsum("ktc,kdc->td", grad_qkv, w_qkv, preferred_element_type=jnp.float32)
    grad_normed_attn = collect_rows(grad_attn_in.reshape(group_shape))
    grad_resid, grad_gain_attn = normalize_back(grad_normed_attn, unit_attn, inv_attn, gain_attn)
    grad_two = grad_three + grad_resid
    grad_sep = spread_rows(grad_two[..., :sep_width].astype(jnp.bfloat16)).reshape(
        group_rows, sep_width
    )
    gathered_branch = spread_rows((valid_own[..., None] * normed_branch).astype(jnp.bfloat16))
    left_pre, right_pre, mid = branch_inner(gathered_branch)
    unit_mid = (mid - mid_mean[..., None]) * inv_mid[..., None]
    depth_in = valid_full[..., None] * unit_mid * gain_mid_f
    depth_low = depth_mix(depth_in)
    grad_w_point = contract_rows(depth_low.reshape(group_rows, inner_cols), grad_sep)
    grad_depth = contract_cols(grad_sep, w_point).reshape(seqs_here, seq_len, inner_cols)
    grad_depth_in = jnp.zeros(grad_depth.shape, jnp.float32)
    depth_rows = []
    for tap_index in range(sep_taps):
        offset = tap_index - sep_taps // 2
        grad_depth_in = grad_depth_in + shifted(grad_depth, -offset) * depth_taps[tap_index]
        depth_rows.append(jnp.sum(shifted(depth_in, offset) * grad_depth, axis=(0, 1)))
    grad_w_depth = jnp.stack(depth_rows)
    grad_unit = grad_depth_in * valid_full[..., None]
    grad_gain_mid = jnp.sum(grad_unit * unit_mid, axis=(0, 1))
    scaled = grad_unit * gain_mid_f
    sum_one, sum_two = channel_sums(scaled, scaled * unit_mid)
    grad_mid = inv_mid[..., None] * (
        scaled - (sum_one / FF)[..., None] - unit_mid * (sum_two / FF)[..., None]
    )
    grad_left = (
        (grad_mid * silu_slope(left_pre)).astype(jnp.bfloat16).reshape(group_rows, inner_cols)
    )
    grad_right_act = grad_mid.reshape(seqs_here, seq_len, right_cols, stride)[..., 0]
    grad_right = (
        (grad_right_act * silu_slope(right_pre))
        .astype(jnp.bfloat16)
        .reshape(group_rows, right_cols)
    )
    branch_flat = gathered_branch.reshape(group_rows, model_width)
    grad_w_left = contract_rows(branch_flat, grad_left)
    grad_branch_in = contract_cols(grad_left, w_left).reshape(group_shape)
    right_rows = []
    for tap_index in range(conv_taps):
        offset = tap_index - conv_taps // 2
        moved = shifted(gathered_branch, offset).reshape(group_rows, model_width)
        right_rows.append(contract_rows(moved, grad_right))
        grad_branch_in = grad_branch_in + shifted(
            contract_cols(grad_right, w_right[tap_index]).reshape(group_shape), -offset
        )
    grad_w_right = jnp.stack(right_rows)
    grad_normed_branch = collect_rows(grad_branch_in) * valid_own[..., None]
    grad_resid, grad_gain_branch = normalize_back(
        grad_normed_branch, unit_branch, inv_branch, gain_branch
    )
    grad_one = grad_two + grad_resid
    grad_glu = lax.all_to_all(
        grad_one.astype(jnp.bfloat16), "mp", split_axis=2, concat_axis=1, tiled=True
    )
    grad_glu_flat = grad_glu.reshape(group_rows, -1).astype(jnp.float32)
    flat_glu = spread_rows(normed_glu.astype(jnp.bfloat16)).reshape(group_rows, model_width)
    value_pre = matmul(flat_glu, w_value)
    gate_sig = jax.nn.sigmoid(matmul(flat_glu, w_gate))
    grad_value = (grad_glu_flat * gate_sig).astype(jnp.bfloat16)
    grad_gate = (grad_glu_flat * value_pre * gate_sig * (1.0 - gate_sig)).astype(jnp.bfloat16)
    grad_w_value = contract_rows(flat_glu, grad_value)
    grad_w_gate = contract_rows(flat_glu, grad_gate)
    grad_glu_in = contract_cols(grad_value, w_value) + contract_cols(grad_gate, w_gate)
    grad_normed_glu = collect_rows(grad_glu_in.reshape(group_shape))
    grad_resid, grad_gain_glu = normalize_back(grad_normed_glu, unit_glu, inv_glu, gain_glu)
    grad_inputs = (grad_one + grad_resid).astype(jnp.bfloat16)
    gains = (grad_gain_glu, grad_gain_branch, grad_gain_attn, grad_gain_ffn)
    shards = (
        grad_w_value,
        grad_w_gate,
        grad_w_left,
        grad_w_right,
        grad_gain_mid,
        grad_w_depth,
        grad_w_point,
        grad_w_qkv,
        grad_w_out,
        grad_w_in,
        grad_w_back,
    )
    return (outputs, grad_inputs, gains, shards)


def local(
    inputs,
    lengths,
    gain_glu,
    w_value,
    w_gate,
    gain_branch,
    w_left,
    w_right,
    gain_mid,
    w_depth,
    w_point,
    gain_attn,
    w_qkv,
    w_out,
    gain_ffn,
    w_in,
    w_back,
    cotangent,
):
    outputs, grad_inputs, gains, shards = split_pass(
        inputs,
        lengths,
        gain_glu,
        w_value,
        w_gate,
        gain_branch,
        w_left,
        w_right,
        gain_mid,
        w_depth,
        w_point,
        gain_attn,
        w_qkv,
        w_out,
        gain_ffn,
        w_in,
        w_back,
        cotangent,
    )
    gain_totals = lax.psum((gains[0], gains[1], gains[2], gains[3]), ("dp", "mp"))
    weight_totals = (
        lax.psum(shards[0].astype(jnp.bfloat16), "dp").astype(jnp.float32),
        lax.psum(shards[1].astype(jnp.bfloat16), "dp").astype(jnp.float32),
        lax.psum(shards[2].astype(jnp.bfloat16), "dp").astype(jnp.float32),
        lax.psum(shards[3].astype(jnp.bfloat16), "dp").astype(jnp.float32),
        lax.psum(shards[4].astype(jnp.bfloat16), "dp").astype(jnp.float32),
        lax.psum(shards[5].astype(jnp.bfloat16), "dp").astype(jnp.float32),
        lax.psum(shards[6].astype(jnp.bfloat16), "dp").astype(jnp.float32),
        lax.psum(shards[7].astype(jnp.bfloat16), "dp").astype(jnp.float32),
        lax.psum(shards[8].astype(jnp.bfloat16), "dp").astype(jnp.float32),
        lax.psum(shards[9].astype(jnp.bfloat16), "dp").astype(jnp.float32),
        lax.psum(shards[10].astype(jnp.bfloat16), "dp").astype(jnp.float32),
    )
    return (
        outputs,
        grad_inputs,
        gain_totals[0],
        weight_totals[0],
        weight_totals[1],
        gain_totals[1],
        weight_totals[2],
        weight_totals[3],
        weight_totals[4],
        weight_totals[5],
        weight_totals[6],
        gain_totals[2],
        weight_totals[7],
        weight_totals[8],
        gain_totals[3],
        weight_totals[9],
        weight_totals[10],
    )


HALF = 256
LANES = 128


def dot_nn(left_side, right_side):
    return lax.dot_general(
        left_side, right_side, (((1,), (0,)), ((), ())), preferred_element_type=jnp.float32
    )


def dot_nt(left_side, right_side):
    return lax.dot_general(
        left_side, right_side, (((1,), (1,)), ((), ())), preferred_element_type=jnp.float32
    )


def dot_tn(left_side, right_side):
    return lax.dot_general(
        left_side, right_side, (((0,), (0,)), ((), ())), preferred_element_type=jnp.float32
    )


def row_stats(values):
    centre = values - jnp.mean(values, axis=-1, keepdims=True)
    inv = lax.rsqrt(jnp.mean(centre * centre, axis=-1, keepdims=True) + epsilon)
    return centre * inv, inv


def norm_grad(grad_out, unit, inv, gain):
    scaled = grad_out * gain
    mean_one = jnp.mean(scaled, axis=-1, keepdims=True)
    mean_two = jnp.mean(scaled * unit, axis=-1, keepdims=True)
    return inv * (scaled - mean_one - unit * mean_two)


def sigmoid(values):
    return 0.5 * jnp.tanh(0.5 * values) + 0.5


def silu(values):
    return values * sigmoid(values)


def turned(values):
    return jnp.transpose(values.astype(jnp.float32)).astype(jnp.bfloat16)


class Loader:
    def __init__(self, sems, first=0):
        self.sems = sems
        self.count = first
        self.waits = []
        self.plain = []
        self.by_core = ([], [])

    def copy(self, source, target, at):
        return pltpu.make_async_copy(source, target, self.sems.at[at])

    def start(self, source, target):
        self.plain.append(self.copy(source, target, self.count))
        self.waits.append(self.plain[-1])
        self.count += 1

    def either(self, got, part, taker, target):
        for core in range(2):
            source = got if core == taker else part
            self.by_core[core].append(self.copy(source, target, self.count))
        self.waits.append(self.by_core[0][-1])
        self.count += 1

    def go(self, core):
        for copy in self.plain:
            copy.start()
        for number, copies in enumerate(self.by_core):
            if copies:

                @pl.when(core == number)
                def _(copies=copies):
                    for copy in copies:
                        copy.start()

    def wait(self):
        for copy in self.waits:
            copy.wait()


def load_pair(loader, own, got, part, taker, core, target, slots=(0, 1)):
    loader.start(own, target.at[slots[0]])
    loader.either(got, part, taker, target.at[slots[1]])


def load_left(loader, w_left, got, part, core, target):
    blocks = w_left.shape[1] // HALF
    rows = w_left.shape[0]
    for block in range(blocks):
        loader.start(w_left.at[:, pl.ds(block * HALF, HALF)], target.at[block])
        at = pl.ds(block * rows, rows)
        loader.either(got.at[at], part.at[at], 0, target.at[blocks + block])


def load_pack(loader, got, part, core, target):
    count, depth = target.shape[:2]
    for block in range(count):
        at = pl.ds(got.shape[0] - (count - block) * depth, depth)
        loader.either(got.at[at], part.at[at], 0, target.at[block])


def load_point(loader, w_point, got, part, core, target):
    at = pl.ds(0, w_point.shape[0])
    load_pair(loader, w_point, got.at[at], part.at[at], 1, core, target)


def load_right(loader, w_right, got, part, core, target):
    loader.start(w_right, target.at[0])
    rows = w_right.shape[1]
    for tap in range(w_right.shape[0]):
        at = (pl.ds(2 * rows + (tap // 2) * rows, rows), pl.ds((tap % 2) * LANES, LANES))
        loader.either(got.at[at], part.at[at], 1, target.at[1, tap])


def load_qkv(loader, w_qkv, got, part, core, target, which):
    rows = w_qkv.shape[1]
    for slot, index in enumerate(which):
        loader.start(w_qkv.at[index], target.at[0, slot])
        at = pl.ds(index * rows, rows)
        loader.either(got.at[at], part.at[at], 0, target.at[1, slot])


def load_out(loader, w_out, got, part, core, target):
    loader.start(w_out, target.at[0])
    rows = w_out.shape[0]
    for block in range(2):
        at = pl.ds(block * rows, rows)
        loader.either(
            got.at[at], part.at[at], 1, target.at[1, :, pl.ds(block * HALF, HALF)]
        )


def load_in(loader, w_in, got2, part2, got3, part3, core, target):
    blocks = w_in.shape[1] // HALF
    rows = w_in.shape[0]
    for block in range(blocks):
        loader.start(w_in.at[:, pl.ds(block * HALF, HALF)], target.at[block])
        got, part = (got2, part2) if block < 2 else (got3, part3)
        at = pl.ds(rows + (block % 2) * rows, rows)
        loader.either(got.at[at], part.at[at], 1, target.at[blocks + block])


def load_back(loader, w_back, got, part, core, target):
    loader.start(w_back, target.at[0])
    rows = w_back.shape[0]
    half = rows // 2
    near, far = pl.ds(0, HALF), pl.ds(HALF, HALF)
    for at, taker, spot in (
        (pl.ds(0, rows), 0, (pl.ds(0, rows), near)),
        (pl.ds(rows, half), 0, (pl.ds(0, half), far)),
        (pl.ds(0, half), 1, (pl.ds(half, half), far)),
    ):
        loader.either(got.at[at], part.at[at], taker, target.at[1].at[spot])


GROUP = 8


def bundle_kernel(
    info, w_left, w_right, w_point, w_depth, gain_mid, w_qkv, w_out, w_in, w_back,
    one_o, two_o, three_o, sems,
):
    core = info[0]

    def copies(pieces):
        at = {id(one_o): 0, id(two_o): 0, id(three_o): 0}
        started = []
        for target, source in pieces:
            base = at[id(target)]
            at[id(target)] = base + source.shape[0]
            spot = target.at[pl.ds(base, source.shape[0]), pl.ds(0, source.shape[1])]
            copy = pltpu.make_async_copy(source, spot, sems.at[len(started)])
            copy.start()
            started.append(copy)
        for copy in started:
            copy.wait()

    def blocks(values):
        return [values.at[:, pl.ds(at, HALF)] for at in range(0, values.shape[1], HALF)]

    near, far = blocks(w_back)
    half = w_back.shape[0] // 2

    @pl.when(core == 0)
    def _():
        base = w_left.shape[0] * (w_left.shape[1] // HALF)
        taps = jnp.concatenate(
            [
                w_depth[...].astype(jnp.float32),
                gain_mid[...].astype(jnp.float32),
                jnp.zeros((15 - w_depth.shape[0], w_depth.shape[1]), jnp.float32),
            ],
            axis=0,
        ).astype(jnp.bfloat16)
        for block in range(w_depth.shape[1] // HALF):
            at = slice(base + block * 16, base + (block + 1) * 16)
            one_o[at] = taps[:, block * HALF : (block + 1) * HALF]
        copies(
            [(one_o, piece) for piece in blocks(w_left)]
            + [(two_o, w_qkv.at[index]) for index in range(3)]
            + [(three_o, near), (three_o, far.at[pl.ds(0, half)])]
        )

    @pl.when(core == 1)
    def _():
        pieces = [(one_o, w_point)]
        pieces += [(two_o, piece) for piece in blocks(w_out) + blocks(w_in)[:2]]
        pieces += [(three_o, far.at[pl.ds(half, half)])]
        pieces += [(three_o, piece) for piece in blocks(w_in)[2:]]
        rows, base = w_right.shape[1], w_point.shape[0]
        started = []
        for tap in range(w_right.shape[0]):
            spot = one_o.at[
                pl.ds(base + (tap // 2) * rows, rows), pl.ds((tap % 2) * LANES, LANES)
            ]
            copy = pltpu.make_async_copy(w_right.at[tap], spot, sems.at[len(pieces) + tap])
            copy.start()
            started.append(copy)
        copies(pieces)
        for copy in started:
            copy.wait()


def row_spot(rows, own, lanes):
    row = lax.broadcasted_iota(jnp.int32, (rows, lanes), 0)
    spot = (row % GROUP) * (own // GROUP) + row // GROUP
    return jnp.where(row < own, spot, jnp.where(row < own + EDGE, row - own - EDGE, row - EDGE))


def row_mask(core, length, ext, lanes):
    own = ext - 2 * EDGE
    spot = row_spot(ext, own, lanes) + core * own
    return jnp.where((spot >= 0) & (spot < length), 1.0, 0.0)


def lane_tiles(width):
    return [slice(at, at + LANES) for at in range(0, width, LANES)]


def load_tiles(source, tiles):
    for index, lanes in enumerate(lane_tiles(source.shape[1])):
        tiles[index] = source[:, lanes].astype(jnp.float32)


def gather_rows(tiles, target):
    own = tiles.shape[1]
    for tile, lanes in enumerate(lane_tiles(target.shape[1])):
        for index in range(own // GROUP):
            target[index * GROUP : (index + 1) * GROUP, lanes] = tiles[
                tile, pl.ds(index, GROUP, stride=own // GROUP)
            ]


def scatter_rows(source, tiles, target):
    own = tiles.shape[1]
    for tile, lanes in enumerate(lane_tiles(target.shape[1])):
        for index in range(own // GROUP):
            tiles[tile, pl.ds(index, GROUP, stride=own // GROUP)] = source[
                index * GROUP : (index + 1) * GROUP, lanes
            ]
        target[:, lanes] = tiles[tile].astype(target.dtype)


def next_group(first, row):
    sub = lax.broadcasted_iota(jnp.int32, first.shape, 0)
    return jnp.where(sub == GROUP - 1, row, pltpu.roll(first, GROUP - 1, 0))


def previous_group(last, row):
    sub = lax.broadcasted_iota(jnp.int32, last.shape, 0)
    return jnp.where(sub == 0, row, pltpu.roll(last, 1, 0))


def shift_rows(values, offset):
    if offset == 0:
        return values
    ext = values.shape[0]
    own = ext - 2 * EDGE
    mid, before, after = values[:own], values[own : own + EDGE], values[own + EDGE :]
    sub = lax.broadcasted_iota(jnp.int32, before.shape, 0)
    if offset > 0:
        moved = jnp.concatenate([mid[GROUP:], next_group(mid[:GROUP], after[:1])], axis=0)
        before = jnp.where(sub == EDGE - 1, mid[:1], pltpu.roll(before, EDGE - 1, 0))
        after = pltpu.roll(after, EDGE - 1, 0)
    else:
        moved = jnp.concatenate(
            [previous_group(mid[own - GROUP :], before[EDGE - 1 :]), mid[: own - GROUP]], axis=0
        )
        after = jnp.where(sub == 0, mid[own - 1 :], pltpu.roll(after, 1, 0))
        before = pltpu.roll(before, 1, 0)
    return jnp.concatenate([moved, before, after], axis=0)


def fill_window(window, values, own, reach):
    before, after = values[own : own + EDGE], values[own + EDGE :]
    window[reach * GROUP : reach * GROUP + own] = values[:own]
    for step in range(1, reach + 1):
        last = values[own - step * GROUP : own - (step - 1) * GROUP]
        at = (reach - step) * GROUP
        window[at : at + GROUP] = previous_group(last, before[EDGE - step : EDGE - step + 1])
        first = values[(step - 1) * GROUP : step * GROUP]
        at = reach * GROUP + own + (step - 1) * GROUP
        window[at : at + GROUP] = next_group(first, after[step - 1 : step])


def glu_kernel(
    info, block, moved, cot_own, cot_moved, edge, gain_glu, gain_branch, w_value, w_gate, got, part_w,
    cot_o, resid_o, branch_o, gluin_o, value_o, sig_o, x_s, c_s, n_s, wv_s, wg_s, sems,
):
    core, member, length = info[0], info[1], info[2]
    loader = Loader(sems)
    load_pair(loader, w_value, got, part_w, 0, core, wv_s, (member, 1 - member))
    load_pair(loader, w_gate, got, part_w, 1, core, wg_s, (member, 1 - member))
    loader.go(core)
    ext = x_s.shape[0]
    rows = ext - 2 * EDGE
    edge_f = edge[...].astype(jnp.float32)
    x_s[rows : rows + EDGE] = jnp.where(core == 1, edge_f, 0.0)
    x_s[rows + EDGE :] = jnp.where(core == 1, 0.0, edge_f)

    @pl.when(core == member)
    def _():
        load_tiles(block, n_s)

    @pl.when(core != member)
    def _():
        load_tiles(moved, n_s)

    gather_rows(n_s, x_s)

    @pl.when(core == member)
    def _():
        load_tiles(cot_own, n_s)

    @pl.when(core != member)
    def _():
        load_tiles(cot_moved, n_s)

    gather_rows(n_s, c_s)
    cot_o[...] = c_s[...].astype(jnp.bfloat16)
    loader.wait()
    valid = row_mask(core, length, ext, LANES)[:, :1]
    part = ext // 2
    for start in (0, part):
        at = slice(start, start + part)
        x = x_s[at]
        glu_in = (row_stats(x)[0] * gain_glu[...]).astype(jnp.bfloat16)
        gluin_o[at] = glu_in
        for half in range(2):
            cols = slice(half * HALF, (half + 1) * HALF)
            value = dot_nn(glu_in, wv_s[half])
            sig = sigmoid(dot_nn(glu_in, wg_s[half]))
            value_o[at, cols] = value.astype(jnp.bfloat16)
            sig_o[at, cols] = sig.astype(jnp.bfloat16)
            resid_o[at, cols] = x[:, cols] + (value * sig).astype(jnp.bfloat16).astype(jnp.float32)
        normed = row_stats(resid_o[at])[0] * gain_branch[...]
        branch_o[at] = (valid[at] * normed).astype(jnp.bfloat16)


def spread_block(index, rights, stride):
    source = lax.broadcasted_iota(jnp.int32, (rights, HALF), 0)
    channel = lax.broadcasted_iota(jnp.int32, (rights, HALF), 1) + index * HALF
    return jnp.where(channel == source * stride, 1.0, 0.0).astype(jnp.bfloat16)


def conv_rows(branch, weights):
    taps = weights.shape[0]
    total = dot_nn(branch, weights[taps // 2])
    for tap in range(taps):
        if tap != taps // 2:
            total = total + shift_rows(dot_nn(branch, weights[tap]), tap - taps // 2)
    return total


def mid_step(branch, into, right_act, index, stride, left_o, mid_o, sums, at):
    left_pre = dot_nn(branch[...], into[index])
    left_o[at] = left_pre.astype(jnp.bfloat16)
    mid = silu(left_pre) + dot_nn(right_act, spread_block(index, right_act.shape[1], stride))
    mid_o[at] = mid
    near, far = mid[:, :LANES], mid[:, LANES:]
    sums[0] += near + far
    sums[1] += near * near + far * far


def branch_own_kernel(
    info, branch, w_left, w_right, left_o, right_o, mid_o, sums_o, wl_s, sems
):
    loader = Loader(sems)
    blocks = wl_s.shape[0]
    for block in range(blocks):
        loader.start(w_left.at[:, pl.ds(block * HALF, HALF)], wl_s.at[block])
    loader.go(info[0])
    right_pre = conv_rows(branch[...], w_right)
    right_o[...] = right_pre
    right_act = silu(right_pre).astype(jnp.bfloat16)
    stride = blocks * HALF // right_pre.shape[1]
    sums_o[...] = jnp.zeros_like(sums_o)
    loader.wait()

    def step(index, carry):
        mid_step(branch, wl_s, right_act, index, stride, left_o, mid_o, sums_o, index)
        return carry

    lax.fori_loop(0, blocks, step, 0, unroll=2)


def fill_taps(pack_own, pack_oth, taps_s):
    count, cols = pack_own.shape
    taps_s[:count, :cols] = pack_own[...].astype(jnp.float32)
    for block in range(pack_oth.shape[0]):
        at = cols + block * HALF
        taps_s[:, at : at + HALF] = pack_oth[block].astype(jnp.float32)


def branch_kernel(
    info, branch, resid_one, pack_own, left_own, right_own, mid_own, sums_own, w_point, got, part,
    resid_two_o, left_o, right_o, stats_o, depth_o,
    wl_s, wr_s, wp_s, po_s, taps_s, mid_s, din_s, sums_s, sep_s, sems,
):
    core, length = info[0], info[2]
    loader = Loader(sems)
    taps_conv, depth_in_rows = wr_s.shape[0], wr_s.shape[1]
    for tap in range(taps_conv):
        at = (
            pl.ds(w_point.shape[0] + (tap // 2) * depth_in_rows, depth_in_rows),
            pl.ds((tap % 2) * LANES, LANES),
        )
        loader.either(got.at[at], part.at[at], 1, wr_s.at[tap])
    blocks = wl_s.shape[0]
    for block in range(blocks):
        at = pl.ds(block * depth_in_rows, depth_in_rows)
        loader.either(got.at[at], part.at[at], 0, wl_s.at[block])
    load_point(loader, w_point, got, part, core, wp_s)
    load_pack(loader, got, part, core, po_s)
    loader.go(core)
    ext = branch.shape[0]
    rows = ext - 2 * EDGE
    chunks = 2 * blocks
    per_shard = blocks
    sep_taps = pack_own.shape[0] - 1
    inner = chunks * HALF
    rights = right_own.shape[1]
    stride = blocks * HALF // rights
    left_o[:blocks] = left_own[...]
    mid_s[:blocks] = mid_own[...]
    sums_s[...] = sums_own[...]
    right_o[:, :rights] = right_own[...]
    loader.wait()
    fill_taps(pack_own, po_s, taps_s)
    right_pre = conv_rows(branch[...], wr_s)
    right_o[:, rights:] = right_pre
    right_act = silu(right_pre).astype(jnp.bfloat16)

    def first(index, carry):
        mid_step(branch, wl_s, right_act, index, stride, left_o, mid_s, sums_s, index + blocks)
        return carry

    lax.fori_loop(0, blocks, first, 0, unroll=2)
    mean = jnp.sum(sums_s[0], axis=-1, keepdims=True) / inner
    inv = lax.rsqrt(
        jnp.sum(sums_s[1], axis=-1, keepdims=True) / inner - mean * mean + epsilon
    )
    lane = lax.broadcasted_iota(jnp.int32, (ext, LANES), 1)
    stats_o[...] = jnp.where(lane == 0, mean, inv)
    sums_s[0] = jnp.broadcast_to(mean, (ext, LANES))
    sums_s[1] = inv * row_mask(core, length, ext, LANES)
    sep_s[...] = jnp.zeros_like(sep_s)

    def second(index, carry):
        cols = pl.ds(pl.multiple_of(index * HALF, HALF), HALF)
        taps = taps_s[:, cols]
        for side in range(2):
            lanes = slice(side * LANES, (side + 1) * LANES)
            depth_in = (
                (mid_s[index, :, lanes] - sums_s[0]) * sums_s[1] * taps[sep_taps : sep_taps + 1, lanes]
            )
            fill_window(din_s.at[:, lanes], depth_in, rows, sep_taps // 2)
        step = 64
        for start in range(0, rows, step):
            for side in range(2):
                lanes = slice(side * LANES, (side + 1) * LANES)
                acc = din_s[start : start + step, lanes] * taps[:1, lanes]
                for tap in range(1, sep_taps):
                    at = start + tap * GROUP
                    acc = acc + din_s[at : at + step, lanes] * taps[tap : tap + 1, lanes]
                depth_o[index, start : start + step, lanes] = acc.astype(jnp.bfloat16)
        shard, chunk = index // per_shard, index % per_shard
        point = wp_s[shard, pl.ds(pl.multiple_of(chunk * HALF, HALF), HALF)]
        sep_s[...] += dot_nn(depth_o[index], point)
        return carry

    lax.fori_loop(0, chunks, second, 0, unroll=2)
    sep_width = sep_s.shape[1]
    resid_two_o[:, :sep_width] = resid_one[:rows, :sep_width] + sep_s[...]
    resid_two_o[:, sep_width:] = resid_one[:rows, sep_width:]


def kv_kernel(info, resid_two, gain, w_qkv, got, part, attn_o, kv_o, w_s, sems):
    loader = Loader(sems)
    load_qkv(loader, w_qkv, got, part, info[0], w_s, (1, 2))
    loader.go(info[0])
    attn_in = (row_stats(resid_two[...])[0] * gain[...]).astype(jnp.bfloat16)
    attn_o[...] = attn_in
    loader.wait()
    width = w_s.shape[3]
    for shard in range(2):
        for index in range(2):
            at = (2 * index + shard) * width
            kv_o[:, at : at + width] = dot_nn(attn_in, w_s[shard, index]).astype(jnp.bfloat16)


def query_kernel(info, attn_in, w_qkv, got, part, q_o, w_s, sems):
    loader = Loader(sems)
    load_qkv(loader, w_qkv, got, part, info[0], w_s, (0,))
    loader.go(info[0])
    loader.wait()
    width = w_s.shape[3]
    scale = 1.0 / math.sqrt(HEAD_DIM)
    for shard in range(2):
        query = dot_nn(attn_in[...], w_s[shard, 0]).astype(jnp.bfloat16).astype(jnp.float32)
        q_o[:, shard * width : (shard + 1) * width] = (query * scale).astype(jnp.bfloat16)


def key_bias(core, length, rows):
    spot = row_spot(rows, rows, LANES) + core * rows
    return jnp.where(spot < length, 0.0, negative_big)


def head_masks(rows, head):
    lane = lax.broadcasted_iota(jnp.int32, (rows, LANES), 1)
    return (lane // HEAD_DIM) == head, lane == HEAD_DIM * (1 - head)


def attend_kernel(info, q, kvo, kvf, ctx0_o, lse0_o, ctx1_o, lse1_o, bias_s):
    core, length = info[0], info[2]
    rows, width = q.shape
    pairs = width // LANES // 2
    bias_s[:rows] = key_bias(core, length, rows)
    bias_s[rows:] = key_bias(1 - core, length, rows)

    def pair_step(shard, ctx_o, lse_o, local, carry):
        pair = local + shard * pairs
        cols = pl.ds(pl.multiple_of(pair * LANES, LANES), LANES)
        vcols = pl.ds(pl.multiple_of(pair * LANES + width, LANES), LANES)
        here = pl.ds(pl.multiple_of(local * LANES, LANES), LANES)
        keys = jnp.concatenate([kvo[:, cols], kvf[:, cols]], axis=0).astype(jnp.float32)
        vals = jnp.concatenate([kvo[:, vcols], kvf[:, vcols]], axis=0)
        vals_t = turned(vals)
        query = q[:, cols].astype(jnp.float32)
        outs = []
        for head in range(2):
            in_k, extra_k = head_masks(2 * rows, head)
            in_q, extra_q = head_masks(rows, head)
            km = jnp.where(in_k, keys, jnp.where(extra_k, bias_s[...], 0.0)).astype(jnp.bfloat16)
            qm = jnp.where(in_q, query, jnp.where(extra_q, 1.0, 0.0)).astype(jnp.bfloat16)
            pieces = []
            for start in range(0, rows, HALF):
                scores = dot_nt(km, qm[start : start + HALF])
                top = jnp.max(scores, axis=0, keepdims=True)
                weights = jnp.exp(scores - top)
                total = jnp.sum(weights, axis=0, keepdims=True)
                out = dot_nn(
                    vals_t[head * HEAD_DIM : (head + 1) * HEAD_DIM], weights.astype(jnp.bfloat16)
                )
                pieces.append(out / total)
                lse_o[pl.ds(local * 2 + head, 1), start : start + HALF] = top + jnp.log(total)
            outs.append(jnp.concatenate(pieces, axis=1))
        ctx_o[:, here] = jnp.transpose(jnp.concatenate(outs, axis=0)).astype(jnp.bfloat16)
        return carry

    lax.fori_loop(0, pairs, functools.partial(pair_step, 0, ctx0_o, lse0_o), 0, unroll=2)
    lax.fori_loop(0, pairs, functools.partial(pair_step, 1, ctx1_o, lse1_o), 0, unroll=2)


def ffn_kernel(
    info, resid_two, ctx0, ctx1, cot, gain, w_out, w_in, w_back, got2, part2,
    got3, part3,
    out_o, grad_three_o, gctx_o, ggain_o, send_o, keep_o,
    wo_s, wi_s, wb_s, fin_s, fint_s, cot_s, acc_s, gacc_s, ctxt_s, n_s, sems,
):
    core = info[0]
    loader = Loader(sems)
    load_out(loader, w_out, got2, part2, core, wo_s)
    late = Loader(sems, loader.count)
    load_in(late, w_in, got2, part2, got3, part3, core, wi_s)
    load_back(late, w_back, got3, part3, core, wb_s)

    loader.go(core)
    late.go(core)
    cot_s[...] = cot[...]
    loader.wait()
    part = ctx0.shape[1]
    chunks = wi_s.shape[0]
    per_shard = chunks // 2
    resid = resid_two[...] + dot_nn(ctx0[...], wo_s[0]) + dot_nn(ctx1[...], wo_s[1])
    acc_s[...] = resid
    gacc_s[...] = jnp.zeros_like(gacc_s)
    unit, inv = row_stats(resid)
    ffn_in = unit * gain[...]
    fin_s[...] = ffn_in.astype(jnp.bfloat16)
    fint_s[...] = jnp.transpose(fin_s[...].astype(jnp.float32)).astype(jnp.bfloat16)
    keep_rows = pl.ds(pl.multiple_of(core * HALF, HALF), HALF)
    send_rows = pl.ds(pl.multiple_of((1 - core) * HALF, HALF), HALF)

    def chunk_step(index, carry):
        shard, chunk = index // per_shard, index % per_shard
        rows = pl.ds(pl.multiple_of(chunk * HALF, HALF), HALF)
        into, back = wi_s[index], wb_s[shard, rows]
        pre = dot_nn(fin_s[...], into)
        sig = sigmoid(pre)
        hidden = (pre * sig).astype(jnp.bfloat16)
        acc_s[...] += dot_nn(hidden, back)
        grad_hidden = dot_nt(cot_s[...], back)
        grad_pre = (grad_hidden * (sig * (1.0 + pre * (1.0 - sig)))).astype(jnp.bfloat16)
        send_o[shard, rows] = dot_nn(fint_s[send_rows], grad_pre).astype(jnp.bfloat16)
        keep_o[shard, rows] = dot_nn(fint_s[keep_rows], grad_pre).astype(jnp.bfloat16)
        hidden_t = turned(hidden)
        base = per_shard * HALF
        rows = pl.ds(pl.multiple_of(base + chunk * HALF, HALF), HALF)
        send_o[shard, rows] = dot_nn(hidden_t, cot_s[:, send_rows]).astype(jnp.bfloat16)
        keep_o[shard, rows] = dot_nn(hidden_t, cot_s[:, keep_rows]).astype(jnp.bfloat16)
        gacc_s[...] += dot_nt(grad_pre, into)
        return carry

    late.wait()
    lax.fori_loop(0, chunks, chunk_step, 0, unroll=4)
    scatter_rows(acc_s, n_s, out_o)
    unit, inv = row_stats(
        resid_two[...] + dot_nn(ctx0[...], wo_s[0]) + dot_nn(ctx1[...], wo_s[1])
    )
    grad_norm = gacc_s[...]
    ggain_o[...] = jnp.sum(grad_norm * unit, axis=0, keepdims=True)
    grad_three = cot_s[...].astype(jnp.float32) + norm_grad(grad_norm, unit, inv, gain[...])
    grad_three_o[...] = grad_three
    fin_s[...] = grad_three.astype(jnp.bfloat16)
    ctxt_s[:part] = turned(ctx0[...])
    ctxt_s[part:] = turned(ctx1[...])
    base = 2 * per_shard * HALF
    for shard in range(2):
        side = slice(shard * part, (shard + 1) * part)
        gctx_o[:, side] = dot_nt(fin_s[...], wo_s[shard]).astype(jnp.bfloat16)
        send_o[shard, base : base + part] = dot_nn(ctxt_s[side], fin_s[:, send_rows]).astype(
            jnp.bfloat16
        )
        keep_o[shard, base : base + part] = dot_nn(ctxt_s[side], fin_s[:, keep_rows]).astype(
            jnp.bfloat16
        )


def attend_back_kernel(side, info, q, kv, ctx0, ctx1, gctx, lse0, lse1, *rest):
    if side:
        gq_o, gkv_o, bias_s, gk_s, gv_s = rest
    else:
        gq_part, gq_o, gkv_o, bias_s, gk_s, gv_s = rest
    core, length = info[0], info[2]
    rows, width = q.shape
    pairs = width // LANES // 2
    scale = 1.0 / math.sqrt(HEAD_DIM)
    bias_s[...] = key_bias(core ^ side, length, rows)

    def pair_step(shard, ctx, lse, local, carry):
        pair = local + shard * pairs
        cols = pl.ds(pl.multiple_of(pair * LANES, LANES), LANES)
        vcols = pl.ds(pl.multiple_of(pair * LANES + width, LANES), LANES)
        here = pl.ds(pl.multiple_of(local * LANES, LANES), LANES)
        keys = kv[:, cols].astype(jnp.float32)
        vals = kv[:, vcols]
        keys_t = jnp.transpose(keys).astype(jnp.bfloat16)
        query = q[:, cols].astype(jnp.float32)
        grad_out = gctx[:, cols].astype(jnp.float32)
        product_t = jnp.transpose(grad_out * ctx[:, here].astype(jnp.float32))
        gk_s[...] = jnp.zeros_like(gk_s)
        gv_s[...] = jnp.zeros_like(gv_s)
        outs = []
        for head in range(2):
            in_q, extra_q = head_masks(rows, head)
            km = jnp.where(in_q, keys, jnp.where(extra_q, bias_s[...], 0.0)).astype(jnp.bfloat16)
            qm = jnp.where(in_q, query, jnp.where(extra_q, 1.0, 0.0)).astype(jnp.bfloat16)
            qz = jnp.where(in_q, query, 0.0).astype(jnp.bfloat16)
            gz = jnp.where(in_q, grad_out, 0.0).astype(jnp.bfloat16)
            span = slice(head * HEAD_DIM, (head + 1) * HEAD_DIM)
            pieces = []
            for start in range(0, rows, HALF):
                at = slice(start, start + HALF)
                level = lse[pl.ds(local * 2 + head, 1), at]
                delta = jnp.sum(product_t[span, at], axis=0, keepdims=True)
                soft = jnp.exp(dot_nt(km, qm[at]) - level)
                gv_s[...] += dot_nn(soft.astype(jnp.bfloat16), gz[at])
                grad_scores = (soft * (dot_nt(vals, gz[at]) - delta)).astype(jnp.bfloat16)
                gk_s[...] += dot_nn(grad_scores, qz[at])
                pieces.append(dot_nn(keys_t[span], grad_scores))
            outs.append(jnp.concatenate(pieces, axis=1))
        grad_q = jnp.transpose(jnp.concatenate(outs, axis=0))
        if not side:
            grad_q = (grad_q + gq_part[:, cols]) * scale
        gq_o[:, cols] = grad_q.astype(gq_o.dtype)
        gkv_o[:, cols] = gk_s[...].astype(gkv_o.dtype)
        gkv_o[:, vcols] = gv_s[...].astype(gkv_o.dtype)
        return carry

    for shard, ctx, lse in ((0, ctx0, lse0), (1, ctx1, lse1)):
        lax.fori_loop(0, pairs, functools.partial(pair_step, shard, ctx, lse), 0, unroll=2)


def qkv_back_kernel(
    info, gq, gown, gfar, attn_in, resid_two, grad_three, gain, w_qkv, got, part,
    grad_two_o, gsep_o, gedge_o, ggain_o, send_o, keep_o, w_s, attnt_s, n_s, sems,
):
    core = info[0]
    loader = Loader(sems)
    load_qkv(loader, w_qkv, got, part, core, w_s, (0, 1, 2))
    loader.go(core)
    attnt_s[...] = turned(attn_in[...])
    width = w_s.shape[3]
    keep_rows = pl.ds(pl.multiple_of(core * HALF, HALF), HALF)
    send_rows = pl.ds(pl.multiple_of((1 - core) * HALF, HALF), HALF)
    loader.wait()
    grad_in = jnp.zeros(resid_two.shape, jnp.float32)
    for index in range(3):
        if index == 0:
            whole = gq[...]
        else:
            cols = slice((index - 1) * 2 * width, index * 2 * width)
            whole = (gown[:, cols] + gfar[:, cols].astype(jnp.float32)).astype(jnp.bfloat16)
        for shard in range(2):
            grad = whole[:, shard * width : (shard + 1) * width]
            at = slice(index * HALF, (index + 1) * HALF)
            send_o[shard, at] = dot_nn(attnt_s[send_rows], grad).astype(jnp.bfloat16)
            keep_o[shard, at] = dot_nn(attnt_s[keep_rows], grad).astype(jnp.bfloat16)
            grad_in = grad_in + dot_nt(grad, w_s[shard, index])
    unit, inv = row_stats(resid_two[...])
    ggain_o[...] = jnp.sum(grad_in * unit, axis=0, keepdims=True)
    grad_two = grad_three[...] + norm_grad(grad_in, unit, inv, gain[...])
    grad_two_o[...] = grad_two
    gsep_o[...] = grad_two[:, : gsep_o.shape[1]].astype(jnp.bfloat16)
    rows = n_s.shape[1]
    for tile, lanes in enumerate(lane_tiles(gsep_o.shape[1])):
        n_s[tile] = grad_two[:, lanes]
        first = n_s[tile, pl.ds(0, EDGE, stride=GROUP)]
        last = n_s[tile, pl.ds(rows - EDGE * GROUP + GROUP - 1, EDGE, stride=GROUP)]
        gedge_o[:, lanes] = jnp.where(core == 0, last, first).astype(jnp.bfloat16)


def point_kernel(info, gsep, depth, send, keep, send_o, keep_o):
    core = info[0]
    grad_sep = gsep[...]
    per_shard = depth.shape[0] // 2
    per_core = per_shard // 2
    base = send.shape[1]
    send_o[:, :base] = send[...]
    keep_o[:, :base] = keep[...]
    for shard in range(2):
        for chunk in range(per_core):
            at = slice(base + chunk * HALF, base + (chunk + 1) * HALF)
            first = shard * per_shard
            send_o[shard, at] = dot_tn(
                depth[first + (1 - core) * per_core + chunk], grad_sep
            ).astype(jnp.bfloat16)
            keep_o[shard, at] = dot_tn(
                depth[first + core * per_core + chunk], grad_sep
            ).astype(jnp.bfloat16)


def as_f32(values):
    return values.astype(jnp.float32)


def slope_of(values):
    sig = sigmoid(values)
    return sig * (1.0 + values * (1.0 - sig))


def depth_back_kernel(
    info, gsep, gedge, left_pre, right_pre, stats, pack_own, w_point, got, part,
    unit_o, scaled_o, sums_s, small_s,
    wp_s, po_s, taps_s, gse_s, gd_s, din_s, near_s, unit_s, scaled_s, wide_s, sems,
):
    core, length = info[0], info[2]
    loader = Loader(sems)
    load_point(loader, w_point, got, part, core, wp_s)
    load_pack(loader, got, part, core, po_s)
    loader.go(core)
    ext = left_pre.shape[1]
    rows = ext - 2 * EDGE
    chunks = left_pre.shape[0]
    per_shard = chunks // 2
    inner = chunks * HALF
    sep_taps = pack_own.shape[0] - 1
    right_cols = right_pre.shape[1]
    stride = inner // right_cols
    reach = sep_taps // 2
    edge = gedge[...].astype(jnp.float32)
    gse_s[:rows] = gsep[...]
    gse_s[rows : rows + EDGE] = jnp.where(core == 1, edge, 0.0).astype(jnp.bfloat16)
    gse_s[rows + EDGE :] = jnp.where(core == 1, 0.0, edge).astype(jnp.bfloat16)
    wide_s[0] = row_mask(core, length, ext, LANES)
    wide_s[1] = jnp.broadcast_to(stats[:, 0:1], (ext, LANES))
    wide_s[2] = jnp.broadcast_to(stats[:, 1:2], (ext, LANES))
    scaled_s[...] = jnp.zeros_like(scaled_s)
    sums_s[...] = jnp.zeros_like(sums_s)
    small_s[...] = jnp.zeros_like(small_s)
    right_act = silu(right_pre[...]).astype(jnp.bfloat16)
    loader.wait()
    fill_taps(pack_own, po_s, taps_s)

    def first(index, carry):
        cols = pl.ds(pl.multiple_of(index * HALF, HALF), HALF)
        taps = taps_s[:, cols]
        shard, chunk = index // per_shard, index % per_shard
        point = wp_s[shard, pl.ds(pl.multiple_of(chunk * HALF, HALF), HALF)]
        grad_depth = dot_nt(gse_s[...], point)
        for side, lanes in enumerate(lane_tiles(HALF)):
            fill_window(gd_s.at[side], grad_depth[:, lanes], rows, reach)
            near_s[side, :EDGE] = grad_depth[rows : rows + EDGE, lanes]
            near_s[side, 3 * EDGE :] = grad_depth[rows + EDGE :, lanes]
            base = reach * GROUP
            near_s[side, EDGE : 2 * EDGE] = gd_s[side, pl.ds(base, EDGE, stride=GROUP)]
            base = reach * GROUP + rows - EDGE * GROUP + GROUP - 1
            near_s[side, 2 * EDGE : 3 * EDGE] = gd_s[side, pl.ds(base, EDGE, stride=GROUP)]
        mid = silu(left_pre[index].astype(jnp.float32)) + dot_nn(
            right_act, spread_block(index, right_cols, stride)
        )
        for side in range(2):
            lanes = slice(side * LANES, (side + 1) * LANES)
            unit = (mid[:, lanes] - wide_s[1]) * wide_s[2]
            unit_s[:, lanes] = unit
            fill_window(
                din_s.at[side],
                unit * wide_s[0] * taps[sep_taps : sep_taps + 1, lanes],
                rows,
                reach,
            )
            for base, target in ((EDGE - GROUP, rows + EDGE - GROUP), (3 * EDGE, rows + EDGE)):
                acc = near_s[side, base + reach : base + reach + GROUP] * taps[:1, lanes]
                for tap in range(1, sep_taps):
                    at = base + reach - tap
                    acc = acc + near_s[side, at : at + GROUP] * taps[tap : tap + 1, lanes]
                at = slice(target, target + GROUP)
                scaled_s[at, lanes] = acc * wide_s[0, at]
        step = 64
        tap_sums = []
        for side in range(2):
            lanes = slice(side * LANES, (side + 1) * LANES)
            sums = [jnp.zeros((GROUP, LANES), jnp.float32) for _ in range(sep_taps)]
            for start in range(0, rows, step):
                at = start + 2 * reach * GROUP
                acc = gd_s[side, at : at + step] * taps[:1, lanes]
                for tap in range(1, sep_taps):
                    at = start + (2 * reach - tap) * GROUP
                    acc = acc + gd_s[side, at : at + step] * taps[tap : tap + 1, lanes]
                scaled_s[start : start + step, lanes] = acc * wide_s[0, start : start + step]
                at = start + reach * GROUP
                grad = gd_s[side, at : at + step]
                for tap in range(sep_taps):
                    at = start + tap * GROUP
                    term = din_s[side, at : at + step] * grad
                    sums[tap] = sums[tap] + jnp.sum(
                        term.reshape(step // GROUP, GROUP, LANES), axis=0
                    )
            tap_sums.append(sums)
        tap_sums = [jnp.concatenate(pair, axis=1) for pair in zip(*tap_sums)]
        tap_rows = [jnp.sum(value, axis=0, keepdims=True) for value in tap_sums]
        gain = taps[sep_taps : sep_taps + 1]
        gain_row = jnp.sum(
            scaled_s[:rows] * unit_s[:rows],
            axis=0,
            keepdims=True,
        )
        filler = jnp.zeros((small_s.shape[0] - sep_taps - 1, HALF), jnp.float32)
        small_s[:, cols] = jnp.concatenate(tap_rows + [gain_row, filler], axis=0)
        scaled = scaled_s[...] * gain
        scaled_o[index] = scaled.astype(jnp.bfloat16)
        unit_o[index] = unit_s[...].astype(jnp.bfloat16)
        near, far = scaled[:, :LANES], scaled[:, LANES:]
        sums_s[0] += near + far
        sums_s[1] += near * unit_s[:, :LANES] + far * unit_s[:, LANES:]
        return carry

    lax.fori_loop(0, chunks, first, 0, unroll=4)


def branch_back_kernel(
    info, unit, scaled, sums, small, left_pre, right_pre, stats, branch, gain_ffn_g, gain_attn_g,
    gleft_o, gright_o, send_o, keep_o,
    wide_s, gra_s, bt_s,
):
    core = info[0]
    ext = left_pre.shape[1]
    rows = ext - 2 * EDGE
    chunks = left_pre.shape[0]
    per_shard = chunks // 2
    inner = chunks * HALF
    right_cols = right_pre.shape[1]
    stride = inner // right_cols
    for index in range(2):
        mean = jnp.sum(sums[index], axis=-1, keepdims=True) / inner
        wide_s[index] = jnp.broadcast_to(mean, (ext, LANES))
    wide_s[2] = jnp.broadcast_to(stats[:, 1:2], (ext, LANES))
    gra_s[...] = jnp.zeros_like(gra_s)
    bt_s[...] = turned(branch[...])
    keep_rows = pl.ds(pl.multiple_of(core * HALF, HALF), HALF)
    send_rows = pl.ds(pl.multiple_of((1 - core) * HALF, HALF), HALF)

    def second(index, carry):
        shard, chunk = index // per_shard, index % per_shard
        sides = []
        for side in range(2):
            lanes = slice(side * LANES, (side + 1) * LANES)
            sides.append(
                wide_s[2]
                * (as_f32(scaled[index, :, lanes]) - wide_s[0] - as_f32(unit[index, :, lanes]) * wide_s[1])
            )
        grad_mid = jnp.concatenate(sides, axis=1)
        grad_left = (
            grad_mid[:rows] * slope_of(left_pre[index, :rows].astype(jnp.float32))
        ).astype(jnp.bfloat16)
        gleft_o[index] = grad_left
        gra_s[...] += dot_nt(
            grad_mid.astype(jnp.bfloat16), spread_block(index, right_cols, stride)
        )
        at = pl.ds(pl.multiple_of(chunk * HALF, HALF), HALF)
        send_o[shard, at] = dot_nn(bt_s[send_rows, :rows], grad_left).astype(
            jnp.bfloat16
        )
        keep_o[shard, at] = dot_nn(bt_s[keep_rows, :rows], grad_left).astype(
            jnp.bfloat16
        )
        return carry

    lax.fori_loop(0, chunks, second, 0, unroll=4)
    grad_right = gra_s[...] * slope_of(right_pre[...])
    gright_o[...] = grad_right.astype(jnp.bfloat16)
    spot = lax.broadcasted_iota(jnp.int32, grad_right.shape, 0)
    own_right = jnp.where(spot < rows, grad_right, 0.0)
    part = right_cols // 2
    base = per_shard * HALF
    for target, picked, side in ((send_o, send_rows, 1 - core), (keep_o, keep_rows, core)):
        taps3 = []
        for tap in range(3):
            moved = shift_rows(own_right, 1 - tap).astype(jnp.bfloat16)
            taps3.append(dot_nn(bt_s[picked, :], moved).astype(jnp.bfloat16))
        for shard in range(2):
            cols = slice(shard * part, (shard + 1) * part)
            target[shard, base : base + HALF, :part] = taps3[0][:, cols]
            target[shard, base : base + HALF, part:] = taps3[1][:, cols]
            target[shard, base + HALF : base + 2 * HALF, :part] = taps3[2][:, cols]
            target[shard, base + HALF : base + 2 * HALF, part:] = jnp.zeros(
                (HALF, part), jnp.bfloat16
            )
            cols_here = inner // 4
            for piece in range(cols_here // LANES):
                lanes = pl.ds(
                    pl.multiple_of(
                        shard * (inner // 2) + side * cols_here + piece * LANES, LANES
                    ),
                    LANES,
                )
                row = base + HALF + piece * 16
                target[shard, row : row + 16, part:] = small[:, lanes].astype(jnp.bfloat16)
            row = base + HALF + 4 * 16
            for piece in range(4):
                lanes = slice(piece * LANES, (piece + 1) * LANES)
                both = jnp.concatenate(
                    [gain_ffn_g[:, lanes], gain_attn_g[:, lanes], jnp.zeros((14, LANES), jnp.float32)],
                    axis=0,
                )
                target[shard, row : row + 16, part:] = both.astype(jnp.bfloat16)
                row += 16


def join_back_kernel(
    info, gleft, gright, resid_one, grad_two, gain_branch, w_left, w_right, got, part_w,
    grad_one_o, ggain_o, wl_s, wr_s, sems,
):
    core, length = info[0], info[2]
    loader = Loader(sems)
    load_left(loader, w_left, got, part_w, core, wl_s)
    load_right(loader, w_right, got, part_w, core, wr_s)
    loader.go(core)
    ext = gright.shape[0]
    rows = ext - 2 * EDGE
    own = slice(0, rows)
    loader.wait()
    grad_in = jnp.zeros((rows, resid_one.shape[1]), jnp.float32)
    for index in range(wl_s.shape[0]):
        grad_in = grad_in + dot_nt(gleft[index], wl_s[index])
    part = wr_s.shape[3]
    for tap in range(wr_s.shape[1]):
        product = dot_nt(gright[:, :part], wr_s[0, tap]) + dot_nt(gright[:, part:], wr_s[1, tap])
        grad_in = grad_in + shift_rows(product, 1 - tap)[own]
    grad_in = grad_in * row_mask(core, length, ext, LANES)[own, :1]
    unit, inv = row_stats(resid_one[own])
    ggain_o[...] = jnp.sum(grad_in * unit, axis=0, keepdims=True)
    grad_one_o[...] = grad_two[...] + norm_grad(grad_in, unit, inv, gain_branch[...])


def glu_back_kernel(
    info, grad_one, gain_branch_row, gain_glu, block, moved, glu_in, value, sig, w_value, w_gate,
    got, part_w,
    gin_o, send_o, keep_o,
    wv_s, wg_s, x_s, n_s, git_s, sems,
):
    core, member = info[0], info[1]
    loader = Loader(sems)
    load_pair(loader, w_value, got, part_w, 0, core, wv_s, (member, 1 - member))
    load_pair(loader, w_gate, got, part_w, 1, core, wg_s, (member, 1 - member))
    loader.go(core)
    rows = grad_one.shape[0]
    own = slice(0, rows)

    @pl.when(core == member)
    def _():
        load_tiles(block, n_s)

    @pl.when(core != member)
    def _():
        load_tiles(moved, n_s)

    gather_rows(n_s, x_s)
    git_s[...] = turned(glu_in[own])
    loader.wait()
    grad_glu = grad_one[...].astype(jnp.bfloat16).astype(jnp.float32)
    keep_rows = pl.ds(pl.multiple_of(core * HALF, HALF), HALF)
    send_rows = pl.ds(pl.multiple_of((1 - core) * HALF, HALF), HALF)
    grad_norm = jnp.zeros(grad_one.shape, jnp.float32)
    for half in range(2):
        cols = slice(half * HALF, (half + 1) * HALF)
        sig_f = sig[own, cols].astype(jnp.float32)
        grad_here = grad_glu[:, cols] * sig_f
        grad_value = grad_here.astype(jnp.bfloat16)
        grad_gate = (grad_here * value[own, cols].astype(jnp.float32) * (1.0 - sig_f)).astype(
            jnp.bfloat16
        )
        slot = jnp.where(member == half, 0, 1)
        send_o[slot, :HALF] = dot_nn(git_s[send_rows], grad_value).astype(jnp.bfloat16)
        keep_o[slot, :HALF] = dot_nn(git_s[keep_rows], grad_value).astype(jnp.bfloat16)
        send_o[slot, HALF : 2 * HALF] = dot_nn(git_s[send_rows], grad_gate).astype(jnp.bfloat16)
        keep_o[slot, HALF : 2 * HALF] = dot_nn(git_s[keep_rows], grad_gate).astype(jnp.bfloat16)
        grad_norm = grad_norm + dot_nt(grad_value, wv_s[half]) + dot_nt(grad_gate, wg_s[half])
    unit, inv = row_stats(x_s[...])
    gain_glu_row = jnp.sum(grad_norm * unit, axis=0, keepdims=True)
    x_s[...] = grad_one[...] + norm_grad(grad_norm, unit, inv, gain_glu[...])
    scatter_rows(x_s, n_s, gin_o)
    tail = send_o.shape[1] - 2 * HALF
    both = jnp.concatenate(
        [gain_glu_row, gain_branch_row[...], jnp.zeros((14, 2 * HALF), jnp.float32)], axis=0
    )
    both = both.astype(jnp.bfloat16)
    for target in (send_o, keep_o):
        for shard in range(2):
            target[shard, 2 * HALF :] = jnp.zeros((tail, HALF), jnp.bfloat16)
            target[shard, 2 * HALF : 2 * HALF + 16] = both[:, :HALF]
            target[shard, 2 * HALF + 16 : 2 * HALF + 32] = both[:, HALF:]


def over_mp(values):
    return lax.ppermute(values, "mp", [(0, 1), (1, 0)])


def flat_pairs(dp_size, rule):
    pairs = []
    for dp_index in range(dp_size):
        for member in range(2):
            pair, core = dp_index // 2, dp_index % 2
            new_core, new_member = rule(core, member)
            pairs.append((dp_index * 2 + member, (pair * 2 + new_core) * 2 + new_member))
    return pairs


def unpack_kernel(layout, sizes, info, both, far, *rest):
    outs, packed, sems = rest[:-2], rest[-2], rest[-1]
    core, ybit, zpos = info[0], info[3], info[4]
    ys = both.shape[0]
    zs, step = (4, both.shape[3]) if len(both.shape) > 3 else (1, both.shape[1])
    loader = Loader(sems)
    for half in range(2):
        for yside in range(ys):
            for zside in range(zs):
                near, far_bit = zside // 2, zside % 2
                at = (yside ^ ybit, near ^ zpos % 2, far_bit ^ zpos // 2)
                if zs == 1:
                    spot = packed.at[half, pl.ds(yside * step, step)]
                    loader.either(both.at[at[0]], far.at[at[0]], half, spot)
                    continue
                first, base = 0, 0
                for size in sizes:
                    low = max(first, far_bit * step)
                    top = min(first + size // 2, (far_bit + 1) * step)
                    if low < top:
                        source = pl.ds(low - far_bit * step, top - low)
                        spot = base + yside * size + near * (size // 2) + low - first
                        loader.either(
                            both.at[at].at[source],
                            far.at[at].at[source],
                            half,
                            packed.at[half, pl.ds(spot, top - low)],
                        )
                    first += size // 2
                    base += 2 * size
    loader.go(core)
    loader.wait()
    layout(packed, outs)


def layout_ffn(packed, outs):
    w_in, w_back, w_out = outs
    blocks = w_in.shape[1] // HALF
    base = blocks * HALF
    for half in range(2):
        side = slice(half * HALF, (half + 1) * HALF)
        for block in range(blocks):
            at = block * HALF
            w_in[side, block * HALF : (block + 1) * HALF] = as_f32(packed[half, at : at + HALF])
        w_back[:, side] = as_f32(packed[half, base : base + w_back.shape[0]])
        last = base + w_back.shape[0]
        w_out[:, side] = as_f32(packed[half, last : last + w_out.shape[0]])


def layout_attn(packed, outs):
    w_qkv, w_point = outs
    for half in range(2):
        for index in range(3):
            at = index * HALF
            w_qkv[index, half * HALF : (half + 1) * HALF] = as_f32(packed[half, at : at + HALF])
        at = 3 * HALF
        w_point[half * 2 * HALF : (half + 1) * 2 * HALF] = as_f32(packed[half, at : at + 2 * HALF])


def layout_branch(packed, outs):
    w_left, w_right, taps, gain, late_ffn, late_attn = outs
    count = taps.shape[0]
    blocks = w_left.shape[1] // HALF
    base = blocks * HALF
    for half in range(2):
        side = slice(half * HALF, (half + 1) * HALF)
        for block in range(blocks):
            w_left[side, block * HALF : (block + 1) * HALF] = as_f32(
                packed[half, block * HALF : (block + 1) * HALF]
            )
        w_right[0, side] = as_f32(packed[half, base : base + HALF, :LANES])
        w_right[1, side] = as_f32(packed[half, base : base + HALF, LANES:])
        w_right[2, side] = as_f32(packed[half, base + HALF : base + 2 * HALF, :LANES])
        for piece in range(4):
            row = base + HALF + piece * 16
            at = half * 4 * LANES + piece * LANES
            rows = as_f32(packed[half, row : row + 16, LANES:])
            taps[:, at : at + LANES] = rows[:count]
            gain[:, at : at + LANES] = rows[count : count + 1]
            row += 4 * 16
            rows = as_f32(packed[half, row : row + 16, LANES:])
            late_ffn[:, piece * LANES : (piece + 1) * LANES] = rows[:1]
            late_attn[:, piece * LANES : (piece + 1) * LANES] = rows[1:2]


def layout_glu(packed, outs):
    w_value, w_gate, late_glu, late_branch = outs
    for half in range(2):
        side = slice(half * HALF, (half + 1) * HALF)
        w_value[side] = as_f32(packed[half, :HALF])
        w_gate[side] = as_f32(packed[half, HALF : 2 * HALF])
        rows = as_f32(packed[0, 2 * HALF + 16 * half : 2 * HALF + 16 * (half + 1)])
        late_glu[:, side] = rows[:1]
        late_branch[:, side] = rows[1:2]


MEGA = 1024 * 1024
SPARE = 8
ALL_VMEM = 62 * MEGA


def call(body, name, ins, outs, scratch, flops, copies=0, room=None, cost=10**11):
    spaces = {"s": pltpu.SMEM, "v": pltpu.VMEM, "h": pltpu.HBM}
    shapes = [jax.ShapeDtypeStruct(shape, dtype) for shape, dtype in outs]
    held = [(a.shape, a.dtype) for a, place in ins if place == "v"] + outs + scratch
    held = sum(math.prod(shape) * jnp.dtype(dtype).itemsize for shape, dtype in held)
    scratch = [pltpu.VMEM(shape, dtype) for shape, dtype in scratch]
    if copies:
        scratch.append(pltpu.SemaphoreType.DMA((copies,)))
    return pl.pallas_call(
        body,
        out_shape=shapes,
        in_specs=[pl.BlockSpec(memory_space=spaces[place]) for _, place in ins],
        out_specs=[pl.BlockSpec(memory_space=pltpu.VMEM) for _ in shapes],
        scratch_shapes=scratch,
        name=name,
        compiler_params=pltpu.CompilerParams(vmem_limit_bytes=room or held + SPARE * MEGA),
        cost_estimate=pl.CostEstimate(flops=cost, bytes_accessed=10**6, transcendentals=0),
    )(*[array for array, _ in ins])


def dp_xor(values, bits):
    size = lax.axis_size("dp")
    return lax.ppermute(values, "dp", [(index, index ^ bits) for index in range(size)])


def over_x_and_y(values):
    pairs = []
    for dp_index in range(lax.axis_size("dp")):
        for member in range(2):
            pairs.append((dp_index * 2 + member, (dp_index ^ 2) * 2 + 1 - member))
    return lax.ppermute(values, ("dp", "mp"), pairs)


def later(values, *first):
    return lax.optimization_barrier((values, first))[0]


class Sums:
    def __init__(self, send, keep, ybit):
        self.keep, self.ybit = keep, ybit
        self.recv = dp_xor(send, 1)

    def over_xy(self, *first):
        recv, keep = later((self.recv, self.keep), *first)
        half = keep.shape[1] // 2

        def piece(shard, bit):
            at = bit * half
            cut = lambda values: as_f32(lax.dynamic_slice_in_dim(values[shard], at, half, axis=0))
            return (cut(keep) + cut(recv)).astype(jnp.bfloat16)

        self.kept = piece(0, self.ybit)
        gone = [piece(1, self.ybit), piece(0, 1 - self.ybit), piece(1, 1 - self.ybit)]
        self.got = [over_mp(gone[0]), dp_xor(gone[1], 2), over_x_and_y(gone[2])]
        return gone

    def over_x(self, *first):
        recv, keep = later((self.recv, self.keep), *first)
        other = (as_f32(keep[1]) + as_f32(recv[1])).astype(jnp.bfloat16)
        self.kept = as_f32(keep[0]) + as_f32(recv[0])
        self.got = over_mp(other)
        return [other]

    def over_y(self, *first):
        got, kept = later((self.got, self.kept), *first)
        mine = (kept + as_f32(got)).astype(jnp.bfloat16)
        half = mine.shape[0] // 2
        gone = lax.dynamic_slice_in_dim(mine, (1 - self.ybit) * half, half, axis=0)
        self.kept = lax.dynamic_slice_in_dim(mine, self.ybit * half, half, axis=0)
        self.got = dp_xor(gone, 2)
        return [gone]

    def last_quarter(self, *first):
        got, kept = later((self.got, self.kept), *first)
        return (as_f32(kept) + as_f32(got)).astype(jnp.bfloat16)

    def quarter(self, *first):
        got, kept = later((self.got, self.kept), *first)
        total = as_f32(kept) + as_f32(got[1]) + (as_f32(got[0]) + as_f32(got[2]))
        return total.astype(jnp.bfloat16)


def halve(mine, bit, across):
    half = mine.shape[0] // 2
    kept = lax.dynamic_slice_in_dim(mine, bit * half, half, axis=0)
    gone = lax.dynamic_slice_in_dim(mine, (1 - bit) * half, half, axis=0)
    return gone, (kept, dp_xor(gone, across))


class Rest:
    def __init__(self, zpos):
        self.zpos, self.pairs, self.sizes = zpos, [], []

    def over_z1(self, quarter):
        gone, pair = halve(quarter, self.zpos % 2, 4)
        self.pairs.append(pair)
        self.sizes.append(quarter.shape[0])
        return [gone]

    def over_z2(self, *first):
        pairs = later(self.pairs, *first)
        mine = [(as_f32(kept) + as_f32(got)).astype(jnp.bfloat16) for kept, got in pairs]
        gone, (self.kept, self.got) = halve(jnp.concatenate(mine, axis=0), self.zpos // 2, 8)
        return [gone]

    def back_z2(self, *first):
        got, kept = later((self.got, self.kept), *first)
        self.mine = (as_f32(kept) + as_f32(got)).astype(jnp.bfloat16)
        self.got = dp_xor(self.mine, 8)
        return [self.mine]

    def back_z1(self, *first):
        return self.double(4, *first)

    def double(self, across, *first):
        got, mine = later((self.got, self.mine), *first)
        self.mine = jnp.stack([mine, got])
        self.got = dp_xor(self.mine, across)
        return [self.mine]

    def back_y(self, *first):
        return self.double(2, *first)

    def back_core(self, *first):
        self.got, mine = later((self.got, self.mine), *first)
        self.both = jnp.stack([mine, self.got])
        self.far = dp_xor(self.both, 1)
        return [self.both]


class Short(Rest):
    def along_z1(self, quarter):
        self.sizes.append(quarter.shape[0])
        self.mine, self.got = quarter, dp_xor(quarter, 4)
        return [quarter]

    def along_z2(self, *first):
        got, mine = later((self.got, self.mine), *first)
        self.mine = (as_f32(mine) + as_f32(got)).astype(jnp.bfloat16)
        self.got = dp_xor(self.mine, 8)
        return [self.mine]

    def back_y(self, *first):
        got, mine = later((self.got, self.mine), *first)
        self.mine = (as_f32(mine) + as_f32(got)).astype(jnp.bfloat16)
        self.got = dp_xor(self.mine, 2)
        return [self.mine]


def unpack(layout, info, sums, outs):
    ys, cols = 2, sums.both.shape[-1]
    zs, part = (4, sums.both.shape[3]) if sums.both.ndim > 3 else (1, sums.both.shape[1])
    return call(
        functools.partial(unpack_kernel, layout, sums.sizes),
        "unpack_" + layout.__name__,
        [(info, "s"), (sums.both, "h"), (sums.far, "h")],
        [(shape, jnp.float32) for shape in outs],
        [((2, ys * zs * part, cols), jnp.bfloat16)],
        1e6,
        4 * ys * (zs + len(sums.sizes)),
    )


def paired(
    inputs, lengths, gain_glu, w_value, w_gate, gain_branch, w_left, w_right, gain_mid, w_depth,
    w_point, gain_attn, w_qkv, w_out, gain_ffn, w_in, w_back, cotangent,
):
    low, full = jnp.bfloat16, jnp.float32
    member = lax.axis_index("mp")
    place = lax.axis_index("dp")
    core, ybit, zpos = place % 2, (place // 2) % 2, place // 4
    rows, width = inputs.shape[1:]
    ext = rows + 2 * EDGE
    inner = 2 * w_left.shape[1]
    chunks = inner // HALF
    right_cols = 2 * w_right.shape[2]
    sep_width = w_point.shape[1]
    heads = 2 * w_qkv.shape[2] // HEAD_DIM
    row = lambda gain: gain.reshape(1, -1)

    block = inputs[0]
    edge = jnp.where(member == 0, block[rows - EDGE :], block[:EDGE])
    size_code = jnp.stack([lengths[0] // 32, lengths[0] % 32]).astype(low)
    code_rows = jnp.broadcast_to(jnp.repeat(size_code, EDGE // 2)[:, None], (EDGE, width))
    edge = jnp.concatenate([edge, code_rows], axis=0)
    edge = lax.ppermute(
        edge, ("dp", "mp"), flat_pairs(lax.axis_size("dp"), lambda c, m: (1 - m, c))
    )
    code = as_f32(edge[EDGE:, 0])
    length = (code[0] * 32 + code[EDGE // 2]).astype(jnp.int32)
    edge = edge[:EDGE]
    swap = [p for p in flat_pairs(lax.axis_size("dp"), lambda c, m: (m, c)) if p[0] != p[1]]
    moved = lax.ppermute(block, ("dp", "mp"), swap)
    info = jnp.stack([core, member, length, ybit, zpos]).astype(jnp.int32)

    v = lambda *arrays: [(array, "v") for array in arrays]
    h = lambda *arrays: [(array, "h") for array in arrays]
    pack = jnp.concatenate([w_depth, gain_mid[None]], axis=0)
    got0 = over_mp(jnp.where(core == 0, w_value, w_gate))
    blocks = w_left.shape[1] // HALF
    bundle1, bundle2, bundle3 = call(
        bundle_kernel, "bundle",
        [(jnp.stack([core, member]).astype(jnp.int32), "s")]
        + h(w_left, w_right, w_point) + v(w_depth, row(gain_mid)) + h(w_qkv, w_out, w_in, w_back),
        [((blocks * (width + 16), HALF), low)] + [((3 * width, HALF), low)] * 2,
        [], 1, 16, ALL_VMEM,
    )
    got1 = over_mp(bundle1)
    part0 = dp_xor(got0, 1)
    cot = cotangent[0]
    cot_moved = lax.ppermute(cot, ("dp", "mp"), swap)

    where = [(info, "s")]
    macs = 2.0 * rows * width
    cot, resid_one, branch_in, glu_in, value, sig = call(
        glu_kernel, "glu",
        where + v(block, moved, cot, cot_moved, edge, row(gain_glu), row(gain_branch))
        + h(w_value, w_gate, got0, part0),
        [((rows, width), low), ((ext, width), full)] + [((ext, width), low)] * 4,
        [((ext, width), full), ((rows, width), full), ((width // LANES, rows, LANES), full)]
        + [((2,) + w_value.shape, low)] * 2,
        macs * width * 2, 8,
    )
    left_own, right_own, mid_own, sums_own = call(
        branch_own_kernel, "branch_own",
        where + v(branch_in) + h(w_left) + v(w_right),
        [
            ((chunks // 2, ext, HALF), low), ((ext, right_cols // 2), full),
            ((chunks // 2, ext, HALF), full), ((2, ext, LANES), full),
        ],
        [((chunks // 2, width, HALF), low)],
        1, chunks // 2,
    )
    got1 = later(got1, sums_own)
    part1 = dp_xor(got1, 1)
    got2 = over_mp(later(bundle2, got1))
    got3 = over_mp(later(bundle3, got1))
    resid_two, left_pre, right_pre, stats, depth = call(
        branch_kernel, "branch",
        where
        + v(branch_in, resid_one, pack, left_own, right_own, mid_own, sums_own)
        + h(w_point, got1, part1),
        [
            ((rows, width), full), ((chunks, ext, HALF), low), ((ext, right_cols), full),
            ((ext, LANES), full), ((chunks, rows, HALF), low),
        ],
        [
            ((chunks // 2, width, HALF), low), (w_right.shape, low), ((2,) + w_point.shape, low),
            ((4, 16, HALF), low), ((16, inner), full), ((chunks, ext, HALF), full),
            ((rows + 64, HALF), full), ((2, ext, LANES), full), ((rows, sep_width), full),
        ],
        1, 20,
    )
    got2 = later(got2, resid_two)
    part2 = dp_xor(got2, 1)
    attn_in, kv_own = call(
        kv_kernel, "keys_values",
        where + v(resid_two, row(gain_attn)) + h(w_qkv, got2, part2),
        [((rows, width), low), ((rows, 2 * width), low)],
        [((2, 2) + w_qkv.shape[1:], low)],
        macs * width * 2, 8,
    )
    (queries,) = call(
        query_kernel, "queries",
        where + v(attn_in) + h(w_qkv, got2, part2),
        [((rows, width), low)],
        [((2, 1) + w_qkv.shape[1:], low)],
        macs * width, 4,
    )
    kv_far = dp_xor(kv_own, 1)
    context0, lse0, context1, lse1 = call(
        attend_kernel, "attend",
        where + v(queries, kv_own, kv_far),
        [((rows, width // 2), low), ((heads // 2, rows), full)] * 2,
        [((2 * rows, LANES), full)],
        macs * 8000,
    )
    part3 = dp_xor(later(got3, lse1), 1)
    r_ffn = 2 * w_in.shape[1] + w_out.shape[0]
    out_rows, grad_three, grad_ctx, ggain_ffn, send, keep = call(
        ffn_kernel, "ffn",
        where + v(resid_two, context0, context1, cot, row(gain_ffn))
        + h(w_out, w_in, w_back, got2, part2, got3, part3),
        [
            ((rows, width), low), ((rows, width), full), ((rows, width), low), ((1, width), full),
            ((2, r_ffn, HALF), low), ((2, r_ffn, HALF), low),
        ],
        [
            ((2,) + w_out.shape, low), ((chunks, width, HALF), low), ((2,) + w_back.shape, low),
            ((rows, width), low), ((width, rows), low), ((rows, width), low), ((rows, width), full),
            ((rows, width), full), ((width, rows), low), ((width // LANES, rows, LANES), full),
        ],
        macs * 16000, 24, 38 * MEGA,
    )
    ffn_sums = Sums(send, keep, ybit)
    swapped_out = lax.ppermute(out_rows, ("dp", "mp"), swap)

    seen = v(context0, context1, grad_ctx, lse0, lse1)
    grad_q, grad_far = call(
        functools.partial(attend_back_kernel, 1), "attend_back_far",
        where + v(queries, kv_far) + seen,
        [((rows, width), full), ((rows, 2 * width), low)],
        [((rows, LANES), full)] * 3, 1,
    )
    recv = dp_xor(grad_far, 1)
    sent = ffn_sums.over_xy(grad_q)
    out_rows, swapped_out = later((out_rows, swapped_out), *sent)
    outputs = jnp.where(member == core, out_rows, swapped_out)
    sent.append(outputs)
    grad_q, grad_own = call(
        functools.partial(attend_back_kernel, 0), "attend_back_own",
        [(later(info, *sent), "s")] + v(queries, kv_own) + seen + v(grad_q),
        [((rows, width), low), ((rows, 2 * width), full)],
        [((rows, LANES), full)] * 3, 1,
    )
    grad_two, grad_sep, sep_edge, ggain_attn, send, keep = call(
        qkv_back_kernel, "qkv_back",
        where
        + v(grad_q, grad_own, recv, attn_in, resid_two, grad_three, row(gain_attn))
        + h(w_qkv, got2, part2),
        [
            ((rows, width), full), ((rows, sep_width), low), ((EDGE, sep_width), low),
            ((1, width), full),
        ]
        + [((2, 3 * HALF, HALF), low)] * 2,
        [
            ((2,) + w_qkv.shape, low), ((width, rows), low),
            ((sep_width // LANES, rows, LANES), full),
        ],
        1, 12,
    )
    sep_edge = dp_xor(sep_edge, 1)
    send, keep = call(
        point_kernel, "point_back",
        where + v(grad_sep, depth, send, keep),
        [((2, 5 * HALF, HALF), low)] * 2, [], macs * 1000,
    )
    attn_sums = Sums(send, keep, ybit)
    unit, scaled, mid_sums, small = call(
        depth_back_kernel, "depth_back",
        where
        + v(grad_sep, sep_edge, left_pre, right_pre, stats, pack)
        + h(w_point, got1, part1),
        [
            ((chunks, ext, HALF), low), ((chunks, ext, HALF), low), ((2, ext, LANES), full),
            ((16, inner), full),
        ],
        [
            ((2,) + w_point.shape, low), ((4, 16, HALF), low), ((16, inner), full),
            ((ext, sep_width), low),
            ((2, rows + 64, LANES), full), ((2, rows + 64, LANES), full),
            ((2, 4 * EDGE, LANES), full), ((ext, HALF), full), ((ext, HALF), full),
            ((3, ext, LANES), full),
        ],
        macs * 8000, 8,
    )
    ffn_rest = Rest(zpos)
    sent = ffn_rest.over_z1(ffn_sums.quarter(mid_sums))
    sent += attn_sums.over_x(*sent)
    r_branch = inner // 2 + 2 * HALF
    grad_left, grad_right, send, keep = call(
        branch_back_kernel, "branch_back",
        [(later(info, *sent), "s")]
        + v(
            unit, scaled, mid_sums, small, left_pre, right_pre, stats, branch_in, ggain_ffn,
            ggain_attn,
        ),
        [
            ((chunks, rows, HALF), low), ((ext, right_cols), low),
            ((2, r_branch, HALF), low), ((2, r_branch, HALF), low),
        ],
        [((3, ext, LANES), full), ((ext, right_cols), full), ((width, ext), low)],
        macs * 4000,
    )
    branch_sums = Sums(send, keep, ybit)
    sent = ffn_rest.over_z2(grad_left)
    sent += attn_sums.over_y(*sent)
    grad_one, ggain_branch = call(
        join_back_kernel, "join_back",
        [(later(info, *sent), "s")]
        + v(grad_left, grad_right, resid_one, grad_two, row(gain_branch))
        + h(w_left, w_right, got1, part1),
        [((rows, width), full), ((1, width), full)],
        [((chunks, width, HALF), low), ((2,) + w_right.shape, low)],
        macs * 4000, 12,
    )
    sent = ffn_rest.back_z2(grad_one)
    sent += branch_sums.over_xy(*sent)
    attn_rest = Rest(zpos)
    grad_in, send, keep = call(
        glu_back_kernel, "glu_back",
        [(later(info, *sent), "s")]
        + v(grad_one, ggain_branch, row(gain_glu), block, moved, glu_in, value, sig)
        + h(w_value, w_gate, got0, part0),
        [((rows, width), low), ((2, 640, HALF), low), ((2, 640, HALF), low)],
        [
            ((2,) + w_value.shape, low), ((2,) + w_gate.shape, low), ((rows, width), full),
            ((width // LANES, rows, LANES), full), ((width, rows), low),
        ],
        macs * 3000, 4,
    )
    glu_sums = Sums(send, keep, ybit)
    branch_rest, glu_rest = Rest(zpos), Short(zpos)
    sent = attn_rest.over_z1(attn_sums.last_quarter(grad_in))
    sent = ffn_rest.back_z1(*sent)
    sent = branch_rest.over_z1(branch_sums.quarter(*sent))
    sent = glu_sums.over_x(*sent)
    swapped_in = lax.ppermute(later(grad_in, *sent), ("dp", "mp"), swap)
    sent = attn_rest.over_z2(*sent)
    sent = branch_rest.over_z2(*sent)
    sent = glu_sums.over_y(*sent)
    sent = ffn_rest.back_y(*sent)
    sent = attn_rest.back_z2(*sent)
    sent = branch_rest.back_z2(*sent)
    sent = glu_rest.along_z1(glu_sums.last_quarter(*sent))
    grad_in, swapped_in = later((grad_in, swapped_in), *sent)
    grad_inputs = jnp.where(member == core, grad_in, swapped_in)
    sent = branch_rest.back_z1(grad_inputs)
    sent = glu_rest.along_z2(*sent)
    sent = branch_rest.back_y(*sent)
    sent = attn_rest.back_z1(*sent)
    sent = ffn_rest.back_core(*sent)
    sent = glu_rest.back_y(*sent)
    sent = attn_rest.back_y(*sent)
    sent = branch_rest.back_core(*sent)
    g_left, g_right, g_taps, g_mid, g_ffn_gain, g_attn_gain = unpack(
        layout_branch, later(info, *sent), branch_rest,
        [
            w_left.shape, w_right.shape, w_depth.shape, (1, inner // 2), (1, width), (1, width),
        ],
    )
    sent = glu_rest.back_core(g_left)
    g_in, g_back, g_out = unpack(
        layout_ffn, later(info, *sent), ffn_rest, [w_in.shape, w_back.shape, w_out.shape]
    )
    sent = attn_rest.back_core(g_in)
    g_value, g_gate, g_glu_gain, g_branch_gain = unpack(
        layout_glu, later(info, *sent), glu_rest,
        [w_value.shape, w_gate.shape, (1, width), (1, width)],
    )
    g_qkv, g_point = unpack(
        layout_attn, later(info, g_value), attn_rest, [w_qkv.shape, w_point.shape]
    )
    flat = lambda gain: gain.reshape(-1)
    return (
        outputs[None],
        grad_inputs[None],
        flat(g_glu_gain),
        g_value,
        g_gate,
        flat(g_branch_gain),
        g_left,
        g_right,
        flat(g_mid),
        g_taps,
        g_point,
        flat(g_attn_gain),
        g_qkv,
        g_out,
        flat(g_ffn_gain),
        g_in,
        g_back,
    )


def solution(mesh):
    placed = (
        P("dp", "mp", None),
        P("dp"),
        P(),
        P(None, "mp"),
        P(None, "mp"),
        P(),
        P(None, "mp"),
        P(None, None, "mp"),
        P("mp"),
        P(None, "mp"),
        P("mp", None),
        P(),
        P(None, None, "mp"),
        P("mp", None),
        P(),
        P(None, "mp"),
        P("mp", None),
        P("dp", "mp", None),
    )
    fast = mesh.shape["mp"] == 2 and mesh.shape["dp"] == 16
    return jax.shard_map(
        paired if fast else local,
        mesh=mesh,
        in_specs=placed,
        out_specs=(
            P("dp", "mp", None),
            P("dp", "mp", None),
            P(),
            P(None, "mp"),
            P(None, "mp"),
            P(),
            P(None, "mp"),
            P(None, None, "mp"),
            P("mp"),
            P(None, "mp"),
            P("mp", None),
            P(),
            P(None, None, "mp"),
            P("mp", None),
            P(),
            P(None, "mp"),
            P("mp", None),
        ),
        check_vma=False,
    )
```
